32 devices in a mesh: dp: 16 (over z, y, x), mp: 2 (over core).
Axes of the slice: x: 2, y: 2, z: 4, core: 2. Of those that a mesh axis runs over, the one named last changes fastest.
Arguments:
- mel_frames: bfloat16 [16384, 1024], P('dp'), may hold values from -6 to 6
- text_features: bfloat16 [16384, 512], P('dp'), may hold values from -6 to 6
- cotangent: bfloat16 [16384, 1024], P('dp'), may hold values from -6 to 6
- time_embedding: bfloat16 [8, 1024], replicated, may hold values from -6 to 6
- lengths: int32 [16], P('dp'), may hold values from 256 to 1024, as said below
- group_ids: int32 [16], P('dp'), may hold values from 0 to 7
- text_keep: int32 [16384], P('dp'), may hold values 0 or 1
- owner_list: int32 [16], replicated, may hold values from 0 to 15, each once
- soap_master: float32 [8192, 1024], P('dp', 'mp'), may hold values from -0.1875 to 0.1875
- soap_first: float32 [8192, 1024], P('dp', 'mp'), may hold values from -2.16 to 2.16
- soap_second: float32 [8192, 1024], P('dp', 'mp'), may hold values from 0.064 to 0.9344, as said below
- left_basis: float32 [8192, 1024], P('dp', 'mp'), may hold values from -1 to 1, as said below
- right_basis: float32 [8192, 1024], P('dp', 'mp'), may hold values from -1 to 1, as said below
- text_matrices: float32 [1536, 1024], P('dp'), may hold values from -0.25 to 0.25
- text_first: float32 [1536, 1024], P('dp'), may hold values from -4 to 4
- text_second: float32 [1536, 1024], P('dp'), may hold values from 0.32 to 1.28
- modulation_weight: float32 [1024, 6144], P('dp'), may hold values from -0.1875 to 0.1875
- modulation_first: float32 [1024, 6144], P('dp'), may hold values from -4 to 4
- modulation_second: float32 [1024, 6144], P('dp'), may hold values from 0.0576 to 0.2304
- vectors: float32 [14848], replicated, may hold values from -2 to 2
- vector_first: float32 [14848], replicated, may hold values from -4 to 4
- vector_second: float32 [14848], replicated, may hold values from 0.16 to 0.64
Outputs:
- block_output: bfloat16 [16384, 1024], P('dp')
- mel_gradient: float32 [16384, 1024], P('dp')
- text_gradient: float32 [16384, 512], P('dp')
- soap_weights: float32 [8192, 1024], P('dp', 'mp')
- soap_moment: float32 [8192, 1024], P('dp', 'mp')
- soap_variance: float32 [8192, 1024], P('dp', 'mp')
- text_weights: float32 [1536, 1024], P('dp')
- text_moment: float32 [1536, 1024], P('dp')
- text_variance: float32 [1536, 1024], P('dp')
- modulation_weights: float32 [1024, 6144], P('dp')
- modulation_moment: float32 [1024, 6144], P('dp')
- modulation_variance: float32 [1024, 6144], P('dp')
- vector_weights: float32 [14848], replicated
- vector_moment: float32 [14848], replicated
- vector_variance: float32 [14848], replicated
The draws below stay inside these ranges and needn't reach their ends.
Inputs may be any that keep to these rules, and one draw needn't show every extreme that they name: Utterance u has valid audio frames 0 to lengths[u] - 1; some utterance has 1024, some has 256. `owner_list`: every index of dp appears once. `soap_second`: entries are positive. `left_basis`: each block of 512 rows and 512 columns is an orthogonal matrix. `right_basis`: each block of 512 rows and 512 columns is an orthogonal matrix.
All inputs are finite; a program needn't handle non-finite values. No bound on the sum of `text_keep` on one device may be relied on, other than what follows from the above.
Results may differ from the reference program's by a relative error of at most 0.013.
The reference program's roundings to bfloat16 on the way count: a program that leaves them out, or rounds other values in their place, can miss the bound.
Values may be sent and summed in bfloat16 or wider, within the bound.
No kernel may reach another device: no remote copies, remote signals or barrier semaphores. Data moves between devices by JAX's collectives and lax.ppermute only.
A program may use at most 256 MiB of HBM per device.

```python
import math
import jax
import jax.numpy as jnp
from jax import lax

D = 1024
HEADS = 16
HEAD = 64
FF = 2048
TEXT = 512
TXT_FF = 1024
KERNEL = 7
LEN = 1024
GROUPS = 8
STEP = 10
WIDE = 512
STACK = 8192
PANEL = 512
UTTS = 16
TOKENS = 16384
NVEC = 14848
N_DP = 16
N_MP = 2


gradient_levels = [0.58, 0.58, 0.32, 0.58, 0.38, 0.38, 0.6, 0.6]


def block_factors(levels):
    row_block = jnp.arange(STACK) // D
    return jnp.asarray(levels, jnp.float32)[row_block][:, None]


def draw_lengths(key, part):
    key = jax.random.fold_in(key, 17)
    position = jnp.arange(UTTS)
    shortest = LEN // 3
    centre = shortest + (LEN - shortest) * position // max(UTTS - 1, 1)
    lowest = centre * 4 // 5
    drawn = jax.random.randint(key, (UTTS,), lowest, centre + 1)
    drawn = jnp.where(position == 0, LEN // 4, drawn)
    return jnp.where(position == UTTS - 1, LEN, drawn).astype(jnp.int32)


def draw_soap_master(key, part):
    key = jax.random.fold_in(key, 11)
    normal_draw = jax.random.truncated_normal(key, -4.0, 4.0, (STACK, D), jnp.float32)
    units_level = math.sqrt(D / FF)
    factors = block_factors([1.0, 1.0, 1.0, 1.5, 1.0, 1.0, units_level, units_level])
    return normal_draw * factors / math.sqrt(D)


def draw_soap_first(key, part):
    key = jax.random.fold_in(key, 12)
    normal_draw = jax.random.truncated_normal(key, -4.0, 4.0, (STACK, D), jnp.float32)
    return normal_draw * block_factors(gradient_levels) * (0.111 * math.sqrt(TOKENS) / UTTS)


def draw_soap_second(key, part):
    key = jax.random.fold_in(key, 13)
    spread = jax.random.uniform(key, (STACK, D), jnp.float32, 0.0, math.log(4.0))
    level_rows = block_factors(gradient_levels) ** 2 * (0.0101 * TOKENS / (UTTS * UTTS))
    return level_rows * jnp.exp(spread)


def orthogonal_blocks(key, row_blocks, col_blocks, block_size):
    sign_key, angle_key = jax.random.split(key)
    row_index = jnp.arange(block_size, dtype=jnp.float32)[:, None]
    col_index = jnp.arange(block_size, dtype=jnp.float32)[None, :]
    cosine_basis = jnp.cos(math.pi * (col_index + 0.5) * row_index / block_size) * math.sqrt(2.0 / block_size)
    cosine_basis = jnp.where(row_index == 0.0, cosine_basis / math.sqrt(2.0), cosine_basis)
    row_signs = 2.0 * jax.random.randint(sign_key, (row_blocks, col_blocks, block_size, 1), 0, 2).astype(jnp.float32) - 1.0
    angles = jax.random.uniform(angle_key, (row_blocks, col_blocks, 1, block_size // 2), jnp.float32, -math.pi, math.pi)
    signed = cosine_basis[None, None] * row_signs
    half_order = block_size // 2
    front_cols = signed[..., :half_order]
    back_cols = signed[..., half_order:]
    turned = jnp.concatenate([jnp.cos(angles) * front_cols + jnp.sin(angles) * back_cols, jnp.cos(angles) * back_cols - jnp.sin(angles) * front_cols], axis=-1)
    return turned.transpose(0, 2, 1, 3).reshape(row_blocks * block_size, col_blocks * block_size)


def draw_left_basis(key, part):
    key = jax.random.fold_in(key, 14)
    return orthogonal_blocks(key, STACK // PANEL, D // WIDE, PANEL)


def draw_right_basis(key, part):
    key = jax.random.fold_in(key, 15)
    return orthogonal_blocks(key, STACK // PANEL, D // WIDE, WIDE)


def draw_vectors(key, part):
    key = jax.random.fold_in(key, 16)
    normal_draw = jax.random.truncated_normal(key, -4.0, 4.0, (NVEC,), jnp.float32)
    position = jnp.arange(NVEC)
    kernel_end = KERNEL * TEXT
    gain_start = kernel_end + TEXT
    gain_end = gain_start + TEXT
    gamma_start = kernel_end + 4 * TEXT + TXT_FF
    gamma_end = gamma_start + TXT_FF
    spread_rows = jnp.where(position < kernel_end, 0.4, 0.3)
    spread_rows = jnp.where((position >= gamma_start) & (position < gamma_end), 0.5, spread_rows)
    values = normal_draw * spread_rows
    is_gain = (position >= gain_start) & (position < gain_end)
    return jnp.where(is_gain, 1.0 + 0.15 * normal_draw, values)


def touch_ends(values, rng, least, top_value):
    spot = [jax.random.randint(jax.random.fold_in(rng, axis), (), 0, length) for axis, length in enumerate(values.shape)]
    widest = values.shape.index(max(values.shape))
    next_to = spot[:widest] + [(spot[widest] + 1) % values.shape[widest]] + spot[widest + 1:]
    return values.at[tuple(spot)].set(least).at[tuple(next_to)].set(top_value)


def level_of(key, dims, shards, smallest, high):
    gain, own = 1.0, jax.random.fold_in(key, 6)
    for dim, parts in shards:
        steps = jnp.exp(jax.random.uniform(jax.random.fold_in(own, dim), (parts,), jnp.float32, smallest / len(shards), high / len(shards)))
        gain = gain * jnp.repeat(steps, dims[dim] // parts).reshape([-1 if axis == dim else 1 for axis in range(len(dims))])
    return gain


def centred(key, shape, deviation, most, shards=(), held_as=jnp.bfloat16):
    values = deviation * jax.random.normal(key, shape, jnp.float32)
    if shards:
        values = values * level_of(key, shape, shards, -0.22, 0.18)
    return jnp.clip(values, -most, most).astype(held_as)


def setup_inputs(seed: int = 0) -> dict:
    seeds = jax.random.split(jax.random.key(seed), 23)
    return {
        "mel_frames": centred(seeds[0], (TOKENS, D), 1.0, 6.0, ((0, 16),)),
        "text_features": centred(seeds[1], (TOKENS, TEXT), 1.0, 6.0, ((0, 16),)),
        "cotangent": centred(seeds[2], (TOKENS, D), 1.0, 6.0, ((0, 16),)),
        "time_embedding": centred(seeds[3], (GROUPS, D), 1.0, 6.0),
        "lengths": draw_lengths(jax.random.fold_in(seeds[22], 71), 0),
        "group_ids": touch_ends(jax.random.randint(seeds[5], (UTTS,), 0, GROUPS), jax.random.fold_in(seeds[5], 1), 0, GROUPS - 1).astype(jnp.int32),
        "text_keep": touch_ends((jax.random.randint(seeds[6], (TOKENS,), 0, 4) < 3).astype(jnp.int32), jax.random.fold_in(seeds[6], 1), 0, 1),
        "owner_list": jax.random.permutation(seeds[7], N_DP).astype(jnp.int32),
        "soap_master": draw_soap_master(jax.random.fold_in(seeds[22], 71), 0),
        "soap_first": draw_soap_first(jax.random.fold_in(seeds[22], 71), 0),
        "soap_second": draw_soap_second(jax.random.fold_in(seeds[22], 71), 0),
        "left_basis": draw_left_basis(jax.random.fold_in(seeds[22], 71), 0),
        "right_basis": draw_right_basis(jax.random.fold_in(seeds[22], 71), 0),
        "text_matrices": centred(seeds[13], (3 * TEXT, D), TEXT ** -0.5, 0.25, ((0, 16),), jnp.float32),
        "text_first": centred(seeds[14], (3 * TEXT, D), (0.078 * TOKENS ** 0.5 / UTTS), 4.0, ((0, 16),), jnp.float32),
        "text_second": jnp.clip(jnp.exp(math.log(1.28) - 1.3862944 * jax.random.uniform(seeds[15], (3 * TEXT, D), jnp.float32) ** level_of(seeds[15], (3 * TEXT, D), ((0, 16),), -0.2, 0.2)), 0.32, 1.28),
        "modulation_weight": centred(seeds[16], (D, 6 * D), D ** -0.5, 0.1875, ((0, 16),), jnp.float32),
        "modulation_first": centred(seeds[17], (D, 6 * D), (0.033 * TOKENS ** 0.5 / UTTS), 4.0, ((0, 16),), jnp.float32),
        "modulation_second": jnp.clip(jnp.exp(math.log(0.2304) - 1.3862944 * jax.random.uniform(seeds[18], (D, 6 * D), jnp.float32) ** level_of(seeds[18], (D, 6 * D), ((0, 16),), -0.2, 0.2)), 0.0576, 0.2304),
        "vectors": draw_vectors(jax.random.fold_in(seeds[22], 71), 0),
        "vector_first": centred(seeds[20], (NVEC,), (0.055 * TOKENS ** 0.5 / UTTS), 4.0, (), jnp.float32),
        "vector_second": jnp.clip(jnp.exp(jax.random.uniform(seeds[21], (NVEC,), jnp.float32, math.log(0.16), math.log(0.64))), 0.16, 0.64),
    }


@jax.custom_vjp
def low(v):
    return lax.optimization_barrier(v.astype(jnp.bfloat16)).astype(jnp.float32)

@jax.custom_vjp
def low_back(v):
    return v

def low_keep(v):
    return (low(v), None)

def low_pass(kept, grad):
    return (grad,)

def back_keep(v):
    return (v, None)

def back_low(kept, grad):
    return (low(grad),)
low.defvjp(low_keep, low_pass)
low_back.defvjp(back_keep, back_low)
precise = lax.Precision.HIGHEST
beta_one = 0.9
beta_two = 0.99
adam_eps = 1e-08
weight_decay = 0.01
learn_rate = 0.03
vector_rate = 0.3

def matmul(left, right):
    return jnp.dot(left, right, precision=precise, preferred_element_type=jnp.float32)

def layer_norm(values):
    center = values - lax.optimization_barrier(jnp.mean(values, axis=-1, keepdims=True))
    variance = lax.optimization_barrier(jnp.mean(center * center, axis=-1, keepdims=True))
    return center * lax.rsqrt(variance + 1e-06)

def vector_parts(vectors):
    kernel_size = KERNEL * TEXT
    pieces = [vectors[:kernel_size].reshape(KERNEL, TEXT)]
    offset = kernel_size
    for extent in (TEXT, TEXT, TEXT, TEXT, TXT_FF, TXT_FF, TXT_FF, 6 * D):
        pieces.append(vectors[offset:offset + extent])
        offset = offset + extent
    return pieces

def text_norm(masked_text, kernel, conv_bias, norm_gain, norm_bias):
    margin = KERNEL // 2
    widths = [(0, 0)] * (masked_text.ndim - 2) + [(margin, margin), (0, 0)]
    padded = jnp.pad(masked_text, widths)
    length = masked_text.shape[-2]
    mixed_sum = conv_bias + padded[..., 0:length, :] * kernel[0]
    for offset in range(1, KERNEL):
        mixed_sum = mixed_sum + padded[..., offset:offset + length, :] * kernel[offset]
    return layer_norm(mixed_sum) * norm_gain + norm_bias

def gelu_grn(pre_act, grn_gamma, grn_beta):
    hidden = jax.nn.gelu(pre_act, approximate=False)
    energy = jnp.sqrt(lax.optimization_barrier(jnp.sum(hidden * hidden, axis=-2, keepdims=True)))
    normed = energy / (lax.optimization_barrier(jnp.mean(energy, axis=-1, keepdims=True)) + 1e-06)
    return grn_gamma * (hidden * normed) + grn_beta + hidden

def modulated(values, shift_part, scale_part):
    return layer_norm(values) * (1.0 + scale_part) + shift_part

def rotary_tables():
    position = jnp.arange(LEN, dtype=jnp.float32)
    frequency = 10000.0 ** (-jnp.arange(HEAD // 2, dtype=jnp.float32) * 2.0 / HEAD)
    angle = position[:, None] * frequency[None, :]
    return (jnp.cos(angle), jnp.sin(angle))

def rotary(values, cosine_table, sine_table):
    half_size = HEAD // 2
    front_half = values[..., :half_size]
    back_half = values[..., half_size:]
    cosine_rows = cosine_table[:, None, :]
    sine_rows = sine_table[:, None, :]
    return jnp.concatenate([front_half * cosine_rows - back_half * sine_rows, back_half * cosine_rows + front_half * sine_rows], axis=-1)

def moments(gradient, first_moment, second_moment):
    first_new = beta_one * first_moment + (1.0 - beta_one) * gradient
    second_new = beta_two * second_moment + (1.0 - beta_two) * gradient * gradient
    bias_first = 1.0 - beta_one ** STEP
    bias_second = 1.0 - beta_two ** STEP
    direction = first_new / bias_first / (jnp.sqrt(second_new / bias_second) + adam_eps)
    return (first_new, second_new, direction)

def apply_step(weight, direction, rate):
    return weight - rate * (direction + weight_decay * weight)

def make_forward(time_embedding, keep_mask, lengths, group_ids):
    cosine_table, sine_table = rotary_tables()
    block_rows = min(512, LEN)

    def forward(mel_frames, text_features, stacked, text_matrices, modulation_weight, vectors):
        kernel, conv_bias, norm_gain, norm_bias, out_bias, in_bias, grn_gamma, grn_beta, modulation_bias = vector_parts(vectors)
        blocks = low(stacked)
        texts = low(text_matrices)
        silu_time = low(jax.nn.silu(time_embedding))
        modulation = low_back(matmul(silu_time, low(modulation_weight))) + modulation_bias
        per_utterance = jnp.take(modulation, group_ids, axis=0)
        unit_first = jnp.concatenate([blocks[4], blocks[5]], axis=1)
        unit_second = jnp.concatenate([blocks[6], blocks[7]], axis=1)

        def utterance(carry_value, item):
            mel_row, text_row, keep_row, length_value, modulation_row = item
            masked_text = text_row * keep_row
            normed_text = text_norm(masked_text, kernel, conv_bias, norm_gain, norm_bias)
            pre_act = low_back(matmul(low(normed_text), texts[0:TEXT])) + in_bias
            grn_out = gelu_grn(pre_act, grn_gamma, grn_beta)
            shrink_out = low_back(matmul(low(grn_out), texts[TEXT:2 * TEXT].T)) + out_bias
            text_out = (masked_text + shrink_out) * keep_row
            stream = mel_row + low_back(matmul(low(text_out), texts[2 * TEXT:3 * TEXT]))
            mod_parts = modulation_row.reshape(6, D)
            normed_one = low(modulated(stream, mod_parts[0], mod_parts[1]))
            queries = low_back(matmul(normed_one, blocks[0])).reshape(LEN, HEADS, HEAD)
            key_rows = low_back(matmul(normed_one, blocks[1])).reshape(LEN, HEADS, HEAD)
            value_rows = low(low_back(matmul(normed_one, blocks[2]))).reshape(LEN, HEADS, HEAD)
            query_rot = low(rotary(queries, cosine_table, sine_table))
            key_rot = low(rotary(key_rows, cosine_table, sine_table))
            live_keys = jnp.arange(LEN) < length_value

            def attend(query_block):
                scores = low_back(jnp.einsum('qhd,khd->hqk', query_block, key_rot, precision=precise) * 0.125)
                scores = jnp.where(live_keys[None, None, :], scores, -1e+30)
                highest = lax.optimization_barrier(jnp.max(scores, axis=-1, keepdims=True))
                weights_exp = jnp.exp(scores - highest)
                probs_full = weights_exp / lax.optimization_barrier(jnp.sum(weights_exp, axis=-1, keepdims=True))
                return jnp.einsum('hqk,khd->qhd', low(probs_full), value_rows, precision=precise)
            attended = lax.map(jax.checkpoint(attend), query_rot.reshape(LEN // block_rows, block_rows, HEADS, HEAD))
            attended = low(low_back(attended.reshape(LEN, D)))
            attention_out = low_back(matmul(attended, blocks[3].T))
            stream_one = stream + mod_parts[2] * attention_out
            normed_two = low(modulated(stream_one, mod_parts[3], mod_parts[4]))
            hidden_pre = low_back(matmul(normed_two, unit_first))
            hidden_act = low(jax.nn.gelu(hidden_pre, approximate=True))
            unit_out = low_back(matmul(hidden_act, unit_second.T))
            return (carry_value, stream_one + mod_parts[5] * unit_out)
        items = (mel_frames.reshape(UTTS, LEN, D), text_features.reshape(UTTS, LEN, TEXT), keep_mask.reshape(UTTS, LEN, 1), lengths, per_utterance)
        unused, outputs = lax.scan(jax.checkpoint(utterance), jnp.zeros((), jnp.float32), items)
        return outputs.reshape(TOKENS, D)
    return forward

def quarter(array, rows_each, cols_each):
    return array.reshape(N_DP, rows_each, N_MP, cols_each).transpose(0, 2, 1, 3)

def unquarter(array):
    return array.transpose(0, 2, 1, 3).reshape(STACK, D)

def reference(mel_frames, text_features, cotangent, time_embedding, lengths, group_ids, text_keep, owner_list, soap_master, soap_first, soap_second, left_basis, right_basis, text_matrices, text_first, text_second, modulation_weight, modulation_first, modulation_second, vectors, vector_first, vector_second):
    slot_blocks = soap_master.reshape(N_DP, PANEL, D)
    stacked = jnp.take(slot_blocks, owner_list, axis=0).reshape(8, D, D)
    forward = make_forward(time_embedding.astype(jnp.float32), text_keep.astype(jnp.float32), lengths, group_ids)
    output, pullback = jax.vjp(forward, mel_frames.astype(jnp.float32), text_features.astype(jnp.float32), stacked, text_matrices, modulation_weight, vectors)
    mel_gradient, text_gradient, stack_grad, text_grad, modulation_grad, vector_grad = pullback(cotangent.astype(jnp.float32))
    stack_grad = stack_grad / UTTS
    text_grad = text_grad / UTTS
    modulation_grad = modulation_grad / UTTS
    vector_grad = vector_grad / UTTS
    slot_grad = jnp.zeros((N_DP, PANEL, D), jnp.float32).at[owner_list].set(stack_grad.reshape(N_DP, PANEL, D))
    grads_q = quarter(slot_grad.reshape(STACK, D), PANEL, WIDE)
    lefts = quarter(left_basis, PANEL, PANEL)
    rights = quarter(right_basis, WIDE, WIDE)
    rotated = jnp.einsum('smpa,smpw->smaw', lefts, grads_q, precision=precise)
    rotated = jnp.einsum('smaw,smwb->smab', rotated, rights, precision=precise)
    moment_q, variance_q, direction = moments(rotated, quarter(soap_first, PANEL, WIDE), quarter(soap_second, PANEL, WIDE))
    turned = jnp.einsum('smpa,smab->smpb', lefts, direction, precision=precise)
    turned = jnp.einsum('smpb,smwb->smpw', turned, rights, precision=precise)
    soap_weights = apply_step(soap_master, unquarter(turned), learn_rate)
    text_moment, text_variance, text_direction = moments(text_grad, text_first, text_second)
    text_weights = apply_step(text_matrices, text_direction, learn_rate)
    modulation_moment, modulation_variance, modulation_direction = moments(modulation_grad, modulation_first, modulation_second)
    modulation_weights = apply_step(modulation_weight, modulation_direction, learn_rate)
    vector_moment, vector_variance, vector_direction = moments(vector_grad, vector_first, vector_second)
    vector_weights = apply_step(vectors, vector_direction, vector_rate)
    return (output.astype(jnp.bfloat16), mel_gradient, text_gradient, soap_weights, unquarter(moment_q), unquarter(variance_q), text_weights, text_moment, text_variance, modulation_weights, modulation_moment, modulation_variance, vector_weights, vector_moment, vector_variance)
```

```python
import jax
import jax.numpy as jnp
from jax import lax
from jax.experimental import pallas as pl
from jax.experimental.pallas import tpu as pltpu
from jax.sharding import PartitionSpec as P

D = 1024
HEAD = 64
TEXT = 512
TXT_FF = 1024
KERNEL = 7
LEN = 1024
GROUPS = 8
STEP = 10

f32 = jnp.float32
bf16 = jnp.bfloat16
beta_one = 0.9
beta_two = 0.99
adam_eps = 1e-08
weight_decay = 0.01
learn_rate = 0.03
vector_rate = 0.3
norm_eps = 1e-06
solver = lax.Precision.HIGH


def swap_core(array):
    return lax.ppermute(array, "mp", [(0, 1), (1, 0)])


def swap_bit(array, bit):
    count = lax.axis_size("dp")
    return lax.ppermute(array, "dp", [(i, i ^ (1 << bit)) for i in range(count)])


def by_core(core, mine, other, axis=0):
    return jnp.where(
        core == 0,
        jnp.concatenate([mine, other], axis=axis),
        jnp.concatenate([other, mine], axis=axis),
    )


def bit_count(count):
    return count.bit_length() - 1


def third_cuts(rows):
    step = rows // 3
    if rows >= 48:
        step = (rows + 24) // 48 * 16
    return (0, step, 2 * step, rows)


axis_orders = ((0, 1, 2), (1, 2, 0), (2, 0, 1))


def tie(*values):
    return lax.optimization_barrier(values)


def spread_step(parts, phase):
    return [
        jnp.stack([part, swap_bit(part, axis_orders[index][phase])])
        for index, part in enumerate(parts)
    ]


def spread_close(parts):
    pieces = []
    for index, part in enumerate(parts):
        order = axis_orders[index]
        held = [order[2], order[1], order[0]]
        axes = [3] + [held.index(bit) for bit in (2, 1, 0)] + [4, 5]
        pieces.append(part.transpose(axes))
    return jnp.concatenate(pieces, axis=4)


def gather_relative(block):
    count = lax.axis_size("dp")
    rows, columns = block.shape
    held = block[None]
    for bit in range(4, bit_count(count)):
        held = jnp.concatenate([held, swap_bit(held, bit)], axis=0)
    cuts = third_cuts(rows)
    split = lambda array: [array[:, cuts[i] : cuts[i + 1]] for i in range(3)]
    far = swap_bit(held, 3)
    near_parts = spread_step(split(held), 0)
    near_parts = spread_step(list(tie(*near_parts)), 1)
    tied = tie(far, *near_parts)
    far, near_parts = tied[0], list(tied[1:])
    near_parts = spread_step(near_parts, 2)
    far_parts = spread_step(split(far), 0)
    tied = tie(*near_parts, *far_parts)
    near_parts, far_parts = list(tied[:3]), list(tied[3:])
    far_parts = spread_step(far_parts, 1)
    far_parts = spread_step(list(tie(*far_parts)), 2)
    near, far = spread_close(near_parts), spread_close(far_parts)
    return jnp.stack([near, far], axis=1).reshape(count, rows, columns)


def add_low(left, right):
    return (left.astype(f32) + right.astype(f32)).astype(bf16)


def fold_step(parts, held, phase):
    folded = []
    for index, part in enumerate(parts):
        bit = axis_orders[index][phase]
        axis = 1 + held[index].index(bit)
        keep = lax.index_in_dim(part, 0, axis, keepdims=False)
        send = lax.index_in_dim(part, 1, axis, keepdims=False)
        folded.append(add_low(keep, swap_bit(send, bit)))
        held[index].remove(bit)
    return folded


def scatter_relative(full):
    count, rows, columns = full.shape
    bits = bit_count(count)
    near, far = [
        full.reshape(count // 16, 2, 2, 2, 2, rows, columns)[:, i] for i in range(2)
    ]
    cuts = third_cuts(rows)
    split = lambda array: [array[..., cuts[i] : cuts[i + 1], :] for i in range(3)]
    near_parts, far_parts = split(near), split(far)
    near_held = [[2, 1, 0] for _ in range(3)]
    far_held = [[2, 1, 0] for _ in range(3)]
    far_parts = fold_step(far_parts, far_held, 2)
    far_parts = fold_step(list(tie(*far_parts)), far_held, 1)
    far_parts = fold_step(list(tie(*far_parts)), far_held, 0)
    near_parts = fold_step(near_parts, near_held, 2)
    tied = tie(*near_parts, *far_parts)
    near_parts, far_parts = list(tied[:3]), list(tied[3:])
    far_sum = swap_bit(jnp.concatenate(far_parts, axis=-2), 3)
    near_parts = fold_step(near_parts, near_held, 1)
    near_parts = fold_step(list(tie(*near_parts)), near_held, 0)
    near_sum = jnp.concatenate(near_parts, axis=-2)
    if bits == 4:
        return near_sum[0].astype(f32) + far_sum[0].astype(f32)
    total = add_low(near_sum, far_sum)
    for bit in range(bits - 1, 3, -1):
        half = 1 << (bit - 4)
        total = total[:half].astype(f32) + swap_bit(total[half:], bit).astype(f32)
        if bit > 4:
            total = total.astype(bf16)
    return total[0]


def sum_dp(array):
    for bit in range(bit_count(lax.axis_size("dp"))):
        array = array + swap_bit(array, bit)
    return array


NT = (((1,), (1,)), ((), ()))
NN = (((1,), (0,)), ((), ()))
ROWS = 256
PAIR = 2 * HEAD
vmem_bytes = 48 * 1024 * 1024


def dot32(left, right, dims=NN):
    return lax.dot_general(left, right, dims, preferred_element_type=f32)


def three_terms(values):
    high = values.astype(bf16).astype(f32)
    rest = values - high
    middle = rest.astype(bf16).astype(f32)
    return high, middle, rest - middle


def rotate(values, cosine, sine, lane):
    partner = jnp.where(
        lane % HEAD < HEAD // 2,
        pltpu.roll(values, PAIR - HEAD // 2, 1),
        pltpu.roll(values, HEAD // 2, 1),
    )
    return values * cosine + partner * sine


def attend_kernel(q_ref, k_ref, v_ref, cos_ref, sin_ref, bias_ref, o_ref, qa_ref, kr_ref):
    lane = lax.broadcasted_iota(jnp.int32, (LEN, PAIR), 1)
    lane_rows = lax.broadcasted_iota(jnp.int32, (ROWS, PAIR), 1)
    row_index = lax.broadcasted_iota(jnp.int32, (PAIR, ROWS), 0)
    cosine, sine = cos_ref[...], sin_ref[...]
    q_turned = (rotate(q_ref[...], cosine, sine, lane).astype(bf16).astype(f32) * 0.125)
    k_turned = rotate(k_ref[...], cosine, sine, lane).astype(bf16)
    kr_ref[...] = k_turned
    k_wide = k_turned.astype(f32)
    values_t = v_ref[...].T
    bias = bias_ref[...].astype(f32)
    keys = []
    for head in range(2):
        own = lane // HEAD == head
        spare = (1 - head) * HEAD
        keys.append(
            jnp.where(
                own, k_wide, jnp.where(lane == spare, bias, 0.0)
            ).astype(bf16)
        )
        qa_ref[:, head * PAIR : (head + 1) * PAIR] = jnp.where(
            own, q_turned, jnp.where(lane == spare, 1.0, 0.0)
        ).astype(bf16)
    for block in range(LEN // ROWS):
        rows = slice(block * ROWS, (block + 1) * ROWS)
        outs = []
        extra = jnp.zeros((PAIR, ROWS), f32)
        for head in range(2):
            spare = (1 - head) * HEAD
            q_block = qa_ref[rows, head * PAIR : (head + 1) * PAIR]
            scores = dot32(keys[head], q_block, NT)
            highest = jnp.max(scores, axis=0, keepdims=True)
            weights = jnp.exp(scores - highest)
            total = jnp.sum(weights, axis=0, keepdims=True)
            out_t = dot32(values_t[head * HEAD : (head + 1) * HEAD], weights.astype(bf16))
            outs.append(out_t / total)
            for place, term in enumerate(three_terms(highest + jnp.log(total))):
                extra = jnp.where(row_index == spare + 1 + place, -term, extra)
        o_ref[rows, :] = jnp.concatenate(outs, axis=0).T.astype(bf16)
        extra_t = extra.T
        for head in range(2):
            spare = (1 - head) * HEAD
            columns = slice(head * PAIR, (head + 1) * PAIR)
            is_extra = (lane_rows > spare) & (lane_rows < spare + 4)
            qa_ref[rows, columns] = jnp.where(
                is_extra, extra_t, qa_ref[rows, columns].astype(f32)
            ).astype(bf16)


def attend_forward(queries, keys, values, cosine, sine, bias):
    width = values.shape[1]
    pairs = width // PAIR
    tall = lambda columns: pl.BlockSpec((LEN, columns), lambda pair: (0, pair))
    whole = pl.BlockSpec((LEN, PAIR), lambda pair: (0, 0))
    return pl.pallas_call(
        attend_kernel,
        grid=(pairs,),
        in_specs=[tall(PAIR), tall(PAIR), tall(PAIR), whole, whole, whole],
        out_specs=[tall(PAIR), tall(2 * PAIR), tall(PAIR)],
        out_shape=[
            jax.ShapeDtypeStruct((LEN, width), bf16),
            jax.ShapeDtypeStruct((LEN, 2 * width), bf16),
            jax.ShapeDtypeStruct((LEN, width), bf16),
        ],
        compiler_params=pltpu.CompilerParams(vmem_limit_bytes=vmem_bytes),
        cost_estimate=pl.CostEstimate(
            flops=2 * 4 * LEN * LEN * width * 4,
            bytes_accessed=10 * LEN * width * 2,
            transcendentals=LEN * LEN * width // HEAD,
        ),
        name="attend",
    )(queries, keys, values, cosine, sine, bias)


def attend_back_kernel(
    qa_ref, kr_ref, v_ref, do_ref, o_ref, cos_ref, sin_ref, bias_ref,
    dq_ref, dk_ref, dv_ref, doa_ref, dka_ref, dva_ref,
):
    lane = lax.broadcasted_iota(jnp.int32, (LEN, PAIR), 1)
    lane_rows = lax.broadcasted_iota(jnp.int32, (ROWS, PAIR), 1)
    cosine, sine = cos_ref[...], sin_ref[...]
    k_wide = kr_ref[...].astype(f32)
    keys_t = kr_ref[...].T
    v_wide = v_ref[...].astype(f32)
    do_wide = do_ref[...].astype(f32)
    bias = bias_ref[...].astype(f32)
    product = do_wide * o_ref[...].astype(f32)
    keys, values = [], []
    for head in range(2):
        own = lane // HEAD == head
        spare = (1 - head) * HEAD
        is_extra = (lane > spare) & (lane < spare + 4)
        ones = jnp.where(is_extra, 1.0, 0.0)
        keys.append(
            jnp.where(own, k_wide, jnp.where(lane == spare, bias, ones)).astype(bf16)
        )
        values.append(jnp.where(own, v_wide, ones).astype(bf16))
        row_dot = jnp.sum(jnp.where(own, product, 0.0), axis=1, keepdims=True)
        grad = jnp.where(own, do_wide, 0.0)
        for place, term in enumerate(three_terms(row_dot)):
            grad = jnp.where(lane == spare + 1 + place, -term, grad)
        doa_ref[:, head * PAIR : (head + 1) * PAIR] = grad.astype(bf16)
    for block in range(LEN // ROWS):
        rows = slice(block * ROWS, (block + 1) * ROWS)
        turned = []
        for head in range(2):
            columns = slice(head * PAIR, (head + 1) * PAIR)
            q_block = qa_ref[rows, columns]
            do_block = doa_ref[rows, columns]
            probs = jnp.exp(dot32(keys[head], q_block, NT))
            prob_grad = dot32(values[head], do_block, NT)
            score_grad = (probs * prob_grad).astype(bf16)
            dv_part = dot32(probs.astype(bf16), do_block)
            dk_part = dot32(score_grad, q_block)
            if block == 0:
                dva_ref[:, columns] = dv_part
                dka_ref[:, columns] = dk_part
            else:
                dva_ref[:, columns] += dv_part
                dka_ref[:, columns] += dk_part
            turned.append(dot32(keys_t[head * HEAD : (head + 1) * HEAD], score_grad))
        dq = jnp.concatenate(turned, axis=0).T * 0.125
        dq_ref[rows, :] = rotate(dq, cosine[rows], -sine[rows], lane_rows).astype(bf16)
    first = lane < HEAD
    dk = jnp.where(first, dka_ref[:, :PAIR], dka_ref[:, PAIR:])
    dk_ref[...] = rotate(dk, cosine, -sine, lane).astype(bf16)
    dv_ref[...] = jnp.where(first, dva_ref[:, :PAIR], dva_ref[:, PAIR:]).astype(bf16)


def attend_backward(queries, keys, values, grads, outputs, cosine, sine, bias):
    width = values.shape[1]
    pairs = width // PAIR
    tall = lambda columns: pl.BlockSpec((LEN, columns), lambda pair: (0, pair))
    whole = pl.BlockSpec((LEN, PAIR), lambda pair: (0, 0))
    return pl.pallas_call(
        attend_back_kernel,
        grid=(pairs,),
        in_specs=[tall(2 * PAIR)] + [tall(PAIR)] * 4 + [whole] * 3,
        out_specs=[tall(PAIR)] * 3,
        out_shape=[jax.ShapeDtypeStruct((LEN, width), bf16)] * 3,
        scratch_shapes=[
            pltpu.VMEM((LEN, 2 * PAIR), bf16),
            pltpu.VMEM((LEN, 2 * PAIR), f32),
            pltpu.VMEM((LEN, 2 * PAIR), f32),
        ],
        compiler_params=pltpu.CompilerParams(vmem_limit_bytes=vmem_bytes),
        cost_estimate=pl.CostEstimate(
            flops=2 * 10 * LEN * LEN * width * 4,
            bytes_accessed=12 * LEN * width * 2,
            transcendentals=LEN * LEN * width // HEAD,
        ),
        name="attend_back",
    )(queries, keys, values, grads, outputs, cosine, sine, bias)


def vector_parts(vectors):
    kernel_size = KERNEL * TEXT
    pieces = [vectors[:kernel_size].reshape(KERNEL, TEXT)]
    offset = kernel_size
    for extent in (TEXT, TEXT, TEXT, TEXT, TXT_FF, TXT_FF, TXT_FF, 6 * D):
        pieces.append(vectors[offset : offset + extent])
        offset = offset + extent
    return pieces


def normalise(values):
    center = values - jnp.mean(values, axis=-1, keepdims=True)
    variance = jnp.mean(center * center, axis=-1, keepdims=True)
    scale = lax.rsqrt(variance + norm_eps)
    return center * scale, scale


def normalise_back(grad, normed, scale):
    mean_grad = jnp.mean(grad, axis=-1, keepdims=True)
    mean_dot = jnp.mean(grad * normed, axis=-1, keepdims=True)
    return scale * (grad - mean_grad - normed * mean_dot)


def gelu_parts(values):
    share = 0.5 * (1.0 + lax.erf(values * 0.7071067811865476))
    density = 0.3989422804014327 * jnp.exp(-0.5 * values * values)
    return share, density


def gelu_tanh(values):
    return jax.nn.gelu(values, approximate=True)


def moments(gradient, first_moment, second_moment):
    first_new = beta_one * first_moment + (1.0 - beta_one) * gradient
    second_new = beta_two * second_moment + (1.0 - beta_two) * gradient * gradient
    bias_first = 1.0 - beta_one**STEP
    bias_second = 1.0 - beta_two**STEP
    direction = first_new / bias_first / (jnp.sqrt(second_new / bias_second) + adam_eps)
    return (first_new, second_new, direction)


def apply_step(weight, direction, rate):
    return weight - rate * (direction + weight_decay * weight)


def rotary_tables(core, half):
    position = ((jnp.arange(LEN) + core * half) % LEN).astype(f32)
    frequency = 10000.0 ** (-jnp.arange(HEAD // 2, dtype=f32) * 2.0 / HEAD)
    angle = position[:, None] * frequency[None, :]
    cosine, sine = jnp.cos(angle), jnp.sin(angle)
    return (
        jnp.concatenate([cosine] * 4, axis=1),
        jnp.concatenate([-sine, sine, -sine, sine], axis=1),
    )


def take_blocks(blocks, index):
    return jnp.take(blocks, index, axis=0, mode="clip")


def both_halves(mine):
    return jnp.concatenate([mine, swap_core(mine)], axis=0)


def sum_halves(multiply, rows, half):
    theirs = multiply(rows[half:]).astype(bf16)
    received = swap_core(theirs)
    return multiply(rows[:half]) + received.astype(f32)


def body(
    mel_frames,
    text_features,
    cotangent,
    time_embedding,
    lengths,
    group_ids,
    text_keep,
    owner_list,
    soap_master,
    soap_first,
    soap_second,
    left_basis,
    right_basis,
    text_matrices,
    text_first,
    text_second,
    modulation_weight,
    modulation_first,
    modulation_second,
    vectors,
    vector_first,
    vector_second,
):
    count = lax.axis_size("dp")
    me, core = lax.axis_index("dp"), lax.axis_index("mp")
    half = LEN // 2
    utterances = lengths.shape[0] * count
    panel_rows, width = soap_master.shape
    share_rows = modulation_weight.shape[0]
    text_rows = text_matrices.shape[0]
    text_half = text_rows // 2
    relative = jnp.arange(count) ^ me

    own_rows = lax.dynamic_slice_in_dim(text_matrices, core * text_half, text_half, 0)
    text_half_all = gather_relative(own_rows.astype(bf16))
    text_other = swap_core(text_half_all)
    slots = gather_relative(soap_master.astype(bf16))
    texts = take_blocks(by_core(core, text_half_all, text_other, axis=1), relative)
    texts = texts.reshape(3 * TEXT, D)
    expand_weight, shrink_rows, text_to_model = texts[:TEXT], texts[TEXT : 2 * TEXT], texts[2 * TEXT :]
    stacked = take_blocks(slots, owner_list ^ me).reshape(8, D, width)
    query_weight, key_weight, value_weight, out_weight = (stacked[i] for i in range(4))
    hidden_in, hidden_out = stacked[4:6], stacked[6:8]

    silu_time = jax.nn.silu(time_embedding.astype(f32)).astype(bf16)
    time_rows = lax.dynamic_slice_in_dim(silu_time, me * share_rows, share_rows, 1)
    weight_half = lax.dynamic_slice_in_dim(modulation_weight, core * 3 * D, 3 * D, 1).astype(bf16)
    modulation_half = sum_dp(dot32(time_rows, weight_half))
    modulation = by_core(core, modulation_half, swap_core(modulation_half), axis=1)
    (
        kernel,
        conv_bias,
        norm_gain,
        norm_bias,
        out_bias,
        in_bias,
        grn_gamma,
        grn_beta,
        modulation_bias,
    ) = vector_parts(vectors)
    group = group_ids[0]
    modulation_row = lax.dynamic_slice_in_dim(modulation, group, 1, 0) + modulation_bias
    shift_one, scale_one, gate_one, shift_two, scale_two, gate_two = (
        modulation_row[:, i * D : (i + 1) * D] for i in range(6)
    )

    first = core * half
    margin = KERNEL // 2
    edge = 8
    keep_all = jnp.pad(text_keep.astype(f32), (edge, edge))[:, None]
    text_all = jnp.pad(text_features, ((edge, edge), (0, 0)))
    window = lax.dynamic_slice_in_dim(text_all, first, half + 2 * edge, 0).astype(f32)
    window = window * lax.dynamic_slice_in_dim(keep_all, first, half + 2 * edge, 0)
    keep = lax.dynamic_slice_in_dim(keep_all, first + edge, half, 0)
    masked_text = window[edge : edge + half]
    taps = [window[edge - margin + j : edge - margin + j + half] for j in range(KERNEL)]
    mixed = conv_bias[None, :]
    for j in range(KERNEL):
        mixed = mixed + taps[j] * kernel[j][None, :]
    conv_normed, conv_scale = normalise(mixed)
    normed_low = (conv_normed * norm_gain + norm_bias).astype(bf16)
    expand_pre = dot32(normed_low, expand_weight) + in_bias
    share, density = gelu_parts(expand_pre)
    hidden = expand_pre * share
    energy_sum = jnp.sum(hidden * hidden, axis=0, keepdims=True)
    energy = jnp.sqrt(energy_sum + swap_core(energy_sum))
    energy_mean = jnp.mean(energy, axis=-1, keepdims=True) + norm_eps
    ratio = energy / energy_mean
    grn_low = (grn_gamma * (hidden * ratio) + grn_beta + hidden).astype(bf16)
    text_out = (masked_text + dot32(grn_low, shrink_rows, NT) + out_bias) * keep
    text_low = text_out.astype(bf16)
    mel_mine = lax.dynamic_slice_in_dim(mel_frames, first, half, 0).astype(f32)
    stream = mel_mine + dot32(text_low, text_to_model)

    normed_one, scale_norm_one = normalise(stream)
    first_normed = both_halves((normed_one * (1.0 + scale_one) + shift_one).astype(bf16))
    cosine, sine = rotary_tables(core, half)
    position = (jnp.arange(LEN) + first) % LEN
    bias = jnp.where(position < lengths[0], 0.0, -1e30).astype(bf16)
    bias = jnp.broadcast_to(bias[:, None], (LEN, PAIR))
    queries = dot32(first_normed, query_weight)
    keys = dot32(first_normed, key_weight)
    value_rows = dot32(first_normed, value_weight).astype(bf16)
    attended, query_aug, key_rot = attend_forward(queries, keys, value_rows, cosine, sine, bias)
    attention_out = sum_halves(lambda rows: dot32(rows, out_weight, NT), attended, half)
    stream_one = stream + gate_one * attention_out

    normed_two, scale_norm_two = normalise(stream_one)
    second_normed = both_halves((normed_two * (1.0 + scale_two) + shift_two).astype(bf16))
    unit_pre = [dot32(second_normed, hidden_in[i]) for i in range(2)]
    unit_act, unit_back = zip(*[jax.vjp(gelu_tanh, pre) for pre in unit_pre])
    unit_low = jnp.concatenate([act.astype(bf16) for act in unit_act], axis=1)
    unit_out = sum_halves(
        lambda rows: dot32(rows[:, :width], hidden_out[0], NT) + dot32(rows[:, width:], hidden_out[1], NT),
        unit_low,
        half,
    )
    output_mine = (stream_one + gate_two * unit_out).astype(bf16)
    block_output = by_core(core, output_mine, swap_core(output_mine))

    cot_mine = lax.dynamic_slice_in_dim(cotangent, first, half, 0)
    cot_other = lax.dynamic_slice_in_dim(cotangent, half - first, half, 0)
    out_grad = cot_mine.astype(f32)
    gate_two_grad = jnp.sum(out_grad * unit_out, axis=0)
    hidden_out_grad = jnp.concatenate(
        [(gate_two * out_grad).astype(bf16), (gate_two * cot_other.astype(f32)).astype(bf16)], axis=0
    )
    TN = (((0,), (0,)), ((), ()))
    out_blocks_grad = [dot32(hidden_out_grad, unit_low[:, i * width : (i + 1) * width], TN) for i in range(2)]
    pre_grad = [
        unit_back[i](dot32(hidden_out_grad, hidden_out[i]))[0].astype(bf16) for i in range(2)
    ]
    in_blocks_grad = [dot32(second_normed, pre_grad[i], TN) for i in range(2)]
    normed_two_grad = sum_halves(
        lambda rows: dot32(rows[:, :width], hidden_in[0], NT) + dot32(rows[:, width:], hidden_in[1], NT),
        jnp.concatenate(pre_grad, axis=1),
        half,
    )
    shift_two_grad = jnp.sum(normed_two_grad, axis=0)
    scale_two_grad = jnp.sum(normed_two_grad * normed_two, axis=0)
    stream_one_grad = out_grad + normalise_back(
        normed_two_grad * (1.0 + scale_two), normed_two, scale_norm_two
    )

    gate_one_grad = jnp.sum(stream_one_grad * attention_out, axis=0)
    attention_grad = both_halves((gate_one * stream_one_grad).astype(bf16))
    out_weight_grad = dot32(attention_grad, attended, TN)
    attended_grad = dot32(attention_grad, out_weight).astype(bf16)
    query_grad, key_grad, value_grad = attend_backward(
        query_aug, key_rot, value_rows, attended_grad, attended, cosine, sine, bias
    )
    head_grads = [dot32(first_normed, grad, TN) for grad in (query_grad, key_grad, value_grad)]
    normed_one_grad = sum_halves(
        lambda rows: dot32(rows[:, :width], query_weight, NT)
        + dot32(rows[:, width : 2 * width], key_weight, NT)
        + dot32(rows[:, 2 * width :], value_weight, NT),
        jnp.concatenate([query_grad, key_grad, value_grad], axis=1),
        half,
    )
    panel_grad = jnp.concatenate(
        [grad.astype(bf16) for grad in head_grads + [out_weight_grad] + in_blocks_grad + out_blocks_grad],
        axis=0,
    ).reshape(count, panel_rows, width)
    slot_index = jnp.arange(count)
    inverse = jnp.sum(jnp.where(owner_list[None, :] == slot_index[:, None], slot_index[None, :], 0), axis=1)
    own_panel = scatter_relative(take_blocks(panel_grad, jnp.take(inverse, relative, mode="clip")))

    shift_one_grad = jnp.sum(normed_one_grad, axis=0)
    scale_one_grad = jnp.sum(normed_one_grad * normed_one, axis=0)
    mel_grad_mine = stream_one_grad + normalise_back(
        normed_one_grad * (1.0 + scale_one), normed_one, scale_norm_one
    )
    mel_gradient = by_core(core, mel_grad_mine, swap_core(mel_grad_mine))

    stream_grad = mel_grad_mine.astype(bf16)
    text_to_model_grad = dot32(text_low, stream_grad, TN)
    shrink_grad = dot32(stream_grad, text_to_model, NT) * keep
    out_bias_grad = jnp.sum(shrink_grad, axis=0)
    shrink_low = shrink_grad.astype(bf16)
    shrink_rows_grad = dot32(shrink_low, grn_low, TN)
    grn_grad = dot32(shrink_low, shrink_rows)
    hidden_dot = jnp.sum(grn_grad * hidden, axis=0, keepdims=True)
    hidden_dot_all = hidden_dot + swap_core(hidden_dot)
    ratio_grad = grn_gamma * hidden_dot_all
    energy_grad = ratio_grad / energy_mean - jnp.mean(ratio_grad * ratio, axis=-1, keepdims=True) / energy_mean
    gamma_grad = (ratio * hidden_dot)[0]
    beta_grad = jnp.sum(grn_grad, axis=0)
    hidden_grad = grn_grad * (grn_gamma * ratio + 1.0) + hidden * (energy_grad / energy)
    expand_grad = hidden_grad * (share + expand_pre * density)
    in_bias_grad = jnp.sum(expand_grad, axis=0)
    expand_low = expand_grad.astype(bf16)
    expand_weight_grad = dot32(normed_low, expand_low, TN)
    text_grads = jnp.concatenate(
        [grad.astype(bf16) for grad in (expand_weight_grad, shrink_rows_grad, text_to_model_grad)], axis=0
    ).reshape(count, 2, text_half, D)
    text_keep_half = lax.dynamic_index_in_dim(text_grads, core, 1, keepdims=False)
    text_send_half = lax.dynamic_index_in_dim(text_grads, 1 - core, 1, keepdims=False)
    text_sum = add_low(text_keep_half, swap_core(text_send_half))
    own_text = scatter_relative(take_blocks(text_sum, relative))
    own_text = by_core(core, own_text, swap_core(own_text))

    normed_text_grad = dot32(expand_low, expand_weight, NT)
    gain_grad = jnp.sum(normed_text_grad * conv_normed, axis=0)
    norm_bias_grad = jnp.sum(normed_text_grad, axis=0)
    mixed_grad = normalise_back(normed_text_grad * norm_gain, conv_normed, conv_scale)
    conv_bias_grad = jnp.sum(mixed_grad, axis=0)
    kernel_grad = jnp.stack([jnp.sum(mixed_grad * taps[j], axis=0) for j in range(KERNEL)])
    border = lax.dynamic_slice_in_dim(mixed_grad, (1 - core) * (half - edge), edge, 0)
    border = swap_core(border)
    before = jnp.where(core == 1, border, 0.0)
    after = jnp.where(core == 0, border, 0.0)
    wide_grad = jnp.concatenate([before, mixed_grad, after], axis=0)
    masked_grad = shrink_grad
    for j in range(KERNEL):
        start = edge + margin - j
        masked_grad = masked_grad + wide_grad[start : start + half] * kernel[j][None, :]
    text_grad_mine = masked_grad * keep
    text_gradient = by_core(core, text_grad_mine, swap_core(text_grad_mine))

    vector_mine = jnp.concatenate(
        [
            kernel_grad.reshape(-1),
            conv_bias_grad,
            gain_grad,
            norm_bias_grad,
            out_bias_grad,
            in_bias_grad,
            gamma_grad,
            beta_grad,
        ]
    )
    token = jnp.concatenate(
        [shift_one_grad, scale_one_grad, gate_one_grad, shift_two_grad, scale_two_grad, gate_two_grad]
    )
    vector_half = vector_mine.shape[0] // 2
    token_half = 3 * D

    def half_of(which):
        return jnp.concatenate(
            [
                lax.dynamic_slice_in_dim(vector_mine, which * vector_half, vector_half, 0),
                lax.dynamic_slice_in_dim(token, which * token_half, token_half, 0),
            ]
        )

    small = half_of(core) + swap_core(half_of(1 - core))
    in_group = (jnp.arange(GROUPS) == group).astype(f32)
    table = in_group[:, None] * small[None, vector_half:]
    small = sum_dp(jnp.concatenate([small[:vector_half], table.reshape(-1)]).reshape(-1, 128))
    small = by_core(core, small[None], swap_core(small)[None]).reshape(2, -1)
    vector_sum = small[:, :vector_half].reshape(-1)
    tables = small[:, vector_half:].reshape(2, GROUPS, token_half)
    modulation_grad = jnp.concatenate([tables[0], tables[1]], axis=1)
    vector_gradient = jnp.concatenate([vector_sum, jnp.sum(modulation_grad, axis=0)]) / utterances
    share_grad = (
        lax.dot_general(
            time_rows, modulation_grad.astype(bf16), TN, preferred_element_type=f32
        )
        / utterances
    )

    own_panel = own_panel / utterances
    own_text = own_text / utterances
    rotated = jnp.dot(jnp.dot(left_basis.T, own_panel, precision=solver), right_basis, precision=solver)
    soap_moment, soap_variance, soap_direction = moments(rotated, soap_first, soap_second)
    turned_back = jnp.dot(
        jnp.dot(left_basis, soap_direction, precision=solver), right_basis.T, precision=solver
    )
    soap_weights = apply_step(soap_master, turned_back, learn_rate)
    text_moment, text_variance, text_direction = moments(own_text, text_first, text_second)
    text_weights = apply_step(text_matrices, text_direction, learn_rate)
    modulation_moment, modulation_variance, modulation_direction = moments(
        share_grad, modulation_first, modulation_second
    )
    modulation_weights = apply_step(modulation_weight, modulation_direction, learn_rate)
    vector_moment, vector_variance, vector_direction = moments(
        vector_gradient, vector_first, vector_second
    )
    vector_weights = apply_step(vectors, vector_direction, vector_rate)
    return (
        block_output,
        mel_gradient,
        text_gradient,
        soap_weights,
        soap_moment,
        soap_variance,
        text_weights,
        text_moment,
        text_variance,
        modulation_weights,
        modulation_moment,
        modulation_variance,
        vector_weights,
        vector_moment,
        vector_variance,
    )


def solution(mesh):
    rows, quarter, same = P("dp", None), P("dp", "mp"), P()
    return jax.shard_map(
        body,
        mesh=mesh,
        in_specs=(
            (rows,) * 3 + (same,) + (P("dp"),) * 3 + (same,) + (quarter,) * 5 + (rows,) * 6 + (same,) * 3
        ),
        out_specs=(rows,) * 3 + (quarter,) * 3 + (rows,) * 6 + (same,) * 3,
        check_vma=False,
    )
```

```python
import jax
import jax.numpy as jnp
from jax import lax
from jax.experimental import pallas as pl
from jax.experimental.pallas import tpu as pltpu
from jax.sharding import PartitionSpec as P

D = 1024
HEAD = 64
TEXT = 512
TXT_FF = 1024
KERNEL = 7
LEN = 1024
GROUPS = 8
STEP = 10

f32 = jnp.float32
bf16 = jnp.bfloat16
beta_one = 0.9
beta_two = 0.99
adam_eps = 1e-08
weight_decay = 0.01
learn_rate = 0.03
vector_rate = 0.3
norm_eps = 1e-06
solver = lax.Precision.HIGH


def swap_core(array):
    return lax.ppermute(array, "mp", [(0, 1), (1, 0)])


def swap_bit(array, bit):
    count = lax.axis_size("dp")
    return lax.ppermute(array, "dp", [(i, i ^ (1 << bit)) for i in range(count)])


def by_core(core, mine, other, axis=0):
    return jnp.where(
        core == 0,
        jnp.concatenate([mine, other], axis=axis),
        jnp.concatenate([other, mine], axis=axis),
    )


def bit_count(count):
    return count.bit_length() - 1


def third_cuts(rows):
    step = rows // 3
    if rows >= 48:
        step = (rows + 24) // 48 * 16
    return (0, step, 2 * step, rows)


axis_orders = ((0, 1, 2), (1, 2, 0), (2, 0, 1))


def tie(*values):
    return lax.optimization_barrier(values)


def spread_step(parts, phase):
    return [
        jnp.stack([part, swap_bit(part, axis_orders[index][phase])])
        for index, part in enumerate(parts)
    ]


def spread_last(parts):
    return [(part, swap_bit(part, axis_orders[index][2])) for index, part in enumerate(parts)]


def split_rows(array, cuts):
    return [array[..., cuts[i] : cuts[i + 1], :] for i in range(3)]


def spread_close(pairs):
    pieces = []
    for index, pair in enumerate(pairs):
        order = axis_orders[index]
        held = [order[2], order[1], order[0]]
        axes = [3] + [held.index(bit) for bit in (2, 1, 0)] + [4, 5]
        pieces.append(jnp.stack(pair).transpose(axes))
    return jnp.concatenate(pieces, axis=4)


def spread_high(block):
    held = block[None]
    for bit in range(4, bit_count(lax.axis_size("dp"))):
        held = jnp.concatenate([held, swap_bit(held, bit)], axis=0)
    return held


def add_low(left, right):
    return (left.astype(f32) + right.astype(f32)).astype(bf16)


def fold_step(parts, held, phase):
    folded = []
    for index, part in enumerate(parts):
        bit = axis_orders[index][phase]
        axis = 1 + held[index].index(bit)
        keep = lax.index_in_dim(part, 0, axis, keepdims=False)
        send = lax.index_in_dim(part, 1, axis, keepdims=False)
        folded.append(add_low(keep, swap_bit(send, bit)))
        held[index].remove(bit)
    return folded


def fold_first(pairs):
    return [add_low(keep, swap_bit(send, axis_orders[index][2])) for index, (keep, send) in enumerate(pairs)]


def fold_next(parts, phase):
    return [add_low(part[0], swap_bit(part[1], axis_orders[index][phase])) for index, part in enumerate(parts)]


def fold_high(total):
    count = total.shape[0]
    if count == 1:
        return total[0]
    for bit in range(bit_count(count) - 1, -1, -1):
        half = 1 << bit
        total = total[:half] + swap_bit(total[half:].astype(bf16), bit + 4).astype(f32)
    return total[0]


def sum_dp(array):
    for bit in range(bit_count(lax.axis_size("dp"))):
        array = array + swap_bit(array, bit)
    return array


NT = (((1,), (1,)), ((), ()))
NN = (((1,), (0,)), ((), ()))
ROWS = 256
PAIR = 2 * HEAD
vmem_bytes = 48 * 1024 * 1024


def dot32(left, right, dims=NN):
    return lax.dot_general(left, right, dims, preferred_element_type=f32)


def three_terms(values):
    high = values.astype(bf16).astype(f32)
    rest = values - high
    middle = rest.astype(bf16).astype(f32)
    return high, middle, rest - middle


def rotate(values, cosine, sine, lane):
    partner = jnp.where(
        lane % HEAD < HEAD // 2,
        pltpu.roll(values, PAIR - HEAD // 2, 1),
        pltpu.roll(values, HEAD // 2, 1),
    )
    return values * cosine + partner * sine


def attend_kernel(q_ref, k_ref, v_ref, bias_ref, o_ref, qa_ref):
    lane = lax.broadcasted_iota(jnp.int32, (LEN, PAIR), 1)
    lane_rows = lax.broadcasted_iota(jnp.int32, (ROWS, PAIR), 1)
    row_index = lax.broadcasted_iota(jnp.int32, (PAIR, ROWS), 0)
    q_wide = q_ref[...].astype(f32)
    k_wide = k_ref[...].astype(f32)
    values_t = v_ref[...].T
    bias = bias_ref[...].astype(f32)
    keys = []
    for head in range(2):
        own = lane // HEAD == head
        spare = (1 - head) * HEAD
        keys.append(
            jnp.where(own, k_wide, jnp.where(lane == spare, bias, 0.0)).astype(bf16)
        )
        qa_ref[:, head * PAIR : (head + 1) * PAIR] = jnp.where(
            own, q_wide, jnp.where(lane == spare, 1.0, 0.0)
        ).astype(bf16)
    steps = [(block, head) for block in range(LEN // ROWS) for head in range(2)]

    def scores_of(step):
        block, head = step
        rows = slice(block * ROWS, (block + 1) * ROWS)
        return dot32(keys[head], qa_ref[rows, head * PAIR : (head + 1) * PAIR], NT)

    following = scores_of(steps[0])
    for position, (block, head) in enumerate(steps):
        scores = following
        if position + 1 < len(steps):
            following = scores_of(steps[position + 1])
        rows = slice(block * ROWS, (block + 1) * ROWS)
        if head == 0:
            outs, extra = [], jnp.zeros((PAIR, ROWS), f32)
        spare = (1 - head) * HEAD
        highest = jnp.max(scores, axis=0, keepdims=True)
        weights = jnp.exp(scores - highest)
        total = jnp.sum(weights, axis=0, keepdims=True)
        out_t = dot32(values_t[head * HEAD : (head + 1) * HEAD], weights.astype(bf16))
        outs.append(out_t / total)
        for place, term in enumerate(three_terms(highest + jnp.log(total))):
            extra = jnp.where(row_index == spare + 1 + place, -term, extra)
        if head == 0:
            continue
        o_ref[rows, :] = jnp.concatenate(outs, axis=0).T.astype(bf16)
        extra_t = extra.T
        for head in range(2):
            spare = (1 - head) * HEAD
            columns = slice(head * PAIR, (head + 1) * PAIR)
            is_extra = (lane_rows > spare) & (lane_rows < spare + 4)
            qa_ref[rows, columns] = jnp.where(
                is_extra, extra_t, qa_ref[rows, columns].astype(f32)
            ).astype(bf16)


def attend_forward(queries, keys, values, bias):
    width = values.shape[1]
    pairs = width // PAIR
    tall = lambda columns: pl.BlockSpec((LEN, columns), lambda pair: (0, pair))
    whole = pl.BlockSpec((LEN, PAIR), lambda pair: (0, 0))
    return pl.pallas_call(
        attend_kernel,
        grid=(pairs,),
        in_specs=[tall(PAIR), tall(PAIR), tall(PAIR), whole],
        out_specs=[tall(PAIR), tall(2 * PAIR)],
        out_shape=[
            jax.ShapeDtypeStruct((LEN, width), bf16),
            jax.ShapeDtypeStruct((LEN, 2 * width), bf16),
        ],
        compiler_params=pltpu.CompilerParams(vmem_limit_bytes=vmem_bytes),
        cost_estimate=pl.CostEstimate(
            flops=2 * 4 * LEN * LEN * width * 4,
            bytes_accessed=6 * LEN * width * 2,
            transcendentals=LEN * LEN * width // HEAD,
        ),
        name="attend",
    )(queries, keys, values, bias)


def attend_back_kernel(
    qa_ref, kr_ref, v_ref, o_ref, mine_ref, other_ref, weight_ref, cos_ref, sin_ref, bias_ref,
    dq_ref, dk_ref, dv_ref, doa_ref, dka_ref, dva_ref,
):
    lane = lax.broadcasted_iota(jnp.int32, (LEN, PAIR), 1)
    lane_rows = lax.broadcasted_iota(jnp.int32, (ROWS, PAIR), 1)
    cosine, sine = cos_ref[...], sin_ref[...]
    k_wide = kr_ref[...].astype(f32)
    keys_t = kr_ref[...].T
    v_wide = v_ref[...].astype(f32)
    do_wide = jnp.concatenate(
        [dot32(ref[...], weight_ref[0]).astype(bf16).astype(f32) for ref in (mine_ref, other_ref)],
        axis=0,
    )
    bias = bias_ref[...].astype(f32)
    product = do_wide * o_ref[...].astype(f32)
    keys, values = [], []
    for head in range(2):
        own = lane // HEAD == head
        spare = (1 - head) * HEAD
        is_extra = (lane > spare) & (lane < spare + 4)
        ones = jnp.where(is_extra, 1.0, 0.0)
        keys.append(
            jnp.where(own, k_wide, jnp.where(lane == spare, bias, ones)).astype(bf16)
        )
        values.append(jnp.where(own, v_wide, ones).astype(bf16))
        row_dot = jnp.sum(jnp.where(own, product, 0.0), axis=1, keepdims=True)
        grad = jnp.where(own, do_wide, 0.0)
        for place, term in enumerate(three_terms(row_dot)):
            grad = jnp.where(lane == spare + 1 + place, -term, grad)
        doa_ref[:, head * PAIR : (head + 1) * PAIR] = grad.astype(bf16)
    for block in range(LEN // ROWS):
        rows = slice(block * ROWS, (block + 1) * ROWS)
        turned = []
        for head in range(2):
            columns = slice(head * PAIR, (head + 1) * PAIR)
            q_block = qa_ref[rows, columns]
            do_block = doa_ref[rows, columns]
            probs = jnp.exp(dot32(keys[head], q_block, NT))
            prob_grad = dot32(values[head], do_block, NT)
            score_grad = (probs * prob_grad).astype(bf16)
            dv_part = dot32(probs.astype(bf16), do_block)
            dk_part = dot32(score_grad, q_block)
            if block == 0:
                dva_ref[:, columns] = dv_part
                dka_ref[:, columns] = dk_part
            else:
                dva_ref[:, columns] += dv_part
                dka_ref[:, columns] += dk_part
            turned.append(dot32(keys_t[head * HEAD : (head + 1) * HEAD], score_grad))
        dq = jnp.concatenate(turned, axis=0).T * 0.125
        dq_ref[rows, :] = rotate(dq, cosine[rows], -sine[rows], lane_rows).astype(bf16)
    first = lane < HEAD
    dk = jnp.where(first, dka_ref[:, :PAIR], dka_ref[:, PAIR:])
    dk_ref[...] = rotate(dk, cosine, -sine, lane).astype(bf16)
    dv_ref[...] = jnp.where(first, dva_ref[:, :PAIR], dva_ref[:, PAIR:]).astype(bf16)


def attend_backward(queries, keys, values, outputs, grad_mine, grad_other, stacked, cosine, sine, bias):
    width = values.shape[1]
    pairs = width // PAIR
    tall = lambda columns: pl.BlockSpec((LEN, columns), lambda pair: (0, pair))
    whole = lambda shape: pl.BlockSpec(shape, lambda pair: (0, 0))
    return pl.pallas_call(
        attend_back_kernel,
        grid=(pairs,),
        in_specs=[tall(2 * PAIR)]
        + [tall(PAIR)] * 3
        + [whole(grad_mine.shape)] * 2
        + [pl.BlockSpec((1, D, PAIR), lambda pair: (3, 0, pair))]
        + [whole((LEN, PAIR))] * 3,
        out_specs=[tall(PAIR)] * 3,
        out_shape=[jax.ShapeDtypeStruct((LEN, width), bf16)] * 3,
        scratch_shapes=[
            pltpu.VMEM((LEN, 2 * PAIR), bf16),
            pltpu.VMEM((LEN, 2 * PAIR), f32),
            pltpu.VMEM((LEN, 2 * PAIR), f32),
        ],
        compiler_params=pltpu.CompilerParams(vmem_limit_bytes=vmem_bytes),
        cost_estimate=pl.CostEstimate(
            flops=2 * 10 * LEN * LEN * width * 4,
            bytes_accessed=12 * LEN * width * 2,
            transcendentals=LEN * LEN * width // HEAD,
        ),
        name="attend_back",
    )(queries, keys, values, outputs, grad_mine, grad_other, stacked, cosine, sine, bias)


def part_place(slot, index, high_count):
    bit = lambda which: (slot >> which) & 1
    order = axis_orders[index]
    lead = (bit(order[1]) * 2 + bit(order[0])) * high_count + (slot >> 4)
    return bit(3), bit(order[2]), lead


def project_kernel(high_count, panel_rows, cuts, slots_ref, *refs):
    parts, refs = refs[:12], refs[12:]
    mine_ref, other_ref, cos_ref, sin_ref, q_ref, k_ref, v_ref, out_ref, held, in_sems, out_sem = refs
    per_block = D // panel_rows

    def fetch(panel, carry):
        slot = slots_ref[panel]
        group = jnp.minimum(panel // per_block, 3)
        for index in range(3):
            far, last, lead = part_place(slot, index, high_count)
            rows = cuts[index + 1] - cuts[index]
            start = pl.multiple_of(panel * panel_rows + cuts[index], 16)
            for which in range(4):

                @pl.when(far * 2 + last == which)
                def _():
                    pltpu.make_async_copy(
                        parts[which * 3 + index].at[lead], held.at[pl.ds(start, rows)], in_sems.at[group]
                    ).start()

        return carry

    lax.fori_loop(0, 8 * per_block, fetch, 0)
    half = mine_ref.shape[0]
    width = held.shape[1]
    lane = lax.broadcasted_iota(jnp.int32, (half, PAIR), 1)
    for block, ref in enumerate((q_ref, k_ref, v_ref)):
        place = pl.ds(block * D, D)
        pltpu.make_async_copy(held.at[place], held.at[place], in_sems.at[block]).wait()
        pltpu.make_async_copy(held.at[place], out_ref.at[place], out_sem).start()
        for part, rows_ref in enumerate((mine_ref, other_ref)):
            rows = slice(part * half, (part + 1) * half)
            product = dot32(rows_ref[...], held[block * D : (block + 1) * D])
            if block == 2:
                ref[rows, :] = product.astype(bf16)
                continue
            cosine, sine = cos_ref[rows, :], sin_ref[rows, :]
            for pair in range(width // PAIR):
                columns = slice(pair * PAIR, (pair + 1) * PAIR)
                turned = rotate(product[:, columns], cosine, sine, lane).astype(bf16)
                if block == 0:
                    turned = (turned.astype(f32) * 0.125).astype(bf16)
                ref[rows, columns] = turned
    place = pl.ds(3 * D, 5 * D)
    pltpu.make_async_copy(held.at[place], held.at[place], in_sems.at[3]).wait()
    pltpu.make_async_copy(held.at[place], out_ref.at[place], out_sem).start()
    pltpu.make_async_copy(held, out_ref, out_sem).wait()


def project(near_pairs, far_pairs, slots, panel_rows, cuts, mine, other, cosine, sine):
    high_count, width = near_pairs[0][0].shape[2], near_pairs[0][0].shape[-1]
    parts = [
        pairs[index][last].reshape(-1, cuts[index + 1] - cuts[index], width)
        for pairs in (near_pairs, far_pairs)
        for last in range(2)
        for index in range(3)
    ]
    whole = pl.BlockSpec(memory_space=pltpu.VMEM)
    anywhere = pl.BlockSpec(memory_space=pl.ANY)
    tall = jax.ShapeDtypeStruct((LEN, width), bf16)
    return pl.pallas_call(
        lambda *refs: project_kernel(high_count, panel_rows, cuts, *refs),
        in_specs=[pl.BlockSpec(memory_space=pltpu.SMEM)] + [anywhere] * 12 + [whole] * 4,
        out_specs=[whole] * 3 + [anywhere],
        out_shape=[tall] * 3 + [jax.ShapeDtypeStruct((8 * D, width), bf16)],
        scratch_shapes=[
            pltpu.VMEM((8 * D, width), bf16),
            pltpu.SemaphoreType.DMA((4,)),
            pltpu.SemaphoreType.DMA,
        ],
        compiler_params=pltpu.CompilerParams(vmem_limit_bytes=vmem_bytes),
        cost_estimate=pl.CostEstimate(
            flops=2 * LEN * 3 * D * width, bytes_accessed=48 * D * width, transcendentals=0
        ),
        name="project",
    )(slots, *parts, mine, other, cosine, sine)


def feed_kernel(n_ref, g_ref, w_ref, f_ref, d_ref, a_ref, u_ref):
    width = w_ref.shape[2]
    rows, grads = n_ref[...], g_ref[...]
    pre = [dot32(rows, w_ref[i]) for i in range(2)]
    act_grad = [dot32(grads, w_ref[2 + i]) for i in range(2)]
    acts, pre_grads = [], []
    for i in range(2):
        value = pre[i]
        square = value * value
        turn = jnp.tanh(0.7978845608028654 * (value + 0.044715 * (square * value)))
        share = 0.5 * (1.0 + turn)
        slope = share + (0.5 * value) * (1.0 - turn * turn) * (
            0.7978845608028654 + (3 * 0.044715 * 0.7978845608028654) * square
        )
        acts.append((value * share).astype(bf16))
        pre_grads.append((act_grad[i] * slope).astype(bf16))
        a_ref[:, i * width : (i + 1) * width] = acts[i]
        u_ref[:, i * width : (i + 1) * width] = pre_grads[i]
    f_ref[...] = (dot32(acts[0], w_ref[2], NT) + dot32(acts[1], w_ref[3], NT)).astype(f_ref.dtype)
    d_ref[...] = (dot32(pre_grads[0], w_ref[0], NT) + dot32(pre_grads[1], w_ref[1], NT)).astype(d_ref.dtype)


def feed(rows, grads, stacked, kind):
    half, width = rows.shape[0], stacked.shape[2]
    whole = pl.BlockSpec((half, D), lambda step: (0, 0))
    low, sums = jax.ShapeDtypeStruct((half, D), bf16), jax.ShapeDtypeStruct((half, D), kind)
    return pl.pallas_call(
        feed_kernel,
        grid=(1,),
        in_specs=[whole, whole, pl.BlockSpec((4, D, width), lambda step: (1, 0, 0))],
        out_specs=[whole] * 4,
        out_shape=[sums, sums, low, low],
        compiler_params=pltpu.CompilerParams(vmem_limit_bytes=vmem_bytes),
        cost_estimate=pl.CostEstimate(
            flops=2 * 4 * half * D * D, bytes_accessed=16 * D * width, transcendentals=half * D
        ),
        name="feed",
    )(rows, grads, stacked)


def inputs_grad_kernel(q_ref, k_ref, v_ref, w_ref, mine_ref, other_ref):
    half = mine_ref.shape[0]
    for start, out_ref in ((half, other_ref), (0, mine_ref)):
        rows = slice(start, start + half)
        total = dot32(q_ref[rows, :], w_ref[0], NT)
        total = total + dot32(k_ref[rows, :], w_ref[1], NT)
        total = total + dot32(v_ref[rows, :], w_ref[2], NT)
        out_ref[...] = total.astype(out_ref.dtype)


def inputs_grad(query_grad, key_grad, value_grad, stacked):
    width = stacked.shape[2]
    half = LEN // 2
    tall = pl.BlockSpec((LEN, width), lambda step: (0, 0))
    out = pl.BlockSpec((half, D), lambda step: (0, 0))
    return pl.pallas_call(
        inputs_grad_kernel,
        grid=(1,),
        in_specs=[tall] * 3 + [pl.BlockSpec((3, D, width), lambda step: (0, 0, 0))],
        out_specs=[out, out],
        out_shape=[jax.ShapeDtypeStruct((half, D), f32), jax.ShapeDtypeStruct((half, D), bf16)],
        compiler_params=pltpu.CompilerParams(vmem_limit_bytes=vmem_bytes),
        cost_estimate=pl.CostEstimate(
            flops=2 * 3 * LEN * D * width, bytes_accessed=12 * LEN * D, transcendentals=0
        ),
        name="inputs_grad",
    )(query_grad, key_grad, value_grad, stacked)


def gradients_kernel(high_count, panel_rows, cuts, lefts, rights, uses, slots_ref, *refs):
    in_count = sum(len(pieces) for pieces in lefts + rights)
    inputs, refs = refs[:in_count], refs[in_count:]
    parts, refs = refs[:12], refs[12:]
    left_held, right_held = refs[: len(lefts)], refs[len(lefts) : len(lefts) + len(rights)]
    turned, block_ref, in_sems, out_sems = refs[len(lefts) + len(rights) :]
    side = block_ref.shape[1]
    operands = [(held, pieces) for held, pieces in zip(left_held + right_held, lefts + rights)]

    def load(operand):
        held, pieces = operands[operand]
        return [
            pltpu.make_async_copy(
                inputs[which],
                held.at[pl.ds(row, inputs[which].shape[0]), pl.ds(column, inputs[which].shape[1])],
                in_sems.at[operand],
            )
            for row, column, which in pieces
        ]

    order = []
    for left, right, right_start in uses:
        for operand in (left, len(lefts) + right):
            if operand not in order:
                order.append(operand)
    for operand in order:
        for copy in load(operand):
            copy.start()
    ready = set()
    pieces = side // panel_rows
    block = 0
    for left, right, right_start in uses:
        for operand in (left, len(lefts) + right):
            if operand not in ready:
                held = operands[operand][0]
                pltpu.make_async_copy(held, held, in_sems.at[operand]).wait()
                ready.add(operand)
                if operand < len(lefts):
                    turned[left % 2] = held[...].T
        for left_start in range(0, D, side):
            place = block % 2
            if block >= 2:
                pltpu.make_async_copy(block_ref.at[place], block_ref.at[place], out_sems.at[place]).wait()
            block_ref[place] = dot32(
                turned[left % 2, left_start : left_start + side],
                right_held[right][:, right_start : right_start + side],
            ).astype(bf16)

            def send(piece, carry, block=block, place=place):
                slot = slots_ref[block * pieces + piece]
                for index in range(3):
                    far, last, lead = part_place(slot, index, high_count)
                    rows = cuts[index + 1] - cuts[index]
                    start = pl.multiple_of(piece * panel_rows + cuts[index], 16)
                    for which in range(4):

                        @pl.when(far * 2 + last == which)
                        def _():
                            pltpu.make_async_copy(
                                block_ref.at[place, pl.ds(start, rows)],
                                parts[which * 3 + index].at[lead],
                                out_sems.at[place],
                            ).start()

                return carry

            lax.fori_loop(0, pieces, send, 0)
            block += 1
    for place in range(2):
        pltpu.make_async_copy(block_ref.at[place], block_ref.at[place], out_sems.at[place]).wait()


def panel_gradients(lefts, rights, uses, slots, panel_rows, cuts, high_count, width):
    arrays, numbered = [], []
    for operands in (lefts, rights):
        made = []
        for pieces in operands:
            made.append([(row, column, len(arrays) + i) for i, (row, column, _) in enumerate(pieces)])
            arrays.extend(array for _, _, array in pieces)
        numbered.append(made)
    extent = lambda pieces: max(column + array.shape[1] for _, column, array in pieces)
    outs = [
        jax.ShapeDtypeStruct((4 * high_count, cuts[index + 1] - cuts[index], width), bf16)
        for _ in range(4)
        for index in range(3)
    ]
    outs = pl.pallas_call(
        lambda *refs: gradients_kernel(
            high_count, panel_rows, cuts, numbered[0], numbered[1], uses, *refs
        ),
        in_specs=[pl.BlockSpec(memory_space=pltpu.SMEM)]
        + [pl.BlockSpec(memory_space=pl.ANY)] * len(arrays),
        out_specs=[pl.BlockSpec(memory_space=pl.ANY)] * 12,
        out_shape=outs,
        scratch_shapes=[pltpu.VMEM((LEN, extent(pieces)), bf16) for pieces in list(lefts) + list(rights)]
        + [
            pltpu.VMEM((2, D, LEN), bf16),
            pltpu.VMEM((2, width, width), bf16),
            pltpu.SemaphoreType.DMA((len(lefts) + len(rights),)),
            pltpu.SemaphoreType.DMA((2,)),
        ],
        compiler_params=pltpu.CompilerParams(vmem_limit_bytes=vmem_bytes),
        cost_estimate=pl.CostEstimate(
            flops=2 * LEN * len(uses) * D * width,
            bytes_accessed=24 * LEN * D,
            transcendentals=0,
        ),
        name="gradients",
    )(slots, *arrays)
    shaped = [out.reshape((2, 2, high_count) + out.shape[1:]) for out in outs]
    pairs = lambda far: [(shaped[far * 6 + index], shaped[far * 6 + 3 + index]) for index in range(3)]
    return pairs(0), pairs(1)


def vector_parts(vectors):
    kernel_size = KERNEL * TEXT
    pieces = [vectors[:kernel_size].reshape(KERNEL, TEXT)]
    offset = kernel_size
    for extent in (TEXT, TEXT, TEXT, TEXT, TXT_FF, TXT_FF, TXT_FF, 6 * D):
        pieces.append(vectors[offset : offset + extent])
        offset = offset + extent
    return pieces


def normalise(values):
    center = values - jnp.mean(values, axis=-1, keepdims=True)
    variance = jnp.mean(center * center, axis=-1, keepdims=True)
    scale = lax.rsqrt(variance + norm_eps)
    return center * scale, scale


def normalise_back(grad, normed, scale):
    mean_grad = jnp.mean(grad, axis=-1, keepdims=True)
    mean_dot = jnp.mean(grad * normed, axis=-1, keepdims=True)
    return scale * (grad - mean_grad - normed * mean_dot)


def gelu_parts(values):
    share = 0.5 * (1.0 + lax.erf(values * 0.7071067811865476))
    density = 0.3989422804014327 * jnp.exp(-0.5 * values * values)
    return share, density


def gelu_tanh(values):
    return jax.nn.gelu(values, approximate=True)


def moments(gradient, first_moment, second_moment):
    first_new = beta_one * first_moment + (1.0 - beta_one) * gradient
    second_new = beta_two * second_moment + (1.0 - beta_two) * gradient * gradient
    bias_first = 1.0 - beta_one**STEP
    bias_second = 1.0 - beta_two**STEP
    direction = first_new / bias_first / (jnp.sqrt(second_new / bias_second) + adam_eps)
    return (first_new, second_new, direction)


def apply_step(weight, direction, rate):
    return weight - rate * (direction + weight_decay * weight)


def rotary_tables(core, half):
    position = ((jnp.arange(LEN) + core * half) % LEN).astype(f32)
    frequency = 10000.0 ** (-jnp.arange(HEAD // 2, dtype=f32) * 2.0 / HEAD)
    angle = position[:, None] * frequency[None, :]
    cosine, sine = jnp.cos(angle), jnp.sin(angle)
    return (
        jnp.concatenate([cosine] * 4, axis=1),
        jnp.concatenate([-sine, sine, -sine, sine], axis=1),
    )


def take_blocks(blocks, index):
    return jnp.take(blocks, index, axis=0, mode="clip")


def both_halves(mine):
    return jnp.concatenate([mine, swap_core(mine)], axis=0)


def sum_halves(multiply, rows, half):
    theirs = multiply(rows[half:]).astype(bf16)
    received = swap_core(theirs)
    return multiply(rows[:half]) + received.astype(f32)


def body(
    mel_frames,
    text_features,
    cotangent,
    time_embedding,
    lengths,
    group_ids,
    text_keep,
    owner_list,
    soap_master,
    soap_first,
    soap_second,
    left_basis,
    right_basis,
    text_matrices,
    text_first,
    text_second,
    modulation_weight,
    modulation_first,
    modulation_second,
    vectors,
    vector_first,
    vector_second,
):
    count = lax.axis_size("dp")
    me, core = lax.axis_index("dp"), lax.axis_index("mp")
    half = LEN // 2
    utterances = lengths.shape[0] * count
    panel_rows, width = soap_master.shape
    share_rows = modulation_weight.shape[0]
    text_rows = text_matrices.shape[0]
    text_half = text_rows // 2
    relative = jnp.arange(count) ^ me

    high_count = count // 16
    cuts, text_cuts = third_cuts(panel_rows), third_cuts(text_half)
    silu_time = jax.nn.silu(time_embedding.astype(f32)).astype(bf16)
    time_rows = lax.dynamic_slice_in_dim(silu_time, me * share_rows, share_rows, 1)
    weight_half = lax.dynamic_slice_in_dim(modulation_weight, core * 3 * D, 3 * D, 1).astype(bf16)
    own_rows = lax.dynamic_slice_in_dim(text_matrices, core * text_half, text_half, 0)
    text_held = spread_high(own_rows.astype(bf16))
    near_held = spread_high(soap_master.astype(bf16))
    text_far = swap_bit(text_held, 3)
    near = spread_step(split_rows(near_held, cuts), 0)
    text_far, near_held, near_a, near_b, near_c = tie(text_far, near_held, *near)
    near = [near_a, near_b, near_c]
    text_parts = split_rows(jnp.concatenate([text_held, text_far], axis=0), text_cuts)
    far_held = swap_bit(near_held, 3)
    text_parts = spread_step(text_parts, 0)
    partial = dot32(time_rows, weight_half)
    *text_parts, partial = tie(*text_parts, partial)
    text_parts = spread_step(text_parts, 1)
    near = spread_step(near, 1)
    *text_parts, partial = tie(*text_parts, partial)
    text_pairs = spread_last(text_parts)
    partial = partial + swap_bit(partial, 0)
    text_tied = tie(*[part for pair in text_pairs for part in pair], *near, far_held, partial)
    text_pairs = [text_tied[0:2], text_tied[2:4], text_tied[4:6]]
    near, far_held, partial = list(text_tied[6:9]), text_tied[9], text_tied[10]
    near_pairs = spread_last(near)
    far = spread_step(split_rows(far_held, cuts), 0)
    partial = partial + swap_bit(partial, 1)
    *far, partial = tie(*far, partial)
    far = spread_step(far, 1)
    partial = partial + swap_bit(partial, 2)
    *far, partial = tie(*far, partial)
    far_pairs = spread_last(far)
    partial = partial + swap_bit(partial, 3)
    for bit in range(4, bit_count(count)):
        partial = partial + swap_bit(partial, bit)
    modulation_half = partial
    text_half_all = spread_close([[part for part in pair] for pair in text_pairs])
    text_half_all = text_half_all.reshape(2, high_count, 2, 2, 2, text_half, D)
    text_half_all = jnp.moveaxis(text_half_all, 0, 1).reshape(count, text_half, D)
    text_other = swap_core(text_half_all)
    texts = take_blocks(by_core(core, text_half_all, text_other, axis=1), relative)
    texts = texts.reshape(3 * TEXT, D)
    expand_weight, shrink_rows, text_to_model = texts[:TEXT], texts[TEXT : 2 * TEXT], texts[2 * TEXT :]
    modulation = by_core(core, modulation_half, swap_core(modulation_half), axis=1)
    (
        kernel,
        conv_bias,
        norm_gain,
        norm_bias,
        out_bias,
        in_bias,
        grn_gamma,
        grn_beta,
        modulation_bias,
    ) = vector_parts(vectors)
    group = group_ids[0]
    modulation_row = lax.dynamic_slice_in_dim(modulation, group, 1, 0) + modulation_bias
    shift_one, scale_one, gate_one, shift_two, scale_two, gate_two = (
        modulation_row[:, i * D : (i + 1) * D] for i in range(6)
    )

    first = core * half
    margin = KERNEL // 2
    edge = 8
    keep_all = jnp.pad(text_keep.astype(f32), (edge, edge))[:, None]
    text_all = jnp.pad(text_features, ((edge, edge), (0, 0)))
    window = lax.dynamic_slice_in_dim(text_all, first, half + 2 * edge, 0).astype(f32)
    window = window * lax.dynamic_slice_in_dim(keep_all, first, half + 2 * edge, 0)
    keep = lax.dynamic_slice_in_dim(keep_all, first + edge, half, 0)
    masked_text = window[edge : edge + half]
    taps = [window[edge - margin + j : edge - margin + j + half] for j in range(KERNEL)]
    mixed = conv_bias[None, :]
    for j in range(KERNEL):
        mixed = mixed + taps[j] * kernel[j][None, :]
    conv_normed, conv_scale = normalise(mixed)
    normed_low = (conv_normed * norm_gain + norm_bias).astype(bf16)
    expand_pre = dot32(normed_low, expand_weight) + in_bias
    share, density = gelu_parts(expand_pre)
    hidden = expand_pre * share
    energy_sum = jnp.sum(hidden * hidden, axis=0, keepdims=True)
    energy = jnp.sqrt(energy_sum + swap_core(energy_sum))
    energy_mean = jnp.mean(energy, axis=-1, keepdims=True) + norm_eps
    ratio = energy / energy_mean
    grn_low = (grn_gamma * (hidden * ratio) + grn_beta + hidden).astype(bf16)
    text_out = (masked_text + dot32(grn_low, shrink_rows, NT) + out_bias) * keep
    text_low = text_out.astype(bf16)
    mel_mine = lax.dynamic_slice_in_dim(mel_frames, first, half, 0).astype(f32)
    stream = mel_mine + dot32(text_low, text_to_model)

    normed_one, scale_norm_one = normalise(stream)
    first_mine = (normed_one * (1.0 + scale_one) + shift_one).astype(bf16)
    first_other = swap_core(first_mine)
    cosine, sine = rotary_tables(core, half)
    position = (jnp.arange(LEN) + first) % LEN
    bias = jnp.where(position < lengths[0], 0.0, -1e30).astype(bf16)
    bias = jnp.broadcast_to(bias[:, None], (LEN, PAIR))
    queries, keys, value_rows, stacked = project(
        near_pairs, far_pairs, owner_list ^ me, panel_rows, cuts, first_mine, first_other, cosine, sine
    )
    stacked = stacked.reshape(8, D, width)
    attended, query_aug = attend_forward(queries, keys, value_rows, bias)
    attention_out = sum_halves(lambda rows: dot32(rows, stacked[3], NT), attended, half)
    stream_one = stream + gate_one * attention_out

    normed_two, scale_norm_two = normalise(stream_one)
    second_mine = (normed_two * (1.0 + scale_two) + shift_two).astype(bf16)
    second_other = swap_core(second_mine)
    cot_mine = lax.dynamic_slice_in_dim(cotangent, first, half, 0)
    cot_other = lax.dynamic_slice_in_dim(cotangent, half - first, half, 0)
    out_grad = cot_mine.astype(f32)
    hidden_mine = (gate_two * out_grad).astype(bf16)
    hidden_other = (gate_two * cot_other.astype(f32)).astype(bf16)
    their_out, their_grad, act_other, pre_other = feed(second_other, hidden_other, stacked, bf16)
    their_out, their_grad = swap_core(their_out), swap_core(their_grad)
    my_out, my_grad, act_mine, pre_mine = feed(second_mine, hidden_mine, stacked, f32)
    unit_out = my_out + their_out.astype(f32)
    normed_two_grad = my_grad + their_grad.astype(f32)
    output_mine = (stream_one + gate_two * unit_out).astype(bf16)
    block_output = by_core(core, output_mine, swap_core(output_mine))
    gate_two_grad = jnp.sum(out_grad * unit_out, axis=0)
    shift_two_grad = jnp.sum(normed_two_grad, axis=0)
    scale_two_grad = jnp.sum(normed_two_grad * normed_two, axis=0)
    stream_one_grad = out_grad + normalise_back(
        normed_two_grad * (1.0 + scale_two), normed_two, scale_norm_two
    )

    gate_one_grad = jnp.sum(stream_one_grad * attention_out, axis=0)
    TN = (((0,), (0,)), ((), ()))
    attention_mine = (gate_one * stream_one_grad).astype(bf16)
    attention_other = swap_core(attention_mine)
    query_grad, key_grad, value_grad = attend_backward(
        query_aug, keys, value_rows, attended, attention_mine, attention_other, stacked, cosine, sine, bias
    )
    my_grad, their_grad = inputs_grad(query_grad, key_grad, value_grad, stacked)
    their_grad = swap_core(their_grad)
    halves = lambda mine, other: [(0, 0, mine), (half, 0, other)]
    whole = lambda array: [(0, 0, array)]
    near_pairs, far_pairs = panel_gradients(
        [
            halves(first_mine, first_other),
            halves(attention_mine, attention_other),
            halves(second_mine, second_other),
            halves(hidden_mine, hidden_other),
        ],
        [
            whole(query_grad),
            whole(key_grad),
            whole(value_grad),
            whole(attended),
            halves(pre_mine, pre_other),
            halves(act_mine, act_other),
        ],
        ((0, 0, 0), (0, 1, 0), (0, 2, 0), (1, 3, 0), (2, 4, 0), (2, 4, width), (3, 5, 0), (3, 5, width)),
        owner_list ^ me,
        panel_rows,
        cuts,
        high_count,
        width,
    )
    normed_one_grad = my_grad + their_grad.astype(f32)
    far = fold_first(far_pairs)
    far = fold_next(tie(*far), 1)
    far = fold_next(tie(*far), 0)
    near = fold_first(near_pairs)
    *far, near_a, near_b, near_c = tie(*far, *near)
    far_sum = swap_bit(jnp.concatenate(far, axis=-2), 3)
    near = fold_next([near_a, near_b, near_c], 1)
    near_last = tie(*near)

    shift_one_grad = jnp.sum(normed_one_grad, axis=0)
    scale_one_grad = jnp.sum(normed_one_grad * normed_one, axis=0)
    mel_grad_mine = stream_one_grad + normalise_back(
        normed_one_grad * (1.0 + scale_one), normed_one, scale_norm_one
    )
    mel_gradient = by_core(core, mel_grad_mine, swap_core(mel_grad_mine))

    stream_grad = mel_grad_mine.astype(bf16)
    text_to_model_grad = dot32(text_low, stream_grad, TN)
    shrink_grad = dot32(stream_grad, text_to_model, NT) * keep
    out_bias_grad = jnp.sum(shrink_grad, axis=0)
    shrink_low = shrink_grad.astype(bf16)
    shrink_rows_grad = dot32(shrink_low, grn_low, TN)
    grn_grad = dot32(shrink_low, shrink_rows)
    hidden_dot = jnp.sum(grn_grad * hidden, axis=0, keepdims=True)
    hidden_dot_all = hidden_dot + swap_core(hidden_dot)
    ratio_grad = grn_gamma * hidden_dot_all
    energy_grad = ratio_grad / energy_mean - jnp.mean(ratio_grad * ratio, axis=-1, keepdims=True) / energy_mean
    gamma_grad = (ratio * hidden_dot)[0]
    beta_grad = jnp.sum(grn_grad, axis=0)
    hidden_grad = grn_grad * (grn_gamma * ratio + 1.0) + hidden * (energy_grad / energy)
    expand_grad = hidden_grad * (share + expand_pre * density)
    in_bias_grad = jnp.sum(expand_grad, axis=0)
    expand_low = expand_grad.astype(bf16)
    expand_weight_grad = dot32(normed_low, expand_low, TN)
    text_grads = jnp.concatenate(
        [grad.astype(bf16) for grad in (expand_weight_grad, shrink_rows_grad, text_to_model_grad)], axis=0
    ).reshape(count, 2, text_half, D)
    text_keep_half = lax.dynamic_index_in_dim(text_grads, core, 1, keepdims=False)
    text_send_half = lax.dynamic_index_in_dim(text_grads, 1 - core, 1, keepdims=False)
    text_sum = add_low(text_keep_half, swap_core(text_send_half))
    text_full = take_blocks(text_sum, relative).reshape(high_count, 2, 2, 2, 2, text_half, D)
    text_full = text_full.transpose(1, 0, 2, 3, 4, 5, 6).reshape(2 * high_count, 2, 2, 2, text_half, D)
    normed_text_grad = dot32(expand_low, expand_weight, NT)
    gain_grad = jnp.sum(normed_text_grad * conv_normed, axis=0)
    norm_bias_grad = jnp.sum(normed_text_grad, axis=0)
    mixed_grad = normalise_back(normed_text_grad * norm_gain, conv_normed, conv_scale)
    conv_bias_grad = jnp.sum(mixed_grad, axis=0)
    kernel_grad = jnp.stack([jnp.sum(mixed_grad * taps[j], axis=0) for j in range(KERNEL)])
    border = lax.dynamic_slice_in_dim(mixed_grad, (1 - core) * (half - edge), edge, 0)
    border = swap_core(border)
    before = jnp.where(core == 1, border, 0.0)
    after = jnp.where(core == 0, border, 0.0)
    wide_grad = jnp.concatenate([before, mixed_grad, after], axis=0)
    masked_grad = shrink_grad
    for j in range(KERNEL):
        start = edge + margin - j
        masked_grad = masked_grad + wide_grad[start : start + half] * kernel[j][None, :]
    text_grad_mine = masked_grad * keep
    text_gradient = by_core(core, text_grad_mine, swap_core(text_grad_mine))

    vector_mine = jnp.concatenate(
        [
            kernel_grad.reshape(-1),
            conv_bias_grad,
            gain_grad,
            norm_bias_grad,
            out_bias_grad,
            in_bias_grad,
            gamma_grad,
            beta_grad,
        ]
    )
    token = jnp.concatenate(
        [shift_one_grad, scale_one_grad, gate_one_grad, shift_two_grad, scale_two_grad, gate_two_grad]
    )
    vector_half = vector_mine.shape[0] // 2
    token_half = 3 * D

    def half_of(which):
        return jnp.concatenate(
            [
                lax.dynamic_slice_in_dim(vector_mine, which * vector_half, vector_half, 0),
                lax.dynamic_slice_in_dim(token, which * token_half, token_half, 0),
            ]
        )

    small = half_of(core) + swap_core(half_of(1 - core))
    in_group = (jnp.arange(GROUPS) == group).astype(f32)
    table = in_group[:, None] * small[None, vector_half:]
    small = jnp.concatenate([small[:vector_half], table.reshape(-1)]).reshape(-1, 128)

    text_held = [[2, 1, 0] for _ in range(3)]
    text_parts = fold_step(split_rows(text_full, text_cuts), text_held, 2)
    small = small + swap_bit(small, 0)
    *text_parts, small = tie(*text_parts, small)
    text_parts = fold_step(text_parts, text_held, 1)
    small = small + swap_bit(small, 1)
    near = fold_next(near_last, 0)
    *text_parts, small = tie(*text_parts, small)
    text_parts = fold_step(text_parts, text_held, 0)
    small = small + swap_bit(small, 2)
    *text_parts, small = tie(*text_parts, small)
    text_near = jnp.concatenate(text_parts, axis=-2)
    text_near, text_far = text_near[:high_count], text_near[high_count:]
    own_text = fold_high(text_near.astype(f32) + swap_bit(text_far, 3).astype(f32))
    small = small + swap_bit(small, 3)
    for bit in range(4, bit_count(count)):
        small = small + swap_bit(small, bit)
    own_text = by_core(core, own_text, swap_core(own_text))
    own_panel = fold_high(jnp.concatenate(near, axis=-2).astype(f32) + far_sum.astype(f32))
    small = by_core(core, small[None], swap_core(small)[None]).reshape(2, -1)
    vector_sum = small[:, :vector_half].reshape(-1)
    tables = small[:, vector_half:].reshape(2, GROUPS, token_half)
    modulation_grad = jnp.concatenate([tables[0], tables[1]], axis=1)
    vector_gradient = jnp.concatenate([vector_sum, jnp.sum(modulation_grad, axis=0)]) / utterances
    share_grad = (
        lax.dot_general(
            time_rows, modulation_grad.astype(bf16), TN, preferred_element_type=f32
        )
        / utterances
    )

    own_panel = own_panel / utterances
    own_text = own_text / utterances
    rotated = jnp.dot(jnp.dot(left_basis.T, own_panel, precision=solver), right_basis, precision=solver)
    soap_moment, soap_variance, soap_direction = moments(rotated, soap_first, soap_second)
    turned_back = jnp.dot(
        jnp.dot(left_basis, soap_direction, precision=solver), right_basis.T, precision=solver
    )
    soap_weights = apply_step(soap_master, turned_back, learn_rate)
    text_moment, text_variance, text_direction = moments(own_text, text_first, text_second)
    text_weights = apply_step(text_matrices, text_direction, learn_rate)
    modulation_moment, modulation_variance, modulation_direction = moments(
        share_grad, modulation_first, modulation_second
    )
    modulation_weights = apply_step(modulation_weight, modulation_direction, learn_rate)
    vector_moment, vector_variance, vector_direction = moments(
        vector_gradient, vector_first, vector_second
    )
    vector_weights = apply_step(vectors, vector_direction, vector_rate)
    return (
        block_output,
        mel_gradient,
        text_gradient,
        soap_weights,
        soap_moment,
        soap_variance,
        text_weights,
        text_moment,
        text_variance,
        modulation_weights,
        modulation_moment,
        modulation_variance,
        vector_weights,
        vector_moment,
        vector_variance,
    )


def solution(mesh):
    rows, quarter, same = P("dp", None), P("dp", "mp"), P()
    return jax.shard_map(
        body,
        mesh=mesh,
        in_specs=(
            (rows,) * 3 + (same,) + (P("dp"),) * 3 + (same,) + (quarter,) * 5 + (rows,) * 6 + (same,) * 3
        ),
        out_specs=(rows,) * 3 + (quarter,) * 3 + (rows,) * 6 + (same,) * 3,
        check_vma=False,
    )
```

```python
import jax
import numpy as np
import jax.numpy as jnp
from jax import lax
from jax.experimental import pallas as pl
from jax.experimental.pallas import tpu as pltpu
from jax.sharding import PartitionSpec as P

D = 1024
HEAD = 64
TEXT = 512
TXT_FF = 1024
KERNEL = 7
LEN = 1024
GROUPS = 8
STEP = 10

f32 = jnp.float32
bf16 = jnp.bfloat16
beta_one = 0.9
beta_two = 0.99
adam_eps = 1e-08
weight_decay = 0.01
learn_rate = 0.03
vector_rate = 0.3
norm_eps = 1e-06
solver = lax.Precision.HIGH


def swap_core(array):
    return lax.ppermute(array, "mp", [(0, 1), (1, 0)])


def swap_bits(array, bits):
    count = lax.axis_size("dp")
    pairs = [
        (i * 2 + core, (i ^ (1 << bits[core])) * 2 + core) for i in range(count) for core in range(2)
    ]
    return lax.ppermute(array, ("dp", "mp"), pairs)


def swap_bit(array, bit):
    return swap_bits(array, (bit, bit))


def by_core(core, mine, other, axis=0):
    return jnp.where(
        core == 0,
        jnp.concatenate([mine, other], axis=axis),
        jnp.concatenate([other, mine], axis=axis),
    )


def bit_count(count):
    return count.bit_length() - 1


def row_cuts(rows):
    return (0, (rows * 2 + 24) // 48 * 16, rows)


axis_orders = (((0, 1, 2), (1, 2, 0)), ((2, 0, 1), (2, 0, 1)))
text_orders = ((2, 0, 1), (2, 1, 0))


def phase_bits(orders, phase):
    return tuple(order[phase] for order in orders)


def tie(*values):
    return lax.optimization_barrier(values)


def tie_lists(*lists):
    flat = [value for values in lists for value in values]
    flat = list(lax.optimization_barrier(tuple(flat)))
    out = []
    for values in lists:
        out.append(flat[: len(values)])
        flat = flat[len(values) :]
    return out


def split_rows(array, cuts):
    return [array[..., cuts[i] : cuts[i + 1], :] for i in range(len(cuts) - 1)]


def spread(part, orders, phase):
    return jnp.stack([part, swap_bits(part, phase_bits(orders, phase))])


def spread_step(parts, phase):
    return [spread(part, axis_orders[index], phase) for index, part in enumerate(parts)]


def spread_last(parts):
    return [(part, swap_bits(part, phase_bits(axis_orders[index], 2))) for index, part in enumerate(parts)]


def spread_high(block):
    held = block[None]
    for bit in range(4, bit_count(lax.axis_size("dp"))):
        held = jnp.concatenate([held, swap_bit(held, bit)], axis=0)
    return held


def add_low(left, right):
    return (left.astype(f32) + right.astype(f32)).astype(bf16)


def receive(sends, phase):
    return [swap_bits(send, phase_bits(axis_orders[index], phase)) for index, send in enumerate(sends)]


def add_all(keeps, received):
    return [add_low(keep, other) for keep, other in zip(keeps, received)]


def firsts(parts):
    return [part[0] for part in parts]


def seconds(parts):
    return [part[1] for part in parts]


def fold(part, orders, phase):
    return add_low(part[0], swap_bits(part[1], phase_bits(orders, phase)))


def fold_high(total):
    count = total.shape[0]
    if count == 1:
        return total[0]
    for bit in range(bit_count(count) - 1, -1, -1):
        half = 1 << bit
        total = total[:half] + swap_bit(total[half:].astype(bf16), bit + 4).astype(f32)
    return total[0]


def bit_of(values, which):
    return (values >> which) & 1


def lead_place(slots, order, high_count):
    return (bit_of(slots, order[1]) * 2 + bit_of(slots, order[0])) * high_count + (slots >> 4)


def panel_places(core, slots, high_count, apart):
    rows = []
    for orders in axis_orders:
        far = bit_of(slots, 3)
        which = [bit_of(slots, order[2]) + 2 * far * apart for order in orders]
        lead = [
            lead_place(slots, order, high_count)
            if apart
            else (bit_of(slots, order[1]) * 2 + bit_of(slots, order[0])) * 2 * high_count
            + far * high_count
            + (slots >> 4)
            for order in orders
        ]
        rows += [jnp.where(core == 0, *which), jnp.where(core == 0, *lead)]
    return jnp.concatenate(rows).astype(jnp.int32)


def text_places(core, slots, high_count):
    places = []
    for order in text_orders:
        high = bit_of(slots, 3) * high_count + (slots >> 4)
        places.append(
            ((bit_of(slots, order[2]) * 2 + bit_of(slots, order[1])) * 2 + bit_of(slots, order[0]))
            * (2 * high_count)
            + high
        )
    return jnp.where(core == 0, *places).astype(jnp.int32)


def text_slots(core, places, high_count):
    lead, rest = places // (2 * high_count), places % (2 * high_count)
    high = ((rest // high_count) << 3) | ((rest % high_count) << 4)
    slots = []
    for order in text_orders:
        low = (bit_of(lead, 2) << order[2]) | (bit_of(lead, 1) << order[1]) | (bit_of(lead, 0) << order[0])
        slots.append(high | low)
    return jnp.where(core == 0, *slots)


NT = (((1,), (1,)), ((), ()))
NN = (((1,), (0,)), ((), ()))
TN = (((0,), (0,)), ((), ()))
ROWS = 256
PAIR = 2 * HEAD
vmem_bytes = 48 * 1024 * 1024


def dot32(left, right, dims=NN):
    return lax.dot_general(left, right, dims, preferred_element_type=f32)


def three_terms(values):
    high = values.astype(bf16).astype(f32)
    rest = values - high
    middle = rest.astype(bf16).astype(f32)
    return high, middle, rest - middle


def rotate(values, cosine, sine, lane):
    partner = jnp.where(
        lane % HEAD < HEAD // 2,
        pltpu.roll(values, PAIR - HEAD // 2, 1),
        pltpu.roll(values, HEAD // 2, 1),
    )
    return values * cosine + partner * sine


def attend_kernel(q_ref, k_ref, v_ref, bias_ref, o_ref, qa_ref):
    lane = lax.broadcasted_iota(jnp.int32, (LEN, PAIR), 1)
    lane_rows = lax.broadcasted_iota(jnp.int32, (ROWS, PAIR), 1)
    row_index = lax.broadcasted_iota(jnp.int32, (PAIR, ROWS), 0)
    q_wide = q_ref[...].astype(f32)
    k_wide = k_ref[...].astype(f32)
    values_t = v_ref[...].T
    bias = bias_ref[...].astype(f32)
    keys = []
    for head in range(2):
        own = lane // HEAD == head
        spare = (1 - head) * HEAD
        keys.append(
            jnp.where(own, k_wide, jnp.where(lane == spare, bias, 0.0)).astype(bf16)
        )
        qa_ref[:, head * PAIR : (head + 1) * PAIR] = jnp.where(
            own, q_wide, jnp.where(lane == spare, 1.0, 0.0)
        ).astype(bf16)
    steps = [(block, head) for block in range(LEN // ROWS) for head in range(2)]

    def scores_of(step):
        block, head = step
        rows = slice(block * ROWS, (block + 1) * ROWS)
        return dot32(keys[head], qa_ref[rows, head * PAIR : (head + 1) * PAIR], NT)

    following = scores_of(steps[0])
    for position, (block, head) in enumerate(steps):
        scores = following
        if position + 1 < len(steps):
            following = scores_of(steps[position + 1])
        rows = slice(block * ROWS, (block + 1) * ROWS)
        if head == 0:
            outs, extra = [], jnp.zeros((PAIR, ROWS), f32)
        spare = (1 - head) * HEAD
        highest = jnp.max(scores, axis=0, keepdims=True)
        weights = jnp.exp(scores - highest)
        total = jnp.sum(weights, axis=0, keepdims=True)
        out_t = dot32(values_t[head * HEAD : (head + 1) * HEAD], weights.astype(bf16))
        outs.append(out_t / total)
        for place, term in enumerate(three_terms(highest + jnp.log(total))):
            extra = jnp.where(row_index == spare + 1 + place, -term, extra)
        if head == 0:
            continue
        o_ref[rows, :] = jnp.concatenate(outs, axis=0).T.astype(bf16)
        extra_t = extra.T
        for head in range(2):
            spare = (1 - head) * HEAD
            columns = slice(head * PAIR, (head + 1) * PAIR)
            is_extra = (lane_rows > spare) & (lane_rows < spare + 4)
            qa_ref[rows, columns] = jnp.where(
                is_extra, extra_t, qa_ref[rows, columns].astype(f32)
            ).astype(bf16)


def attend_forward(queries, keys, values, bias):
    width = values.shape[1]
    pairs = width // PAIR
    tall = lambda columns: pl.BlockSpec((LEN, columns), lambda pair: (0, pair))
    whole = pl.BlockSpec((LEN, PAIR), lambda pair: (0, 0))
    return pl.pallas_call(
        attend_kernel,
        grid=(pairs,),
        in_specs=[tall(PAIR), tall(PAIR), tall(PAIR), whole],
        out_specs=[tall(PAIR), tall(2 * PAIR)],
        out_shape=[
            jax.ShapeDtypeStruct((LEN, width), bf16),
            jax.ShapeDtypeStruct((LEN, 2 * width), bf16),
        ],
        compiler_params=pltpu.CompilerParams(vmem_limit_bytes=vmem_bytes),
        cost_estimate=pl.CostEstimate(
            flops=2 * 4 * LEN * LEN * width * 4,
            bytes_accessed=6 * LEN * width * 2,
            transcendentals=LEN * LEN * width // HEAD,
        ),
        name="attend",
    )(queries, keys, values, bias)


def attend_back_kernel(
    qa_ref, kr_ref, v_ref, o_ref, mine_ref, other_ref, weight_ref, cos_ref, sin_ref, bias_ref,
    dq_ref, dk_ref, dv_ref, doa_ref, dka_ref, dva_ref,
):
    lane = lax.broadcasted_iota(jnp.int32, (LEN, PAIR), 1)
    lane_rows = lax.broadcasted_iota(jnp.int32, (ROWS, PAIR), 1)
    cosine, sine = cos_ref[...], sin_ref[...]
    k_wide = kr_ref[...].astype(f32)
    keys_t = kr_ref[...].T
    v_wide = v_ref[...].astype(f32)
    do_wide = jnp.concatenate(
        [dot32(ref[...], weight_ref[0]).astype(bf16).astype(f32) for ref in (mine_ref, other_ref)],
        axis=0,
    )
    bias = bias_ref[...].astype(f32)
    product = do_wide * o_ref[...].astype(f32)
    keys, values = [], []
    for head in range(2):
        own = lane // HEAD == head
        spare = (1 - head) * HEAD
        is_extra = (lane > spare) & (lane < spare + 4)
        ones = jnp.where(is_extra, 1.0, 0.0)
        keys.append(
            jnp.where(own, k_wide, jnp.where(lane == spare, bias, ones)).astype(bf16)
        )
        values.append(jnp.where(own, v_wide, ones).astype(bf16))
        row_dot = jnp.sum(jnp.where(own, product, 0.0), axis=1, keepdims=True)
        grad = jnp.where(own, do_wide, 0.0)
        for place, term in enumerate(three_terms(row_dot)):
            grad = jnp.where(lane == spare + 1 + place, -term, grad)
        doa_ref[:, head * PAIR : (head + 1) * PAIR] = grad.astype(bf16)
    for block in range(LEN // ROWS):
        rows = slice(block * ROWS, (block + 1) * ROWS)
        turned = []
        for head in range(2):
            columns = slice(head * PAIR, (head + 1) * PAIR)
            q_block = qa_ref[rows, columns]
            do_block = doa_ref[rows, columns]
            probs = jnp.exp(dot32(keys[head], q_block, NT))
            prob_grad = dot32(values[head], do_block, NT)
            score_grad = (probs * prob_grad).astype(bf16)
            dv_part = dot32(probs.astype(bf16), do_block)
            dk_part = dot32(score_grad, q_block)
            if block == 0:
                dva_ref[:, columns] = dv_part
                dka_ref[:, columns] = dk_part
            else:
                dva_ref[:, columns] += dv_part
                dka_ref[:, columns] += dk_part
            turned.append(dot32(keys_t[head * HEAD : (head + 1) * HEAD], score_grad))
        dq = jnp.concatenate(turned, axis=0).T * 0.125
        dq_ref[rows, :] = rotate(dq, cosine[rows], -sine[rows], lane_rows).astype(bf16)
    first = lane < HEAD
    dk = jnp.where(first, dka_ref[:, :PAIR], dka_ref[:, PAIR:])
    dk_ref[...] = rotate(dk, cosine, -sine, lane).astype(bf16)
    dv_ref[...] = jnp.where(first, dva_ref[:, :PAIR], dva_ref[:, PAIR:]).astype(bf16)


def attend_backward(queries, keys, values, outputs, grad_mine, grad_other, stacked, cosine, sine, bias):
    width = values.shape[1]
    pairs = width // PAIR
    tall = lambda columns: pl.BlockSpec((LEN, columns), lambda pair: (0, pair))
    whole = lambda shape: pl.BlockSpec(shape, lambda pair: (0, 0))
    return pl.pallas_call(
        attend_back_kernel,
        grid=(pairs,),
        in_specs=[tall(2 * PAIR)]
        + [tall(PAIR)] * 3
        + [whole(grad_mine.shape)] * 2
        + [pl.BlockSpec((1, D, PAIR), lambda pair: (3, 0, pair))]
        + [whole((LEN, PAIR))] * 3,
        out_specs=[tall(PAIR)] * 3,
        out_shape=[jax.ShapeDtypeStruct((LEN, width), bf16)] * 3,
        scratch_shapes=[
            pltpu.VMEM((LEN, 2 * PAIR), bf16),
            pltpu.VMEM((LEN, 2 * PAIR), f32),
            pltpu.VMEM((LEN, 2 * PAIR), f32),
        ],
        compiler_params=pltpu.CompilerParams(vmem_limit_bytes=vmem_bytes),
        cost_estimate=pl.CostEstimate(
            flops=2 * 10 * LEN * LEN * width * 4,
            bytes_accessed=12 * LEN * width * 2,
            transcendentals=LEN * LEN * width // HEAD,
        ),
        name="attend_back",
    )(queries, keys, values, outputs, grad_mine, grad_other, stacked, cosine, sine, bias)


PARTS = 2


def part_copies(table_ref, panels, panel, cuts, start_row, copy, arrays=4):
    for index in range(PARTS):
        which = table_ref[2 * index * panels + panel]
        lead = table_ref[(2 * index + 1) * panels + panel]
        start = pl.multiple_of(start_row + cuts[index], 16)
        for number in range(arrays):

            @pl.when(which == number)
            def _():
                copy(number * PARTS + index, lead, start, cuts[index + 1] - cuts[index])


def project_kernel(panel_rows, cuts, slots_ref, *refs):
    parts, refs = refs[: 2 * PARTS], refs[2 * PARTS :]
    mine_ref, other_ref, cos_ref, sin_ref, q_ref, k_ref, v_ref, out_ref, held, in_sems, out_sem = refs
    per_block = D // panel_rows

    def fetch(panel, carry):
        group = jnp.minimum(panel // per_block, 3)

        def copy(number, lead, start, rows):
            pltpu.make_async_copy(
                parts[number].at[lead], held.at[pl.ds(start, rows)], in_sems.at[group]
            ).start()

        part_copies(slots_ref, 8 * per_block, panel, cuts, panel * panel_rows, copy, 2)
        return carry

    lax.fori_loop(0, 8 * per_block, fetch, 0)
    half = mine_ref.shape[0]
    width = held.shape[1]
    lane = lax.broadcasted_iota(jnp.int32, (half, PAIR), 1)
    for block, ref in enumerate((q_ref, k_ref, v_ref)):
        place = pl.ds(block * D, D)
        pltpu.make_async_copy(held.at[place], held.at[place], in_sems.at[block]).wait()
        pltpu.make_async_copy(held.at[place], out_ref.at[place], out_sem).start()
        for part, rows_ref in enumerate((mine_ref, other_ref)):
            rows = slice(part * half, (part + 1) * half)
            product = dot32(rows_ref[...], held[block * D : (block + 1) * D])
            if block == 2:
                ref[rows, :] = product.astype(bf16)
                continue
            cosine, sine = cos_ref[rows, :], sin_ref[rows, :]
            for pair in range(width // PAIR):
                columns = slice(pair * PAIR, (pair + 1) * PAIR)
                turned = rotate(product[:, columns], cosine, sine, lane).astype(bf16)
                if block == 0:
                    turned = (turned.astype(f32) * 0.125).astype(bf16)
                ref[rows, columns] = turned
    place = pl.ds(3 * D, 5 * D)
    pltpu.make_async_copy(held.at[place], held.at[place], in_sems.at[3]).wait()
    pltpu.make_async_copy(held.at[place], out_ref.at[place], out_sem).start()
    pltpu.make_async_copy(held, out_ref, out_sem).wait()


def project(part_pairs, slots, panel_rows, cuts, mine, other, cosine, sine):
    width = part_pairs[0][0].shape[-1]
    parts = [
        part_pairs[index][last].reshape(-1, cuts[index + 1] - cuts[index], width)
        for last in range(2)
        for index in range(PARTS)
    ]
    whole = pl.BlockSpec(memory_space=pltpu.VMEM)
    anywhere = pl.BlockSpec(memory_space=pl.ANY)
    tall = jax.ShapeDtypeStruct((LEN, width), bf16)
    return pl.pallas_call(
        lambda *refs: project_kernel(panel_rows, cuts, *refs),
        in_specs=[pl.BlockSpec(memory_space=pltpu.SMEM)] + [anywhere] * (2 * PARTS) + [whole] * 4,
        out_specs=[whole] * 3 + [anywhere],
        out_shape=[tall] * 3 + [jax.ShapeDtypeStruct((8 * D, width), bf16)],
        scratch_shapes=[
            pltpu.VMEM((8 * D, width), bf16),
            pltpu.SemaphoreType.DMA((4,)),
            pltpu.SemaphoreType.DMA,
        ],
        compiler_params=pltpu.CompilerParams(vmem_limit_bytes=vmem_bytes),
        cost_estimate=pl.CostEstimate(
            flops=2 * LEN * 3 * D * width, bytes_accessed=48 * D * width, transcendentals=0
        ),
        name="project",
    )(slots, *parts, mine, other, cosine, sine)


def feed_kernel(n_ref, g_ref, w_ref, f_ref, d_ref, a_ref, u_ref):
    width = w_ref.shape[2]
    rows, grads = n_ref[...], g_ref[...]
    pre = [dot32(rows, w_ref[i]) for i in range(2)]
    act_grad = [dot32(grads, w_ref[2 + i]) for i in range(2)]
    acts, pre_grads = [], []
    for i in range(2):
        value = pre[i]
        square = value * value
        turn = jnp.tanh(0.7978845608028654 * (value + 0.044715 * (square * value)))
        share = 0.5 * (1.0 + turn)
        slope = share + (0.5 * value) * (1.0 - turn * turn) * (
            0.7978845608028654 + (3 * 0.044715 * 0.7978845608028654) * square
        )
        acts.append((value * share).astype(bf16))
        pre_grads.append((act_grad[i] * slope).astype(bf16))
        a_ref[:, i * width : (i + 1) * width] = acts[i]
        u_ref[:, i * width : (i + 1) * width] = pre_grads[i]
    f_ref[...] = (dot32(acts[0], w_ref[2], NT) + dot32(acts[1], w_ref[3], NT)).astype(f_ref.dtype)
    d_ref[...] = (dot32(pre_grads[0], w_ref[0], NT) + dot32(pre_grads[1], w_ref[1], NT)).astype(d_ref.dtype)


def feed(rows, grads, stacked, kind):
    half, width = rows.shape[0], stacked.shape[2]
    whole = pl.BlockSpec((half, D), lambda step: (0, 0))
    low, sums = jax.ShapeDtypeStruct((half, D), bf16), jax.ShapeDtypeStruct((half, D), kind)
    return pl.pallas_call(
        feed_kernel,
        grid=(1,),
        in_specs=[whole, whole, pl.BlockSpec((4, D, width), lambda step: (1, 0, 0))],
        out_specs=[whole] * 4,
        out_shape=[sums, sums, low, low],
        compiler_params=pltpu.CompilerParams(vmem_limit_bytes=vmem_bytes),
        cost_estimate=pl.CostEstimate(
            flops=2 * 4 * half * D * D, bytes_accessed=16 * D * width, transcendentals=half * D
        ),
        name="feed",
    )(rows, grads, stacked)


def inputs_grad_kernel(q_ref, k_ref, v_ref, w_ref, mine_ref, other_ref):
    half = mine_ref.shape[0]
    for start, out_ref in ((half, other_ref), (0, mine_ref)):
        rows = slice(start, start + half)
        total = dot32(q_ref[rows, :], w_ref[0], NT)
        total = total + dot32(k_ref[rows, :], w_ref[1], NT)
        total = total + dot32(v_ref[rows, :], w_ref[2], NT)
        out_ref[...] = total.astype(out_ref.dtype)


def inputs_grad(query_grad, key_grad, value_grad, stacked):
    width = stacked.shape[2]
    half = LEN // 2
    tall = pl.BlockSpec((LEN, width), lambda step: (0, 0))
    out = pl.BlockSpec((half, D), lambda step: (0, 0))
    return pl.pallas_call(
        inputs_grad_kernel,
        grid=(1,),
        in_specs=[tall] * 3 + [pl.BlockSpec((3, D, width), lambda step: (0, 0, 0))],
        out_specs=[out, out],
        out_shape=[jax.ShapeDtypeStruct((half, D), f32), jax.ShapeDtypeStruct((half, D), bf16)],
        compiler_params=pltpu.CompilerParams(vmem_limit_bytes=vmem_bytes),
        cost_estimate=pl.CostEstimate(
            flops=2 * 3 * LEN * D * width, bytes_accessed=12 * LEN * D, transcendentals=0
        ),
        name="inputs_grad",
    )(query_grad, key_grad, value_grad, stacked)


def gradients_kernel(panel_rows, cuts, lefts, rights, uses, slots_ref, *refs):
    in_count = sum(len(pieces) for pieces in lefts + rights)
    inputs, refs = refs[:in_count], refs[in_count:]
    parts, refs = refs[: 4 * PARTS], refs[4 * PARTS :]
    left_held, right_held = refs[: len(lefts)], refs[len(lefts) : len(lefts) + len(rights)]
    turned, block_ref, in_sems, out_sems = refs[len(lefts) + len(rights) :]
    side = block_ref.shape[1]
    operands = [(held, pieces) for held, pieces in zip(left_held + right_held, lefts + rights)]

    def load(operand):
        held, pieces = operands[operand]
        return [
            pltpu.make_async_copy(
                inputs[which],
                held.at[pl.ds(row, inputs[which].shape[0]), pl.ds(column, inputs[which].shape[1])],
                in_sems.at[operand],
            )
            for row, column, which in pieces
        ]

    order = []
    for left, right, right_start in uses:
        for operand in (left, len(lefts) + right):
            if operand not in order:
                order.append(operand)
    for operand in order:
        for copy in load(operand):
            copy.start()
    ready = set()
    pieces = side // panel_rows
    block = 0
    for left, right, right_start in uses:
        for operand in (left, len(lefts) + right):
            if operand not in ready:
                held = operands[operand][0]
                pltpu.make_async_copy(held, held, in_sems.at[operand]).wait()
                ready.add(operand)
                if operand < len(lefts):
                    turned[left % 2] = held[...].T
        for left_start in range(0, D, side):
            place = block % 2
            if block >= 2:
                pltpu.make_async_copy(block_ref.at[place], block_ref.at[place], out_sems.at[place]).wait()
            block_ref[place] = dot32(
                turned[left % 2, left_start : left_start + side],
                right_held[right][:, right_start : right_start + side],
            ).astype(bf16)

            def send(piece, carry, block=block, place=place):
                def copy(number, lead, start, rows):
                    pltpu.make_async_copy(
                        block_ref.at[place, pl.ds(start, rows)], parts[number].at[lead], out_sems.at[place]
                    ).start()

                part_copies(
                    slots_ref, 8 * D // panel_rows, block * pieces + piece, cuts, piece * panel_rows, copy
                )
                return carry

            lax.fori_loop(0, pieces, send, 0)
            block += 1
    for place in range(2):
        pltpu.make_async_copy(block_ref.at[place], block_ref.at[place], out_sems.at[place]).wait()


def panel_gradients(lefts, rights, uses, slots, panel_rows, cuts, high_count, width):
    arrays, numbered = [], []
    for operands in (lefts, rights):
        made = []
        for pieces in operands:
            made.append([(row, column, len(arrays) + i) for i, (row, column, _) in enumerate(pieces)])
            arrays.extend(array for _, _, array in pieces)
        numbered.append(made)
    extent = lambda pieces: max(column + array.shape[1] for _, column, array in pieces)
    outs = [
        jax.ShapeDtypeStruct((4 * high_count, cuts[index + 1] - cuts[index], width), bf16)
        for _ in range(4)
        for index in range(PARTS)
    ]
    outs = pl.pallas_call(
        lambda *refs: gradients_kernel(panel_rows, cuts, numbered[0], numbered[1], uses, *refs),
        in_specs=[pl.BlockSpec(memory_space=pltpu.SMEM)]
        + [pl.BlockSpec(memory_space=pl.ANY)] * len(arrays),
        out_specs=[pl.BlockSpec(memory_space=pl.ANY)] * (4 * PARTS),
        out_shape=outs,
        scratch_shapes=[pltpu.VMEM((LEN, extent(pieces)), bf16) for pieces in list(lefts) + list(rights)]
        + [
            pltpu.VMEM((2, D, LEN), bf16),
            pltpu.VMEM((2, width, width), bf16),
            pltpu.SemaphoreType.DMA((len(lefts) + len(rights),)),
            pltpu.SemaphoreType.DMA((2,)),
        ],
        compiler_params=pltpu.CompilerParams(vmem_limit_bytes=vmem_bytes),
        cost_estimate=pl.CostEstimate(
            flops=2 * LEN * len(uses) * D * width,
            bytes_accessed=24 * LEN * D,
            transcendentals=0,
        ),
        name="gradients",
    )(slots, *arrays)
    shaped = [out.reshape((2, 2, high_count) + out.shape[1:]) for out in outs]
    pairs = lambda far: [
        (shaped[far * 2 * PARTS + index], shaped[far * 2 * PARTS + PARTS + index]) for index in range(PARTS)
    ]
    return pairs(0), pairs(1)


beside = pl.CostEstimate(flops=1000, bytes_accessed=1000, transcendentals=0)


def gelu_parts(values):
    share = 0.5 * (1.0 + lax.erf(values * 0.7071067811865476))
    density = 0.3989422804014327 * jnp.exp(-0.5 * values * values)
    return share, density


def in_vmem(kernel, name, inputs, outs, scratch=(), specs=None, out_specs=None):
    whole = pl.BlockSpec(memory_space=pltpu.VMEM)
    return pl.pallas_call(
        kernel,
        in_specs=specs or [whole] * len(inputs),
        out_specs=out_specs or [whole] * len(outs),
        out_shape=[jax.ShapeDtypeStruct(shape, kind) for shape, kind in outs],
        scratch_shapes=list(scratch),
        compiler_params=pltpu.CompilerParams(vmem_limit_bytes=vmem_bytes),
        cost_estimate=beside,
        name=name,
    )(*inputs)


def text_forward_kernel(
    core_ref, table_ref, mine_ref, other_ref, normed_ref, masked_ref, keep_ref, mel_mine_ref, mel_other_ref,
    in_bias_ref, gamma_ref, beta_ref, bias_ref, shift_ref, scale_ref,
    pre_ref, energy_ref, grn_ref, text_ref, stream_ref, first_ref, other_first_ref, texts_ref, hidden_held, held, sem, out_sem,
):
    rows = mine_ref.shape[1]
    half = stream_ref.shape[0]

    def fetch(block, carry):
        place = held.at[pl.ds(pl.multiple_of(block * rows, 16), rows)]
        for part, ref in enumerate((mine_ref, other_ref)):

            @pl.when((block + core_ref[0]) % 2 == part)
            def _():
                pltpu.make_async_copy(ref.at[table_ref[block]], place, sem).start()

        return carry

    lax.fori_loop(0, table_ref.shape[0], fetch, 0)
    pltpu.make_async_copy(held, held, sem).wait()
    out = pltpu.make_async_copy(held, texts_ref, out_sem)
    out.start()
    energy_sum = jnp.zeros((1, TXT_FF), f32)
    for part in range(2):
        frames = slice(part * half, (part + 1) * half)
        pre = dot32(normed_ref[frames, :], held[:TEXT]) + in_bias_ref[...]
        if part == 0:
            pre_ref[...] = pre
        hidden = pre * gelu_parts(pre)[0]
        hidden_held[frames, :] = hidden
        energy_sum = energy_sum + jnp.sum(hidden * hidden, axis=0, keepdims=True)
    energy_ref[...] = energy_sum
    energy = jnp.sqrt(energy_sum)
    ratio = energy / (jnp.mean(energy, axis=-1, keepdims=True) + norm_eps)
    weight = gamma_ref[...] * ratio + 1.0
    for part, mel_ref in enumerate((mel_mine_ref, mel_other_ref)):
        frames = slice(part * half, (part + 1) * half)
        grn_low = (weight * hidden_held[frames, :] + beta_ref[...]).astype(bf16)
        text_out = masked_ref[frames, :] + dot32(grn_low, held[TEXT : 2 * TEXT], NT) + bias_ref[...]
        text_low = (text_out * keep_ref[frames, :]).astype(bf16)
        stream = mel_ref[...].astype(f32) + dot32(text_low, held[2 * TEXT :])
        normed, _ = normalise(stream)
        first = (normed * (1.0 + scale_ref[...]) + shift_ref[...]).astype(bf16)
        if part == 0:
            grn_ref[...] = grn_low
            text_ref[...] = text_low
            stream_ref[...] = stream
            first_ref[...] = first
        else:
            other_first_ref[...] = first
    out.wait()


def text_forward(core, table, *inputs):
    whole, anywhere = pl.BlockSpec(memory_space=pltpu.VMEM), pl.BlockSpec(memory_space=pl.ANY)
    scalars = pl.BlockSpec(memory_space=pltpu.SMEM)
    half = LEN // 2
    return in_vmem(
        text_forward_kernel,
        "text_forward",
        (core.reshape(1).astype(jnp.int32), table) + inputs,
        [
            ((half, TXT_FF), f32),
            ((1, TXT_FF), f32),
            ((half, TXT_FF), bf16),
            ((half, TEXT), bf16),
            ((half, D), f32),
            ((half, D), bf16),
            ((half, D), bf16),
            ((3 * TEXT, D), bf16),
        ],
        [
            pltpu.VMEM((LEN, TXT_FF), f32),
            pltpu.VMEM((3 * TEXT, D), bf16),
            pltpu.SemaphoreType.DMA,
            pltpu.SemaphoreType.DMA,
        ],
        [scalars, scalars, anywhere, anywhere] + [whole] * (len(inputs) - 2),
        [whole] * 7 + [anywhere],
    )


def stream_back_kernel(
    core_ref, my_ref, their_ref, stream_ref, later_ref, scale_ref, texts_ref, keep_ref, pre_ref,
    mel_ref, low_ref, shrink_ref, shrink_low_ref, grn_grad_ref, sums_ref, bias_sum_ref, full_ref, sem,
):
    half = mel_ref.shape[0]
    grad = my_ref[...] + their_ref[...].astype(f32)
    normed, scale = normalise(stream_ref[...])
    sums_ref[0:1] = jnp.sum(grad, axis=0, keepdims=True)
    sums_ref[1:2] = jnp.sum(grad * normed, axis=0, keepdims=True)
    mel_grad = later_ref[...] + normalise_back(grad * (1.0 + scale_ref[...]), normed, scale)
    mel_ref[...] = mel_grad
    place = pl.ds(pl.multiple_of(core_ref[0] * half, half), half)
    out = pltpu.make_async_copy(mel_ref, full_ref.at[place], sem)
    out.start()
    low = mel_grad.astype(bf16)
    low_ref[...] = low
    shrink_grad = dot32(low, texts_ref[2 * TEXT :], NT) * keep_ref[...]
    shrink_ref[...] = shrink_grad
    bias_sum_ref[...] = jnp.sum(shrink_grad, axis=0, keepdims=True)
    shrink_low = shrink_grad.astype(bf16)
    shrink_low_ref[...] = shrink_low
    grn_grad = dot32(shrink_low, texts_ref[TEXT : 2 * TEXT])
    grn_grad_ref[...] = grn_grad
    pre = pre_ref[...]
    sums_ref[2:3] = jnp.sum(grn_grad * (pre * gelu_parts(pre)[0]), axis=0, keepdims=True)
    sums_ref[3:4] = jnp.sum(grn_grad, axis=0, keepdims=True)
    sums_ref[4:8] = jnp.zeros((4, D), f32)
    out.wait()


def stream_back(core, *inputs):
    half = inputs[0].shape[0]
    whole = pl.BlockSpec(memory_space=pltpu.VMEM)
    return in_vmem(
        stream_back_kernel,
        "stream_back",
        (core.reshape(1).astype(jnp.int32),) + inputs,
        [
            ((half, D), f32),
            ((half, D), bf16),
            ((half, TEXT), f32),
            ((half, TEXT), bf16),
            ((half, TXT_FF), f32),
            ((8, D), f32),
            ((1, TEXT), f32),
            ((2 * half, D), f32),
        ],
        [pltpu.SemaphoreType.DMA],
        [pl.BlockSpec(memory_space=pltpu.SMEM)] + [whole] * len(inputs),
        [whole] * 7 + [pl.BlockSpec(memory_space=pl.ANY)],
    )


def text_back_kernel(
    pre_ref, grn_grad_ref, energy_ref, dot_ref, gamma_ref, texts_ref, normed_ref, conv_normed_ref, conv_scale_ref, gain_ref,
    shrink_low_ref, grn_ref, text_ref, low_ref,
    mixed_ref, sums_ref, wide_sums_ref, grads_ref,
):
    pre = pre_ref[...]
    share, density = gelu_parts(pre)
    energy = jnp.sqrt(energy_ref[...])
    energy_mean = jnp.mean(energy, axis=-1, keepdims=True) + norm_eps
    ratio = energy / energy_mean
    ratio_grad = gamma_ref[...] * dot_ref[...]
    energy_grad = (ratio_grad - jnp.mean(ratio_grad * ratio, axis=-1, keepdims=True)) / energy_mean
    hidden_grad = grn_grad_ref[...] * (gamma_ref[...] * ratio + 1.0) + (pre * share) * (energy_grad / energy)
    expand_grad = hidden_grad * (share + pre * density)
    wide_sums_ref[0:1] = jnp.sum(expand_grad, axis=0, keepdims=True)
    wide_sums_ref[1:2] = ratio
    expand_low = expand_grad.astype(bf16)
    grads_ref[:TEXT] = dot32(normed_ref[...], expand_low, TN).astype(bf16)
    grads_ref[TEXT : 2 * TEXT] = dot32(shrink_low_ref[...], grn_ref[...], TN).astype(bf16)
    grads_ref[2 * TEXT :] = dot32(text_ref[...], low_ref[...], TN).astype(bf16)
    normed_grad = dot32(expand_low, texts_ref[:TEXT], NT)
    conv_normed = conv_normed_ref[...]
    sums_ref[0:1] = jnp.sum(normed_grad * conv_normed, axis=0, keepdims=True)
    sums_ref[1:2] = jnp.sum(normed_grad, axis=0, keepdims=True)
    mixed_grad = normalise_back(normed_grad * gain_ref[...], conv_normed, conv_scale_ref[...])
    sums_ref[2:3] = jnp.sum(mixed_grad, axis=0, keepdims=True)
    mixed_ref[...] = mixed_grad


def text_back(*inputs):
    half = inputs[0].shape[0]
    return in_vmem(
        text_back_kernel,
        "text_back",
        inputs,
        [((half, TEXT), f32), ((3, TEXT), f32), ((2, TXT_FF), f32), ((3 * TEXT, D), bf16)],
    )


def vector_parts(vectors):
    kernel_size = KERNEL * TEXT
    pieces = [vectors[:kernel_size].reshape(KERNEL, TEXT)]
    offset = kernel_size
    for extent in (TEXT, TEXT, TEXT, TEXT, TXT_FF, TXT_FF, TXT_FF, 6 * D):
        pieces.append(vectors[offset : offset + extent])
        offset = offset + extent
    return pieces


def normalise(values):
    center = values - jnp.mean(values, axis=-1, keepdims=True)
    variance = jnp.mean(center * center, axis=-1, keepdims=True)
    scale = lax.rsqrt(variance + norm_eps)
    return center * scale, scale


def normalise_back(grad, normed, scale):
    mean_grad = jnp.mean(grad, axis=-1, keepdims=True)
    mean_dot = jnp.mean(grad * normed, axis=-1, keepdims=True)
    return scale * (grad - mean_grad - normed * mean_dot)


def moments(gradient, first_moment, second_moment):
    first_new = beta_one * first_moment + (1.0 - beta_one) * gradient
    second_new = beta_two * second_moment + (1.0 - beta_two) * gradient * gradient
    bias_first = 1.0 - beta_one**STEP
    bias_second = 1.0 - beta_two**STEP
    direction = first_new / bias_first / (jnp.sqrt(second_new / bias_second) + adam_eps)
    return (first_new, second_new, direction)


def apply_step(weight, direction, rate):
    return weight - rate * (direction + weight_decay * weight)


def rotary_tables(first):
    position = np.arange(LEN)
    frequency = 10000.0 ** (-np.arange(HEAD // 2) * 2.0 / HEAD)
    angle = position[:, None] * frequency[None, :]
    cosine, sine = np.cos(angle), np.sin(angle)
    tables = np.concatenate([cosine] * 4 + [-sine, sine, -sine, sine], axis=1).astype(np.float32)
    tables = lax.dynamic_slice_in_dim(jnp.asarray(np.concatenate([tables, tables])), first, LEN, 0)
    return tables[:, :PAIR], tables[:, PAIR:]


def take_blocks(blocks, index):
    return jnp.take(blocks, index, axis=0, mode="clip")


def both_halves(mine):
    return jnp.concatenate([mine, swap_core(mine)], axis=0)


def sum_halves(multiply, rows, half):
    theirs = multiply(rows[half:]).astype(bf16)
    received = swap_core(theirs)
    return multiply(rows[:half]) + received.astype(f32)


def body(
    mel_frames,
    text_features,
    cotangent,
    time_embedding,
    lengths,
    group_ids,
    text_keep,
    owner_list,
    soap_master,
    soap_first,
    soap_second,
    left_basis,
    right_basis,
    text_matrices,
    text_first,
    text_second,
    modulation_weight,
    modulation_first,
    modulation_second,
    vectors,
    vector_first,
    vector_second,
):
    count = lax.axis_size("dp")
    me, core = lax.axis_index("dp"), lax.axis_index("mp")
    half = LEN // 2
    utterances = lengths.shape[0] * count
    panel_rows, width = soap_master.shape
    share_rows = modulation_weight.shape[0]
    text_rows = text_matrices.shape[0]
    text_half = text_rows // 2
    relative = jnp.arange(count) ^ me

    high_count = count // 16
    cuts = row_cuts(panel_rows)
    gather_table = panel_places(core, owner_list ^ me, high_count, 0)
    panel_table = panel_places(core, owner_list ^ me, high_count, 1)
    silu_time = jax.nn.silu(time_embedding.astype(f32)).astype(bf16)
    time_rows = lax.dynamic_slice_in_dim(silu_time, me * share_rows, share_rows, 1)
    weight_half = lax.dynamic_slice_in_dim(modulation_weight, core * 3 * D, 3 * D, 1).astype(bf16)
    own_rows = lax.dynamic_slice_in_dim(text_matrices, core * text_half, text_half, 0)
    text_held = spread_high(own_rows.astype(bf16))
    partial = dot32(time_rows, weight_half)
    held = spread_high(soap_master.astype(bf16))
    text_received, partial_received = tie(swap_bit(text_held, 3), swap_bit(partial, 3))
    text_held = jnp.concatenate([text_held, text_received], axis=0)
    partial = partial + partial_received
    text_received, partial_received, held = tie(
        swap_bits(text_held, phase_bits(text_orders, 0)), swap_bits(partial, phase_bits(text_orders, 0)), held
    )
    held = split_rows(held, cuts)
    text_held = jnp.stack([text_held, text_received])
    partial = partial + partial_received
    text_received, partial_received, far_last = tie(
        swap_bits(text_held, phase_bits(text_orders, 1)),
        swap_bits(partial, phase_bits(text_orders, 1)),
        swap_bit(held[1], 3),
    )
    text_held = jnp.stack([text_held, text_received])
    partial = partial + partial_received
    text_received, partial_received, far_first = tie(
        swap_bits(text_held, phase_bits(text_orders, 2)),
        swap_bits(partial, phase_bits(text_orders, 2)),
        swap_bit(held[0], 3),
    )
    partial = partial + partial_received
    parts = [jnp.concatenate(pair, axis=0) for pair in zip(held, (far_first, far_last))]
    received = receive(parts, 0)
    text_mine = jnp.stack([text_held, text_received]).reshape(count, text_half, D)
    text_other = swap_core(text_mine)
    received, (text_mine, text_other, partial, text_features, mel_frames, cotangent) = tie_lists(
        received, (text_mine, text_other, partial, text_features, mel_frames, cotangent)
    )
    parts = [jnp.stack(pair) for pair in zip(parts, received)]
    received = receive(parts, 1)
    for bit in range(4, bit_count(count)):
        partial = partial + swap_bit(partial, bit)
    modulation_half = partial
    mine_places, other_places = text_places(core, relative, high_count), text_places(1 - core, relative, high_count)
    text_table = jnp.where(
        core == 0, jnp.stack([mine_places, other_places], 1), jnp.stack([other_places, mine_places], 1)
    ).reshape(-1)
    if text_half % 16:
        source = jnp.arange(2 * count) % 2 != core
        texts = take_blocks(jnp.concatenate([text_mine, text_other]), text_table + count * source)
        text_mine = text_other = texts.reshape(1, 3 * TEXT, D)
        text_table = jnp.zeros((1,), jnp.int32)

    modulation = by_core(core, modulation_half, swap_core(modulation_half), axis=1)
    (
        kernel,
        conv_bias,
        norm_gain,
        norm_bias,
        out_bias,
        in_bias,
        grn_gamma,
        grn_beta,
        modulation_bias,
    ) = vector_parts(vectors)
    group = group_ids[0]
    modulation_row = lax.dynamic_slice_in_dim(modulation, group, 1, 0) + modulation_bias


    first = core * half
    margin = KERNEL // 2
    edge = 8
    keep_all = jnp.pad(text_keep.astype(f32), (edge, edge))[:, None]
    text_all = jnp.pad(text_features, ((edge, edge), (0, 0)))

    def text_start(start):
        window = lax.dynamic_slice_in_dim(text_all, start, half + 2 * edge, 0).astype(f32)
        window = window * lax.dynamic_slice_in_dim(keep_all, start, half + 2 * edge, 0)
        keep = lax.dynamic_slice_in_dim(keep_all, start + edge, half, 0)
        taps = [window[edge - margin + j : edge - margin + j + half] for j in range(KERNEL)]
        mixed = conv_bias[None, :]
        for j in range(KERNEL):
            mixed = mixed + taps[j] * kernel[j][None, :]
        normed, scale = normalise(mixed)
        return window[edge : edge + half], keep, taps, normed, scale, (normed * norm_gain + norm_bias).astype(bf16)

    masked_text, keep, taps, conv_normed, conv_scale, normed_low = text_start(first)
    masked_other, keep_other, _, _, _, normed_other = text_start(half - first)
    masked_both = jnp.concatenate([masked_text, masked_other], axis=0)
    keep_both = jnp.concatenate([keep, keep_other], axis=0)
    normed_both = jnp.concatenate([normed_low, normed_other], axis=0)
    mel_mine = lax.dynamic_slice_in_dim(mel_frames, first, half, 0)
    mel_other = lax.dynamic_slice_in_dim(mel_frames, half - first, half, 0)
    cosine, sine = rotary_tables(first)
    received, (text_other, modulation_row, normed_both, masked_both, cosine, sine) = tie_lists(
        received, (text_other, modulation_row, normed_both, masked_both, cosine, sine)
    )
    pairs = spread_last([jnp.stack(pair) for pair in zip(parts, received)])
    shift_one, scale_one, gate_one, shift_two, scale_two, gate_two = (
        modulation_row[:, i * D : (i + 1) * D] for i in range(6)
    )
    expand_pre, energy_sum, grn_low, text_low, stream, first_mine, first_other, texts = text_forward(
        core,
        text_table,
        text_mine,
        text_other,
        normed_both,
        masked_both,
        keep_both,
        mel_mine,
        mel_other,
        in_bias[None],
        grn_gamma[None],
        grn_beta[None],
        out_bias[None],
        shift_one,
        scale_one,
    )

    cot_mine = lax.dynamic_slice_in_dim(cotangent, first, half, 0)
    cot_other = lax.dynamic_slice_in_dim(cotangent, half - first, half, 0)
    hidden_mine = (gate_two * cot_mine.astype(f32)).astype(bf16)
    hidden_other = (gate_two * cot_other.astype(f32)).astype(bf16)
    first_mine, hidden_mine, hidden_other = tie(first_mine, hidden_mine, hidden_other)
    position = (jnp.arange(LEN) + first) % LEN
    bias = jnp.where(position < lengths[0], 0.0, -1e30).astype(bf16)
    bias = jnp.broadcast_to(bias[:, None], (LEN, PAIR))
    queries, keys, value_rows, stacked = project(
        pairs, gather_table, panel_rows, cuts, first_mine, first_other, cosine, sine
    )
    stacked = stacked.reshape(8, D, width)
    attended, query_aug = attend_forward(queries, keys, value_rows, bias)
    attention_out = sum_halves(lambda rows: dot32(rows, stacked[3], NT), attended, half)
    stream_one = stream + gate_one * attention_out

    normed_two, scale_norm_two = normalise(stream_one)
    second_mine = (normed_two * (1.0 + scale_two) + shift_two).astype(bf16)
    second_other = swap_core(second_mine)
    out_grad = cot_mine.astype(f32)
    their_out, their_grad, act_other, pre_other = feed(second_other, hidden_other, stacked, bf16)
    their_out, their_grad = swap_core(their_out), swap_core(their_grad)
    my_out, my_grad, act_mine, pre_mine = feed(second_mine, hidden_mine, stacked, f32)
    unit_out = my_out + their_out.astype(f32)
    normed_two_grad = my_grad + their_grad.astype(f32)
    output_mine = (stream_one + gate_two * unit_out).astype(bf16)
    block_output = by_core(core, output_mine, swap_core(output_mine))
    gate_two_grad = jnp.sum(out_grad * unit_out, axis=0)
    shift_two_grad = jnp.sum(normed_two_grad, axis=0)
    scale_two_grad = jnp.sum(normed_two_grad * normed_two, axis=0)
    stream_one_grad = out_grad + normalise_back(
        normed_two_grad * (1.0 + scale_two), normed_two, scale_norm_two
    )

    gate_one_grad = jnp.sum(stream_one_grad * attention_out, axis=0)
    attention_mine = (gate_one * stream_one_grad).astype(bf16)
    attention_other = swap_core(attention_mine)
    query_grad, key_grad, value_grad = attend_backward(
        query_aug, keys, value_rows, attended, attention_mine, attention_other, stacked, cosine, sine, bias
    )
    my_grad, their_grad = inputs_grad(query_grad, key_grad, value_grad, stacked)
    their_grad, query_grad = tie(their_grad, query_grad)
    their_grad = swap_core(their_grad)
    halves = lambda mine, other: [(0, 0, mine), (half, 0, other)]
    whole = lambda array: [(0, 0, array)]
    near_pairs, far_pairs = panel_gradients(
        [
            halves(first_mine, first_other),
            halves(attention_mine, attention_other),
            halves(second_mine, second_other),
            halves(hidden_mine, hidden_other),
        ],
        [
            whole(query_grad),
            whole(key_grad),
            whole(value_grad),
            whole(attended),
            halves(pre_mine, pre_other),
            halves(act_mine, act_other),
        ],
        ((0, 0, 0), (0, 1, 0), (0, 2, 0), (1, 3, 0), (2, 4, 0), (2, 4, width), (3, 5, 0), (3, 5, width)),
        panel_table,
        panel_rows,
        cuts,
        high_count,
        width,
    )

    far_keep, far_send = firsts(far_pairs), seconds(far_pairs)
    near_keep, near_send = firsts(near_pairs), seconds(near_pairs)
    far_received = receive(far_send, 2)
    mel_grad_mine, stream_low, shrink_grad, shrink_low, grn_grad, sums, out_bias_grad, mel_gradient = stream_back(
        core, my_grad, their_grad, stream, stream_one_grad, scale_one, texts, keep, expand_pre
    )
    far_received, (sums, mel_grad_mine) = tie_lists(far_received, (sums, mel_grad_mine))
    shift_one_grad, scale_one_grad, hidden_dot, beta_grad = sums[0], sums[1], sums[2:3], sums[3]
    out_bias_grad = out_bias_grad[0]
    far = add_all(far_keep, far_received)
    far_received = receive(seconds(far), 1)
    hidden_dot_all = hidden_dot + swap_core(hidden_dot)
    mixed_grad, text_sums, wide_sums, text_grads = text_back(
        expand_pre,
        grn_grad,
        energy_sum,
        hidden_dot_all,
        grn_gamma[None],
        texts,
        normed_low,
        conv_normed,
        conv_scale,
        norm_gain[None],
        shrink_low,
        grn_low,
        text_low,
        stream_low,
    )
    mel_grad_theirs = swap_core(mel_grad_mine)
    gain_grad, norm_bias_grad, conv_bias_grad = text_sums[0], text_sums[1], text_sums[2]
    in_bias_grad, gamma_grad = wide_sums[0], wide_sums[1] * hidden_dot[0]
    far_received, near_send, (mixed_grad, text_grads, mel_grad_theirs) = tie_lists(
        far_received, near_send, (mixed_grad, text_grads, mel_grad_theirs)
    )
    far = add_all(firsts(far), far_received)
    far_received = receive(seconds(far), 0)
    near_received = receive(near_send, 2)
    text_grads = text_grads.reshape(count, 2, text_half, D)
    text_keep_half = lax.dynamic_index_in_dim(text_grads, core, 1, keepdims=False)
    text_send_half = lax.dynamic_index_in_dim(text_grads, 1 - core, 1, keepdims=False)
    text_received = swap_core(text_send_half)
    kernel_grad = jnp.stack([jnp.sum(mixed_grad * taps[j], axis=0) for j in range(KERNEL)])
    border = lax.dynamic_slice_in_dim(mixed_grad, (1 - core) * (half - edge), edge, 0)
    border = swap_core(border)
    before = jnp.where(core == 1, border, 0.0)
    after = jnp.where(core == 0, border, 0.0)
    wide_grad = jnp.concatenate([before, mixed_grad, after], axis=0)
    masked_grad = shrink_grad
    for j in range(KERNEL):
        start = edge + margin - j
        masked_grad = masked_grad + wide_grad[start : start + half] * kernel[j][None, :]
    text_grad_mine = masked_grad * keep

    vector_mine = jnp.concatenate(
        [
            kernel_grad.reshape(-1),
            conv_bias_grad,
            gain_grad,
            norm_bias_grad,
            out_bias_grad,
            in_bias_grad,
            gamma_grad,
            beta_grad,
        ]
    )
    token = jnp.concatenate(
        [shift_one_grad, scale_one_grad, gate_one_grad, shift_two_grad, scale_two_grad, gate_two_grad]
    )
    vector_half = vector_mine.shape[0] // 2
    token_half = 3 * D

    def half_of(which):
        return jnp.concatenate(
            [
                lax.dynamic_slice_in_dim(vector_mine, which * vector_half, vector_half, 0),
                lax.dynamic_slice_in_dim(token, which * token_half, token_half, 0),
            ]
        )

    small_send = half_of(1 - core)
    small = half_of(core)
    in_group = (jnp.arange(GROUPS) == group).astype(f32)

    far_received, near_received, (text_received, small, small_send) = tie_lists(
        far_received, near_received, (text_received, small, small_send)
    )
    far = add_all(firsts(far), far_received)
    far_last = swap_bit(far[1], 3)
    near = add_all(near_keep, near_received)
    near_received = receive(seconds(near), 1)
    text_part = take_blocks(
        add_low(text_keep_half, text_received), text_slots(core, jnp.arange(count), high_count) ^ me
    )
    text_part = text_part.reshape(2, 2, 2, 2 * high_count, text_half, D)
    text_received = swap_bits(text_part[1], phase_bits(text_orders, 2))
    small_received = swap_core(small_send)
    mel_gradient = lax.dynamic_update_slice_in_dim(mel_gradient, mel_grad_theirs, half - first, 0)
    near_received, (text_received, small_received, mel_gradient, far_last) = tie_lists(
        near_received, (text_received, small_received, mel_gradient, far_last)
    )
    far_first = swap_bit(far[0], 3)
    near = add_all(firsts(near), near_received)
    near_received = receive(seconds(near), 0)
    text_part = add_low(text_part[0], text_received)
    text_part = fold(text_part, text_orders, 1)
    small = small + small_received
    table = in_group[:, None] * small[None, vector_half:]
    small = jnp.concatenate([small[:vector_half], table.reshape(-1)]).reshape(-1, 128)
    small = small + swap_bits(small, (2, 0))
    text_gradient = by_core(core, text_grad_mine, swap_core(text_grad_mine))
    near_received, (text_part, small, text_gradient, far_first, block_output) = tie_lists(
        near_received, (text_part, small, text_gradient, far_first, block_output)
    )
    near = add_all(firsts(near), near_received)
    own_panel = jnp.concatenate(
        [keep.astype(f32) + other.astype(f32) for keep, other in zip(near, (far_first, far_last))], axis=-2
    )
    own_panel = fold_high(own_panel)
    text_part = fold(text_part, text_orders, 0)
    text_received = swap_bit(text_part[high_count:], 3)
    small = small + swap_bits(small, (0, 1))
    small = small + swap_bits(small, (1, 2))
    small = small + swap_bit(small, 3)
    own_text = text_part[:high_count].astype(f32) + text_received.astype(f32)
    for bit in range(4, bit_count(count)):
        small = small + swap_bit(small, bit)
    own_text = fold_high(own_text)
    own_text = by_core(core, own_text, swap_core(own_text))
    small = by_core(core, small[None], swap_core(small)[None]).reshape(2, -1)
    vector_sum = small[:, :vector_half].reshape(-1)
    tables = small[:, vector_half:].reshape(2, GROUPS, token_half)
    modulation_grad = jnp.concatenate([tables[0], tables[1]], axis=1)
    vector_gradient = jnp.concatenate([vector_sum, jnp.sum(modulation_grad, axis=0)]) / utterances
    share_grad = (
        lax.dot_general(
            time_rows, modulation_grad.astype(bf16), TN, preferred_element_type=f32
        )
        / utterances
    )

    own_panel = own_panel / utterances
    own_text = own_text / utterances
    rotated = jnp.dot(jnp.dot(left_basis.T, own_panel, precision=solver), right_basis, precision=solver)
    soap_moment, soap_variance, soap_direction = moments(rotated, soap_first, soap_second)
    turned_back = jnp.dot(
        jnp.dot(left_basis, soap_direction, precision=solver), right_basis.T, precision=solver
    )
    soap_weights = apply_step(soap_master, turned_back, learn_rate)
    text_moment, text_variance, text_direction = moments(own_text, text_first, text_second)
    text_weights = apply_step(text_matrices, text_direction, learn_rate)
    modulation_moment, modulation_variance, modulation_direction = moments(
        share_grad, modulation_first, modulation_second
    )
    modulation_weights = apply_step(modulation_weight, modulation_direction, learn_rate)
    vector_moment, vector_variance, vector_direction = moments(
        vector_gradient, vector_first, vector_second
    )
    vector_weights = apply_step(vectors, vector_direction, vector_rate)
    return (
        block_output,
        mel_gradient,
        text_gradient,
        soap_weights,
        soap_moment,
        soap_variance,
        text_weights,
        text_moment,
        text_variance,
        modulation_weights,
        modulation_moment,
        modulation_variance,
        vector_weights,
        vector_moment,
        vector_variance,
    )


def solution(mesh):
    rows, quarter, same = P("dp", None), P("dp", "mp"), P()
    return jax.shard_map(
        body,
        mesh=mesh,
        in_specs=(
            (rows,) * 3 + (same,) + (P("dp"),) * 3 + (same,) + (quarter,) * 5 + (rows,) * 6 + (same,) * 3
        ),
        out_specs=(rows,) * 3 + (quarter,) * 3 + (rows,) * 6 + (same,) * 3,
        check_vma=False,
    )
```

```python
import jax
import numpy as np
import jax.numpy as jnp
from jax import lax
from jax.experimental import pallas as pl
from jax.experimental.pallas import tpu as pltpu
from jax.sharding import PartitionSpec as P

D = 1024
HEAD = 64
TEXT = 512
TXT_FF = 1024
KERNEL = 7
LEN = 1024
GROUPS = 8
STEP = 10

f32 = jnp.float32
bf16 = jnp.bfloat16
beta_one = 0.9
beta_two = 0.99
adam_eps = 1e-08
weight_decay = 0.01
learn_rate = 0.03
vector_rate = 0.3
norm_eps = 1e-06


def swap_core(array):
    return lax.ppermute(array, "mp", [(0, 1), (1, 0)])


def swap_bits(array, bits):
    count = lax.axis_size("dp")
    pairs = [
        (i * 2 + core, (i ^ (1 << bits[core])) * 2 + core) for i in range(count) for core in range(2)
    ]
    return lax.ppermute(array, ("dp", "mp"), pairs)


def swap_bit(array, bit):
    return swap_bits(array, (bit, bit))


def by_core(core, mine, other, axis=0):
    return jnp.where(
        core == 0,
        jnp.concatenate([mine, other], axis=axis),
        jnp.concatenate([other, mine], axis=axis),
    )


def bit_count(count):
    return count.bit_length() - 1


def row_cuts(rows):
    return (0, (rows * 2 + 24) // 48 * 16, rows)


axis_orders = (((0, 1, 2), (1, 2, 0)), ((2, 0, 1), (2, 0, 1)))
text_orders = ((2, 0, 1), (2, 1, 0))


def phase_bits(orders, phase):
    return tuple(order[phase] for order in orders)


def tie(*values):
    return lax.optimization_barrier(values)


def tie_lists(*lists):
    flat = [value for values in lists for value in values]
    flat = list(lax.optimization_barrier(tuple(flat)))
    out = []
    for values in lists:
        out.append(flat[: len(values)])
        flat = flat[len(values) :]
    return out


def split_rows(array, cuts):
    return [array[..., cuts[i] : cuts[i + 1], :] for i in range(len(cuts) - 1)]


def spread(part, orders, phase):
    return jnp.stack([part, swap_bits(part, phase_bits(orders, phase))])


def spread_step(parts, phase):
    return [spread(part, axis_orders[index], phase) for index, part in enumerate(parts)]


def spread_last(parts):
    return [(part, swap_bits(part, phase_bits(axis_orders[index], 2))) for index, part in enumerate(parts)]


def spread_high(block):
    held = block[None]
    for bit in range(4, bit_count(lax.axis_size("dp"))):
        held = jnp.concatenate([held, swap_bit(held, bit)], axis=0)
    return held


def add_low(left, right):
    return (left.astype(f32) + right.astype(f32)).astype(bf16)


def receive(sends, phase):
    return [swap_bits(send, phase_bits(axis_orders[index], phase)) for index, send in enumerate(sends)]


def add_all(keeps, received):
    return [add_low(keep, other) for keep, other in zip(keeps, received)]


def firsts(parts):
    return [part[0] for part in parts]


def seconds(parts):
    return [part[1] for part in parts]


def fold(part, orders, phase):
    return add_low(part[0], swap_bits(part[1], phase_bits(orders, phase)))


def fold_high(total):
    count = total.shape[0]
    if count == 1:
        return total[0]
    for bit in range(bit_count(count) - 1, -1, -1):
        half = 1 << bit
        total = total[:half] + swap_bit(total[half:].astype(bf16), bit + 4).astype(f32)
    return total[0]


def bit_of(values, which):
    return (values >> which) & 1


def panel_places(core, slots, high_count, apart=False):
    rows = []
    for orders in axis_orders:
        far = bit_of(slots, 3)
        which = [bit_of(slots, order[2]) + (2 * far if apart else 0) for order in orders]
        lead = [bit_of(slots, order[1]) * 2 + bit_of(slots, order[0]) for order in orders]
        if not apart:
            lead = [place * 2 + far for place in lead]
        lead = [place * high_count + (slots >> 4) for place in lead]
        rows += [jnp.where(core == 0, *which), jnp.where(core == 0, *lead)]
    return jnp.concatenate(rows).astype(jnp.int32)


def text_places(core, slots, high_count):
    places = []
    for order in text_orders:
        high = bit_of(slots, 3) * high_count + (slots >> 4)
        places.append(
            ((bit_of(slots, order[2]) * 2 + bit_of(slots, order[1])) * 2 + bit_of(slots, order[0]))
            * (2 * high_count)
            + high
        )
    return jnp.where(core == 0, *places).astype(jnp.int32)


def text_slots(core, places, high_count):
    lead, rest = places // (2 * high_count), places % (2 * high_count)
    high = ((rest // high_count) << 3) | ((rest % high_count) << 4)
    slots = []
    for order in text_orders:
        low = (bit_of(lead, 2) << order[2]) | (bit_of(lead, 1) << order[1]) | (bit_of(lead, 0) << order[0])
        slots.append(high | low)
    return jnp.where(core == 0, *slots)


beside = pl.CostEstimate(flops=1000, bytes_accessed=1000, transcendentals=0)

NT = (((1,), (1,)), ((), ()))
NN = (((1,), (0,)), ((), ()))
TN = (((0,), (0,)), ((), ()))
ROWS = 256
LONG_ROWS = 512
PAIR = 2 * HEAD
vmem_bytes = 12 * 1024 * 1024
gradient_bytes = 20 * 1024 * 1024


def dot32(left, right, dims=NN):
    return lax.dot_general(left, right, dims, preferred_element_type=f32)


def three_terms(values):
    high = values.astype(bf16).astype(f32)
    rest = values - high
    middle = rest.astype(bf16).astype(f32)
    return high, middle, rest - middle


def rotate(values, cosine, sine, lane):
    partner = jnp.where(
        lane % HEAD < HEAD // 2,
        pltpu.roll(values, PAIR - HEAD // 2, 1),
        pltpu.roll(values, HEAD // 2, 1),
    )
    return values * cosine + partner * sine


def attend_kernel(q_ref, k_ref, v_ref, bias_ref, o_ref, qa_ref):
    lane = lax.broadcasted_iota(jnp.int32, (LEN, PAIR), 1)
    lane_rows = lax.broadcasted_iota(jnp.int32, (LONG_ROWS, PAIR), 1)
    row_index = lax.broadcasted_iota(jnp.int32, (PAIR, LONG_ROWS), 0)
    q_wide = q_ref[...].astype(f32)
    k_wide = k_ref[...].astype(f32)
    values_t = v_ref[...].T
    bias = bias_ref[...].astype(f32)
    keys = []
    for head in range(2):
        own = lane // HEAD == head
        spare = (1 - head) * HEAD
        keys.append(
            jnp.where(own, k_wide, jnp.where(lane == spare, bias, 0.0)).astype(bf16)
        )
        qa_ref[:, head * PAIR : (head + 1) * PAIR] = jnp.where(
            own, q_wide, jnp.where(lane == spare, 1.0, 0.0)
        ).astype(bf16)
    steps = [(block, head) for block in range(LEN // LONG_ROWS) for head in range(2)]

    def scores_of(step):
        block, head = step
        rows = slice(block * LONG_ROWS, (block + 1) * LONG_ROWS)
        return dot32(keys[head], qa_ref[rows, head * PAIR : (head + 1) * PAIR], NT)

    following = scores_of(steps[0])
    for position, (block, head) in enumerate(steps):
        scores = following
        if position + 1 < len(steps):
            following = scores_of(steps[position + 1])
        rows = slice(block * LONG_ROWS, (block + 1) * LONG_ROWS)
        if head == 0:
            outs, extra = [], jnp.zeros((PAIR, LONG_ROWS), f32)
        spare = (1 - head) * HEAD
        highest = jnp.max(scores, axis=0, keepdims=True)
        weights = jnp.exp(scores - highest)
        total = jnp.sum(weights, axis=0, keepdims=True)
        out_t = dot32(values_t[head * HEAD : (head + 1) * HEAD], weights.astype(bf16))
        outs.append(out_t / total)
        for place, term in enumerate(three_terms(highest + jnp.log(total))):
            extra = jnp.where(row_index == spare + 1 + place, -term, extra)
        if head == 0:
            continue
        o_ref[rows, :] = jnp.concatenate(outs, axis=0).T.astype(bf16)
        extra_t = extra.T
        for head in range(2):
            spare = (1 - head) * HEAD
            columns = slice(head * PAIR, (head + 1) * PAIR)
            is_extra = (lane_rows > spare) & (lane_rows < spare + 4)
            qa_ref[rows, columns] = jnp.where(
                is_extra, extra_t, qa_ref[rows, columns].astype(f32)
            ).astype(bf16)


def attend_forward(queries, keys, values, bias):
    width = values.shape[1]
    pairs = width // PAIR
    tall = lambda columns: pl.BlockSpec((LEN, columns), lambda pair: (0, pair))
    whole = pl.BlockSpec((LEN, PAIR), lambda pair: (0, 0))
    return pl.pallas_call(
        attend_kernel,
        grid=(pairs,),
        in_specs=[tall(PAIR), tall(PAIR), tall(PAIR), whole],
        out_specs=[tall(PAIR), tall(2 * PAIR)],
        out_shape=[
            jax.ShapeDtypeStruct((LEN, width), bf16),
            jax.ShapeDtypeStruct((LEN, 2 * width), bf16),
        ],
        compiler_params=pltpu.CompilerParams(vmem_limit_bytes=vmem_bytes),
        cost_estimate=pl.CostEstimate(
            flops=2 * 4 * LEN * LEN * width * 4,
            bytes_accessed=6 * LEN * width * 2,
            transcendentals=LEN * LEN * width // HEAD,
        ),
        name="attend",
    )(queries, keys, values, bias)


def attend_back_kernel(
    qa_ref, kr_ref, v_ref, o_ref, mine_ref, other_ref, weight_ref, cos_ref, sin_ref, bias_ref,
    dq_ref, dk_ref, dv_ref, doa_ref, dka_ref, dva_ref,
):
    lane = lax.broadcasted_iota(jnp.int32, (LEN, PAIR), 1)
    lane_rows = lax.broadcasted_iota(jnp.int32, (ROWS, PAIR), 1)
    cosine, sine = cos_ref[...], sin_ref[...]
    k_wide = kr_ref[...].astype(f32)
    keys_t = kr_ref[...].T
    v_wide = v_ref[...].astype(f32)
    do_wide = jnp.concatenate(
        [dot32(ref[...], weight_ref[0]).astype(bf16).astype(f32) for ref in (mine_ref, other_ref)],
        axis=0,
    )
    bias = bias_ref[...].astype(f32)
    product = do_wide * o_ref[...].astype(f32)
    keys, values = [], []
    for head in range(2):
        own = lane // HEAD == head
        spare = (1 - head) * HEAD
        is_extra = (lane > spare) & (lane < spare + 4)
        ones = jnp.where(is_extra, 1.0, 0.0)
        keys.append(
            jnp.where(own, k_wide, jnp.where(lane == spare, bias, ones)).astype(bf16)
        )
        values.append(jnp.where(own, v_wide, ones).astype(bf16))
        row_dot = jnp.sum(jnp.where(own, product, 0.0), axis=1, keepdims=True)
        grad = jnp.where(own, do_wide, 0.0)
        for place, term in enumerate(three_terms(row_dot)):
            grad = jnp.where(lane == spare + 1 + place, -term, grad)
        doa_ref[:, head * PAIR : (head + 1) * PAIR] = grad.astype(bf16)
    for block in range(LEN // ROWS):
        rows = slice(block * ROWS, (block + 1) * ROWS)
        turned = []
        for head in range(2):
            columns = slice(head * PAIR, (head + 1) * PAIR)
            q_block = qa_ref[rows, columns]
            do_block = doa_ref[rows, columns]
            probs = jnp.exp(dot32(keys[head], q_block, NT))
            prob_grad = dot32(values[head], do_block, NT)
            score_grad = (probs * prob_grad).astype(bf16)
            dv_part = dot32(probs.astype(bf16), do_block)
            dk_part = dot32(score_grad, q_block)
            if block == 0:
                dva_ref[:, columns] = dv_part
                dka_ref[:, columns] = dk_part
            else:
                dva_ref[:, columns] += dv_part
                dka_ref[:, columns] += dk_part
            turned.append(dot32(keys_t[head * HEAD : (head + 1) * HEAD], score_grad))
        dq = jnp.concatenate(turned, axis=0).T * 0.125
        dq_ref[rows, :] = rotate(dq, cosine[rows], -sine[rows], lane_rows).astype(bf16)
    first = lane < HEAD
    dk = jnp.where(first, dka_ref[:, :PAIR], dka_ref[:, PAIR:])
    dk_ref[...] = rotate(dk, cosine, -sine, lane).astype(bf16)
    dv_ref[...] = jnp.where(first, dva_ref[:, :PAIR], dva_ref[:, PAIR:]).astype(bf16)


def attend_backward(side, queries, keys, values, outputs, grad_mine, grad_other, stacked, cosine, sine, bias):
    width = values.shape[1] // 2
    pairs = width // PAIR
    tall = lambda columns: pl.BlockSpec((LEN, columns), lambda pair: (0, pair + side * pairs))
    whole = lambda shape: pl.BlockSpec(shape, lambda pair: (0, 0))
    return pl.pallas_call(
        attend_back_kernel,
        grid=(pairs,),
        in_specs=[tall(2 * PAIR)]
        + [tall(PAIR)] * 3
        + [whole(grad_mine.shape)] * 2
        + [pl.BlockSpec((1, D, PAIR), lambda pair: (3, 0, pair + side * pairs))]
        + [whole((LEN, PAIR))] * 3,
        out_specs=[pl.BlockSpec((LEN, PAIR), lambda pair: (0, pair))] * 3,
        out_shape=[jax.ShapeDtypeStruct((LEN, width), bf16)] * 3,
        scratch_shapes=[
            pltpu.VMEM((LEN, 2 * PAIR), bf16),
            pltpu.VMEM((LEN, 2 * PAIR), f32),
            pltpu.VMEM((LEN, 2 * PAIR), f32),
        ],
        compiler_params=pltpu.CompilerParams(vmem_limit_bytes=vmem_bytes),
        cost_estimate=beside,
        name="attend_back",
    )(queries, keys, values, outputs, grad_mine, grad_other, stacked, cosine, sine, bias)


PARTS = 2


def part_copies(table_ref, panels, panel, cuts, start_row, copy, arrays=4):
    for index in range(PARTS):
        which = table_ref[2 * index * panels + panel]
        lead = table_ref[(2 * index + 1) * panels + panel]
        start = pl.multiple_of(start_row + cuts[index], 16)
        for number in range(arrays):

            @pl.when(which == number)
            def _():
                copy(number * PARTS + index, lead, start, cuts[index + 1] - cuts[index])


def project_kernel(panel_rows, cuts, slots_ref, *refs):
    parts, refs = refs[: 4 * PARTS], refs[4 * PARTS :]
    mine_ref, other_ref, cos_ref, sin_ref, q_ref, k_ref, v_ref, out_ref, held, in_sems, out_sem = refs
    per_block = D // panel_rows

    def fetch(panel, carry):
        group = jnp.minimum(panel // per_block, 3)

        def copy(number, lead, start, rows):
            pltpu.make_async_copy(
                parts[number].at[lead], held.at[pl.ds(start, rows)], in_sems.at[group]
            ).start()

        part_copies(slots_ref, 8 * per_block, panel, cuts, panel * panel_rows, copy)
        return carry

    lax.fori_loop(0, 8 * per_block, fetch, 0)
    half = mine_ref.shape[0]
    width = held.shape[1]
    lane = lax.broadcasted_iota(jnp.int32, (half, PAIR), 1)
    for block, ref in enumerate((q_ref, k_ref, v_ref)):
        place = pl.ds(block * D, D)
        pltpu.make_async_copy(held.at[place], held.at[place], in_sems.at[block]).wait()
        pltpu.make_async_copy(held.at[place], out_ref.at[place], out_sem).start()
        for part, rows_ref in enumerate((mine_ref, other_ref)):
            rows = slice(part * half, (part + 1) * half)
            product = dot32(rows_ref[...], held[block * D : (block + 1) * D])
            if block == 2:
                ref[rows, :] = product.astype(bf16)
                continue
            cosine, sine = cos_ref[rows, :], sin_ref[rows, :]
            for pair in range(width // PAIR):
                columns = slice(pair * PAIR, (pair + 1) * PAIR)
                turned = rotate(product[:, columns], cosine, sine, lane).astype(bf16)
                if block == 0:
                    turned = (turned.astype(f32) * 0.125).astype(bf16)
                ref[rows, columns] = turned
    place = pl.ds(3 * D, 5 * D)
    pltpu.make_async_copy(held.at[place], held.at[place], in_sems.at[3]).wait()
    pltpu.make_async_copy(held.at[place], out_ref.at[place], out_sem).start()
    pltpu.make_async_copy(held, out_ref, out_sem).wait()


def project(groups, slots, panel_rows, cuts, mine, other, cosine, sine):
    width = groups[0][0].shape[-1]
    parts = [array.reshape((-1,) + array.shape[-2:]) for group in groups for array in group]
    whole = pl.BlockSpec(memory_space=pltpu.VMEM)
    anywhere = pl.BlockSpec(memory_space=pl.ANY)
    tall = jax.ShapeDtypeStruct((LEN, width), bf16)
    return pl.pallas_call(
        lambda *refs: project_kernel(panel_rows, cuts, *refs),
        in_specs=[pl.BlockSpec(memory_space=pltpu.SMEM)] + [anywhere] * (4 * PARTS) + [whole] * 4,
        out_specs=[whole] * 3 + [anywhere],
        out_shape=[tall] * 3 + [jax.ShapeDtypeStruct((8 * D, width), bf16)],
        scratch_shapes=[
            pltpu.VMEM((8 * D, width), bf16),
            pltpu.SemaphoreType.DMA((4,)),
            pltpu.SemaphoreType.DMA,
        ],
        compiler_params=pltpu.CompilerParams(vmem_limit_bytes=vmem_bytes),
        cost_estimate=pl.CostEstimate(
            flops=2 * LEN * 3 * D * width, bytes_accessed=48 * D * width, transcendentals=0
        ),
        name="project",
    )(slots, *parts, mine, other, cosine, sine)


def feed_kernel(n_ref, g_ref, w_ref, f_ref, d_ref, a_ref, u_ref):
    width = w_ref.shape[2]
    rows, grads = n_ref[...], g_ref[...]
    pre = [dot32(rows, w_ref[i]) for i in range(2)]
    act_grad = [dot32(grads, w_ref[2 + i]) for i in range(2)]
    acts, pre_grads = [], []
    for i in range(2):
        value = pre[i]
        square = value * value
        turn = jnp.tanh(0.7978845608028654 * (value + 0.044715 * (square * value)))
        share = 0.5 * (1.0 + turn)
        slope = share + (0.5 * value) * (1.0 - turn * turn) * (
            0.7978845608028654 + (3 * 0.044715 * 0.7978845608028654) * square
        )
        acts.append((value * share).astype(bf16))
        pre_grads.append((act_grad[i] * slope).astype(bf16))
        a_ref[:, i * width : (i + 1) * width] = acts[i]
        u_ref[:, i * width : (i + 1) * width] = pre_grads[i]
    f_ref[...] = (dot32(acts[0], w_ref[2], NT) + dot32(acts[1], w_ref[3], NT)).astype(f_ref.dtype)
    d_ref[...] = (dot32(pre_grads[0], w_ref[0], NT) + dot32(pre_grads[1], w_ref[1], NT)).astype(d_ref.dtype)


def feed(rows, grads, stacked, kind):
    half, width = rows.shape[0], stacked.shape[2]
    whole = pl.BlockSpec((half, D), lambda step: (0, 0))
    low, sums = jax.ShapeDtypeStruct((half, D), bf16), jax.ShapeDtypeStruct((half, D), kind)
    return pl.pallas_call(
        feed_kernel,
        grid=(1,),
        in_specs=[whole, whole, pl.BlockSpec((4, D, width), lambda step: (1, 0, 0))],
        out_specs=[whole] * 4,
        out_shape=[sums, sums, low, low],
        compiler_params=pltpu.CompilerParams(vmem_limit_bytes=vmem_bytes),
        cost_estimate=pl.CostEstimate(
            flops=2 * 4 * half * D * D, bytes_accessed=16 * D * width, transcendentals=half * D
        ),
        name="feed",
    )(rows, grads, stacked)


def inputs_grad_kernel(*refs):
    grads, w_ref, mine_ref, other_ref = refs[:6], refs[6], refs[7], refs[8]
    half = mine_ref.shape[0]
    narrow = grads[0].shape[1]
    for start, out_ref in ((half, other_ref), (0, mine_ref)):
        rows = slice(start, start + half)
        total = None
        for which in range(3):
            for side in range(2):
                weight = w_ref[which, :, side * narrow : (side + 1) * narrow]
                part = dot32(grads[side * 3 + which][rows, :], weight, NT)
                total = part if total is None else total + part
        out_ref[...] = total.astype(out_ref.dtype)


def inputs_grad(grads, stacked):
    width = stacked.shape[2]
    half = LEN // 2
    out = pl.BlockSpec((half, D), lambda step: (0, 0))
    return pl.pallas_call(
        inputs_grad_kernel,
        grid=(1,),
        in_specs=[pl.BlockSpec((LEN, width // 2), lambda step: (0, 0))] * 6
        + [pl.BlockSpec((3, D, width), lambda step: (0, 0, 0))],
        out_specs=[out, out],
        out_shape=[jax.ShapeDtypeStruct((half, D), f32), jax.ShapeDtypeStruct((half, D), bf16)],
        compiler_params=pltpu.CompilerParams(vmem_limit_bytes=vmem_bytes),
        cost_estimate=beside,
        name="inputs_grad",
    )(*grads, stacked)


def gradients_kernel(panel_rows, cuts, lefts, rights, uses, slots_ref, *refs):
    in_count = 1 + max(max(max(pair) for pair in lefts), max(max(pair) for group in rights for _, pair in group))
    inputs, refs = refs[:in_count], refs[in_count:]
    parts, (block_ref, out_sems) = refs[: 2 * PARTS], refs[2 * PARTS :]
    tall, side = block_ref.shape[2:]
    half = LEN // 2
    pieces = tall // panel_rows
    step = 0
    drained = {}

    def rows_of(pair, part, columns):
        if pair[0] == pair[1]:
            return inputs[pair[0]][part * half : (part + 1) * half, columns]
        return inputs[pair[part]][:, columns]

    for left, right, blocks in uses:
        for left_start in range(0, D, tall):
            place = step % 2
            for number in drained.get(place, ()):
                pltpu.make_async_copy(
                    block_ref.at[place, number], block_ref.at[place, number], out_sems.at[place]
                ).wait()
            product = None
            for part in range(2):
                columns = [rows_of(pair, part, slice(start, start + side)) for start, pair in rights[right]]
                wide = columns[0] if len(columns) == 1 else jnp.concatenate(columns, axis=1)
                term = dot32(rows_of(lefts[left], part, slice(left_start, left_start + tall)), wide, TN)
                product = term if product is None else product + term
            for number, block in enumerate(blocks):
                block_ref[place, number] = product[:, number * side : (number + 1) * side].astype(bf16)

            def send(piece, carry, place=place, left_start=left_start, blocks=blocks):
                for number, block in enumerate(blocks):

                    def copy(array, lead, start, rows):
                        pltpu.make_async_copy(
                            block_ref.at[place, number, pl.ds(start, rows)],
                            parts[array].at[lead],
                            out_sems.at[place],
                        ).start()

                    panel = (block * D + left_start) // panel_rows + piece
                    part_copies(slots_ref, 8 * D // panel_rows, panel, cuts, piece * panel_rows, copy, 2)
                return carry

            lax.fori_loop(0, pieces, send, 0)
            drained[place] = range(len(blocks))
            step += 1
    for place, numbers in drained.items():
        for number in numbers:
            pltpu.make_async_copy(
                block_ref.at[place, number], block_ref.at[place, number], out_sems.at[place]
            ).wait()


def panel_gradients(arrays, lefts, rights, uses, slots, panel_rows, cuts, high_count, width):
    tall = LEN // 2
    outs = [
        jax.ShapeDtypeStruct((8 * high_count, cuts[index + 1] - cuts[index], width), bf16)
        for _ in range(2)
        for index in range(PARTS)
    ]
    outs = pl.pallas_call(
        lambda *refs: gradients_kernel(panel_rows, cuts, lefts, rights, uses, *refs),
        in_specs=[pl.BlockSpec(memory_space=pltpu.SMEM)]
        + [pl.BlockSpec(memory_space=pltpu.VMEM)] * len(arrays),
        out_specs=[pl.BlockSpec(memory_space=pl.ANY)] * (2 * PARTS),
        out_shape=outs,
        scratch_shapes=[pltpu.VMEM((2, 2, tall, width), bf16), pltpu.SemaphoreType.DMA((2,))],
        compiler_params=pltpu.CompilerParams(vmem_limit_bytes=gradient_bytes),
        cost_estimate=beside,
        name="gradients",
    )(slots, *arrays)
    shaped = [out.reshape((2, 2, 2 * high_count) + out.shape[1:]) for out in outs]
    return shaped[:PARTS], shaped[PARTS:]


def gelu_parts(values):
    share = 0.5 * (1.0 + lax.erf(values * 0.7071067811865476))
    density = 0.3989422804014327 * jnp.exp(-0.5 * values * values)
    return share, density


def in_vmem(kernel, name, inputs, outs, scratch=(), specs=None, out_specs=None):
    whole = pl.BlockSpec(memory_space=pltpu.VMEM)
    return pl.pallas_call(
        kernel,
        in_specs=specs or [whole] * len(inputs),
        out_specs=out_specs or [whole] * len(outs),
        out_shape=[jax.ShapeDtypeStruct(shape, kind) for shape, kind in outs],
        scratch_shapes=list(scratch),
        compiler_params=pltpu.CompilerParams(vmem_limit_bytes=vmem_bytes),
        cost_estimate=beside,
        name=name,
    )(*inputs)


def text_forward_kernel(
    core_ref, table_ref, mine_ref, other_ref, normed_ref, masked_ref, keep_ref, mel_mine_ref, mel_other_ref,
    in_bias_ref, gamma_ref, beta_ref, bias_ref, shift_ref, scale_ref,
    pre_ref, energy_ref, grn_ref, text_ref, stream_ref, first_ref, other_first_ref, texts_ref, hidden_held, held, sem, out_sem,
):
    rows = mine_ref.shape[1]
    half = stream_ref.shape[0]

    def fetch(block, carry):
        place = held.at[pl.ds(pl.multiple_of(block * rows, 16), rows)]
        for part, ref in enumerate((mine_ref, other_ref)):

            @pl.when((block + core_ref[0]) % 2 == part)
            def _():
                pltpu.make_async_copy(ref.at[table_ref[block]], place, sem).start()

        return carry

    lax.fori_loop(0, table_ref.shape[0], fetch, 0)
    pltpu.make_async_copy(held, held, sem).wait()
    out = pltpu.make_async_copy(held, texts_ref, out_sem)
    out.start()
    energy_sum = jnp.zeros((1, TXT_FF), f32)
    for part in range(2):
        frames = slice(part * half, (part + 1) * half)
        pre = dot32(normed_ref[frames, :], held[:TEXT]) + in_bias_ref[...]
        if part == 0:
            pre_ref[...] = pre
        hidden = pre * gelu_parts(pre)[0]
        hidden_held[frames, :] = hidden
        energy_sum = energy_sum + jnp.sum(hidden * hidden, axis=0, keepdims=True)
    energy_ref[...] = energy_sum
    energy = jnp.sqrt(energy_sum)
    ratio = energy / (jnp.mean(energy, axis=-1, keepdims=True) + norm_eps)
    weight = gamma_ref[...] * ratio + 1.0
    for part, mel_ref in enumerate((mel_mine_ref, mel_other_ref)):
        frames = slice(part * half, (part + 1) * half)
        grn_low = (weight * hidden_held[frames, :] + beta_ref[...]).astype(bf16)
        text_out = masked_ref[frames, :] + dot32(grn_low, held[TEXT : 2 * TEXT], NT) + bias_ref[...]
        text_low = (text_out * keep_ref[frames, :]).astype(bf16)
        stream = mel_ref[...].astype(f32) + dot32(text_low, held[2 * TEXT :])
        normed, _ = normalise(stream)
        first = (normed * (1.0 + scale_ref[...]) + shift_ref[...]).astype(bf16)
        if part == 0:
            grn_ref[...] = grn_low
            text_ref[...] = text_low
            stream_ref[...] = stream
            first_ref[...] = first
        else:
            other_first_ref[...] = first
    out.wait()


def text_forward(core, table, *inputs):
    whole, anywhere = pl.BlockSpec(memory_space=pltpu.VMEM), pl.BlockSpec(memory_space=pl.ANY)
    scalars = pl.BlockSpec(memory_space=pltpu.SMEM)
    half = LEN // 2
    return in_vmem(
        text_forward_kernel,
        "text_forward",
        (core.reshape(1).astype(jnp.int32), table) + inputs,
        [
            ((half, TXT_FF), f32),
            ((1, TXT_FF), f32),
            ((half, TXT_FF), bf16),
            ((half, TEXT), bf16),
            ((half, D), f32),
            ((half, D), bf16),
            ((half, D), bf16),
            ((3 * TEXT, D), bf16),
        ],
        [
            pltpu.VMEM((LEN, TXT_FF), f32),
            pltpu.VMEM((3 * TEXT, D), bf16),
            pltpu.SemaphoreType.DMA,
            pltpu.SemaphoreType.DMA,
        ],
        [scalars, scalars, anywhere, anywhere] + [whole] * (len(inputs) - 2),
        [whole] * 7 + [anywhere],
    )


def stream_back_kernel(
    core_ref, my_ref, their_ref, stream_ref, later_ref, scale_ref, texts_ref, keep_ref, pre_ref,
    mel_ref, low_ref, shrink_ref, shrink_low_ref, grn_grad_ref, sums_ref, bias_sum_ref, full_ref, sem,
):
    half = mel_ref.shape[0]
    grad = my_ref[...] + their_ref[...].astype(f32)
    normed, scale = normalise(stream_ref[...])
    sums_ref[0:1] = jnp.sum(grad, axis=0, keepdims=True)
    sums_ref[1:2] = jnp.sum(grad * normed, axis=0, keepdims=True)
    mel_grad = later_ref[...] + normalise_back(grad * (1.0 + scale_ref[...]), normed, scale)
    mel_ref[...] = mel_grad
    place = pl.ds(pl.multiple_of(core_ref[0] * half, half), half)
    out = pltpu.make_async_copy(mel_ref, full_ref.at[place], sem)
    out.start()
    low = mel_grad.astype(bf16)
    low_ref[...] = low
    shrink_grad = dot32(low, texts_ref[2 * TEXT :], NT) * keep_ref[...]
    shrink_ref[...] = shrink_grad
    bias_sum_ref[...] = jnp.sum(shrink_grad, axis=0, keepdims=True)
    shrink_low = shrink_grad.astype(bf16)
    shrink_low_ref[...] = shrink_low
    grn_grad = dot32(shrink_low, texts_ref[TEXT : 2 * TEXT])
    grn_grad_ref[...] = grn_grad
    pre = pre_ref[...]
    sums_ref[2:3] = jnp.sum(grn_grad * (pre * gelu_parts(pre)[0]), axis=0, keepdims=True)
    sums_ref[3:4] = jnp.sum(grn_grad, axis=0, keepdims=True)
    sums_ref[4:8] = jnp.zeros((4, D), f32)
    out.wait()


def stream_back(core, *inputs):
    half = inputs[0].shape[0]
    whole = pl.BlockSpec(memory_space=pltpu.VMEM)
    return in_vmem(
        stream_back_kernel,
        "stream_back",
        (core.reshape(1).astype(jnp.int32),) + inputs,
        [
            ((half, D), f32),
            ((half, D), bf16),
            ((half, TEXT), f32),
            ((half, TEXT), bf16),
            ((half, TXT_FF), f32),
            ((8, D), f32),
            ((1, TEXT), f32),
            ((2 * half, D), f32),
        ],
        [pltpu.SemaphoreType.DMA],
        [pl.BlockSpec(memory_space=pltpu.SMEM)] + [whole] * len(inputs),
        [whole] * 7 + [pl.BlockSpec(memory_space=pl.ANY)],
    )


def text_back_kernel(
    pre_ref, grn_grad_ref, energy_ref, dot_ref, gamma_ref, texts_ref, normed_ref, conv_normed_ref, conv_scale_ref, gain_ref,
    shrink_low_ref, grn_ref, text_ref, low_ref, core_ref, table_ref,
    mixed_ref, sums_ref, wide_sums_ref, *rest,
):
    grads_ref = rest[2] if len(rest) > 1 else rest[0]
    pre = pre_ref[...]
    share, density = gelu_parts(pre)
    energy = jnp.sqrt(energy_ref[...])
    energy_mean = jnp.mean(energy, axis=-1, keepdims=True) + norm_eps
    ratio = energy / energy_mean
    ratio_grad = gamma_ref[...] * dot_ref[...]
    energy_grad = (ratio_grad - jnp.mean(ratio_grad * ratio, axis=-1, keepdims=True)) / energy_mean
    hidden_grad = grn_grad_ref[...] * (gamma_ref[...] * ratio + 1.0) + (pre * share) * (energy_grad / energy)
    expand_grad = hidden_grad * (share + pre * density)
    wide_sums_ref[0:1] = jnp.sum(expand_grad, axis=0, keepdims=True)
    wide_sums_ref[1:2] = ratio
    expand_low = expand_grad.astype(bf16)
    grads_ref[:TEXT] = dot32(normed_ref[...], expand_low, TN).astype(bf16)
    grads_ref[TEXT : 2 * TEXT] = dot32(shrink_low_ref[...], grn_ref[...], TN).astype(bf16)
    grads_ref[2 * TEXT :] = dot32(text_ref[...], low_ref[...], TN).astype(bf16)
    normed_grad = dot32(expand_low, texts_ref[:TEXT], NT)
    conv_normed = conv_normed_ref[...]
    sums_ref[0:1] = jnp.sum(normed_grad * conv_normed, axis=0, keepdims=True)
    sums_ref[1:2] = jnp.sum(normed_grad, axis=0, keepdims=True)
    mixed_grad = normalise_back(normed_grad * gain_ref[...], conv_normed, conv_scale_ref[...])
    sums_ref[2:3] = jnp.sum(mixed_grad, axis=0, keepdims=True)
    mixed_ref[...] = mixed_grad
    if len(rest) == 1:
        return
    keep_ref, send_ref, _, sem = rest
    rows = keep_ref.shape[1]

    def place(block, carry):
        piece = grads_ref.at[pl.ds(pl.multiple_of(block * rows, 16), rows)]
        for part, ref in enumerate((keep_ref, send_ref)):

            @pl.when((block + core_ref[0]) % 2 == part)
            def _():
                pltpu.make_async_copy(piece, ref.at[table_ref[block]], sem).start()

        return carry

    lax.fori_loop(0, table_ref.shape[0], place, 0)
    pltpu.make_async_copy(grads_ref, grads_ref, sem).wait()


def text_back(core, table, rows, *inputs):
    half = inputs[0].shape[0]
    whole, anywhere = pl.BlockSpec(memory_space=pltpu.VMEM), pl.BlockSpec(memory_space=pl.ANY)
    scalars = pl.BlockSpec(memory_space=pltpu.SMEM)
    outs = [((half, TEXT), f32), ((3, TEXT), f32), ((2, TXT_FF), f32)]
    apart = rows % 16 == 0
    blocks = ((3 * TEXT // (2 * rows), rows, D), bf16)
    return in_vmem(
        text_back_kernel,
        "text_back",
        inputs + (core.reshape(1).astype(jnp.int32), table),
        outs + ([blocks] * 2 if apart else [((3 * TEXT, D), bf16)]),
        [pltpu.VMEM((3 * TEXT, D), bf16), pltpu.SemaphoreType.DMA] if apart else [],
        [whole] * len(inputs) + [scalars] * 2,
        [whole] * 3 + ([anywhere] * 2 if apart else [whole]),
    )


def conv_back_kernel(
    core_ref, mixed_ref, border_ref, window_ref, kernel_ref, shrink_ref, keep_ref,
    mine_ref, kernel_grad_ref, full_ref, wide, sem,
):
    half = mixed_ref.shape[0]
    edge, margin = border_ref.shape[0], KERNEL // 2
    mixed = mixed_ref[...]
    border = border_ref[...]
    wide[:edge] = jnp.where(core_ref[0] == 1, border, 0.0)
    wide[edge : edge + half] = mixed
    wide[edge + half :] = jnp.where(core_ref[0] == 0, border, 0.0)
    total = shrink_ref[...]
    for j in range(KERNEL):
        start = edge + margin - j
        total = total + wide[start : start + half] * kernel_ref[j : j + 1]
        tap = window_ref[edge - margin + j : edge - margin + j + half]
        kernel_grad_ref[j : j + 1] = jnp.sum(mixed * tap, axis=0, keepdims=True)
    mine_ref[...] = total * keep_ref[...]
    place = pl.ds(pl.multiple_of(core_ref[0] * half, half), half)
    out = pltpu.make_async_copy(mine_ref, full_ref.at[place], sem)
    out.start()
    out.wait()


def conv_back(core, *inputs):
    half = inputs[0].shape[0]
    whole, anywhere = pl.BlockSpec(memory_space=pltpu.VMEM), pl.BlockSpec(memory_space=pl.ANY)
    return in_vmem(
        conv_back_kernel,
        "conv_back",
        (core.reshape(1).astype(jnp.int32),) + inputs,
        [((half, TEXT), f32), ((KERNEL, TEXT), f32), ((2 * half, TEXT), f32)],
        [pltpu.VMEM((half + 2 * inputs[1].shape[0], TEXT), f32), pltpu.SemaphoreType.DMA],
        [pl.BlockSpec(memory_space=pltpu.SMEM)] + [whole] * len(inputs),
        [whole] * 2 + [anywhere],
    )


def settle_kernel(
    core_ref, my_out_ref, their_out_ref, my_grad_ref, their_grad_ref, stream_ref, attention_ref, cot_ref,
    gate_one_ref, scale_ref, gate_two_ref,
    output_ref, later_ref, attention_grad_ref, sums_ref, full_ref, sem,
):
    half = output_ref.shape[0]
    unit_out = my_out_ref[...] + their_out_ref[...].astype(f32)
    stream = stream_ref[...]
    output_ref[...] = (stream + gate_two_ref[...] * unit_out).astype(bf16)
    place = pl.ds(pl.multiple_of(core_ref[0] * half, half), half)
    out = pltpu.make_async_copy(output_ref, full_ref.at[place], sem)
    out.start()
    out_grad = cot_ref[...].astype(f32)
    sums_ref[0:1] = jnp.sum(out_grad * unit_out, axis=0, keepdims=True)
    grad = my_grad_ref[...] + their_grad_ref[...].astype(f32)
    normed, scale = normalise(stream)
    sums_ref[1:2] = jnp.sum(grad, axis=0, keepdims=True)
    sums_ref[2:3] = jnp.sum(grad * normed, axis=0, keepdims=True)
    later = out_grad + normalise_back(grad * (1.0 + scale_ref[...]), normed, scale)
    later_ref[...] = later
    sums_ref[3:4] = jnp.sum(later * attention_ref[...], axis=0, keepdims=True)
    attention_grad_ref[...] = (gate_one_ref[...] * later).astype(bf16)
    out.wait()


def settle(core, *inputs):
    half = inputs[0].shape[0]
    whole, anywhere = pl.BlockSpec(memory_space=pltpu.VMEM), pl.BlockSpec(memory_space=pl.ANY)
    return in_vmem(
        settle_kernel,
        "settle",
        (core.reshape(1).astype(jnp.int32),) + inputs,
        [((half, D), bf16), ((half, D), f32), ((half, D), bf16), ((4, D), f32), ((2 * half, D), bf16)],
        [pltpu.SemaphoreType.DMA],
        [pl.BlockSpec(memory_space=pltpu.SMEM)] + [whole] * len(inputs),
        [whole] * 4 + [anywhere],
    )


def dot_split(left, right, dims=NN):
    split = lambda array: (array.astype(bf16), (array - array.astype(bf16).astype(f32)).astype(bf16))
    left_high, left_low = split(left)
    right_high, right_low = split(right)
    return (
        dot32(left_high, right_high, dims)
        + dot32(left_high, right_low, dims)
        + dot32(left_low, right_high, dims)
    )


def rotated_kernel(places, utterances, *refs):
    pieces, refs = refs[: sum(count for _, _, count in places)], refs[sum(count for _, _, count in places) :]
    left_ref, right_ref, master_ref, first_ref, second_ref, weights_ref, moment_ref, variance_ref, grad_ref = refs
    which = 0
    for row, column, count in places:
        total = pieces[which][...].astype(f32)
        for ref in pieces[which + 1 : which + count]:
            total = total + ref[...].astype(f32)
        rows, columns = total.shape
        grad_ref[row : row + rows, column : column + columns] = total / utterances
        which += count
    left, right = left_ref[...], right_ref[...]
    rotated = dot_split(dot_split(left, grad_ref[...], TN), right)
    moment, variance, direction = moments(rotated, first_ref[...], second_ref[...])
    moment_ref[...] = moment
    variance_ref[...] = variance
    turned = dot_split(dot_split(left, direction), right, NT)
    master = master_ref[...]
    weights_ref[...] = apply_step(master, turned, learn_rate)


def rotated_step(pieces, utterances, left, right, master, first, second):
    places = [(row, column, len(arrays)) for row, column, arrays in pieces]
    arrays = [array for _, _, group in pieces for array in group]
    return in_vmem(
        lambda *refs: rotated_kernel(places, utterances, *refs),
        "rotated_step",
        tuple(arrays) + (left, right, master, first, second),
        [(master.shape, f32)] * 3,
        [pltpu.VMEM(master.shape, f32)],
    )


def modulation_kernel(utterances, time_ref, table_ref, old_ref, first_ref, second_ref, weights_ref, moment_ref, variance_ref):
    grad = dot32(time_ref[...], table_ref[...], TN) / utterances
    moment, variance, direction = moments(grad, first_ref[...], second_ref[...])
    moment_ref[...] = moment
    variance_ref[...] = variance
    weights_ref[...] = apply_step(old_ref[...], direction, learn_rate)


def modulation_step(utterances, time_rows, table, old, first, second):
    rows, columns = old.shape
    step = columns // 6
    tall = pl.BlockSpec((rows, step), lambda i: (0, i))
    return pl.pallas_call(
        lambda *refs: modulation_kernel(utterances, *refs),
        grid=(6,),
        in_specs=[
            pl.BlockSpec((GROUPS, rows), lambda i: (0, 0)),
            pl.BlockSpec((GROUPS, step), lambda i: (0, i)),
        ]
        + [tall] * 3,
        out_specs=[tall] * 3,
        out_shape=[jax.ShapeDtypeStruct(old.shape, f32)] * 3,
        compiler_params=pltpu.CompilerParams(vmem_limit_bytes=vmem_bytes),
        cost_estimate=beside,
        name="modulation_step",
    )(time_rows, table, old, first, second)


def vector_parts(vectors):
    kernel_size = KERNEL * TEXT
    pieces = [vectors[:kernel_size].reshape(KERNEL, TEXT)]
    offset = kernel_size
    for extent in (TEXT, TEXT, TEXT, TEXT, TXT_FF, TXT_FF, TXT_FF, 6 * D):
        pieces.append(vectors[offset : offset + extent])
        offset = offset + extent
    return pieces


def normalise(values):
    center = values - jnp.mean(values, axis=-1, keepdims=True)
    variance = jnp.mean(center * center, axis=-1, keepdims=True)
    scale = lax.rsqrt(variance + norm_eps)
    return center * scale, scale


def normalise_back(grad, normed, scale):
    mean_grad = jnp.mean(grad, axis=-1, keepdims=True)
    mean_dot = jnp.mean(grad * normed, axis=-1, keepdims=True)
    return scale * (grad - mean_grad - normed * mean_dot)


def moments(gradient, first_moment, second_moment):
    first_new = beta_one * first_moment + (1.0 - beta_one) * gradient
    second_new = beta_two * second_moment + (1.0 - beta_two) * gradient * gradient
    bias_first = 1.0 - beta_one**STEP
    bias_second = 1.0 - beta_two**STEP
    direction = first_new / bias_first / (jnp.sqrt(second_new / bias_second) + adam_eps)
    return (first_new, second_new, direction)


def apply_step(weight, direction, rate):
    return weight - rate * (direction + weight_decay * weight)


def rotary_tables(first):
    position = np.arange(LEN)
    frequency = 10000.0 ** (-np.arange(HEAD // 2) * 2.0 / HEAD)
    angle = position[:, None] * frequency[None, :]
    cosine, sine = np.cos(angle), np.sin(angle)
    tables = np.concatenate([cosine] * 4 + [-sine, sine, -sine, sine], axis=1).astype(np.float32)
    tables = lax.dynamic_slice_in_dim(jnp.asarray(np.concatenate([tables, tables])), first, LEN, 0)
    return tables[:, :PAIR], tables[:, PAIR:]


def take_blocks(blocks, index):
    return jnp.take(blocks, index, axis=0, mode="clip")


def both_halves(mine):
    return jnp.concatenate([mine, swap_core(mine)], axis=0)


def sum_halves(multiply, rows, half):
    theirs = multiply(rows[half:]).astype(bf16)
    received = swap_core(theirs)
    return multiply(rows[:half]) + received.astype(f32)


def body(
    mel_frames,
    text_features,
    cotangent,
    time_embedding,
    lengths,
    group_ids,
    text_keep,
    owner_list,
    soap_master,
    soap_first,
    soap_second,
    left_basis,
    right_basis,
    text_matrices,
    text_first,
    text_second,
    modulation_weight,
    modulation_first,
    modulation_second,
    vectors,
    vector_first,
    vector_second,
):
    count = lax.axis_size("dp")
    me, core = lax.axis_index("dp"), lax.axis_index("mp")
    half = LEN // 2
    utterances = lengths.shape[0] * count
    panel_rows, width = soap_master.shape
    share_rows = modulation_weight.shape[0]
    text_rows = text_matrices.shape[0]
    text_half = text_rows // 2
    relative = jnp.arange(count) ^ me

    high_count = count // 16
    cuts = row_cuts(panel_rows)
    panel_table = panel_places(core, owner_list ^ me, high_count)
    gather_table = panel_places(core, owner_list ^ me, high_count, True)
    silu_time = jax.nn.silu(time_embedding.astype(f32)).astype(bf16)
    time_rows = lax.dynamic_slice_in_dim(silu_time, me * share_rows, share_rows, 1)
    weight_half = lax.dynamic_slice_in_dim(modulation_weight, core * 3 * D, 3 * D, 1).astype(bf16)
    own_rows = lax.dynamic_slice_in_dim(text_matrices, core * text_half, text_half, 0)
    text_held = spread_high(own_rows.astype(bf16))
    partial = dot32(time_rows, weight_half)
    held = spread_high(soap_master.astype(bf16))
    text_received, partial_received = tie(swap_bit(text_held, 3), swap_bit(partial, 3))
    text_held = jnp.concatenate([text_held, text_received], axis=0)
    partial = partial + partial_received
    text_received, partial_received, held = tie(
        swap_bits(text_held, phase_bits(text_orders, 0)), swap_bits(partial, phase_bits(text_orders, 0)), held
    )
    held = split_rows(held, cuts)
    text_held = jnp.stack([text_held, text_received])
    partial = partial + partial_received
    received, (text_received, partial_received, far_last) = tie_lists(
        receive(held, 0),
        (
            swap_bits(text_held, phase_bits(text_orders, 1)),
            swap_bits(partial, phase_bits(text_orders, 1)),
            swap_bit(held[1], 3),
        ),
    )
    near = [jnp.stack(pair) for pair in zip(held, received)]
    text_held = jnp.stack([text_held, text_received])
    partial = partial + partial_received
    received, (text_received, partial_received, far_first) = tie_lists(
        receive(near, 1),
        (
            swap_bits(text_held, phase_bits(text_orders, 2)),
            swap_bits(partial, phase_bits(text_orders, 2)),
            swap_bit(held[0], 3),
        ),
    )
    partial = partial + partial_received
    near = [jnp.stack(pair) for pair in zip(near, received)]
    near_received = receive(near, 2)
    far = spread_step([far_first, far_last], 0)
    received = receive(far, 1)
    text_mine = jnp.stack([text_held, text_received]).reshape(count, text_half, D)
    text_other = swap_core(text_mine)
    text_features, mel_frames, cotangent, far = tie(text_features, mel_frames, cotangent, far)
    for bit in range(4, bit_count(count)):
        partial = partial + swap_bit(partial, bit)
    modulation_half = partial
    mine_places, other_places = text_places(core, relative, high_count), text_places(1 - core, relative, high_count)
    text_table = jnp.where(
        core == 0, jnp.stack([mine_places, other_places], 1), jnp.stack([other_places, mine_places], 1)
    ).reshape(-1)
    if text_half % 16:
        source = jnp.arange(2 * count) % 2 != core
        texts = take_blocks(jnp.concatenate([text_mine, text_other]), text_table + count * source)
        text_mine = text_other = texts.reshape(1, 3 * TEXT, D)
        text_table = jnp.zeros((1,), jnp.int32)

    modulation = by_core(core, modulation_half, swap_core(modulation_half), axis=1)
    (
        kernel,
        conv_bias,
        norm_gain,
        norm_bias,
        out_bias,
        in_bias,
        grn_gamma,
        grn_beta,
        modulation_bias,
    ) = vector_parts(vectors)
    group = group_ids[0]
    modulation_row = lax.dynamic_slice_in_dim(modulation, group, 1, 0) + modulation_bias


    first = core * half
    margin = KERNEL // 2
    edge = 8
    keep_all = jnp.pad(text_keep.astype(f32), (edge, edge))[:, None]
    text_all = jnp.pad(text_features, ((edge, edge), (0, 0)))

    def text_start(start):
        window = lax.dynamic_slice_in_dim(text_all, start, half + 2 * edge, 0).astype(f32)
        window = window * lax.dynamic_slice_in_dim(keep_all, start, half + 2 * edge, 0)
        keep = lax.dynamic_slice_in_dim(keep_all, start + edge, half, 0)
        taps = [window[edge - margin + j : edge - margin + j + half] for j in range(KERNEL)]
        mixed = conv_bias[None, :]
        for j in range(KERNEL):
            mixed = mixed + taps[j] * kernel[j][None, :]
        normed, scale = normalise(mixed)
        return window, keep, normed, scale, (normed * norm_gain + norm_bias).astype(bf16)

    window, keep, conv_normed, conv_scale, normed_low = text_start(first)
    window_other, keep_other, _, _, normed_other = text_start(half - first)
    masked_both = jnp.concatenate([window[edge : edge + half], window_other[edge : edge + half]], axis=0)
    keep_both = jnp.concatenate([keep, keep_other], axis=0)
    normed_both = jnp.concatenate([normed_low, normed_other], axis=0)
    mel_mine = lax.dynamic_slice_in_dim(mel_frames, first, half, 0)
    mel_other = lax.dynamic_slice_in_dim(mel_frames, half - first, half, 0)
    cosine, sine = rotary_tables(first)
    received, near_received, (text_other, modulation_row, normed_both, masked_both, cosine, sine) = tie_lists(
        received, near_received, (text_other, modulation_row, normed_both, masked_both, cosine, sine)
    )
    far = [jnp.stack(pair) for pair in zip(far, received)]
    far_received = receive(far, 2)
    shift_one, scale_one, gate_one, shift_two, scale_two, gate_two = (
        modulation_row[:, i * D : (i + 1) * D] for i in range(6)
    )
    expand_pre, energy_sum, grn_low, text_low, stream, first_mine, first_other, texts = text_forward(
        core,
        text_table,
        text_mine,
        text_other,
        normed_both,
        masked_both,
        keep_both,
        mel_mine,
        mel_other,
        in_bias[None],
        grn_gamma[None],
        grn_beta[None],
        out_bias[None],
        shift_one,
        scale_one,
    )

    cot_mine = lax.dynamic_slice_in_dim(cotangent, first, half, 0)
    cot_other = lax.dynamic_slice_in_dim(cotangent, half - first, half, 0)
    hidden_mine = (gate_two * cot_mine.astype(f32)).astype(bf16)
    hidden_other = (gate_two * cot_other.astype(f32)).astype(bf16)
    first_mine, hidden_mine, hidden_other = tie(first_mine, hidden_mine, hidden_other)
    position = (jnp.arange(LEN) + first) % LEN
    bias = jnp.where(position < lengths[0], 0.0, -1e30).astype(bf16)
    bias = jnp.broadcast_to(bias[:, None], (LEN, PAIR))
    queries, keys, value_rows, stacked = project(
        (near, near_received, far, far_received), gather_table, panel_rows, cuts, first_mine, first_other, cosine, sine
    )
    stacked = stacked.reshape(8, D, width)
    attended, query_aug = attend_forward(queries, keys, value_rows, bias)
    attention_out = sum_halves(lambda rows: dot32(rows, stacked[3], NT), attended, half)
    stream_one = stream + gate_one * attention_out

    normed_two, _ = normalise(stream_one)
    second_mine = (normed_two * (1.0 + scale_two) + shift_two).astype(bf16)
    second_other = swap_core(second_mine)
    their_out, their_grad, act_other, pre_other = feed(second_other, hidden_other, stacked, bf16)
    their_out, their_grad = swap_core(their_out), swap_core(their_grad)
    my_out, my_grad, act_mine, pre_mine = feed(second_mine, hidden_mine, stacked, f32)
    output_mine, stream_one_grad, attention_mine, settle_sums, block_output = settle(
        core,
        my_out,
        their_out,
        my_grad,
        their_grad,
        stream_one,
        attention_out,
        cot_mine,
        gate_one,
        scale_two,
        gate_two,
    )
    gate_two_grad, shift_two_grad, scale_two_grad, gate_one_grad = (settle_sums[i] for i in range(4))
    output_theirs = swap_core(output_mine)

    attention_other = swap_core(attention_mine)
    narrow = width // 2

    def back(side, queries):
        return attend_backward(
            side, queries, keys, value_rows, attended, attention_mine, attention_other, stacked, cosine, sine, bias
        )

    def weight_gradients(side, head_grads):
        column = side * narrow
        return panel_gradients(
            [
                first_mine, first_other, attention_mine, attention_other, second_mine, second_other,
                hidden_mine, hidden_other, *head_grads, attended, pre_mine, pre_other, act_mine, act_other,
            ],
            [(0, 1), (2, 3), (4, 5), (6, 7)],
            [
                [(0, (8, 8)), (0, (9, 9))],
                [(0, (10, 10))],
                [(column, (11, 11))],
                [(column, (12, 13)), (width + column, (12, 13))],
                [(column, (14, 15)), (width + column, (14, 15))],
            ],
            ((0, 0, (0, 1)), (0, 1, (2,)), (1, 2, (3,)), (2, 3, (4, 5)), (3, 4, (6, 7))),
            panel_table,
            panel_rows,
            cuts,
            high_count,
            narrow,
        )

    head_grads = list(back(0, query_aug))
    keep_a, send_a = weight_gradients(0, head_grads)
    send_a, (query_aug,) = tie_lists(send_a, (query_aug,))
    received_a = receive(send_a, 2)
    head_grads += list(back(1, query_aug))
    received_a, head_grads = tie_lists(received_a, head_grads)
    part_a = add_all(keep_a, received_a)
    received_a = receive(seconds(part_a), 1)
    my_grad, their_grad = inputs_grad(head_grads, stacked)
    received_a, head_grads, (my_grad, their_grad) = tie_lists(received_a, head_grads, (my_grad, their_grad))
    part_a = add_all(firsts(part_a), received_a)
    received_a = receive(seconds(part_a), 0)
    keep_b, send_b = weight_gradients(1, head_grads[3:])
    their_grad = swap_core(their_grad)
    received_a, send_b, (their_grad,) = tie_lists(received_a, send_b, (their_grad,))

    part_a = add_all(firsts(part_a), received_a)
    received_b = receive(send_b, 2)
    mel_grad_mine, stream_low, shrink_grad, shrink_low, grn_grad, sums, out_bias_grad, mel_gradient = stream_back(
        core, my_grad, their_grad, stream, stream_one_grad, scale_one, texts, keep, expand_pre
    )
    received_b, part_a, (sums, mel_grad_mine) = tie_lists(received_b, part_a, (sums, mel_grad_mine))
    shift_one_grad, scale_one_grad, hidden_dot, beta_grad = sums[0], sums[1], sums[2:3], sums[3]
    out_bias_grad = out_bias_grad[0]
    far_a = [swap_bit(part[high_count:], 3) for part in part_a]
    part_b = add_all(keep_b, received_b)
    received_b = receive(seconds(part_b), 1)
    hidden_dot_all = hidden_dot + swap_core(hidden_dot)
    mixed_grad, text_sums, wide_sums, *text_grads = text_back(
        core,
        text_table,
        text_half,
        expand_pre,
        grn_grad,
        energy_sum,
        hidden_dot_all,
        grn_gamma[None],
        texts,
        normed_low,
        conv_normed,
        conv_scale,
        norm_gain[None],
        shrink_low,
        grn_low,
        text_low,
        stream_low,
    )
    mel_grad_theirs = swap_core(mel_grad_mine)
    gain_grad, norm_bias_grad, conv_bias_grad = text_sums[0], text_sums[1], text_sums[2]
    in_bias_grad, gamma_grad = wide_sums[0], wide_sums[1] * hidden_dot[0]
    if len(text_grads) == 1:
        blocks = text_grads[0].reshape(count, 2, text_half, D)
        order = lambda which: text_slots(which, jnp.arange(count), high_count) ^ me
        text_grads = [
            take_blocks(lax.dynamic_index_in_dim(blocks, which, 1, keepdims=False), order(which))
            for which in (core, 1 - core)
        ]
    received_b, far_a, (mixed_grad, text_keep_half, text_send_half, mel_grad_theirs) = tie_lists(
        received_b, far_a, (mixed_grad, *text_grads, mel_grad_theirs)
    )
    part_b = add_all(firsts(part_b), received_b)
    received_b = receive(seconds(part_b), 0)
    text_received = swap_core(text_send_half)
    border = swap_core(lax.dynamic_slice_in_dim(mixed_grad, (1 - core) * (half - edge), edge, 0))
    text_grad_mine, kernel_grad, text_gradient = conv_back(
        core, mixed_grad, border, window, kernel, shrink_grad, keep
    )

    vector_mine = jnp.concatenate(
        [
            kernel_grad.reshape(-1),
            conv_bias_grad,
            gain_grad,
            norm_bias_grad,
            out_bias_grad,
            in_bias_grad,
            gamma_grad,
            beta_grad,
        ]
    )
    token = jnp.concatenate(
        [shift_one_grad, scale_one_grad, gate_one_grad, shift_two_grad, scale_two_grad, gate_two_grad]
    )
    vector_half = vector_mine.shape[0] // 2
    token_half = 3 * D

    def half_of(which):
        return jnp.concatenate(
            [
                lax.dynamic_slice_in_dim(vector_mine, which * vector_half, vector_half, 0),
                lax.dynamic_slice_in_dim(token, which * token_half, token_half, 0),
            ]
        )

    small_send = half_of(1 - core)
    small = half_of(core)
    in_group = (jnp.arange(GROUPS) == group).astype(f32)

    text_grad_theirs = swap_core(text_grad_mine)
    text_part = add_low(text_keep_half, text_received).reshape(2, 2, 2, 2 * high_count, text_half, D)
    mel_gradient = lax.dynamic_update_slice_in_dim(mel_gradient, mel_grad_theirs, half - first, 0)
    received_b, (text_part, small, small_send, mel_gradient) = tie_lists(
        received_b, (text_part, small, small_send, mel_gradient)
    )
    part_b = add_all(firsts(part_b), received_b)
    far_b = [swap_bit(part[high_count:], 3) for part in part_b]
    text_received = swap_bits(text_part[1], phase_bits(text_orders, 2))
    small_received = swap_core(small_send)
    block_output = lax.dynamic_update_slice_in_dim(block_output, output_theirs, half - first, 0)
    text_gradient = lax.dynamic_update_slice_in_dim(text_gradient, text_grad_theirs, half - first, 0)
    far_b, (text_received, small_received, text_gradient, block_output) = tie_lists(
        far_b, (text_received, small_received, text_gradient, block_output)
    )
    text_part = add_low(text_part[0], text_received)
    text_received = swap_bits(text_part[1], phase_bits(text_orders, 1))
    small = small + small_received
    table = in_group[:, None] * small[None, vector_half:]
    small = jnp.concatenate([small[:vector_half], table.reshape(-1)]).reshape(-1, 128)
    small_received = swap_bits(small, (2, 0))
    panel_pieces = []
    for side, (parts, others) in enumerate(((part_a, far_a), (part_b, far_b))):
        for index, (part, other) in enumerate(zip(parts, others)):
            if high_count == 1:
                arrays = [part[0], other[0]]
            else:
                arrays = [fold_high(part[:high_count].astype(f32) + other.astype(f32))]
            panel_pieces.append((cuts[index], side * narrow, arrays))
    text_received, small_received = tie(text_received, small_received)
    text_part = add_low(text_part[0], text_received)
    small = small + small_received
    text_part = fold(text_part, text_orders, 0)
    text_received = swap_bit(text_part[high_count:], 3)
    small = small + swap_bits(small, (0, 1))
    small = small + swap_bits(small, (1, 2))
    small = small + swap_bit(small, 3)
    own_text = text_part[:high_count].astype(f32) + text_received.astype(f32)
    for bit in range(4, bit_count(count)):
        small = small + swap_bit(small, bit)
    own_text = fold_high(own_text)
    own_text = by_core(core, own_text, swap_core(own_text))
    small = by_core(core, small[None], swap_core(small)[None]).reshape(2, -1)
    vector_sum = small[:, :vector_half].reshape(-1)
    tables = small[:, vector_half:].reshape(2, GROUPS, token_half)
    modulation_grad = jnp.concatenate([tables[0], tables[1]], axis=1)
    vector_gradient = jnp.concatenate([vector_sum, jnp.sum(modulation_grad, axis=0)]) / utterances

    own_text = own_text / utterances
    soap_weights, soap_moment, soap_variance = rotated_step(
        panel_pieces, utterances, left_basis, right_basis, soap_master, soap_first, soap_second
    )
    text_moment, text_variance, text_direction = moments(own_text, text_first, text_second)
    text_weights = apply_step(text_matrices, text_direction, learn_rate)
    modulation_weights, modulation_moment, modulation_variance = modulation_step(
        utterances,
        time_rows,
        modulation_grad.astype(bf16),
        modulation_weight,
        modulation_first,
        modulation_second,
    )
    vector_moment, vector_variance, vector_direction = moments(
        vector_gradient, vector_first, vector_second
    )
    vector_weights = apply_step(vectors, vector_direction, vector_rate)
    return (
        block_output,
        mel_gradient,
        text_gradient,
        soap_weights,
        soap_moment,
        soap_variance,
        text_weights,
        text_moment,
        text_variance,
        modulation_weights,
        modulation_moment,
        modulation_variance,
        vector_weights,
        vector_moment,
        vector_variance,
    )


def solution(mesh):
    rows, quarter, same = P("dp", None), P("dp", "mp"), P()
    return jax.shard_map(
        body,
        mesh=mesh,
        in_specs=(
            (rows,) * 3 + (same,) + (P("dp"),) * 3 + (same,) + (quarter,) * 5 + (rows,) * 6 + (same,) * 3
        ),
        out_specs=(rows,) * 3 + (quarter,) * 3 + (rows,) * 6 + (same,) * 3,
        check_vma=False,
    )
```

```python
import jax
import numpy as np
import jax.numpy as jnp
from jax import lax
from jax.experimental import pallas as pl
from jax.experimental.pallas import tpu as pltpu
from jax.sharding import PartitionSpec as P

D = 1024
HEAD = 64
TEXT = 512
TXT_FF = 1024
KERNEL = 7
LEN = 1024
GROUPS = 8
STEP = 10

f32 = jnp.float32
bf16 = jnp.bfloat16
beta_one = 0.9
beta_two = 0.99
adam_eps = 1e-08
weight_decay = 0.01
learn_rate = 0.03
vector_rate = 0.3
norm_eps = 1e-06


def swap_core(array):
    return lax.ppermute(array, "mp", [(0, 1), (1, 0)])


def swap_bits(array, bits):
    count = lax.axis_size("dp")
    pairs = [
        (i * 2 + core, (i ^ (1 << bits[core])) * 2 + core) for i in range(count) for core in range(2)
    ]
    return lax.ppermute(array, ("dp", "mp"), pairs)


def swap_bit(array, bit):
    return swap_bits(array, (bit, bit))


def by_core(core, mine, other, axis=0):
    return jnp.where(
        core == 0,
        jnp.concatenate([mine, other], axis=axis),
        jnp.concatenate([other, mine], axis=axis),
    )


def bit_count(count):
    return count.bit_length() - 1


def row_cuts(rows):
    return (0, (rows * 2 + 24) // 48 * 16, rows)


axis_orders = (((0, 1, 2), (1, 2, 0)), ((2, 0, 1), (2, 0, 1)))
text_orders = ((2, 0, 1), (2, 1, 0))


def phase_bits(orders, phase):
    return tuple(order[phase] for order in orders)


def tie(*values):
    return lax.optimization_barrier(values)


def tie_lists(*lists):
    flat = [value for values in lists for value in values]
    flat = list(lax.optimization_barrier(tuple(flat)))
    out = []
    for values in lists:
        out.append(flat[: len(values)])
        flat = flat[len(values) :]
    return out


def split_rows(array, cuts):
    return [array[..., cuts[i] : cuts[i + 1], :] for i in range(len(cuts) - 1)]


def spread(part, orders, phase):
    return jnp.stack([part, swap_bits(part, phase_bits(orders, phase))])


def spread_step(parts, phase):
    return [spread(part, axis_orders[index], phase) for index, part in enumerate(parts)]


def spread_last(parts):
    return [(part, swap_bits(part, phase_bits(axis_orders[index], 2))) for index, part in enumerate(parts)]


def spread_high(block):
    held = block[None]
    for bit in range(4, bit_count(lax.axis_size("dp"))):
        held = jnp.concatenate([held, swap_bit(held, bit)], axis=0)
    return held


def add_low(left, right):
    return (left.astype(f32) + right.astype(f32)).astype(bf16)


def receive(sends, phase):
    return [swap_bits(send, phase_bits(axis_orders[index], phase)) for index, send in enumerate(sends)]


def add_all(keeps, received):
    return [add_low(keep, other) for keep, other in zip(keeps, received)]


def firsts(parts):
    return [part[0] for part in parts]


def seconds(parts):
    return [part[1] for part in parts]


def fold(part, orders, phase):
    return add_low(part[0], swap_bits(part[1], phase_bits(orders, phase)))


def fold_high(total):
    count = total.shape[0]
    if count == 1:
        return total[0]
    for bit in range(bit_count(count) - 1, -1, -1):
        half = 1 << bit
        total = total[:half] + swap_bit(total[half:].astype(bf16), bit + 4).astype(f32)
    return total[0]


def bit_of(values, which):
    return (values >> which) & 1


def panel_places(core, slots, high_count, apart=False):
    rows = []
    for orders in axis_orders:
        far = bit_of(slots, 3)
        which = [bit_of(slots, order[2]) + (2 * far if apart else 0) for order in orders]
        lead = [bit_of(slots, order[1]) * 2 + bit_of(slots, order[0]) for order in orders]
        if not apart:
            lead = [place * 2 + far for place in lead]
        lead = [place * high_count + (slots >> 4) for place in lead]
        rows += [jnp.where(core == 0, *which), jnp.where(core == 0, *lead)]
    return jnp.concatenate(rows).astype(jnp.int32)


def text_places(core, slots, high_count):
    places = []
    for order in text_orders:
        high = bit_of(slots, 3) * high_count + (slots >> 4)
        places.append(
            ((bit_of(slots, order[2]) * 2 + bit_of(slots, order[1])) * 2 + bit_of(slots, order[0]))
            * (2 * high_count)
            + high
        )
    return jnp.where(core == 0, *places).astype(jnp.int32)


def text_slots(core, places, high_count):
    lead, rest = places // (2 * high_count), places % (2 * high_count)
    high = ((rest // high_count) << 3) | ((rest % high_count) << 4)
    slots = []
    for order in text_orders:
        low = (bit_of(lead, 2) << order[2]) | (bit_of(lead, 1) << order[1]) | (bit_of(lead, 0) << order[0])
        slots.append(high | low)
    return jnp.where(core == 0, *slots)


beside = pl.CostEstimate(flops=1000, bytes_accessed=1000, transcendentals=0)

NT = (((1,), (1,)), ((), ()))
NN = (((1,), (0,)), ((), ()))
TN = (((0,), (0,)), ((), ()))
ROWS = 256
LONG_ROWS = 512
PAIR = 2 * HEAD
vmem_bytes = 16 * 1024 * 1024
gradient_bytes = 24 * 1024 * 1024
project_bytes = 32 * 1024 * 1024


def dot32(left, right, dims=NN):
    return lax.dot_general(left, right, dims, preferred_element_type=f32)


def three_terms(values):
    high = values.astype(bf16).astype(f32)
    rest = values - high
    middle = rest.astype(bf16).astype(f32)
    return high, middle, rest - middle


def rotate(values, cosine, sine, lane):
    partner = jnp.where(
        lane % HEAD < HEAD // 2,
        pltpu.roll(values, PAIR - HEAD // 2, 1),
        pltpu.roll(values, HEAD // 2, 1),
    )
    return values * cosine + partner * sine


def attend_kernel(q_ref, k_ref, v_ref, bias_ref, o_ref, qa_ref):
    lane = lax.broadcasted_iota(jnp.int32, (LEN, PAIR), 1)
    lane_rows = lax.broadcasted_iota(jnp.int32, (LONG_ROWS, PAIR), 1)
    row_index = lax.broadcasted_iota(jnp.int32, (PAIR, LONG_ROWS), 0)
    q_wide = q_ref[...].astype(f32)
    k_wide = k_ref[...].astype(f32)
    values_t = v_ref[...].T
    bias = bias_ref[...].astype(f32)
    keys = []
    for head in range(2):
        own = lane // HEAD == head
        spare = (1 - head) * HEAD
        keys.append(
            jnp.where(own, k_wide, jnp.where(lane == spare, bias, 0.0)).astype(bf16)
        )
        qa_ref[:, head * PAIR : (head + 1) * PAIR] = jnp.where(
            own, q_wide, jnp.where(lane == spare, 1.0, 0.0)
        ).astype(bf16)
    steps = [(block, head) for block in range(LEN // LONG_ROWS) for head in range(2)]

    def scores_of(step):
        block, head = step
        rows = slice(block * LONG_ROWS, (block + 1) * LONG_ROWS)
        return dot32(keys[head], qa_ref[rows, head * PAIR : (head + 1) * PAIR], NT)

    following = scores_of(steps[0])
    for position, (block, head) in enumerate(steps):
        scores = following
        if position + 1 < len(steps):
            following = scores_of(steps[position + 1])
        rows = slice(block * LONG_ROWS, (block + 1) * LONG_ROWS)
        if head == 0:
            outs, extra = [], jnp.zeros((PAIR, LONG_ROWS), f32)
        spare = (1 - head) * HEAD
        highest = jnp.max(scores, axis=0, keepdims=True)
        weights = jnp.exp(scores - highest)
        total = jnp.sum(weights, axis=0, keepdims=True)
        out_t = dot32(values_t[head * HEAD : (head + 1) * HEAD], weights.astype(bf16))
        outs.append(out_t / total)
        for place, term in enumerate(three_terms(highest + jnp.log(total))):
            extra = jnp.where(row_index == spare + 1 + place, -term, extra)
        if head == 0:
            continue
        o_ref[rows, :] = jnp.concatenate(outs, axis=0).T.astype(bf16)
        extra_t = extra.T
        for head in range(2):
            spare = (1 - head) * HEAD
            columns = slice(head * PAIR, (head + 1) * PAIR)
            is_extra = (lane_rows > spare) & (lane_rows < spare + 4)
            qa_ref[rows, columns] = jnp.where(
                is_extra, extra_t, qa_ref[rows, columns].astype(f32)
            ).astype(bf16)


def attend_forward(queries, keys, values, bias):
    width = values.shape[1]
    pairs = width // PAIR
    tall = lambda columns: pl.BlockSpec((LEN, columns), lambda pair: (0, pair))
    whole = pl.BlockSpec((LEN, PAIR), lambda pair: (0, 0))
    return pl.pallas_call(
        attend_kernel,
        grid=(pairs,),
        in_specs=[tall(PAIR), tall(PAIR), tall(PAIR), whole],
        out_specs=[tall(PAIR), tall(2 * PAIR)],
        out_shape=[
            jax.ShapeDtypeStruct((LEN, width), bf16),
            jax.ShapeDtypeStruct((LEN, 2 * width), bf16),
        ],
        compiler_params=pltpu.CompilerParams(vmem_limit_bytes=vmem_bytes),
        cost_estimate=pl.CostEstimate(
            flops=2 * 4 * LEN * LEN * width * 4,
            bytes_accessed=6 * LEN * width * 2,
            transcendentals=LEN * LEN * width // HEAD,
        ),
        name="attend",
    )(queries, keys, values, bias)


def attend_back_kernel(
    qa_ref, kr_ref, v_ref, o_ref, mine_ref, other_ref, weight_ref, cos_ref, sin_ref, bias_ref,
    dq_ref, dk_ref, dv_ref, *rest,
):
    doa_ref, dka_ref, dva_ref = rest[-3:]
    if len(rest) > 3:

        @pl.when(pl.program_id(0) == 0)
        def _():
            rest[0][...] = mine_ref[...].T
            rest[1][...] = other_ref[...].T

    lane = lax.broadcasted_iota(jnp.int32, (LEN, PAIR), 1)
    lane_rows = lax.broadcasted_iota(jnp.int32, (ROWS, PAIR), 1)
    cosine, sine = cos_ref[...], sin_ref[...]
    k_wide = kr_ref[...].astype(f32)
    keys_t = kr_ref[...].T
    v_wide = v_ref[...].astype(f32)
    do_wide = jnp.concatenate(
        [dot32(ref[...], weight_ref[0]).astype(bf16).astype(f32) for ref in (mine_ref, other_ref)],
        axis=0,
    )
    bias = bias_ref[...].astype(f32)
    product = do_wide * o_ref[...].astype(f32)
    keys, values = [], []
    for head in range(2):
        own = lane // HEAD == head
        spare = (1 - head) * HEAD
        is_extra = (lane > spare) & (lane < spare + 4)
        ones = jnp.where(is_extra, 1.0, 0.0)
        keys.append(
            jnp.where(own, k_wide, jnp.where(lane == spare, bias, ones)).astype(bf16)
        )
        values.append(jnp.where(own, v_wide, ones).astype(bf16))
        row_dot = jnp.sum(jnp.where(own, product, 0.0), axis=1, keepdims=True)
        grad = jnp.where(own, do_wide, 0.0)
        for place, term in enumerate(three_terms(row_dot)):
            grad = jnp.where(lane == spare + 1 + place, -term, grad)
        doa_ref[:, head * PAIR : (head + 1) * PAIR] = grad.astype(bf16)
    for block in range(LEN // ROWS):
        rows = slice(block * ROWS, (block + 1) * ROWS)
        turned = []
        for head in range(2):
            columns = slice(head * PAIR, (head + 1) * PAIR)
            q_block = qa_ref[rows, columns]
            do_block = doa_ref[rows, columns]
            probs = jnp.exp(dot32(keys[head], q_block, NT))
            prob_grad = dot32(values[head], do_block, NT)
            score_grad = (probs * prob_grad).astype(bf16)
            dv_part = dot32(probs.astype(bf16), do_block)
            dk_part = dot32(score_grad, q_block)
            if block == 0:
                dva_ref[:, columns] = dv_part
                dka_ref[:, columns] = dk_part
            else:
                dva_ref[:, columns] += dv_part
                dka_ref[:, columns] += dk_part
            turned.append(dot32(keys_t[head * HEAD : (head + 1) * HEAD], score_grad))
        dq = jnp.concatenate(turned, axis=0).T * 0.125
        dq_ref[rows, :] = rotate(dq, cosine[rows], -sine[rows], lane_rows).astype(bf16)
    first = lane < HEAD
    dk = jnp.where(first, dka_ref[:, :PAIR], dka_ref[:, PAIR:])
    dk_ref[...] = rotate(dk, cosine, -sine, lane).astype(bf16)
    dv_ref[...] = jnp.where(first, dva_ref[:, :PAIR], dva_ref[:, PAIR:]).astype(bf16)


def attend_backward(side, queries, keys, values, outputs, grad_mine, grad_other, stacked, cosine, sine, bias):
    width = values.shape[1] // 2
    pairs = width // PAIR
    turned = grad_mine.shape[::-1]
    tall = lambda columns: pl.BlockSpec((LEN, columns), lambda pair: (0, pair + side * pairs))
    whole = lambda shape: pl.BlockSpec(shape, lambda pair: (0, 0))
    return pl.pallas_call(
        attend_back_kernel,
        grid=(pairs,),
        in_specs=[tall(2 * PAIR)]
        + [tall(PAIR)] * 3
        + [whole(grad_mine.shape)] * 2
        + [pl.BlockSpec((1, D, PAIR), lambda pair: (3, 0, pair + side * pairs))]
        + [whole((LEN, PAIR))] * 3,
        out_specs=[pl.BlockSpec((LEN, PAIR), lambda pair: (0, pair))] * 3 + [whole(turned)] * (2 - 2 * side),
        out_shape=[jax.ShapeDtypeStruct((LEN, width), bf16)] * 3
        + [jax.ShapeDtypeStruct(turned, bf16)] * (2 - 2 * side),
        scratch_shapes=[
            pltpu.VMEM((LEN, 2 * PAIR), bf16),
            pltpu.VMEM((LEN, 2 * PAIR), f32),
            pltpu.VMEM((LEN, 2 * PAIR), f32),
        ],
        compiler_params=pltpu.CompilerParams(vmem_limit_bytes=vmem_bytes),
        cost_estimate=beside,
        name="attend_back",
    )(queries, keys, values, outputs, grad_mine, grad_other, stacked, cosine, sine, bias)


PARTS = 2


def part_copies(table_ref, panels, panel, cuts, start_row, copy, arrays=4):
    for index in range(PARTS):
        which = table_ref[2 * index * panels + panel]
        lead = table_ref[(2 * index + 1) * panels + panel]
        start = pl.multiple_of(start_row + cuts[index], 16)
        for number in range(arrays):

            @pl.when(which == number)
            def _():
                copy(number * PARTS + index, lead, start, cuts[index + 1] - cuts[index])


def project_kernel(panel_rows, cuts, slots_ref, *refs):
    parts, refs = refs[: 4 * PARTS], refs[4 * PARTS :]
    mine_ref, other_ref, cos_ref, sin_ref, q_ref, k_ref, v_ref, out_ref = refs
    per_block = D // panel_rows

    def fetch(panel, carry):
        def copy(number, lead, start, rows):
            out_ref[pl.ds(start, rows), :] = parts[number][lead]

        part_copies(slots_ref, 8 * per_block, panel, cuts, panel * panel_rows, copy)
        return carry

    lax.fori_loop(0, 8 * per_block, fetch, 0)
    half = mine_ref.shape[0]
    width = out_ref.shape[1]
    lane = lax.broadcasted_iota(jnp.int32, (half, PAIR), 1)
    for block, ref in enumerate((q_ref, k_ref, v_ref)):
        for part, rows_ref in enumerate((mine_ref, other_ref)):
            rows = slice(part * half, (part + 1) * half)
            product = dot32(rows_ref[...], out_ref[block * D : (block + 1) * D, :])
            if block == 2:
                ref[rows, :] = product.astype(bf16)
                continue
            cosine, sine = cos_ref[rows, :], sin_ref[rows, :]
            for pair in range(width // PAIR):
                columns = slice(pair * PAIR, (pair + 1) * PAIR)
                turned = rotate(product[:, columns], cosine, sine, lane).astype(bf16)
                if block == 0:
                    turned = (turned.astype(f32) * 0.125).astype(bf16)
                ref[rows, columns] = turned


def project(groups, slots, panel_rows, cuts, mine, other, cosine, sine):
    width = groups[0][0].shape[-1]
    parts = [array.reshape((-1,) + array.shape[-2:]) for group in groups for array in group]
    whole = pl.BlockSpec(memory_space=pltpu.VMEM)
    tall = jax.ShapeDtypeStruct((LEN, width), bf16)
    return pl.pallas_call(
        lambda *refs: project_kernel(panel_rows, cuts, *refs),
        in_specs=[pl.BlockSpec(memory_space=pltpu.SMEM)] + [whole] * (4 * PARTS + 4),
        out_specs=[whole] * 4,
        out_shape=[tall] * 3 + [jax.ShapeDtypeStruct((8 * D, width), bf16)],
        compiler_params=pltpu.CompilerParams(vmem_limit_bytes=project_bytes),
        cost_estimate=pl.CostEstimate(
            flops=2 * LEN * 3 * D * width, bytes_accessed=48 * D * width, transcendentals=0
        ),
        name="project",
    )(slots, *parts, mine, other, cosine, sine)


def feed_kernel(n_ref, g_ref, w_ref, f_ref, d_ref, a_ref, u_ref, n_t_ref, g_t_ref):
    width = w_ref.shape[2]
    rows, grads = n_ref[...], g_ref[...]
    n_t_ref[...] = rows.T
    g_t_ref[...] = grads.T
    pre = [dot32(rows, w_ref[i]) for i in range(2)]
    act_grad = [dot32(grads, w_ref[2 + i]) for i in range(2)]
    acts, pre_grads = [], []
    for i in range(2):
        value = pre[i]
        square = value * value
        turn = jnp.tanh(0.7978845608028654 * (value + 0.044715 * (square * value)))
        share = 0.5 * (1.0 + turn)
        slope = share + (0.5 * value) * (1.0 - turn * turn) * (
            0.7978845608028654 + (3 * 0.044715 * 0.7978845608028654) * square
        )
        acts.append((value * share).astype(bf16))
        pre_grads.append((act_grad[i] * slope).astype(bf16))
        a_ref[:, i * width : (i + 1) * width] = acts[i]
        u_ref[:, i * width : (i + 1) * width] = pre_grads[i]
    f_ref[...] = (dot32(acts[0], w_ref[2], NT) + dot32(acts[1], w_ref[3], NT)).astype(f_ref.dtype)
    d_ref[...] = (dot32(pre_grads[0], w_ref[0], NT) + dot32(pre_grads[1], w_ref[1], NT)).astype(d_ref.dtype)


def feed(rows, grads, stacked, kind):
    half, width = rows.shape[0], stacked.shape[2]
    whole = pl.BlockSpec((half, D), lambda step: (0, 0))
    low, sums = jax.ShapeDtypeStruct((half, D), bf16), jax.ShapeDtypeStruct((half, D), kind)
    return pl.pallas_call(
        feed_kernel,
        grid=(1,),
        in_specs=[whole, whole, pl.BlockSpec((4, D, width), lambda step: (1, 0, 0))],
        out_specs=[whole] * 4 + [pl.BlockSpec((D, half), lambda step: (0, 0))] * 2,
        out_shape=[sums, sums, low, low] + [jax.ShapeDtypeStruct((D, half), bf16)] * 2,
        compiler_params=pltpu.CompilerParams(vmem_limit_bytes=vmem_bytes),
        cost_estimate=pl.CostEstimate(
            flops=2 * 4 * half * D * D, bytes_accessed=16 * D * width, transcendentals=half * D
        ),
        name="feed",
    )(rows, grads, stacked)


def inputs_grad_kernel(*refs):
    grads, w_ref, mine_ref, other_ref = refs[:6], refs[6], refs[7], refs[8]
    half = mine_ref.shape[0]
    narrow = grads[0].shape[1]
    for start, out_ref in ((half, other_ref), (0, mine_ref)):
        rows = slice(start, start + half)
        total = None
        for which in range(3):
            for side in range(2):
                weight = w_ref[which, :, side * narrow : (side + 1) * narrow]
                part = dot32(grads[side * 3 + which][rows, :], weight, NT)
                total = part if total is None else total + part
        out_ref[...] = total.astype(out_ref.dtype)


def inputs_grad(grads, stacked):
    width = stacked.shape[2]
    half = LEN // 2
    out = pl.BlockSpec((half, D), lambda step: (0, 0))
    return pl.pallas_call(
        inputs_grad_kernel,
        grid=(1,),
        in_specs=[pl.BlockSpec((LEN, width // 2), lambda step: (0, 0))] * 6
        + [pl.BlockSpec((3, D, width), lambda step: (0, 0, 0))],
        out_specs=[out, out],
        out_shape=[jax.ShapeDtypeStruct((half, D), f32), jax.ShapeDtypeStruct((half, D), bf16)],
        compiler_params=pltpu.CompilerParams(vmem_limit_bytes=vmem_bytes),
        cost_estimate=beside,
        name="inputs_grad",
    )(*grads, stacked)


def gradients_kernel(panel_rows, cuts, lefts, rights, uses, slots_ref, *refs):
    in_count = 1 + max(max(max(pair) for pair in lefts), max(max(pair) for group in rights for _, pair in group))
    inputs, refs = refs[:in_count], refs[in_count:]
    parts, (block_ref,) = refs[: 2 * PARTS], refs[2 * PARTS :]
    tall, side = block_ref.shape[1:]
    half = LEN // 2
    pieces = tall // panel_rows

    def rows_of(pair, part, columns):
        if pair[0] == pair[1]:
            return inputs[pair[0]][part * half : (part + 1) * half, columns]
        return inputs[pair[part]][:, columns]

    for left, right, blocks in uses:
        for left_start in range(0, D, tall):
            product = None
            for part in range(2):
                columns = [rows_of(pair, part, slice(start, start + side)) for start, pair in rights[right]]
                wide = columns[0] if len(columns) == 1 else jnp.concatenate(columns, axis=1)
                term = dot32(inputs[lefts[left][part]][left_start : left_start + tall, :], wide)
                product = term if product is None else product + term
            places = [(block * D + left_start) // tall for block in blocks]
            for number, place in enumerate(places):
                block_ref[place] = product[:, number * side : (number + 1) * side].astype(bf16)

            def send(piece, carry, places=places):
                for place in places:

                    def copy(array, lead, start, rows):
                        parts[array][lead] = block_ref[place, pl.ds(start, rows), :]

                    part_copies(
                        slots_ref, 8 * D // panel_rows, place * pieces + piece, cuts, piece * panel_rows, copy, 2
                    )
                return carry

            lax.fori_loop(0, pieces, send, 0)


def panel_gradients(arrays, lefts, rights, uses, slots, panel_rows, cuts, high_count, width):
    tall = LEN // 2
    outs = [
        jax.ShapeDtypeStruct((8 * high_count, cuts[index + 1] - cuts[index], width), bf16)
        for _ in range(2)
        for index in range(PARTS)
    ]
    outs = pl.pallas_call(
        lambda *refs: gradients_kernel(panel_rows, cuts, lefts, rights, uses, *refs),
        in_specs=[pl.BlockSpec(memory_space=pltpu.SMEM)]
        + [pl.BlockSpec(memory_space=pltpu.VMEM)] * len(arrays),
        out_specs=[pl.BlockSpec(memory_space=pltpu.VMEM)] * (2 * PARTS),
        out_shape=outs,
        scratch_shapes=[pltpu.VMEM((8 * D // tall, tall, width), bf16)],
        compiler_params=pltpu.CompilerParams(vmem_limit_bytes=gradient_bytes),
        cost_estimate=beside,
        name="gradients",
    )(slots, *arrays)
    shaped = [out.reshape((2, 2, 2 * high_count) + out.shape[1:]) for out in outs]
    return shaped[:PARTS], shaped[PARTS:]


def gelu_parts(values):
    share = 0.5 * (1.0 + lax.erf(values * 0.7071067811865476))
    density = 0.3989422804014327 * jnp.exp(-0.5 * values * values)
    return share, density


def in_vmem(kernel, name, inputs, outs, scratch=(), specs=None, out_specs=None):
    whole = pl.BlockSpec(memory_space=pltpu.VMEM)
    return pl.pallas_call(
        kernel,
        in_specs=specs or [whole] * len(inputs),
        out_specs=out_specs or [whole] * len(outs),
        out_shape=[jax.ShapeDtypeStruct(shape, kind) for shape, kind in outs],
        scratch_shapes=list(scratch),
        compiler_params=pltpu.CompilerParams(vmem_limit_bytes=vmem_bytes),
        cost_estimate=beside,
        name=name,
    )(*inputs)


def text_forward_kernel(
    core_ref, table_ref, mine_ref, other_ref, normed_ref, masked_ref, keep_ref, mel_mine_ref, mel_other_ref,
    in_bias_ref, gamma_ref, beta_ref, bias_ref, shift_ref, scale_ref,
    pre_ref, energy_ref, grn_ref, text_ref, stream_ref, first_ref, other_first_ref, first_t_ref, other_first_t_ref, texts_ref,
    hidden_held,
):
    rows = mine_ref.shape[1]
    half = stream_ref.shape[0]

    held = texts_ref

    def fetch(block, carry):
        place = pl.ds(pl.multiple_of(block * rows, 16), rows)
        for part, ref in enumerate((mine_ref, other_ref)):

            @pl.when((block + core_ref[0]) % 2 == part)
            def _():
                texts_ref[place, :] = ref[table_ref[block]]

        return carry

    lax.fori_loop(0, table_ref.shape[0], fetch, 0)
    energy_sum = jnp.zeros((1, TXT_FF), f32)
    for part in range(2):
        frames = slice(part * half, (part + 1) * half)
        pre = dot32(normed_ref[frames, :], held[:TEXT]) + in_bias_ref[...]
        if part == 0:
            pre_ref[...] = pre
        hidden = pre * gelu_parts(pre)[0]
        hidden_held[frames, :] = hidden
        energy_sum = energy_sum + jnp.sum(hidden * hidden, axis=0, keepdims=True)
    energy_ref[...] = energy_sum
    energy = jnp.sqrt(energy_sum)
    ratio = energy / (jnp.mean(energy, axis=-1, keepdims=True) + norm_eps)
    weight = gamma_ref[...] * ratio + 1.0
    for part, mel_ref in enumerate((mel_mine_ref, mel_other_ref)):
        frames = slice(part * half, (part + 1) * half)
        grn_low = (weight * hidden_held[frames, :] + beta_ref[...]).astype(bf16)
        text_out = masked_ref[frames, :] + dot32(grn_low, held[TEXT : 2 * TEXT], NT) + bias_ref[...]
        text_low = (text_out * keep_ref[frames, :]).astype(bf16)
        stream = mel_ref[...].astype(f32) + dot32(text_low, held[2 * TEXT :])
        normed, _ = normalise(stream)
        first = (normed * (1.0 + scale_ref[...]) + shift_ref[...]).astype(bf16)
        if part == 0:
            grn_ref[...] = grn_low
            text_ref[...] = text_low
            stream_ref[...] = stream
            first_ref[...] = first
            first_t_ref[...] = first.T
        else:
            other_first_ref[...] = first
            other_first_t_ref[...] = first.T


def text_forward(core, table, *inputs):
    whole = pl.BlockSpec(memory_space=pltpu.VMEM)
    scalars = pl.BlockSpec(memory_space=pltpu.SMEM)
    half = LEN // 2
    return in_vmem(
        text_forward_kernel,
        "text_forward",
        (core.reshape(1).astype(jnp.int32), table) + inputs,
        [
            ((half, TXT_FF), f32),
            ((1, TXT_FF), f32),
            ((half, TXT_FF), bf16),
            ((half, TEXT), bf16),
            ((half, D), f32),
            ((half, D), bf16),
            ((half, D), bf16),
            ((D, half), bf16),
            ((D, half), bf16),
            ((3 * TEXT, D), bf16),
        ],
        [pltpu.VMEM((LEN, TXT_FF), f32)],
        [scalars, scalars] + [whole] * len(inputs),
        [whole] * 10,
    )


def stream_back_kernel(
    core_ref, my_ref, their_ref, stream_ref, later_ref, scale_ref, texts_ref, keep_ref, pre_ref,
    mel_ref, low_ref, shrink_ref, shrink_low_ref, grn_grad_ref, sums_ref, bias_sum_ref, full_ref,
):
    half = mel_ref.shape[0]
    grad = my_ref[...] + their_ref[...].astype(f32)
    normed, scale = normalise(stream_ref[...])
    sums_ref[0:1] = jnp.sum(grad, axis=0, keepdims=True)
    sums_ref[1:2] = jnp.sum(grad * normed, axis=0, keepdims=True)
    mel_grad = later_ref[...] + normalise_back(grad * (1.0 + scale_ref[...]), normed, scale)
    mel_ref[...] = mel_grad
    place = pl.ds(pl.multiple_of(core_ref[0] * half, half), half)
    full_ref[place, :] = mel_ref[...]
    low = mel_grad.astype(bf16)
    low_ref[...] = low
    shrink_grad = dot32(low, texts_ref[2 * TEXT :], NT) * keep_ref[...]
    shrink_ref[...] = shrink_grad
    bias_sum_ref[...] = jnp.sum(shrink_grad, axis=0, keepdims=True)
    shrink_low = shrink_grad.astype(bf16)
    shrink_low_ref[...] = shrink_low
    grn_grad = dot32(shrink_low, texts_ref[TEXT : 2 * TEXT])
    grn_grad_ref[...] = grn_grad
    pre = pre_ref[...]
    sums_ref[2:3] = jnp.sum(grn_grad * (pre * gelu_parts(pre)[0]), axis=0, keepdims=True)
    sums_ref[3:4] = jnp.sum(grn_grad, axis=0, keepdims=True)
    sums_ref[4:8] = jnp.zeros((4, D), f32)


def stream_back(core, *inputs):
    half = inputs[0].shape[0]
    whole = pl.BlockSpec(memory_space=pltpu.VMEM)
    return in_vmem(
        stream_back_kernel,
        "stream_back",
        (core.reshape(1).astype(jnp.int32),) + inputs,
        [
            ((half, D), f32),
            ((half, D), bf16),
            ((half, TEXT), f32),
            ((half, TEXT), bf16),
            ((half, TXT_FF), f32),
            ((8, D), f32),
            ((1, TEXT), f32),
            ((2 * half, D), f32),
        ],
        [],
        [pl.BlockSpec(memory_space=pltpu.SMEM)] + [whole] * len(inputs),
        [whole] * 8,
    )


def text_back_kernel(
    pre_ref, grn_grad_ref, energy_ref, dot_ref, gamma_ref, texts_ref, normed_ref, conv_normed_ref, conv_scale_ref, gain_ref,
    shrink_low_ref, grn_ref, text_ref, low_ref, core_ref, table_ref,
    mixed_ref, sums_ref, wide_sums_ref, *rest,
):
    grads_ref = rest[2] if len(rest) > 1 else rest[0]
    pre = pre_ref[...]
    share, density = gelu_parts(pre)
    energy = jnp.sqrt(energy_ref[...])
    energy_mean = jnp.mean(energy, axis=-1, keepdims=True) + norm_eps
    ratio = energy / energy_mean
    ratio_grad = gamma_ref[...] * dot_ref[...]
    energy_grad = (ratio_grad - jnp.mean(ratio_grad * ratio, axis=-1, keepdims=True)) / energy_mean
    hidden_grad = grn_grad_ref[...] * (gamma_ref[...] * ratio + 1.0) + (pre * share) * (energy_grad / energy)
    expand_grad = hidden_grad * (share + pre * density)
    wide_sums_ref[0:1] = jnp.sum(expand_grad, axis=0, keepdims=True)
    wide_sums_ref[1:2] = ratio
    expand_low = expand_grad.astype(bf16)
    grads_ref[:TEXT] = dot32(normed_ref[...], expand_low, TN).astype(bf16)
    grads_ref[TEXT : 2 * TEXT] = dot32(shrink_low_ref[...], grn_ref[...], TN).astype(bf16)
    grads_ref[2 * TEXT :] = dot32(text_ref[...], low_ref[...], TN).astype(bf16)
    normed_grad = dot32(expand_low, texts_ref[:TEXT], NT)
    conv_normed = conv_normed_ref[...]
    sums_ref[0:1] = jnp.sum(normed_grad * conv_normed, axis=0, keepdims=True)
    sums_ref[1:2] = jnp.sum(normed_grad, axis=0, keepdims=True)
    mixed_grad = normalise_back(normed_grad * gain_ref[...], conv_normed, conv_scale_ref[...])
    sums_ref[2:3] = jnp.sum(mixed_grad, axis=0, keepdims=True)
    mixed_ref[...] = mixed_grad
    if len(rest) == 1:
        return
    keep_ref, send_ref, _ = rest
    rows = keep_ref.shape[1]

    def place(block, carry):
        piece = pl.ds(pl.multiple_of(block * rows, 16), rows)
        for part, ref in enumerate((keep_ref, send_ref)):

            @pl.when((block + core_ref[0]) % 2 == part)
            def _():
                ref[table_ref[block]] = grads_ref[piece, :]

        return carry

    lax.fori_loop(0, table_ref.shape[0], place, 0)


def text_back(core, table, rows, *inputs):
    half = inputs[0].shape[0]
    whole = pl.BlockSpec(memory_space=pltpu.VMEM)
    scalars = pl.BlockSpec(memory_space=pltpu.SMEM)
    outs = [((half, TEXT), f32), ((3, TEXT), f32), ((2, TXT_FF), f32)]
    apart = rows % 16 == 0
    blocks = ((3 * TEXT // (2 * rows), rows, D), bf16)
    return in_vmem(
        text_back_kernel,
        "text_back",
        inputs + (core.reshape(1).astype(jnp.int32), table),
        outs + ([blocks] * 2 if apart else [((3 * TEXT, D), bf16)]),
        [pltpu.VMEM((3 * TEXT, D), bf16)] if apart else [],
        [whole] * len(inputs) + [scalars] * 2,
        [whole] * (5 if apart else 4),
    )


def conv_back_kernel(
    core_ref, mixed_ref, border_ref, window_ref, kernel_ref, shrink_ref, keep_ref,
    mine_ref, kernel_grad_ref, full_ref, wide,
):
    half = mixed_ref.shape[0]
    edge, margin = border_ref.shape[0], KERNEL // 2
    mixed = mixed_ref[...]
    border = border_ref[...]
    wide[:edge] = jnp.where(core_ref[0] == 1, border, 0.0)
    wide[edge : edge + half] = mixed
    wide[edge + half :] = jnp.where(core_ref[0] == 0, border, 0.0)
    total = shrink_ref[...]
    for j in range(KERNEL):
        start = edge + margin - j
        total = total + wide[start : start + half] * kernel_ref[j : j + 1]
        tap = window_ref[edge - margin + j : edge - margin + j + half]
        kernel_grad_ref[j : j + 1] = jnp.sum(mixed * tap, axis=0, keepdims=True)
    mine_ref[...] = total * keep_ref[...]
    place = pl.ds(pl.multiple_of(core_ref[0] * half, half), half)
    full_ref[place, :] = mine_ref[...]


def conv_back(core, *inputs):
    half = inputs[0].shape[0]
    whole = pl.BlockSpec(memory_space=pltpu.VMEM)
    return in_vmem(
        conv_back_kernel,
        "conv_back",
        (core.reshape(1).astype(jnp.int32),) + inputs,
        [((half, TEXT), f32), ((KERNEL, TEXT), f32), ((2 * half, TEXT), f32)],
        [pltpu.VMEM((half + 2 * inputs[1].shape[0], TEXT), f32)],
        [pl.BlockSpec(memory_space=pltpu.SMEM)] + [whole] * len(inputs),
        [whole] * 3,
    )


def settle_kernel(
    core_ref, my_out_ref, their_out_ref, my_grad_ref, their_grad_ref, stream_ref, attention_ref, cot_ref,
    gate_one_ref, scale_ref, gate_two_ref,
    output_ref, later_ref, attention_grad_ref, sums_ref, full_ref,
):
    half = output_ref.shape[0]
    unit_out = my_out_ref[...] + their_out_ref[...].astype(f32)
    stream = stream_ref[...]
    output_ref[...] = (stream + gate_two_ref[...] * unit_out).astype(bf16)
    place = pl.ds(pl.multiple_of(core_ref[0] * half, half), half)
    full_ref[place, :] = output_ref[...]
    out_grad = cot_ref[...].astype(f32)
    sums_ref[0:1] = jnp.sum(out_grad * unit_out, axis=0, keepdims=True)
    grad = my_grad_ref[...] + their_grad_ref[...].astype(f32)
    normed, scale = normalise(stream)
    sums_ref[1:2] = jnp.sum(grad, axis=0, keepdims=True)
    sums_ref[2:3] = jnp.sum(grad * normed, axis=0, keepdims=True)
    later = out_grad + normalise_back(grad * (1.0 + scale_ref[...]), normed, scale)
    later_ref[...] = later
    sums_ref[3:4] = jnp.sum(later * attention_ref[...], axis=0, keepdims=True)
    attention_grad_ref[...] = (gate_one_ref[...] * later).astype(bf16)


def settle(core, *inputs):
    half = inputs[0].shape[0]
    whole = pl.BlockSpec(memory_space=pltpu.VMEM)
    return in_vmem(
        settle_kernel,
        "settle",
        (core.reshape(1).astype(jnp.int32),) + inputs,
        [((half, D), bf16), ((half, D), f32), ((half, D), bf16), ((4, D), f32), ((2 * half, D), bf16)],
        [],
        [pl.BlockSpec(memory_space=pltpu.SMEM)] + [whole] * len(inputs),
        [whole] * 5,
    )


def dot_split(left, right, dims=NN):
    split = lambda array: (array.astype(bf16), (array - array.astype(bf16).astype(f32)).astype(bf16))
    left_high, left_low = split(left)
    right_high, right_low = split(right)
    return (
        dot32(left_high, right_high, dims)
        + dot32(left_high, right_low, dims)
        + dot32(left_low, right_high, dims)
    )


def rotated_kernel(places, utterances, *refs):
    pieces, refs = refs[: sum(count for _, _, count in places)], refs[sum(count for _, _, count in places) :]
    left_ref, right_ref, master_ref, first_ref, second_ref, weights_ref, moment_ref, variance_ref, grad_ref = refs
    which = 0
    for row, column, count in places:
        total = pieces[which][...].astype(f32)
        for ref in pieces[which + 1 : which + count]:
            total = total + ref[...].astype(f32)
        rows, columns = total.shape
        grad_ref[row : row + rows, column : column + columns] = total / utterances
        which += count
    left, right = left_ref[...], right_ref[...]
    rotated = dot_split(dot_split(left, grad_ref[...], TN), right)
    moment, variance, direction = moments(rotated, first_ref[...], second_ref[...])
    moment_ref[...] = moment
    variance_ref[...] = variance
    turned = dot_split(dot_split(left, direction), right, NT)
    master = master_ref[...]
    weights_ref[...] = apply_step(master, turned, learn_rate)


def rotated_step(pieces, utterances, left, right, master, first, second):
    places = [(row, column, len(arrays)) for row, column, arrays in pieces]
    arrays = [array for _, _, group in pieces for array in group]
    return in_vmem(
        lambda *refs: rotated_kernel(places, utterances, *refs),
        "rotated_step",
        tuple(arrays) + (left, right, master, first, second),
        [(master.shape, f32)] * 3,
        [pltpu.VMEM(master.shape, f32)],
    )


def modulation_kernel(utterances, time_ref, table_ref, old_ref, first_ref, second_ref, weights_ref, moment_ref, variance_ref):
    grad = dot32(time_ref[...], table_ref[...], TN) / utterances
    moment, variance, direction = moments(grad, first_ref[...], second_ref[...])
    moment_ref[...] = moment
    variance_ref[...] = variance
    weights_ref[...] = apply_step(old_ref[...], direction, learn_rate)


def modulation_step(utterances, time_rows, table, old, first, second):
    rows, columns = old.shape
    step = columns // 6
    tall = pl.BlockSpec((rows, step), lambda i: (0, i))
    return pl.pallas_call(
        lambda *refs: modulation_kernel(utterances, *refs),
        grid=(6,),
        in_specs=[
            pl.BlockSpec((GROUPS, rows), lambda i: (0, 0)),
            pl.BlockSpec((GROUPS, step), lambda i: (0, i)),
        ]
        + [tall] * 3,
        out_specs=[tall] * 3,
        out_shape=[jax.ShapeDtypeStruct(old.shape, f32)] * 3,
        compiler_params=pltpu.CompilerParams(vmem_limit_bytes=vmem_bytes),
        cost_estimate=beside,
        name="modulation_step",
    )(time_rows, table, old, first, second)


def vector_parts(vectors):
    kernel_size = KERNEL * TEXT
    pieces = [vectors[:kernel_size].reshape(KERNEL, TEXT)]
    offset = kernel_size
    for extent in (TEXT, TEXT, TEXT, TEXT, TXT_FF, TXT_FF, TXT_FF, 6 * D):
        pieces.append(vectors[offset : offset + extent])
        offset = offset + extent
    return pieces


def normalise(values):
    center = values - jnp.mean(values, axis=-1, keepdims=True)
    variance = jnp.mean(center * center, axis=-1, keepdims=True)
    scale = lax.rsqrt(variance + norm_eps)
    return center * scale, scale


def normalise_back(grad, normed, scale):
    mean_grad = jnp.mean(grad, axis=-1, keepdims=True)
    mean_dot = jnp.mean(grad * normed, axis=-1, keepdims=True)
    return scale * (grad - mean_grad - normed * mean_dot)


def moments(gradient, first_moment, second_moment):
    first_new = beta_one * first_moment + (1.0 - beta_one) * gradient
    second_new = beta_two * second_moment + (1.0 - beta_two) * gradient * gradient
    bias_first = 1.0 - beta_one**STEP
    bias_second = 1.0 - beta_two**STEP
    direction = first_new / bias_first / (jnp.sqrt(second_new / bias_second) + adam_eps)
    return (first_new, second_new, direction)


def apply_step(weight, direction, rate):
    return weight - rate * (direction + weight_decay * weight)


def rotary_tables(first):
    position = np.arange(LEN)
    frequency = 10000.0 ** (-np.arange(HEAD // 2) * 2.0 / HEAD)
    angle = position[:, None] * frequency[None, :]
    cosine, sine = np.cos(angle), np.sin(angle)
    tables = np.concatenate([cosine] * 4 + [-sine, sine, -sine, sine], axis=1).astype(np.float32)
    tables = lax.dynamic_slice_in_dim(jnp.asarray(np.concatenate([tables, tables])), first, LEN, 0)
    return tables[:, :PAIR], tables[:, PAIR:]


def take_blocks(blocks, index):
    return jnp.take(blocks, index, axis=0, mode="clip")


def both_halves(mine):
    return jnp.concatenate([mine, swap_core(mine)], axis=0)


def sum_halves(multiply, rows, half):
    theirs = multiply(rows[half:]).astype(bf16)
    received = swap_core(theirs)
    return multiply(rows[:half]) + received.astype(f32)


def body(
    mel_frames,
    text_features,
    cotangent,
    time_embedding,
    lengths,
    group_ids,
    text_keep,
    owner_list,
    soap_master,
    soap_first,
    soap_second,
    left_basis,
    right_basis,
    text_matrices,
    text_first,
    text_second,
    modulation_weight,
    modulation_first,
    modulation_second,
    vectors,
    vector_first,
    vector_second,
):
    count = lax.axis_size("dp")
    me, core = lax.axis_index("dp"), lax.axis_index("mp")
    half = LEN // 2
    utterances = lengths.shape[0] * count
    panel_rows, width = soap_master.shape
    share_rows = modulation_weight.shape[0]
    text_rows = text_matrices.shape[0]
    text_half = text_rows // 2
    relative = jnp.arange(count) ^ me

    high_count = count // 16
    cuts = row_cuts(panel_rows)
    panel_table = panel_places(core, owner_list ^ me, high_count)
    gather_table = panel_places(core, owner_list ^ me, high_count, True)
    silu_time = jax.nn.silu(time_embedding.astype(f32)).astype(bf16)
    time_rows = lax.dynamic_slice_in_dim(silu_time, me * share_rows, share_rows, 1)
    weight_half = lax.dynamic_slice_in_dim(modulation_weight, core * 3 * D, 3 * D, 1).astype(bf16)
    own_rows = lax.dynamic_slice_in_dim(text_matrices, core * text_half, text_half, 0)
    text_held = spread_high(own_rows.astype(bf16))
    partial = dot32(time_rows, weight_half)
    held = spread_high(soap_master.astype(bf16))
    text_received, partial_received = tie(swap_bit(text_held, 3), swap_bit(partial, 3))
    text_held = jnp.concatenate([text_held, text_received], axis=0)
    partial = partial + partial_received
    text_received, partial_received, held = tie(
        swap_bits(text_held, phase_bits(text_orders, 0)), swap_bits(partial, phase_bits(text_orders, 0)), held
    )
    held = split_rows(held, cuts)
    text_held = jnp.stack([text_held, text_received])
    partial = partial + partial_received
    received, (text_received, partial_received, far_last) = tie_lists(
        receive(held, 0),
        (
            swap_bits(text_held, phase_bits(text_orders, 1)),
            swap_bits(partial, phase_bits(text_orders, 1)),
            swap_bit(held[1], 3),
        ),
    )
    near = [jnp.stack(pair) for pair in zip(held, received)]
    text_held = jnp.stack([text_held, text_received])
    partial = partial + partial_received
    received, (text_received, partial_received, far_first) = tie_lists(
        receive(near, 1),
        (
            swap_bits(text_held, phase_bits(text_orders, 2)),
            swap_bits(partial, phase_bits(text_orders, 2)),
            swap_bit(held[0], 3),
        ),
    )
    partial = partial + partial_received
    near = [jnp.stack(pair) for pair in zip(near, received)]
    near_received = receive(near, 2)
    far = spread_step([far_first, far_last], 0)
    received = receive(far, 1)
    text_mine = jnp.stack([text_held, text_received]).reshape(count, text_half, D)
    text_other = swap_core(text_mine)
    text_features, mel_frames, cotangent, far = tie(text_features, mel_frames, cotangent, far)
    for bit in range(4, bit_count(count)):
        partial = partial + swap_bit(partial, bit)
    modulation_half = partial
    mine_places, other_places = text_places(core, relative, high_count), text_places(1 - core, relative, high_count)
    text_table = jnp.where(
        core == 0, jnp.stack([mine_places, other_places], 1), jnp.stack([other_places, mine_places], 1)
    ).reshape(-1)
    if text_half % 16:
        source = jnp.arange(2 * count) % 2 != core
        texts = take_blocks(jnp.concatenate([text_mine, text_other]), text_table + count * source)
        text_mine = text_other = texts.reshape(1, 3 * TEXT, D)
        text_table = jnp.zeros((1,), jnp.int32)

    modulation = by_core(core, modulation_half, swap_core(modulation_half), axis=1)
    (
        kernel,
        conv_bias,
        norm_gain,
        norm_bias,
        out_bias,
        in_bias,
        grn_gamma,
        grn_beta,
        modulation_bias,
    ) = vector_parts(vectors)
    group = group_ids[0]
    modulation_row = lax.dynamic_slice_in_dim(modulation, group, 1, 0) + modulation_bias


    first = core * half
    margin = KERNEL // 2
    edge = 8
    keep_all = jnp.pad(text_keep.astype(f32), (edge, edge))[:, None]
    text_all = jnp.pad(text_features, ((edge, edge), (0, 0)))

    def text_start(start):
        window = lax.dynamic_slice_in_dim(text_all, start, half + 2 * edge, 0).astype(f32)
        window = window * lax.dynamic_slice_in_dim(keep_all, start, half + 2 * edge, 0)
        keep = lax.dynamic_slice_in_dim(keep_all, start + edge, half, 0)
        taps = [window[edge - margin + j : edge - margin + j + half] for j in range(KERNEL)]
        mixed = conv_bias[None, :]
        for j in range(KERNEL):
            mixed = mixed + taps[j] * kernel[j][None, :]
        normed, scale = normalise(mixed)
        return window, keep, normed, scale, (normed * norm_gain + norm_bias).astype(bf16)

    window, keep, conv_normed, conv_scale, normed_low = text_start(first)
    window_other, keep_other, _, _, normed_other = text_start(half - first)
    masked_both = jnp.concatenate([window[edge : edge + half], window_other[edge : edge + half]], axis=0)
    keep_both = jnp.concatenate([keep, keep_other], axis=0)
    normed_both = jnp.concatenate([normed_low, normed_other], axis=0)
    mel_mine = lax.dynamic_slice_in_dim(mel_frames, first, half, 0)
    mel_other = lax.dynamic_slice_in_dim(mel_frames, half - first, half, 0)
    cosine, sine = rotary_tables(first)
    received, near_received, (text_other, modulation_row, normed_both, masked_both, cosine, sine) = tie_lists(
        received, near_received, (text_other, modulation_row, normed_both, masked_both, cosine, sine)
    )
    far = [jnp.stack(pair) for pair in zip(far, received)]
    far_received = receive(far, 2)
    shift_one, scale_one, gate_one, shift_two, scale_two, gate_two = (
        modulation_row[:, i * D : (i + 1) * D] for i in range(6)
    )
    expand_pre, energy_sum, grn_low, text_low, stream, first_mine, first_other, first_t, first_other_t, texts = text_forward(
        core,
        text_table,
        text_mine,
        text_other,
        normed_both,
        masked_both,
        keep_both,
        mel_mine,
        mel_other,
        in_bias[None],
        grn_gamma[None],
        grn_beta[None],
        out_bias[None],
        shift_one,
        scale_one,
    )

    cot_mine = lax.dynamic_slice_in_dim(cotangent, first, half, 0)
    cot_other = lax.dynamic_slice_in_dim(cotangent, half - first, half, 0)
    hidden_mine = (gate_two * cot_mine.astype(f32)).astype(bf16)
    hidden_other = (gate_two * cot_other.astype(f32)).astype(bf16)
    first_mine, hidden_mine, hidden_other = tie(first_mine, hidden_mine, hidden_other)
    position = (jnp.arange(LEN) + first) % LEN
    bias = jnp.where(position < lengths[0], 0.0, -1e30).astype(bf16)
    bias = jnp.broadcast_to(bias[:, None], (LEN, PAIR))
    queries, keys, value_rows, stacked = project(
        (near, near_received, far, far_received), gather_table, panel_rows, cuts, first_mine, first_other, cosine, sine
    )
    stacked = stacked.reshape(8, D, width)
    attended, query_aug = attend_forward(queries, keys, value_rows, bias)
    attention_out = sum_halves(lambda rows: dot32(rows, stacked[3], NT), attended, half)
    stream_one = stream + gate_one * attention_out

    normed_two, _ = normalise(stream_one)
    second_mine = (normed_two * (1.0 + scale_two) + shift_two).astype(bf16)
    second_other = swap_core(second_mine)
    their_out, their_grad, act_other, pre_other, second_other_t, hidden_other_t = feed(second_other, hidden_other, stacked, bf16)
    their_out, their_grad = swap_core(their_out), swap_core(their_grad)
    my_out, my_grad, act_mine, pre_mine, second_t, hidden_t = feed(second_mine, hidden_mine, stacked, f32)
    output_mine, stream_one_grad, attention_mine, settle_sums, block_output = settle(
        core,
        my_out,
        their_out,
        my_grad,
        their_grad,
        stream_one,
        attention_out,
        cot_mine,
        gate_one,
        scale_two,
        gate_two,
    )
    gate_two_grad, shift_two_grad, scale_two_grad, gate_one_grad = (settle_sums[i] for i in range(4))
    output_theirs = swap_core(output_mine)

    attention_other = swap_core(attention_mine)
    narrow = width // 2

    def back(side, queries):
        return attend_backward(
            side, queries, keys, value_rows, attended, attention_mine, attention_other, stacked, cosine, sine, bias
        )

    def weight_gradients(side, head_grads):
        column = side * narrow
        return panel_gradients(
            [
                first_t, first_other_t, attention_t, attention_other_t, second_t, second_other_t,
                hidden_t, hidden_other_t, *head_grads, attended, pre_mine, pre_other, act_mine, act_other,
            ],
            [(0, 1), (2, 3), (4, 5), (6, 7)],
            [
                [(0, (8, 8)), (0, (9, 9))],
                [(0, (10, 10))],
                [(column, (11, 11))],
                [(column, (12, 13)), (width + column, (12, 13))],
                [(column, (14, 15)), (width + column, (14, 15))],
            ],
            ((0, 0, (0, 1)), (0, 1, (2,)), (1, 2, (3,)), (2, 3, (4, 5)), (3, 4, (6, 7))),
            panel_table,
            panel_rows,
            cuts,
            high_count,
            narrow,
        )

    *head_grads, attention_t, attention_other_t = back(0, query_aug)
    keep_a, send_a = weight_gradients(0, head_grads)
    send_a, (query_aug,) = tie_lists(send_a, (query_aug,))
    received_a = receive(send_a, 2)
    head_grads += list(back(1, query_aug))
    received_a, head_grads = tie_lists(received_a, head_grads)
    part_a = add_all(keep_a, received_a)
    received_a = receive(seconds(part_a), 1)
    my_grad, their_grad = inputs_grad(head_grads, stacked)
    received_a, head_grads, (my_grad, their_grad) = tie_lists(received_a, head_grads, (my_grad, their_grad))
    part_a = add_all(firsts(part_a), received_a)
    received_a = receive(seconds(part_a), 0)
    keep_b, send_b = weight_gradients(1, head_grads[3:])
    their_grad = swap_core(their_grad)
    received_a, send_b, (their_grad,) = tie_lists(received_a, send_b, (their_grad,))

    part_a = add_all(firsts(part_a), received_a)
    received_b = receive(send_b, 2)
    mel_grad_mine, stream_low, shrink_grad, shrink_low, grn_grad, sums, out_bias_grad, mel_gradient = stream_back(
        core, my_grad, their_grad, stream, stream_one_grad, scale_one, texts, keep, expand_pre
    )
    received_b, part_a, (sums, mel_grad_mine) = tie_lists(received_b, part_a, (sums, mel_grad_mine))
    shift_one_grad, scale_one_grad, hidden_dot, beta_grad = sums[0], sums[1], sums[2:3], sums[3]
    out_bias_grad = out_bias_grad[0]
    far_a = [swap_bit(part[high_count:], 3) for part in part_a]
    part_b = add_all(keep_b, received_b)
    received_b = receive(seconds(part_b), 1)
    hidden_dot_all = hidden_dot + swap_core(hidden_dot)
    mixed_grad, text_sums, wide_sums, *text_grads = text_back(
        core,
        text_table,
        text_half,
        expand_pre,
        grn_grad,
        energy_sum,
        hidden_dot_all,
        grn_gamma[None],
        texts,
        normed_low,
        conv_normed,
        conv_scale,
        norm_gain[None],
        shrink_low,
        grn_low,
        text_low,
        stream_low,
    )
    mel_grad_theirs = swap_core(mel_grad_mine)
    gain_grad, norm_bias_grad, conv_bias_grad = text_sums[0], text_sums[1], text_sums[2]
    in_bias_grad, gamma_grad = wide_sums[0], wide_sums[1] * hidden_dot[0]
    if len(text_grads) == 1:
        blocks = text_grads[0].reshape(count, 2, text_half, D)
        order = lambda which: text_slots(which, jnp.arange(count), high_count) ^ me
        text_grads = [
            take_blocks(lax.dynamic_index_in_dim(blocks, which, 1, keepdims=False), order(which))
            for which in (core, 1 - core)
        ]
    received_b, far_a, (mixed_grad, text_keep_half, text_send_half, mel_grad_theirs) = tie_lists(
        received_b, far_a, (mixed_grad, *text_grads, mel_grad_theirs)
    )
    part_b = add_all(firsts(part_b), received_b)
    received_b = receive(seconds(part_b), 0)
    text_received = swap_core(text_send_half)
    border = swap_core(lax.dynamic_slice_in_dim(mixed_grad, (1 - core) * (half - edge), edge, 0))
    text_grad_mine, kernel_grad, text_gradient = conv_back(
        core, mixed_grad, border, window, kernel, shrink_grad, keep
    )

    vector_mine = jnp.concatenate(
        [
            kernel_grad.reshape(-1),
            conv_bias_grad,
            gain_grad,
            norm_bias_grad,
            out_bias_grad,
            in_bias_grad,
            gamma_grad,
            beta_grad,
        ]
    )
    token = jnp.concatenate(
        [shift_one_grad, scale_one_grad, gate_one_grad, shift_two_grad, scale_two_grad, gate_two_grad]
    )
    vector_half = vector_mine.shape[0] // 2
    token_half = 3 * D

    def half_of(which):
        return jnp.concatenate(
            [
                lax.dynamic_slice_in_dim(vector_mine, which * vector_half, vector_half, 0),
                lax.dynamic_slice_in_dim(token, which * token_half, token_half, 0),
            ]
        )

    small_send = half_of(1 - core)
    small = half_of(core)
    in_group = (jnp.arange(GROUPS) == group).astype(f32)

    text_grad_theirs = swap_core(text_grad_mine)
    text_part = add_low(text_keep_half, text_received).reshape(2, 2, 2, 2 * high_count, text_half, D)
    mel_gradient = lax.dynamic_update_slice_in_dim(mel_gradient, mel_grad_theirs, half - first, 0)
    received_b, (text_part, small, small_send, mel_gradient) = tie_lists(
        received_b, (text_part, small, small_send, mel_gradient)
    )
    part_b = add_all(firsts(part_b), received_b)
    far_b = [swap_bit(part[high_count:], 3) for part in part_b]
    text_received = swap_bits(text_part[1], phase_bits(text_orders, 2))
    small_received = swap_core(small_send)
    block_output = lax.dynamic_update_slice_in_dim(block_output, output_theirs, half - first, 0)
    text_gradient = lax.dynamic_update_slice_in_dim(text_gradient, text_grad_theirs, half - first, 0)
    far_b, (text_received, small_received, text_gradient, block_output) = tie_lists(
        far_b, (text_received, small_received, text_gradient, block_output)
    )
    text_part = add_low(text_part[0], text_received)
    text_received = swap_bits(text_part[1], phase_bits(text_orders, 1))
    small = small + small_received
    table = in_group[:, None] * small[None, vector_half:]
    small = jnp.concatenate([small[:vector_half], table.reshape(-1)]).reshape(-1, 128)
    small_received = swap_bits(small, (2, 0))
    panel_pieces = []
    for side, (parts, others) in enumerate(((part_a, far_a), (part_b, far_b))):
        for index, (part, other) in enumerate(zip(parts, others)):
            if high_count == 1:
                arrays = [part[0], other[0]]
            else:
                arrays = [fold_high(part[:high_count].astype(f32) + other.astype(f32))]
            panel_pieces.append((cuts[index], side * narrow, arrays))
    soap_weights, soap_moment, soap_variance = rotated_step(
        panel_pieces, utterances, left_basis, right_basis, soap_master, soap_first, soap_second
    )
    text_received, small_received, soap_weights, soap_moment, soap_variance = tie(
        text_received, small_received, soap_weights, soap_moment, soap_variance
    )
    text_part = add_low(text_part[0], text_received)
    small = small + small_received
    text_part = fold(text_part, text_orders, 0)
    text_received = swap_bit(text_part[high_count:], 3)
    small = small + swap_bits(small, (0, 1))
    small = small + swap_bits(small, (1, 2))
    small = small + swap_bit(small, 3)
    own_text = text_part[:high_count].astype(f32) + text_received.astype(f32)
    for bit in range(4, bit_count(count)):
        small = small + swap_bit(small, bit)
    own_text = fold_high(own_text)
    own_text = by_core(core, own_text, swap_core(own_text))
    small = by_core(core, small[None], swap_core(small)[None]).reshape(2, -1)
    vector_sum = small[:, :vector_half].reshape(-1)
    tables = small[:, vector_half:].reshape(2, GROUPS, token_half)
    modulation_grad = jnp.concatenate([tables[0], tables[1]], axis=1)
    vector_gradient = jnp.concatenate([vector_sum, jnp.sum(modulation_grad, axis=0)]) / utterances

    own_text = own_text / utterances
    text_moment, text_variance, text_direction = moments(own_text, text_first, text_second)
    text_weights = apply_step(text_matrices, text_direction, learn_rate)
    modulation_weights, modulation_moment, modulation_variance = modulation_step(
        utterances,
        time_rows,
        modulation_grad.astype(bf16),
        modulation_weight,
        modulation_first,
        modulation_second,
    )
    vector_moment, vector_variance, vector_direction = moments(
        vector_gradient, vector_first, vector_second
    )
    vector_weights = apply_step(vectors, vector_direction, vector_rate)
    return (
        block_output,
        mel_gradient,
        text_gradient,
        soap_weights,
        soap_moment,
        soap_variance,
        text_weights,
        text_moment,
        text_variance,
        modulation_weights,
        modulation_moment,
        modulation_variance,
        vector_weights,
        vector_moment,
        vector_variance,
    )


def solution(mesh):
    rows, quarter, same = P("dp", None), P("dp", "mp"), P()
    return jax.shard_map(
        body,
        mesh=mesh,
        in_specs=(
            (rows,) * 3 + (same,) + (P("dp"),) * 3 + (same,) + (quarter,) * 5 + (rows,) * 6 + (same,) * 3
        ),
        out_specs=(rows,) * 3 + (quarter,) * 3 + (rows,) * 6 + (same,) * 3,
        check_vma=False,
    )
```

```python
import jax
import numpy as np
import jax.numpy as jnp
from jax import lax
from jax.experimental import pallas as pl
from jax.experimental.pallas import tpu as pltpu
from jax.sharding import PartitionSpec as P

D = 1024
HEAD = 64
TEXT = 512
TXT_FF = 1024
KERNEL = 7
LEN = 1024
GROUPS = 8
STEP = 10

f32 = jnp.float32
bf16 = jnp.bfloat16
beta_one = 0.9
beta_two = 0.99
adam_eps = 1e-08
weight_decay = 0.01
learn_rate = 0.03
vector_rate = 0.3
norm_eps = 1e-06


def swap_core(array):
    return lax.ppermute(array, "mp", [(0, 1), (1, 0)])


def swap_bits(array, bits):
    count = lax.axis_size("dp")
    pairs = [
        (i * 2 + core, (i ^ (1 << bits[core])) * 2 + core) for i in range(count) for core in range(2)
    ]
    return lax.ppermute(array, ("dp", "mp"), pairs)


def swap_bit(array, bit):
    return swap_bits(array, (bit, bit))


def by_core(core, mine, other, axis=0):
    return jnp.where(
        core == 0,
        jnp.concatenate([mine, other], axis=axis),
        jnp.concatenate([other, mine], axis=axis),
    )


def bit_count(count):
    return count.bit_length() - 1


def row_cuts(rows):
    return (0, (rows * 2 + 24) // 48 * 16, rows)


axis_orders = (((0, 1, 2), (1, 2, 0)), ((2, 0, 1), (2, 0, 1)))
text_orders = ((2, 0, 1), (2, 1, 0))


def phase_bits(orders, phase):
    return tuple(order[phase] for order in orders)


def tie(*values):
    return lax.optimization_barrier(values)


def tie_lists(*lists):
    flat = [value for values in lists for value in values]
    flat = list(lax.optimization_barrier(tuple(flat)))
    out = []
    for values in lists:
        out.append(flat[: len(values)])
        flat = flat[len(values) :]
    return out


def split_rows(array, cuts):
    return [array[..., cuts[i] : cuts[i + 1], :] for i in range(len(cuts) - 1)]


def spread(part, orders, phase):
    return jnp.stack([part, swap_bits(part, phase_bits(orders, phase))])


def spread_step(parts, phase):
    return [spread(part, axis_orders[index], phase) for index, part in enumerate(parts)]


def spread_last(parts):
    return [(part, swap_bits(part, phase_bits(axis_orders[index], 2))) for index, part in enumerate(parts)]


def spread_high(block):
    held = block[None]
    for bit in range(4, bit_count(lax.axis_size("dp"))):
        held = jnp.concatenate([held, swap_bit(held, bit)], axis=0)
    return held


def add_low(left, right):
    return (left.astype(f32) + right.astype(f32)).astype(bf16)


def receive(sends, phase):
    return [swap_bits(send, phase_bits(axis_orders[index], phase)) for index, send in enumerate(sends)]


def add_all(keeps, received):
    return [add_low(keep, other) for keep, other in zip(keeps, received)]


def firsts(parts):
    return [part[0] for part in parts]


def seconds(parts):
    return [part[1] for part in parts]


def fold(part, orders, phase):
    return add_low(part[0], swap_bits(part[1], phase_bits(orders, phase)))


def fold_high(total):
    count = total.shape[0]
    if count == 1:
        return total[0]
    for bit in range(bit_count(count) - 1, -1, -1):
        half = 1 << bit
        total = total[:half] + swap_bit(total[half:].astype(bf16), bit + 4).astype(f32)
    return total[0]


def bit_of(values, which):
    return (values >> which) & 1


def panel_places(core, slots, high_count, apart=False):
    rows = []
    for orders in axis_orders:
        far = bit_of(slots, 3)
        which = [bit_of(slots, order[2]) + (2 * far if apart else 0) for order in orders]
        lead = [bit_of(slots, order[1]) * 2 + bit_of(slots, order[0]) for order in orders]
        if not apart:
            lead = [place * 2 + far for place in lead]
        lead = [place * high_count + (slots >> 4) for place in lead]
        rows += [jnp.where(core == 0, *which), jnp.where(core == 0, *lead)]
    return jnp.concatenate(rows).astype(jnp.int32)


def text_places(core, slots, high_count):
    places = []
    for order in text_orders:
        high = bit_of(slots, 3) * high_count + (slots >> 4)
        places.append(
            ((bit_of(slots, order[2]) * 2 + bit_of(slots, order[1])) * 2 + bit_of(slots, order[0]))
            * (2 * high_count)
            + high
        )
    return jnp.where(core == 0, *places).astype(jnp.int32)


def text_slots(core, places, high_count):
    lead, rest = places // (2 * high_count), places % (2 * high_count)
    high = ((rest // high_count) << 3) | ((rest % high_count) << 4)
    slots = []
    for order in text_orders:
        low = (bit_of(lead, 2) << order[2]) | (bit_of(lead, 1) << order[1]) | (bit_of(lead, 0) << order[0])
        slots.append(high | low)
    return jnp.where(core == 0, *slots)


beside = pl.CostEstimate(flops=1000, bytes_accessed=1000, transcendentals=0)

NT = (((1,), (1,)), ((), ()))
NN = (((1,), (0,)), ((), ()))
TN = (((0,), (0,)), ((), ()))
ROWS = 256
LONG_ROWS = 512
PAIR = 2 * HEAD
mebibyte = 1024 * 1024
vmem_bytes = 12 * mebibyte
feed_bytes = 16 * mebibyte
attend_back_bytes = 16 * mebibyte
text_forward_bytes = 20 * mebibyte
text_back_bytes = 16 * mebibyte
gradient_bytes = 20 * mebibyte
project_bytes = 24 * mebibyte


def dot32(left, right, dims=NN):
    return lax.dot_general(left, right, dims, preferred_element_type=f32)


def three_terms(values):
    high = values.astype(bf16).astype(f32)
    rest = values - high
    middle = rest.astype(bf16).astype(f32)
    return high, middle, rest - middle


def rotate(values, cosine, sine, lane):
    partner = jnp.where(
        lane % HEAD < HEAD // 2,
        pltpu.roll(values, PAIR - HEAD // 2, 1),
        pltpu.roll(values, HEAD // 2, 1),
    )
    return values * cosine + partner * sine


def attend_kernel(q_ref, k_ref, v_ref, bias_ref, o_ref, qa_ref):
    lane = lax.broadcasted_iota(jnp.int32, (LEN, PAIR), 1)
    lane_rows = lax.broadcasted_iota(jnp.int32, (LONG_ROWS, PAIR), 1)
    row_index = lax.broadcasted_iota(jnp.int32, (PAIR, LONG_ROWS), 0)
    q_wide = q_ref[...].astype(f32)
    k_wide = k_ref[...].astype(f32)
    values_t = v_ref[...].T
    bias = bias_ref[...].astype(f32)
    keys = []
    for head in range(2):
        own = lane // HEAD == head
        spare = (1 - head) * HEAD
        keys.append(
            jnp.where(own, k_wide, jnp.where(lane == spare, bias, 0.0)).astype(bf16)
        )
        qa_ref[:, head * PAIR : (head + 1) * PAIR] = jnp.where(
            own, q_wide, jnp.where(lane == spare, 1.0, 0.0)
        ).astype(bf16)
    steps = [(block, head) for block in range(LEN // LONG_ROWS) for head in range(2)]

    def scores_of(step):
        block, head = step
        rows = slice(block * LONG_ROWS, (block + 1) * LONG_ROWS)
        return dot32(keys[head], qa_ref[rows, head * PAIR : (head + 1) * PAIR], NT)

    following = scores_of(steps[0])
    for position, (block, head) in enumerate(steps):
        scores = following
        if position + 1 < len(steps):
            following = scores_of(steps[position + 1])
        rows = slice(block * LONG_ROWS, (block + 1) * LONG_ROWS)
        if head == 0:
            outs, extra = [], jnp.zeros((PAIR, LONG_ROWS), f32)
        spare = (1 - head) * HEAD
        highest = jnp.max(scores, axis=0, keepdims=True)
        weights = jnp.exp(scores - highest)
        total = jnp.sum(weights, axis=0, keepdims=True)
        out_t = dot32(values_t[head * HEAD : (head + 1) * HEAD], weights.astype(bf16))
        outs.append(out_t / total)
        for place, term in enumerate(three_terms(highest + jnp.log(total))):
            extra = jnp.where(row_index == spare + 1 + place, -term, extra)
        if head == 0:
            continue
        o_ref[rows, :] = jnp.concatenate(outs, axis=0).T.astype(bf16)
        extra_t = extra.T
        for head in range(2):
            spare = (1 - head) * HEAD
            columns = slice(head * PAIR, (head + 1) * PAIR)
            is_extra = (lane_rows > spare) & (lane_rows < spare + 4)
            qa_ref[rows, columns] = jnp.where(
                is_extra, extra_t, qa_ref[rows, columns].astype(f32)
            ).astype(bf16)


def attend_forward(queries, keys, values, bias):
    width = values.shape[1]
    pairs = width // PAIR
    tall = lambda columns: pl.BlockSpec((LEN, columns), lambda pair: (0, pair))
    whole = pl.BlockSpec((LEN, PAIR), lambda pair: (0, 0))
    return pl.pallas_call(
        attend_kernel,
        grid=(pairs,),
        in_specs=[tall(PAIR), tall(PAIR), tall(PAIR), whole],
        out_specs=[tall(PAIR), tall(2 * PAIR)],
        out_shape=[
            jax.ShapeDtypeStruct((LEN, width), bf16),
            jax.ShapeDtypeStruct((LEN, 2 * width), bf16),
        ],
        compiler_params=pltpu.CompilerParams(vmem_limit_bytes=vmem_bytes),
        cost_estimate=pl.CostEstimate(
            flops=2 * 4 * LEN * LEN * width * 4,
            bytes_accessed=6 * LEN * width * 2,
            transcendentals=LEN * LEN * width // HEAD,
        ),
        name="attend",
    )(queries, keys, values, bias)


def attend_back_kernel(
    qa_ref, kr_ref, v_ref, o_ref, mine_ref, other_ref, weight_ref, cos_ref, sin_ref, bias_ref,
    dq_ref, dk_ref, dv_ref, *rest,
):
    doa_ref, dka_ref, dva_ref = rest[-3:]
    if len(rest) > 3:

        @pl.when(pl.program_id(0) == 0)
        def _():
            rest[0][...] = mine_ref[...].T
            rest[1][...] = other_ref[...].T

    lane = lax.broadcasted_iota(jnp.int32, (LEN, PAIR), 1)
    lane_rows = lax.broadcasted_iota(jnp.int32, (ROWS, PAIR), 1)
    cosine, sine = cos_ref[...], sin_ref[...]
    k_wide = kr_ref[...].astype(f32)
    keys_t = kr_ref[...].T
    v_wide = v_ref[...].astype(f32)
    do_wide = jnp.concatenate(
        [dot32(ref[...], weight_ref[0]).astype(bf16).astype(f32) for ref in (mine_ref, other_ref)],
        axis=0,
    )
    bias = bias_ref[...].astype(f32)
    product = do_wide * o_ref[...].astype(f32)
    keys, values = [], []
    for head in range(2):
        own = lane // HEAD == head
        spare = (1 - head) * HEAD
        is_extra = (lane > spare) & (lane < spare + 4)
        ones = jnp.where(is_extra, 1.0, 0.0)
        keys.append(
            jnp.where(own, k_wide, jnp.where(lane == spare, bias, ones)).astype(bf16)
        )
        values.append(jnp.where(own, v_wide, ones).astype(bf16))
        row_dot = jnp.sum(jnp.where(own, product, 0.0), axis=1, keepdims=True)
        grad = jnp.where(own, do_wide, 0.0)
        for place, term in enumerate(three_terms(row_dot)):
            grad = jnp.where(lane == spare + 1 + place, -term, grad)
        doa_ref[:, head * PAIR : (head + 1) * PAIR] = grad.astype(bf16)
    for block in range(LEN // ROWS):
        rows = slice(block * ROWS, (block + 1) * ROWS)
        turned = []
        for head in range(2):
            columns = slice(head * PAIR, (head + 1) * PAIR)
            q_block = qa_ref[rows, columns]
            do_block = doa_ref[rows, columns]
            probs = jnp.exp(dot32(keys[head], q_block, NT))
            prob_grad = dot32(values[head], do_block, NT)
            score_grad = (probs * prob_grad).astype(bf16)
            dv_part = dot32(probs.astype(bf16), do_block)
            dk_part = dot32(score_grad, q_block)
            if block == 0:
                dva_ref[:, columns] = dv_part
                dka_ref[:, columns] = dk_part
            else:
                dva_ref[:, columns] += dv_part
                dka_ref[:, columns] += dk_part
            turned.append(dot32(keys_t[head * HEAD : (head + 1) * HEAD], score_grad))
        dq = jnp.concatenate(turned, axis=0).T * 0.125
        dq_ref[rows, :] = rotate(dq, cosine[rows], -sine[rows], lane_rows).astype(bf16)
    first = lane < HEAD
    dk = jnp.where(first, dka_ref[:, :PAIR], dka_ref[:, PAIR:])
    dk_ref[...] = rotate(dk, cosine, -sine, lane).astype(bf16)
    dv_ref[...] = jnp.where(first, dva_ref[:, :PAIR], dva_ref[:, PAIR:]).astype(bf16)


def attend_backward(side, queries, keys, values, outputs, grad_mine, grad_other, stacked, cosine, sine, bias):
    width = values.shape[1] // 2
    pairs = width // PAIR
    turned = grad_mine.shape[::-1]
    tall = lambda columns: pl.BlockSpec((LEN, columns), lambda pair: (0, pair + side * pairs))
    whole = lambda shape: pl.BlockSpec(shape, lambda pair: (0, 0))
    return pl.pallas_call(
        attend_back_kernel,
        grid=(pairs,),
        in_specs=[tall(2 * PAIR)]
        + [tall(PAIR)] * 3
        + [whole(grad_mine.shape)] * 2
        + [pl.BlockSpec((1, D, PAIR), lambda pair: (3, 0, pair + side * pairs))]
        + [whole((LEN, PAIR))] * 3,
        out_specs=[pl.BlockSpec((LEN, PAIR), lambda pair: (0, pair))] * 3 + [whole(turned)] * (2 - 2 * side),
        out_shape=[jax.ShapeDtypeStruct((LEN, width), bf16)] * 3
        + [jax.ShapeDtypeStruct(turned, bf16)] * (2 - 2 * side),
        scratch_shapes=[
            pltpu.VMEM((LEN, 2 * PAIR), bf16),
            pltpu.VMEM((LEN, 2 * PAIR), f32),
            pltpu.VMEM((LEN, 2 * PAIR), f32),
        ],
        compiler_params=pltpu.CompilerParams(vmem_limit_bytes=attend_back_bytes),
        cost_estimate=beside,
        name="attend_back",
    )(queries, keys, values, outputs, grad_mine, grad_other, stacked, cosine, sine, bias)


PARTS = 2


def part_copies(table_ref, panels, panel, cuts, start_row, copy, arrays=4):
    for index in range(PARTS):
        which = table_ref[2 * index * panels + panel]
        lead = table_ref[(2 * index + 1) * panels + panel]
        start = pl.multiple_of(start_row + cuts[index], 16)
        for number in range(arrays):

            @pl.when(which == number)
            def _():
                copy(number * PARTS + index, lead, start, cuts[index + 1] - cuts[index])


def project_kernel(panel_rows, cuts, slots_ref, *refs):
    parts, refs = refs[: 4 * PARTS], refs[4 * PARTS :]
    mine_ref, other_ref, cos_ref, sin_ref, q_ref, k_ref, v_ref, out_ref = refs
    per_block = D // panel_rows

    def fetch(panel, carry):
        def copy(number, lead, start, rows):
            out_ref[pl.ds(start, rows), :] = parts[number][lead]

        part_copies(slots_ref, 8 * per_block, panel, cuts, panel * panel_rows, copy)
        return carry

    lax.fori_loop(0, 8 * per_block, fetch, 0)
    half = mine_ref.shape[0]
    width = out_ref.shape[1]
    lane = lax.broadcasted_iota(jnp.int32, (half, PAIR), 1)
    for block, ref in enumerate((q_ref, k_ref, v_ref)):
        for part, rows_ref in enumerate((mine_ref, other_ref)):
            rows = slice(part * half, (part + 1) * half)
            product = dot32(rows_ref[...], out_ref[block * D : (block + 1) * D, :])
            if block == 2:
                ref[rows, :] = product.astype(bf16)
                continue
            cosine, sine = cos_ref[rows, :], sin_ref[rows, :]
            for pair in range(width // PAIR):
                columns = slice(pair * PAIR, (pair + 1) * PAIR)
                turned = rotate(product[:, columns], cosine, sine, lane).astype(bf16)
                if block == 0:
                    turned = (turned.astype(f32) * 0.125).astype(bf16)
                ref[rows, columns] = turned


def project(groups, slots, panel_rows, cuts, mine, other, cosine, sine):
    width = groups[0][0].shape[-1]
    parts = [array.reshape((-1,) + array.shape[-2:]) for group in groups for array in group]
    whole = pl.BlockSpec(memory_space=pltpu.VMEM)
    tall = jax.ShapeDtypeStruct((LEN, width), bf16)
    return pl.pallas_call(
        lambda *refs: project_kernel(panel_rows, cuts, *refs),
        in_specs=[pl.BlockSpec(memory_space=pltpu.SMEM)] + [whole] * (4 * PARTS + 4),
        out_specs=[whole] * 4,
        out_shape=[tall] * 3 + [jax.ShapeDtypeStruct((8 * D, width), bf16)],
        compiler_params=pltpu.CompilerParams(vmem_limit_bytes=project_bytes),
        cost_estimate=pl.CostEstimate(
            flops=2 * LEN * 3 * D * width, bytes_accessed=48 * D * width, transcendentals=0
        ),
        name="project",
    )(slots, *parts, mine, other, cosine, sine)


def feed_kernel(n_ref, g_ref, w_ref, f_ref, d_ref, a_ref, u_ref, n_t_ref, g_t_ref):
    width = w_ref.shape[2]
    rows, grads = n_ref[...], g_ref[...]
    n_t_ref[...] = rows.T
    g_t_ref[...] = grads.T
    pre = [dot32(rows, w_ref[i]) for i in range(2)]
    act_grad = [dot32(grads, w_ref[2 + i]) for i in range(2)]
    acts, pre_grads = [], []
    for i in range(2):
        value = pre[i]
        square = value * value
        turn = jnp.tanh(0.7978845608028654 * (value + 0.044715 * (square * value)))
        share = 0.5 * (1.0 + turn)
        slope = share + (0.5 * value) * (1.0 - turn * turn) * (
            0.7978845608028654 + (3 * 0.044715 * 0.7978845608028654) * square
        )
        acts.append((value * share).astype(bf16))
        pre_grads.append((act_grad[i] * slope).astype(bf16))
        a_ref[:, i * width : (i + 1) * width] = acts[i]
        u_ref[:, i * width : (i + 1) * width] = pre_grads[i]
    f_ref[...] = (dot32(acts[0], w_ref[2], NT) + dot32(acts[1], w_ref[3], NT)).astype(f_ref.dtype)
    d_ref[...] = (dot32(pre_grads[0], w_ref[0], NT) + dot32(pre_grads[1], w_ref[1], NT)).astype(d_ref.dtype)


def feed(rows, grads, stacked, kind):
    half, width = rows.shape[0], stacked.shape[2]
    whole = pl.BlockSpec((half, D), lambda step: (0, 0))
    low, sums = jax.ShapeDtypeStruct((half, D), bf16), jax.ShapeDtypeStruct((half, D), kind)
    return pl.pallas_call(
        feed_kernel,
        grid=(1,),
        in_specs=[whole, whole, pl.BlockSpec((4, D, width), lambda step: (1, 0, 0))],
        out_specs=[whole] * 4 + [pl.BlockSpec((D, half), lambda step: (0, 0))] * 2,
        out_shape=[sums, sums, low, low] + [jax.ShapeDtypeStruct((D, half), bf16)] * 2,
        compiler_params=pltpu.CompilerParams(vmem_limit_bytes=feed_bytes),
        cost_estimate=pl.CostEstimate(
            flops=2 * 4 * half * D * D, bytes_accessed=16 * D * width, transcendentals=half * D
        ),
        name="feed",
    )(rows, grads, stacked)


def inputs_grad_kernel(*refs):
    grads, w_ref, mine_ref, other_ref = refs[:6], refs[6], refs[7], refs[8]
    half = mine_ref.shape[0]
    narrow = grads[0].shape[1]
    for start, out_ref in ((half, other_ref), (0, mine_ref)):
        rows = slice(start, start + half)
        total = None
        for which in range(3):
            for side in range(2):
                weight = w_ref[which, :, side * narrow : (side + 1) * narrow]
                part = dot32(grads[side * 3 + which][rows, :], weight, NT)
                total = part if total is None else total + part
        out_ref[...] = total.astype(out_ref.dtype)


def inputs_grad(grads, stacked):
    width = stacked.shape[2]
    half = LEN // 2
    out = pl.BlockSpec((half, D), lambda step: (0, 0))
    return pl.pallas_call(
        inputs_grad_kernel,
        grid=(1,),
        in_specs=[pl.BlockSpec((LEN, width // 2), lambda step: (0, 0))] * 6
        + [pl.BlockSpec((3, D, width), lambda step: (0, 0, 0))],
        out_specs=[out, out],
        out_shape=[jax.ShapeDtypeStruct((half, D), f32), jax.ShapeDtypeStruct((half, D), bf16)],
        compiler_params=pltpu.CompilerParams(vmem_limit_bytes=vmem_bytes),
        cost_estimate=beside,
        name="inputs_grad",
    )(*grads, stacked)


def gradients_kernel(panel_rows, cuts, lefts, rights, uses, slots_ref, *refs):
    in_count = 1 + max(max(max(pair) for pair in lefts), max(max(pair) for group in rights for _, pair in group))
    inputs, refs = refs[:in_count], refs[in_count:]
    parts, (block_ref,) = refs[: 2 * PARTS], refs[2 * PARTS :]
    tall, side = block_ref.shape[1:]
    half = LEN // 2
    pieces = tall // panel_rows

    def rows_of(pair, part, columns):
        if pair[0] == pair[1]:
            return inputs[pair[0]][part * half : (part + 1) * half, columns]
        return inputs[pair[part]][:, columns]

    for left, right, blocks in uses:
        for left_start in range(0, D, tall):
            product = None
            for part in range(2):
                columns = [rows_of(pair, part, slice(start, start + side)) for start, pair in rights[right]]
                wide = columns[0] if len(columns) == 1 else jnp.concatenate(columns, axis=1)
                term = dot32(inputs[lefts[left][part]][left_start : left_start + tall, :], wide)
                product = term if product is None else product + term
            places = [(block * D + left_start) // tall for block in blocks]
            for number, place in enumerate(places):
                block_ref[place] = product[:, number * side : (number + 1) * side].astype(bf16)

            def send(piece, carry, places=places):
                for place in places:

                    def copy(array, lead, start, rows):
                        parts[array][lead] = block_ref[place, pl.ds(start, rows), :]

                    part_copies(
                        slots_ref, 8 * D // panel_rows, place * pieces + piece, cuts, piece * panel_rows, copy, 2
                    )
                return carry

            lax.fori_loop(0, pieces, send, 0)


def panel_gradients(arrays, lefts, rights, uses, slots, panel_rows, cuts, high_count, width):
    tall = LEN // 2
    outs = [
        jax.ShapeDtypeStruct((8 * high_count, cuts[index + 1] - cuts[index], width), bf16)
        for _ in range(2)
        for index in range(PARTS)
    ]
    outs = pl.pallas_call(
        lambda *refs: gradients_kernel(panel_rows, cuts, lefts, rights, uses, *refs),
        in_specs=[pl.BlockSpec(memory_space=pltpu.SMEM)]
        + [pl.BlockSpec(memory_space=pltpu.VMEM)] * len(arrays),
        out_specs=[pl.BlockSpec(memory_space=pltpu.VMEM)] * (2 * PARTS),
        out_shape=outs,
        scratch_shapes=[pltpu.VMEM((8 * D // tall, tall, width), bf16)],
        compiler_params=pltpu.CompilerParams(vmem_limit_bytes=gradient_bytes),
        cost_estimate=beside,
        name="gradients",
    )(slots, *arrays)
    shaped = [out.reshape((2, 2, 2 * high_count) + out.shape[1:]) for out in outs]
    return shaped[:PARTS], shaped[PARTS:]


def gelu_parts(values):
    share = 0.5 * (1.0 + lax.erf(values * 0.7071067811865476))
    density = 0.3989422804014327 * jnp.exp(-0.5 * values * values)
    return share, density


def in_vmem(kernel, name, inputs, outs, scratch=(), specs=None, out_specs=None, limit=vmem_bytes):
    whole = pl.BlockSpec(memory_space=pltpu.VMEM)
    return pl.pallas_call(
        kernel,
        in_specs=specs or [whole] * len(inputs),
        out_specs=out_specs or [whole] * len(outs),
        out_shape=[jax.ShapeDtypeStruct(shape, kind) for shape, kind in outs],
        scratch_shapes=list(scratch),
        compiler_params=pltpu.CompilerParams(vmem_limit_bytes=limit),
        cost_estimate=beside,
        name=name,
    )(*inputs)


def text_forward_kernel(
    core_ref, table_ref, mine_ref, other_ref, normed_ref, masked_ref, keep_ref, mel_mine_ref, mel_other_ref,
    in_bias_ref, gamma_ref, beta_ref, bias_ref, shift_ref, scale_ref,
    pre_ref, energy_ref, grn_ref, text_ref, stream_ref, first_ref, other_first_ref, first_t_ref, other_first_t_ref, texts_ref,
    hidden_held,
):
    rows = mine_ref.shape[1]
    half = stream_ref.shape[0]

    held = texts_ref

    def fetch(block, carry):
        place = pl.ds(pl.multiple_of(block * rows, 16), rows)
        for part, ref in enumerate((mine_ref, other_ref)):

            @pl.when((block + core_ref[0]) % 2 == part)
            def _():
                texts_ref[place, :] = ref[table_ref[block]]

        return carry

    lax.fori_loop(0, table_ref.shape[0], fetch, 0)
    energy_sum = jnp.zeros((1, TXT_FF), f32)
    for part in range(2):
        frames = slice(part * half, (part + 1) * half)
        pre = dot32(normed_ref[frames, :], held[:TEXT]) + in_bias_ref[...]
        if part == 0:
            pre_ref[...] = pre
        hidden = pre * gelu_parts(pre)[0]
        hidden_held[frames, :] = hidden
        energy_sum = energy_sum + jnp.sum(hidden * hidden, axis=0, keepdims=True)
    energy_ref[...] = energy_sum
    energy = jnp.sqrt(energy_sum)
    ratio = energy / (jnp.mean(energy, axis=-1, keepdims=True) + norm_eps)
    weight = gamma_ref[...] * ratio + 1.0
    for part, mel_ref in enumerate((mel_mine_ref, mel_other_ref)):
        frames = slice(part * half, (part + 1) * half)
        grn_low = (weight * hidden_held[frames, :] + beta_ref[...]).astype(bf16)
        text_out = masked_ref[frames, :] + dot32(grn_low, held[TEXT : 2 * TEXT], NT) + bias_ref[...]
        text_low = (text_out * keep_ref[frames, :]).astype(bf16)
        stream = mel_ref[...].astype(f32) + dot32(text_low, held[2 * TEXT :])
        normed, _ = normalise(stream)
        first = (normed * (1.0 + scale_ref[...]) + shift_ref[...]).astype(bf16)
        if part == 0:
            grn_ref[...] = grn_low
            text_ref[...] = text_low
            stream_ref[...] = stream
            first_ref[...] = first
            first_t_ref[...] = first.T
        else:
            other_first_ref[...] = first
            other_first_t_ref[...] = first.T


def text_forward(core, table, *inputs):
    whole = pl.BlockSpec(memory_space=pltpu.VMEM)
    scalars = pl.BlockSpec(memory_space=pltpu.SMEM)
    half = LEN // 2
    return in_vmem(
        text_forward_kernel,
        "text_forward",
        (core.reshape(1).astype(jnp.int32), table) + inputs,
        [
            ((half, TXT_FF), f32),
            ((1, TXT_FF), f32),
            ((half, TXT_FF), bf16),
            ((half, TEXT), bf16),
            ((half, D), f32),
            ((half, D), bf16),
            ((half, D), bf16),
            ((D, half), bf16),
            ((D, half), bf16),
            ((3 * TEXT, D), bf16),
        ],
        [pltpu.VMEM((LEN, TXT_FF), f32)],
        [scalars, scalars] + [whole] * len(inputs),
        [whole] * 10,
        text_forward_bytes,
    )


def stream_back_kernel(
    core_ref, my_ref, their_ref, stream_ref, later_ref, scale_ref, texts_ref, keep_ref, pre_ref,
    mel_ref, low_ref, shrink_ref, shrink_low_ref, grn_grad_ref, sums_ref, bias_sum_ref, full_ref,
):
    half = mel_ref.shape[0]
    grad = my_ref[...] + their_ref[...].astype(f32)
    normed, scale = normalise(stream_ref[...])
    sums_ref[0:1] = jnp.sum(grad, axis=0, keepdims=True)
    sums_ref[1:2] = jnp.sum(grad * normed, axis=0, keepdims=True)
    mel_grad = later_ref[...] + normalise_back(grad * (1.0 + scale_ref[...]), normed, scale)
    mel_ref[...] = mel_grad
    place = pl.ds(pl.multiple_of(core_ref[0] * half, half), half)
    full_ref[place, :] = mel_ref[...]
    low = mel_grad.astype(bf16)
    low_ref[...] = low
    shrink_grad = dot32(low, texts_ref[2 * TEXT :], NT) * keep_ref[...]
    shrink_ref[...] = shrink_grad
    bias_sum_ref[...] = jnp.sum(shrink_grad, axis=0, keepdims=True)
    shrink_low = shrink_grad.astype(bf16)
    shrink_low_ref[...] = shrink_low
    grn_grad = dot32(shrink_low, texts_ref[TEXT : 2 * TEXT])
    grn_grad_ref[...] = grn_grad
    pre = pre_ref[...]
    sums_ref[2:3] = jnp.sum(grn_grad * (pre * gelu_parts(pre)[0]), axis=0, keepdims=True)
    sums_ref[3:4] = jnp.sum(grn_grad, axis=0, keepdims=True)
    sums_ref[4:8] = jnp.zeros((4, D), f32)


def stream_back(core, *inputs):
    half = inputs[0].shape[0]
    whole = pl.BlockSpec(memory_space=pltpu.VMEM)
    return in_vmem(
        stream_back_kernel,
        "stream_back",
        (core.reshape(1).astype(jnp.int32),) + inputs,
        [
            ((half, D), f32),
            ((half, D), bf16),
            ((half, TEXT), f32),
            ((half, TEXT), bf16),
            ((half, TXT_FF), f32),
            ((8, D), f32),
            ((1, TEXT), f32),
            ((2 * half, D), f32),
        ],
        [],
        [pl.BlockSpec(memory_space=pltpu.SMEM)] + [whole] * len(inputs),
        [whole] * 8,
    )


def text_back_kernel(
    pre_ref, grn_grad_ref, energy_ref, dot_ref, gamma_ref, texts_ref, normed_ref, conv_normed_ref, conv_scale_ref, gain_ref,
    shrink_low_ref, grn_ref, text_ref, low_ref, core_ref, table_ref,
    mixed_ref, sums_ref, wide_sums_ref, *rest,
):
    grads_ref = rest[2] if len(rest) > 1 else rest[0]
    pre = pre_ref[...]
    share, density = gelu_parts(pre)
    energy = jnp.sqrt(energy_ref[...])
    energy_mean = jnp.mean(energy, axis=-1, keepdims=True) + norm_eps
    ratio = energy / energy_mean
    ratio_grad = gamma_ref[...] * dot_ref[...]
    energy_grad = (ratio_grad - jnp.mean(ratio_grad * ratio, axis=-1, keepdims=True)) / energy_mean
    hidden_grad = grn_grad_ref[...] * (gamma_ref[...] * ratio + 1.0) + (pre * share) * (energy_grad / energy)
    expand_grad = hidden_grad * (share + pre * density)
    wide_sums_ref[0:1] = jnp.sum(expand_grad, axis=0, keepdims=True)
    wide_sums_ref[1:2] = ratio
    expand_low = expand_grad.astype(bf16)
    grads_ref[:TEXT] = dot32(normed_ref[...], expand_low, TN).astype(bf16)
    grads_ref[TEXT : 2 * TEXT] = dot32(shrink_low_ref[...], grn_ref[...], TN).astype(bf16)
    grads_ref[2 * TEXT :] = dot32(text_ref[...], low_ref[...], TN).astype(bf16)
    normed_grad = dot32(expand_low, texts_ref[:TEXT], NT)
    conv_normed = conv_normed_ref[...]
    sums_ref[0:1] = jnp.sum(normed_grad * conv_normed, axis=0, keepdims=True)
    sums_ref[1:2] = jnp.sum(normed_grad, axis=0, keepdims=True)
    mixed_grad = normalise_back(normed_grad * gain_ref[...], conv_normed, conv_scale_ref[...])
    sums_ref[2:3] = jnp.sum(mixed_grad, axis=0, keepdims=True)
    mixed_ref[...] = mixed_grad
    if len(rest) == 1:
        return
    keep_ref, send_ref, _ = rest
    rows = keep_ref.shape[1]

    def place(block, carry):
        piece = pl.ds(pl.multiple_of(block * rows, 16), rows)
        for part, ref in enumerate((keep_ref, send_ref)):

            @pl.when((block + core_ref[0]) % 2 == part)
            def _():
                ref[table_ref[block]] = grads_ref[piece, :]

        return carry

    lax.fori_loop(0, table_ref.shape[0], place, 0)


def text_back(core, table, rows, *inputs):
    half = inputs[0].shape[0]
    whole = pl.BlockSpec(memory_space=pltpu.VMEM)
    scalars = pl.BlockSpec(memory_space=pltpu.SMEM)
    outs = [((half, TEXT), f32), ((3, TEXT), f32), ((2, TXT_FF), f32)]
    apart = rows % 16 == 0
    blocks = ((3 * TEXT // (2 * rows), rows, D), bf16)
    return in_vmem(
        text_back_kernel,
        "text_back",
        inputs + (core.reshape(1).astype(jnp.int32), table),
        outs + ([blocks] * 2 if apart else [((3 * TEXT, D), bf16)]),
        [pltpu.VMEM((3 * TEXT, D), bf16)] if apart else [],
        [whole] * len(inputs) + [scalars] * 2,
        [whole] * (5 if apart else 4),
        text_back_bytes,
    )


def conv_back_kernel(
    core_ref, mixed_ref, border_ref, window_ref, kernel_ref, shrink_ref, keep_ref,
    mine_ref, kernel_grad_ref, full_ref, wide,
):
    half = mixed_ref.shape[0]
    edge, margin = border_ref.shape[0], KERNEL // 2
    mixed = mixed_ref[...]
    border = border_ref[...]
    wide[:edge] = jnp.where(core_ref[0] == 1, border, 0.0)
    wide[edge : edge + half] = mixed
    wide[edge + half :] = jnp.where(core_ref[0] == 0, border, 0.0)
    total = shrink_ref[...]
    for j in range(KERNEL):
        start = edge + margin - j
        total = total + wide[start : start + half] * kernel_ref[j : j + 1]
        tap = window_ref[edge - margin + j : edge - margin + j + half]
        kernel_grad_ref[j : j + 1] = jnp.sum(mixed * tap, axis=0, keepdims=True)
    mine_ref[...] = total * keep_ref[...]
    place = pl.ds(pl.multiple_of(core_ref[0] * half, half), half)
    full_ref[place, :] = mine_ref[...]


def conv_back(core, *inputs):
    half = inputs[0].shape[0]
    whole = pl.BlockSpec(memory_space=pltpu.VMEM)
    return in_vmem(
        conv_back_kernel,
        "conv_back",
        (core.reshape(1).astype(jnp.int32),) + inputs,
        [((half, TEXT), f32), ((KERNEL, TEXT), f32), ((2 * half, TEXT), f32)],
        [pltpu.VMEM((half + 2 * inputs[1].shape[0], TEXT), f32)],
        [pl.BlockSpec(memory_space=pltpu.SMEM)] + [whole] * len(inputs),
        [whole] * 3,
    )


def settle_kernel(
    core_ref, my_out_ref, their_out_ref, my_grad_ref, their_grad_ref, stream_ref, attention_ref, cot_ref,
    gate_one_ref, scale_ref, gate_two_ref,
    output_ref, later_ref, attention_grad_ref, sums_ref, full_ref,
):
    half = output_ref.shape[0]
    unit_out = my_out_ref[...] + their_out_ref[...].astype(f32)
    stream = stream_ref[...]
    output_ref[...] = (stream + gate_two_ref[...] * unit_out).astype(bf16)
    place = pl.ds(pl.multiple_of(core_ref[0] * half, half), half)
    full_ref[place, :] = output_ref[...]
    out_grad = cot_ref[...].astype(f32)
    sums_ref[0:1] = jnp.sum(out_grad * unit_out, axis=0, keepdims=True)
    grad = my_grad_ref[...] + their_grad_ref[...].astype(f32)
    normed, scale = normalise(stream)
    sums_ref[1:2] = jnp.sum(grad, axis=0, keepdims=True)
    sums_ref[2:3] = jnp.sum(grad * normed, axis=0, keepdims=True)
    later = out_grad + normalise_back(grad * (1.0 + scale_ref[...]), normed, scale)
    later_ref[...] = later
    sums_ref[3:4] = jnp.sum(later * attention_ref[...], axis=0, keepdims=True)
    attention_grad_ref[...] = (gate_one_ref[...] * later).astype(bf16)


def settle(core, *inputs):
    half = inputs[0].shape[0]
    whole = pl.BlockSpec(memory_space=pltpu.VMEM)
    return in_vmem(
        settle_kernel,
        "settle",
        (core.reshape(1).astype(jnp.int32),) + inputs,
        [((half, D), bf16), ((half, D), f32), ((half, D), bf16), ((4, D), f32), ((2 * half, D), bf16)],
        [],
        [pl.BlockSpec(memory_space=pltpu.SMEM)] + [whole] * len(inputs),
        [whole] * 5,
    )


def dot_split(left, right, dims=NN):
    split = lambda array: (array.astype(bf16), (array - array.astype(bf16).astype(f32)).astype(bf16))
    left_high, left_low = split(left)
    right_high, right_low = split(right)
    return (
        dot32(left_high, right_high, dims)
        + dot32(left_high, right_low, dims)
        + dot32(left_low, right_high, dims)
    )


def rotated_kernel(places, utterances, *refs):
    pieces, refs = refs[: sum(count for _, _, count in places)], refs[sum(count for _, _, count in places) :]
    left_ref, right_ref, master_ref, first_ref, second_ref, weights_ref, moment_ref, variance_ref, grad_ref = refs
    which = 0
    for row, column, count in places:
        total = pieces[which][...].astype(f32)
        for ref in pieces[which + 1 : which + count]:
            total = total + ref[...].astype(f32)
        rows, columns = total.shape
        grad_ref[row : row + rows, column : column + columns] = total / utterances
        which += count
    left, right = left_ref[...], right_ref[...]
    rotated = dot_split(dot_split(left, grad_ref[...], TN), right)
    moment, variance, direction = moments(rotated, first_ref[...], second_ref[...])
    moment_ref[...] = moment
    variance_ref[...] = variance
    turned = dot_split(dot_split(left, direction), right, NT)
    master = master_ref[...]
    weights_ref[...] = apply_step(master, turned, learn_rate)


def rotated_step(pieces, utterances, left, right, master, first, second):
    places = [(row, column, len(arrays)) for row, column, arrays in pieces]
    arrays = [array for _, _, group in pieces for array in group]
    return in_vmem(
        lambda *refs: rotated_kernel(places, utterances, *refs),
        "rotated_step",
        tuple(arrays) + (left, right, master, first, second),
        [(master.shape, f32)] * 3,
        [pltpu.VMEM(master.shape, f32)],
    )


def modulation_kernel(utterances, time_ref, table_ref, old_ref, first_ref, second_ref, weights_ref, moment_ref, variance_ref):
    grad = dot32(time_ref[...], table_ref[...], TN) / utterances
    moment, variance, direction = moments(grad, first_ref[...], second_ref[...])
    moment_ref[...] = moment
    variance_ref[...] = variance
    weights_ref[...] = apply_step(old_ref[...], direction, learn_rate)


def modulation_step(utterances, time_rows, table, old, first, second):
    rows, columns = old.shape
    step = columns // 6
    tall = pl.BlockSpec((rows, step), lambda i: (0, i))
    return pl.pallas_call(
        lambda *refs: modulation_kernel(utterances, *refs),
        grid=(6,),
        in_specs=[
            pl.BlockSpec((GROUPS, rows), lambda i: (0, 0)),
            pl.BlockSpec((GROUPS, step), lambda i: (0, i)),
        ]
        + [tall] * 3,
        out_specs=[tall] * 3,
        out_shape=[jax.ShapeDtypeStruct(old.shape, f32)] * 3,
        compiler_params=pltpu.CompilerParams(vmem_limit_bytes=vmem_bytes),
        cost_estimate=beside,
        name="modulation_step",
    )(time_rows, table, old, first, second)


def vector_parts(vectors):
    kernel_size = KERNEL * TEXT
    pieces = [vectors[:kernel_size].reshape(KERNEL, TEXT)]
    offset = kernel_size
    for extent in (TEXT, TEXT, TEXT, TEXT, TXT_FF, TXT_FF, TXT_FF, 6 * D):
        pieces.append(vectors[offset : offset + extent])
        offset = offset + extent
    return pieces


def normalise(values):
    center = values - jnp.mean(values, axis=-1, keepdims=True)
    variance = jnp.mean(center * center, axis=-1, keepdims=True)
    scale = lax.rsqrt(variance + norm_eps)
    return center * scale, scale


def normalise_back(grad, normed, scale):
    mean_grad = jnp.mean(grad, axis=-1, keepdims=True)
    mean_dot = jnp.mean(grad * normed, axis=-1, keepdims=True)
    return scale * (grad - mean_grad - normed * mean_dot)


def moments(gradient, first_moment, second_moment):
    first_new = beta_one * first_moment + (1.0 - beta_one) * gradient
    second_new = beta_two * second_moment + (1.0 - beta_two) * gradient * gradient
    bias_first = 1.0 - beta_one**STEP
    bias_second = 1.0 - beta_two**STEP
    direction = first_new / bias_first / (jnp.sqrt(second_new / bias_second) + adam_eps)
    return (first_new, second_new, direction)


def apply_step(weight, direction, rate):
    return weight - rate * (direction + weight_decay * weight)


def rotary_tables(first):
    position = np.arange(LEN)
    frequency = 10000.0 ** (-np.arange(HEAD // 2) * 2.0 / HEAD)
    angle = position[:, None] * frequency[None, :]
    cosine, sine = np.cos(angle), np.sin(angle)
    tables = np.concatenate([cosine] * 4 + [-sine, sine, -sine, sine], axis=1).astype(np.float32)
    tables = lax.dynamic_slice_in_dim(jnp.asarray(np.concatenate([tables, tables])), first, LEN, 0)
    return tables[:, :PAIR], tables[:, PAIR:]


def take_blocks(blocks, index):
    return jnp.take(blocks, index, axis=0, mode="clip")


def both_halves(mine):
    return jnp.concatenate([mine, swap_core(mine)], axis=0)


def sum_halves(multiply, rows, half):
    theirs = multiply(rows[half:]).astype(bf16)
    received = swap_core(theirs)
    return multiply(rows[:half]) + received.astype(f32)


def body(
    mel_frames,
    text_features,
    cotangent,
    time_embedding,
    lengths,
    group_ids,
    text_keep,
    owner_list,
    soap_master,
    soap_first,
    soap_second,
    left_basis,
    right_basis,
    text_matrices,
    text_first,
    text_second,
    modulation_weight,
    modulation_first,
    modulation_second,
    vectors,
    vector_first,
    vector_second,
):
    count = lax.axis_size("dp")
    me, core = lax.axis_index("dp"), lax.axis_index("mp")
    half = LEN // 2
    utterances = lengths.shape[0] * count
    panel_rows, width = soap_master.shape
    share_rows = modulation_weight.shape[0]
    text_rows = text_matrices.shape[0]
    text_half = text_rows // 2
    relative = jnp.arange(count) ^ me

    high_count = count // 16
    cuts = row_cuts(panel_rows)
    panel_table = panel_places(core, owner_list ^ me, high_count)
    gather_table = panel_places(core, owner_list ^ me, high_count, True)
    silu_time = jax.nn.silu(time_embedding.astype(f32)).astype(bf16)
    time_rows = lax.dynamic_slice_in_dim(silu_time, me * share_rows, share_rows, 1)
    weight_half = lax.dynamic_slice_in_dim(modulation_weight, core * 3 * D, 3 * D, 1).astype(bf16)
    own_rows = lax.dynamic_slice_in_dim(text_matrices, core * text_half, text_half, 0)
    text_held = spread_high(own_rows.astype(bf16))
    partial = dot32(time_rows, weight_half)
    held = spread_high(soap_master.astype(bf16))
    text_received, partial_received = tie(swap_bit(text_held, 3), swap_bit(partial, 3))
    text_held = jnp.concatenate([text_held, text_received], axis=0)
    partial = partial + partial_received
    text_received, partial_received, held = tie(
        swap_bits(text_held, phase_bits(text_orders, 0)), swap_bits(partial, phase_bits(text_orders, 0)), held
    )
    held = split_rows(held, cuts)
    text_held = jnp.stack([text_held, text_received])
    partial = partial + partial_received
    received, (text_received, partial_received, far_last) = tie_lists(
        receive(held, 0),
        (
            swap_bits(text_held, phase_bits(text_orders, 1)),
            swap_bits(partial, phase_bits(text_orders, 1)),
            swap_bit(held[1], 3),
        ),
    )
    near = [jnp.stack(pair) for pair in zip(held, received)]
    text_held = jnp.stack([text_held, text_received])
    partial = partial + partial_received
    received, (text_received, partial_received, far_first) = tie_lists(
        receive(near, 1),
        (
            swap_bits(text_held, phase_bits(text_orders, 2)),
            swap_bits(partial, phase_bits(text_orders, 2)),
            swap_bit(held[0], 3),
        ),
    )
    partial = partial + partial_received
    near = [jnp.stack(pair) for pair in zip(near, received)]
    near_received = receive(near, 2)
    far = spread_step([far_first, far_last], 0)
    received = receive(far, 1)
    text_mine = jnp.stack([text_held, text_received]).reshape(count, text_half, D)
    text_other = swap_core(text_mine)
    text_features, mel_frames, cotangent, far = tie(text_features, mel_frames, cotangent, far)
    for bit in range(4, bit_count(count)):
        partial = partial + swap_bit(partial, bit)
    modulation_half = partial
    mine_places, other_places = text_places(core, relative, high_count), text_places(1 - core, relative, high_count)
    text_table = jnp.where(
        core == 0, jnp.stack([mine_places, other_places], 1), jnp.stack([other_places, mine_places], 1)
    ).reshape(-1)
    if text_half % 16:
        source = jnp.arange(2 * count) % 2 != core
        texts = take_blocks(jnp.concatenate([text_mine, text_other]), text_table + count * source)
        text_mine = text_other = texts.reshape(1, 3 * TEXT, D)
        text_table = jnp.zeros((1,), jnp.int32)

    modulation = by_core(core, modulation_half, swap_core(modulation_half), axis=1)
    (
        kernel,
        conv_bias,
        norm_gain,
        norm_bias,
        out_bias,
        in_bias,
        grn_gamma,
        grn_beta,
        modulation_bias,
    ) = vector_parts(vectors)
    group = group_ids[0]
    modulation_row = lax.dynamic_slice_in_dim(modulation, group, 1, 0) + modulation_bias


    first = core * half
    margin = KERNEL // 2
    edge = 8
    keep_all = jnp.pad(text_keep.astype(f32), (edge, edge))[:, None]
    text_all = jnp.pad(text_features, ((edge, edge), (0, 0)))

    def text_start(start):
        window = lax.dynamic_slice_in_dim(text_all, start, half + 2 * edge, 0).astype(f32)
        window = window * lax.dynamic_slice_in_dim(keep_all, start, half + 2 * edge, 0)
        keep = lax.dynamic_slice_in_dim(keep_all, start + edge, half, 0)
        taps = [window[edge - margin + j : edge - margin + j + half] for j in range(KERNEL)]
        mixed = conv_bias[None, :]
        for j in range(KERNEL):
            mixed = mixed + taps[j] * kernel[j][None, :]
        normed, scale = normalise(mixed)
        return window, keep, normed, scale, (normed * norm_gain + norm_bias).astype(bf16)

    window, keep, conv_normed, conv_scale, normed_low = text_start(first)
    window_other, keep_other, _, _, normed_other = text_start(half - first)
    masked_both = jnp.concatenate([window[edge : edge + half], window_other[edge : edge + half]], axis=0)
    keep_both = jnp.concatenate([keep, keep_other], axis=0)
    normed_both = jnp.concatenate([normed_low, normed_other], axis=0)
    mel_mine = lax.dynamic_slice_in_dim(mel_frames, first, half, 0)
    mel_other = lax.dynamic_slice_in_dim(mel_frames, half - first, half, 0)
    cosine, sine = rotary_tables(first)
    received, near_received, (text_other, modulation_row, normed_both, masked_both, cosine, sine) = tie_lists(
        received, near_received, (text_other, modulation_row, normed_both, masked_both, cosine, sine)
    )
    far = [jnp.stack(pair) for pair in zip(far, received)]
    far_received = receive(far, 2)
    shift_one, scale_one, gate_one, shift_two, scale_two, gate_two = (
        modulation_row[:, i * D : (i + 1) * D] for i in range(6)
    )
    expand_pre, energy_sum, grn_low, text_low, stream, first_mine, first_other, first_t, first_other_t, texts = text_forward(
        core,
        text_table,
        text_mine,
        text_other,
        normed_both,
        masked_both,
        keep_both,
        mel_mine,
        mel_other,
        in_bias[None],
        grn_gamma[None],
        grn_beta[None],
        out_bias[None],
        shift_one,
        scale_one,
    )

    cot_mine = lax.dynamic_slice_in_dim(cotangent, first, half, 0)
    cot_other = lax.dynamic_slice_in_dim(cotangent, half - first, half, 0)
    hidden_mine = (gate_two * cot_mine.astype(f32)).astype(bf16)
    hidden_other = (gate_two * cot_other.astype(f32)).astype(bf16)
    first_mine, hidden_mine, hidden_other = tie(first_mine, hidden_mine, hidden_other)
    position = (jnp.arange(LEN) + first) % LEN
    bias = jnp.where(position < lengths[0], 0.0, -1e30).astype(bf16)
    bias = jnp.broadcast_to(bias[:, None], (LEN, PAIR))
    queries, keys, value_rows, stacked = project(
        (near, near_received, far, far_received), gather_table, panel_rows, cuts, first_mine, first_other, cosine, sine
    )
    stacked = stacked.reshape(8, D, width)
    attended, query_aug = attend_forward(queries, keys, value_rows, bias)
    attention_out = sum_halves(lambda rows: dot32(rows, stacked[3], NT), attended, half)
    stream_one = stream + gate_one * attention_out

    normed_two, _ = normalise(stream_one)
    second_mine = (normed_two * (1.0 + scale_two) + shift_two).astype(bf16)
    second_other = swap_core(second_mine)
    their_out, their_grad, act_other, pre_other, second_other_t, hidden_other_t = feed(second_other, hidden_other, stacked, bf16)
    their_out, their_grad = swap_core(their_out), swap_core(their_grad)
    my_out, my_grad, act_mine, pre_mine, second_t, hidden_t = feed(second_mine, hidden_mine, stacked, f32)
    output_mine, stream_one_grad, attention_mine, settle_sums, block_output = settle(
        core,
        my_out,
        their_out,
        my_grad,
        their_grad,
        stream_one,
        attention_out,
        cot_mine,
        gate_one,
        scale_two,
        gate_two,
    )
    gate_two_grad, shift_two_grad, scale_two_grad, gate_one_grad = (settle_sums[i] for i in range(4))
    output_theirs = swap_core(output_mine)

    attention_other = swap_core(attention_mine)
    narrow = width // 2

    def back(side, queries):
        return attend_backward(
            side, queries, keys, value_rows, attended, attention_mine, attention_other, stacked, cosine, sine, bias
        )

    def weight_gradients(side, head_grads):
        column = side * narrow
        return panel_gradients(
            [
                first_t, first_other_t, attention_t, attention_other_t, second_t, second_other_t,
                hidden_t, hidden_other_t, *head_grads, attended, pre_mine, pre_other, act_mine, act_other,
            ],
            [(0, 1), (2, 3), (4, 5), (6, 7)],
            [
                [(0, (8, 8)), (0, (9, 9))],
                [(0, (10, 10))],
                [(column, (11, 11))],
                [(column, (12, 13)), (width + column, (12, 13))],
                [(column, (14, 15)), (width + column, (14, 15))],
            ],
            ((0, 0, (0, 1)), (0, 1, (2,)), (1, 2, (3,)), (2, 3, (4, 5)), (3, 4, (6, 7))),
            panel_table,
            panel_rows,
            cuts,
            high_count,
            narrow,
        )

    *head_grads, attention_t, attention_other_t = back(0, query_aug)
    keep_a, send_a = weight_gradients(0, head_grads)
    send_a, (query_aug,) = tie_lists(send_a, (query_aug,))
    received_a = receive(send_a, 2)
    head_grads += list(back(1, query_aug))
    received_a, head_grads = tie_lists(received_a, head_grads)
    part_a = add_all(keep_a, received_a)
    received_a = receive(seconds(part_a), 1)
    keep_b, send_b = weight_gradients(1, head_grads[3:])
    received_a, send_b, head_grads = tie_lists(received_a, send_b, head_grads)
    part_a = add_all(firsts(part_a), received_a)
    received_a = receive(seconds(part_a), 0)
    my_grad, their_grad = inputs_grad(head_grads, stacked)
    received_a, send_b, (my_grad, their_grad) = tie_lists(received_a, send_b, (my_grad, their_grad))

    part_a = add_all(firsts(part_a), received_a)
    received_b = receive(send_b, 2)
    their_grad = swap_core(their_grad)
    mel_grad_mine, stream_low, shrink_grad, shrink_low, grn_grad, sums, out_bias_grad, mel_gradient = stream_back(
        core, my_grad, their_grad, stream, stream_one_grad, scale_one, texts, keep, expand_pre
    )
    received_b, part_a, (sums, mel_grad_mine) = tie_lists(received_b, part_a, (sums, mel_grad_mine))
    shift_one_grad, scale_one_grad, hidden_dot, beta_grad = sums[0], sums[1], sums[2:3], sums[3]
    out_bias_grad = out_bias_grad[0]
    far_a = [swap_bit(part[high_count:], 3) for part in part_a]
    part_b = add_all(keep_b, received_b)
    received_b = receive(seconds(part_b), 1)
    hidden_dot_all = hidden_dot + swap_core(hidden_dot)
    mixed_grad, text_sums, wide_sums, *text_grads = text_back(
        core,
        text_table,
        text_half,
        expand_pre,
        grn_grad,
        energy_sum,
        hidden_dot_all,
        grn_gamma[None],
        texts,
        normed_low,
        conv_normed,
        conv_scale,
        norm_gain[None],
        shrink_low,
        grn_low,
        text_low,
        stream_low,
    )
    mel_grad_theirs = swap_core(mel_grad_mine)
    gain_grad, norm_bias_grad, conv_bias_grad = text_sums[0], text_sums[1], text_sums[2]
    in_bias_grad, gamma_grad = wide_sums[0], wide_sums[1] * hidden_dot[0]
    if len(text_grads) == 1:
        blocks = text_grads[0].reshape(count, 2, text_half, D)
        order = lambda which: text_slots(which, jnp.arange(count), high_count) ^ me
        text_grads = [
            take_blocks(lax.dynamic_index_in_dim(blocks, which, 1, keepdims=False), order(which))
            for which in (core, 1 - core)
        ]
    received_b, far_a, (mixed_grad, text_keep_half, text_send_half, mel_grad_theirs) = tie_lists(
        received_b, far_a, (mixed_grad, *text_grads, mel_grad_theirs)
    )
    part_b = add_all(firsts(part_b), received_b)
    received_b = receive(seconds(part_b), 0)
    text_received = swap_core(text_send_half)
    border = swap_core(lax.dynamic_slice_in_dim(mixed_grad, (1 - core) * (half - edge), edge, 0))
    text_grad_mine, kernel_grad, text_gradient = conv_back(
        core, mixed_grad, border, window, kernel, shrink_grad, keep
    )

    vector_mine = jnp.concatenate(
        [
            kernel_grad.reshape(-1),
            conv_bias_grad,
            gain_grad,
            norm_bias_grad,
            out_bias_grad,
            in_bias_grad,
            gamma_grad,
            beta_grad,
        ]
    )
    token = jnp.concatenate(
        [shift_one_grad, scale_one_grad, gate_one_grad, shift_two_grad, scale_two_grad, gate_two_grad]
    )
    vector_half = vector_mine.shape[0] // 2
    token_half = 3 * D

    def half_of(which):
        half_vector = lax.dynamic_slice_in_dim(vector_mine, which * vector_half, vector_half, 0)
        return jnp.concatenate(
            [
                jnp.pad(half_vector, (0, 2 * token_half - vector_half)).reshape(2, token_half),
                lax.dynamic_slice_in_dim(token, which * token_half, token_half, 0)[None],
            ]
        )

    small = half_of(core)
    small_received = swap_core(half_of(1 - core))
    in_group = (jnp.arange(GROUPS) == group).astype(f32)
    text_grad_theirs = swap_core(text_grad_mine)
    text_part = add_low(text_keep_half, text_received).reshape(2, 2, 2, 2 * high_count, text_half, D)
    mel_gradient = lax.dynamic_update_slice_in_dim(mel_gradient, mel_grad_theirs, half - first, 0)
    received_b, (text_part, small, small_received, mel_gradient) = tie_lists(
        received_b, (text_part, small, small_received, mel_gradient)
    )
    small = small + small_received
    small = jnp.concatenate([in_group[:, None] * small[2:], small[:2]])
    part_b = add_all(firsts(part_b), received_b)
    far_b = [swap_bit(part[high_count:], 3) for part in part_b]
    text_received = swap_bits(text_part[1], phase_bits(text_orders, 2))
    small_received = swap_bits(small, (2, 0))
    block_output = lax.dynamic_update_slice_in_dim(block_output, output_theirs, half - first, 0)
    text_gradient = lax.dynamic_update_slice_in_dim(text_gradient, text_grad_theirs, half - first, 0)
    far_b, (text_received, small_received, text_gradient, block_output) = tie_lists(
        far_b, (text_received, small_received, text_gradient, block_output)
    )
    text_part = add_low(text_part[0], text_received)
    text_received = swap_bits(text_part[1], phase_bits(text_orders, 1))
    small = small + small_received
    small_received = swap_bits(small, (0, 1))
    panel_pieces = []
    for side, (parts, others) in enumerate(((part_a, far_a), (part_b, far_b))):
        for index, (part, other) in enumerate(zip(parts, others)):
            if high_count == 1:
                arrays = [part[0], other[0]]
            else:
                arrays = [fold_high(part[:high_count].astype(f32) + other.astype(f32))]
            panel_pieces.append((cuts[index], side * narrow, arrays))
    soap_weights, soap_moment, soap_variance = rotated_step(
        panel_pieces, utterances, left_basis, right_basis, soap_master, soap_first, soap_second
    )
    text_received, small_received, soap_weights, soap_moment, soap_variance = tie(
        text_received, small_received, soap_weights, soap_moment, soap_variance
    )
    text_part = add_low(text_part[0], text_received)
    small = small + small_received
    text_part = fold(text_part, text_orders, 0)
    text_received = swap_bit(text_part[high_count:], 3)
    small = small + swap_bits(small, (1, 2))
    small = small + swap_bit(small, 3)
    own_text = text_part[:high_count].astype(f32) + text_received.astype(f32)
    for bit in range(4, bit_count(count)):
        small = small + swap_bit(small, bit)
    own_text = fold_high(own_text)
    own_text = by_core(core, own_text, swap_core(own_text))
    small = by_core(core, small, swap_core(small), axis=1)
    modulation_grad = small[:GROUPS]
    vector_sum = jnp.concatenate(
        [
            small[GROUPS + row, which * token_half : which * token_half + min(token_half, vector_half - row * token_half)]
            for which in range(2)
            for row in range(2)
        ]
    )
    vector_gradient = jnp.concatenate([vector_sum, jnp.sum(modulation_grad, axis=0)]) / utterances

    own_text = own_text / utterances
    text_moment, text_variance, text_direction = moments(own_text, text_first, text_second)
    text_weights = apply_step(text_matrices, text_direction, learn_rate)
    modulation_weights, modulation_moment, modulation_variance = modulation_step(
        utterances,
        time_rows,
        modulation_grad.astype(bf16),
        modulation_weight,
        modulation_first,
        modulation_second,
    )
    vector_moment, vector_variance, vector_direction = moments(
        vector_gradient, vector_first, vector_second
    )
    vector_weights = apply_step(vectors, vector_direction, vector_rate)
    return (
        block_output,
        mel_gradient,
        text_gradient,
        soap_weights,
        soap_moment,
        soap_variance,
        text_weights,
        text_moment,
        text_variance,
        modulation_weights,
        modulation_moment,
        modulation_variance,
        vector_weights,
        vector_moment,
        vector_variance,
    )


def solution(mesh):
    rows, quarter, same = P("dp", None), P("dp", "mp"), P()
    return jax.shard_map(
        body,
        mesh=mesh,
        in_specs=(
            (rows,) * 3 + (same,) + (P("dp"),) * 3 + (same,) + (quarter,) * 5 + (rows,) * 6 + (same,) * 3
        ),
        out_specs=(rows,) * 3 + (quarter,) * 3 + (rows,) * 6 + (same,) * 3,
        check_vma=False,
    )
```

```python
import jax
import numpy as np
import jax.numpy as jnp
from jax import lax
from jax.experimental import pallas as pl
from jax.experimental.pallas import tpu as pltpu
from jax.sharding import PartitionSpec as P

D = 1024
HEAD = 64
TEXT = 512
TXT_FF = 1024
KERNEL = 7
LEN = 1024
GROUPS = 8
STEP = 10

f32 = jnp.float32
bf16 = jnp.bfloat16
beta_one = 0.9
beta_two = 0.99
adam_eps = 1e-08
weight_decay = 0.01
learn_rate = 0.03
vector_rate = 0.3
norm_eps = 1e-06


def swap_core(array):
    return lax.ppermute(array, "mp", [(0, 1), (1, 0)])


def swap_bits(array, bits):
    count = lax.axis_size("dp")
    pairs = [
        (i * 2 + core, (i ^ (1 << bits[core])) * 2 + core) for i in range(count) for core in range(2)
    ]
    return lax.ppermute(array, ("dp", "mp"), pairs)


def swap_bit(array, bit):
    return swap_bits(array, (bit, bit))


def by_core(core, mine, other, axis=0):
    return jnp.where(
        core == 0,
        jnp.concatenate([mine, other], axis=axis),
        jnp.concatenate([other, mine], axis=axis),
    )


def bit_count(count):
    return count.bit_length() - 1


def row_cuts(rows):
    return (0, (rows * 2 + 24) // 48 * 16, rows)


axis_orders = (((0, 1, 2), (1, 2, 0)), ((2, 0, 1), (2, 0, 1)))
text_orders = ((2, 0, 1), (2, 1, 0))


def phase_bits(orders, phase):
    return tuple(order[phase] for order in orders)


def tie(*values):
    return lax.optimization_barrier(values)


def tie_lists(*lists):
    flat = [value for values in lists for value in values]
    flat = list(lax.optimization_barrier(tuple(flat)))
    out = []
    for values in lists:
        out.append(flat[: len(values)])
        flat = flat[len(values) :]
    return out


def split_rows(array, cuts):
    return [array[..., cuts[i] : cuts[i + 1], :] for i in range(len(cuts) - 1)]


def spread(part, orders, phase):
    return jnp.stack([part, swap_bits(part, phase_bits(orders, phase))])


def spread_step(parts, phase):
    return [spread(part, axis_orders[index], phase) for index, part in enumerate(parts)]


def spread_last(parts):
    return [(part, swap_bits(part, phase_bits(axis_orders[index], 2))) for index, part in enumerate(parts)]


def spread_high(block):
    held = block[None]
    for bit in range(4, bit_count(lax.axis_size("dp"))):
        held = jnp.concatenate([held, swap_bit(held, bit)], axis=0)
    return held


def add_low(left, right):
    return (left.astype(f32) + right.astype(f32)).astype(bf16)


def receive(sends, phase):
    return [swap_bits(send, phase_bits(axis_orders[index], phase)) for index, send in enumerate(sends)]


def add_all(keeps, received):
    return [add_low(keep, other) for keep, other in zip(keeps, received)]


def firsts(parts):
    return [part[0] for part in parts]


def seconds(parts):
    return [part[1] for part in parts]


def fold(part, orders, phase):
    return add_low(part[0], swap_bits(part[1], phase_bits(orders, phase)))


def fold_high(total):
    count = total.shape[0]
    if count == 1:
        return total[0]
    for bit in range(bit_count(count) - 1, -1, -1):
        half = 1 << bit
        total = total[:half] + swap_bit(total[half:].astype(bf16), bit + 4).astype(f32)
    return total[0]


def bit_of(values, which):
    return (values >> which) & 1


def panel_places(core, slots, high_count, apart=False):
    rows = []
    for orders in axis_orders:
        far = bit_of(slots, 3)
        which = [bit_of(slots, order[2]) + (2 * far if apart else 0) for order in orders]
        lead = [bit_of(slots, order[1]) * 2 + bit_of(slots, order[0]) for order in orders]
        if not apart:
            lead = [place * 2 + far for place in lead]
        lead = [place * high_count + (slots >> 4) for place in lead]
        rows += [jnp.where(core == 0, *which), jnp.where(core == 0, *lead)]
    return jnp.concatenate(rows).astype(jnp.int32)


def text_places(core, slots, high_count):
    places = []
    for order in text_orders:
        high = bit_of(slots, 3) * high_count + (slots >> 4)
        places.append(
            ((bit_of(slots, order[2]) * 2 + bit_of(slots, order[1])) * 2 + bit_of(slots, order[0]))
            * (2 * high_count)
            + high
        )
    return jnp.where(core == 0, *places).astype(jnp.int32)


def text_slots(core, places, high_count):
    lead, rest = places // (2 * high_count), places % (2 * high_count)
    high = ((rest // high_count) << 3) | ((rest % high_count) << 4)
    slots = []
    for order in text_orders:
        low = (bit_of(lead, 2) << order[2]) | (bit_of(lead, 1) << order[1]) | (bit_of(lead, 0) << order[0])
        slots.append(high | low)
    return jnp.where(core == 0, *slots)


beside = pl.CostEstimate(flops=1000, bytes_accessed=1000, transcendentals=0)

NT = (((1,), (1,)), ((), ()))
NN = (((1,), (0,)), ((), ()))
TN = (((0,), (0,)), ((), ()))
ROWS = 256
LONG_ROWS = 512
PAIR = 2 * HEAD
mebibyte = 1024 * 1024
vmem_bytes = 12 * mebibyte
feed_bytes = 12 * mebibyte
attend_back_bytes = 14 * mebibyte
text_forward_bytes = 16 * mebibyte
text_back_bytes = 12 * mebibyte
gradient_bytes = 18 * mebibyte
project_bytes = 22 * mebibyte


def dot32(left, right, dims=NN):
    return lax.dot_general(left, right, dims, preferred_element_type=f32)


def three_terms(values):
    high = values.astype(bf16).astype(f32)
    rest = values - high
    middle = rest.astype(bf16).astype(f32)
    return high, middle, rest - middle


def rotate(values, cosine, sine, lane):
    partner = jnp.where(
        lane % HEAD < HEAD // 2,
        pltpu.roll(values, PAIR - HEAD // 2, 1),
        pltpu.roll(values, HEAD // 2, 1),
    )
    return values * cosine + partner * sine


def attend_kernel(q_ref, k_ref, v_ref, bias_ref, o_ref, qa_ref):
    lane = lax.broadcasted_iota(jnp.int32, (LEN, PAIR), 1)
    lane_rows = lax.broadcasted_iota(jnp.int32, (LONG_ROWS, PAIR), 1)
    row_index = lax.broadcasted_iota(jnp.int32, (PAIR, LONG_ROWS), 0)
    q_wide = q_ref[...].astype(f32)
    k_wide = k_ref[...].astype(f32)
    values_t = v_ref[...].T
    bias = bias_ref[...].astype(f32)
    keys = []
    for head in range(2):
        own = lane // HEAD == head
        spare = (1 - head) * HEAD
        keys.append(
            jnp.where(own, k_wide, jnp.where(lane == spare, bias, 0.0)).astype(bf16)
        )
        qa_ref[:, head * PAIR : (head + 1) * PAIR] = jnp.where(
            own, q_wide, jnp.where(lane == spare, 1.0, 0.0)
        ).astype(bf16)
    steps = [(block, head) for block in range(LEN // LONG_ROWS) for head in range(2)]

    def scores_of(step):
        block, head = step
        rows = slice(block * LONG_ROWS, (block + 1) * LONG_ROWS)
        return dot32(keys[head], qa_ref[rows, head * PAIR : (head + 1) * PAIR], NT)

    following = scores_of(steps[0])
    for position, (block, head) in enumerate(steps):
        scores = following
        if position + 1 < len(steps):
            following = scores_of(steps[position + 1])
        rows = slice(block * LONG_ROWS, (block + 1) * LONG_ROWS)
        if head == 0:
            outs, extra = [], jnp.zeros((PAIR, LONG_ROWS), f32)
        spare = (1 - head) * HEAD
        highest = jnp.max(scores, axis=0, keepdims=True)
        weights = jnp.exp(scores - highest)
        total = jnp.sum(weights, axis=0, keepdims=True)
        out_t = dot32(values_t[head * HEAD : (head + 1) * HEAD], weights.astype(bf16))
        outs.append(out_t / total)
        for place, term in enumerate(three_terms(highest + jnp.log(total))):
            extra = jnp.where(row_index == spare + 1 + place, -term, extra)
        if head == 0:
            continue
        o_ref[rows, :] = jnp.concatenate(outs, axis=0).T.astype(bf16)
        extra_t = extra.T
        for head in range(2):
            spare = (1 - head) * HEAD
            columns = slice(head * PAIR, (head + 1) * PAIR)
            is_extra = (lane_rows > spare) & (lane_rows < spare + 4)
            qa_ref[rows, columns] = jnp.where(
                is_extra, extra_t, qa_ref[rows, columns].astype(f32)
            ).astype(bf16)


def attend_forward(queries, keys, values, bias):
    width = values.shape[1]
    pairs = width // PAIR
    tall = lambda columns: pl.BlockSpec((LEN, columns), lambda pair: (0, pair))
    whole = pl.BlockSpec((LEN, PAIR), lambda pair: (0, 0))
    return pl.pallas_call(
        attend_kernel,
        grid=(pairs,),
        in_specs=[tall(PAIR), tall(PAIR), tall(PAIR), whole],
        out_specs=[tall(PAIR), tall(2 * PAIR)],
        out_shape=[
            jax.ShapeDtypeStruct((LEN, width), bf16),
            jax.ShapeDtypeStruct((LEN, 2 * width), bf16),
        ],
        compiler_params=pltpu.CompilerParams(vmem_limit_bytes=vmem_bytes),
        cost_estimate=pl.CostEstimate(
            flops=2 * 4 * LEN * LEN * width * 4,
            bytes_accessed=6 * LEN * width * 2,
            transcendentals=LEN * LEN * width // HEAD,
        ),
        name="attend",
    )(queries, keys, values, bias)


def attend_back_kernel(
    qa_ref, kr_ref, v_ref, o_ref, mine_ref, other_ref, weight_ref, cos_ref, sin_ref, bias_ref,
    dq_ref, dk_ref, dv_ref, *rest,
):
    doa_ref, dka_ref, dva_ref = rest[-3:]
    if len(rest) > 3:

        @pl.when(pl.program_id(0) == 0)
        def _():
            rest[0][...] = mine_ref[...].T
            rest[1][...] = other_ref[...].T

    lane = lax.broadcasted_iota(jnp.int32, (LEN, PAIR), 1)
    lane_rows = lax.broadcasted_iota(jnp.int32, (ROWS, PAIR), 1)
    cosine, sine = cos_ref[...], sin_ref[...]
    k_wide = kr_ref[...].astype(f32)
    keys_t = kr_ref[...].T
    v_wide = v_ref[...].astype(f32)
    do_wide = jnp.concatenate(
        [dot32(ref[...], weight_ref[0]).astype(bf16).astype(f32) for ref in (mine_ref, other_ref)],
        axis=0,
    )
    bias = bias_ref[...].astype(f32)
    product = do_wide * o_ref[...].astype(f32)
    keys, values = [], []
    for head in range(2):
        own = lane // HEAD == head
        spare = (1 - head) * HEAD
        is_extra = (lane > spare) & (lane < spare + 4)
        ones = jnp.where(is_extra, 1.0, 0.0)
        keys.append(
            jnp.where(own, k_wide, jnp.where(lane == spare, bias, ones)).astype(bf16)
        )
        values.append(jnp.where(own, v_wide, ones).astype(bf16))
        row_dot = jnp.sum(jnp.where(own, product, 0.0), axis=1, keepdims=True)
        grad = jnp.where(own, do_wide, 0.0)
        for place, term in enumerate(three_terms(row_dot)):
            grad = jnp.where(lane == spare + 1 + place, -term, grad)
        doa_ref[:, head * PAIR : (head + 1) * PAIR] = grad.astype(bf16)
    for block in range(LEN // ROWS):
        rows = slice(block * ROWS, (block + 1) * ROWS)
        turned = []
        for head in range(2):
            columns = slice(head * PAIR, (head + 1) * PAIR)
            q_block = qa_ref[rows, columns]
            do_block = doa_ref[rows, columns]
            probs = jnp.exp(dot32(keys[head], q_block, NT))
            prob_grad = dot32(values[head], do_block, NT)
            score_grad = (probs * prob_grad).astype(bf16)
            dv_part = dot32(probs.astype(bf16), do_block)
            dk_part = dot32(score_grad, q_block)
            if block == 0:
                dva_ref[:, columns] = dv_part
                dka_ref[:, columns] = dk_part
            else:
                dva_ref[:, columns] += dv_part
                dka_ref[:, columns] += dk_part
            turned.append(dot32(keys_t[head * HEAD : (head + 1) * HEAD], score_grad))
        dq = jnp.concatenate(turned, axis=0).T * 0.125
        dq_ref[rows, :] = rotate(dq, cosine[rows], -sine[rows], lane_rows).astype(bf16)
    first = lane < HEAD
    dk = jnp.where(first, dka_ref[:, :PAIR], dka_ref[:, PAIR:])
    dk_ref[...] = rotate(dk, cosine, -sine, lane).astype(bf16)
    dv_ref[...] = jnp.where(first, dva_ref[:, :PAIR], dva_ref[:, PAIR:]).astype(bf16)


def attend_backward(side, queries, keys, values, outputs, grad_mine, grad_other, stacked, cosine, sine, bias):
    width = values.shape[1] // 2
    pairs = width // PAIR
    turned = grad_mine.shape[::-1]
    tall = lambda columns: pl.BlockSpec((LEN, columns), lambda pair: (0, pair + side * pairs))
    whole = lambda shape: pl.BlockSpec(shape, lambda pair: (0, 0))
    return pl.pallas_call(
        attend_back_kernel,
        grid=(pairs,),
        in_specs=[tall(2 * PAIR)]
        + [tall(PAIR)] * 3
        + [whole(grad_mine.shape)] * 2
        + [pl.BlockSpec((1, D, PAIR), lambda pair: (3, 0, pair + side * pairs))]
        + [whole((LEN, PAIR))] * 3,
        out_specs=[pl.BlockSpec((LEN, PAIR), lambda pair: (0, pair))] * 3 + [whole(turned)] * (2 - 2 * side),
        out_shape=[jax.ShapeDtypeStruct((LEN, width), bf16)] * 3
        + [jax.ShapeDtypeStruct(turned, bf16)] * (2 - 2 * side),
        scratch_shapes=[
            pltpu.VMEM((LEN, 2 * PAIR), bf16),
            pltpu.VMEM((LEN, 2 * PAIR), f32),
            pltpu.VMEM((LEN, 2 * PAIR), f32),
        ],
        compiler_params=pltpu.CompilerParams(vmem_limit_bytes=attend_back_bytes),
        cost_estimate=beside,
        name="attend_back",
    )(queries, keys, values, outputs, grad_mine, grad_other, stacked, cosine, sine, bias)


PARTS = 2


def part_copies(table_ref, panels, panel, cuts, start_row, copy, arrays=4):
    for index in range(PARTS):
        which = table_ref[2 * index * panels + panel]
        lead = table_ref[(2 * index + 1) * panels + panel]
        start = pl.multiple_of(start_row + cuts[index], 16)
        for number in range(arrays):

            @pl.when(which == number)
            def _():
                copy(number * PARTS + index, lead, start, cuts[index + 1] - cuts[index])


def project_kernel(panel_rows, cuts, slots_ref, *refs):
    parts, refs = refs[: 4 * PARTS], refs[4 * PARTS :]
    mine_ref, other_ref, cos_ref, sin_ref, q_ref, k_ref, v_ref, out_ref = refs
    per_block = D // panel_rows

    def fetch(panel, carry):
        def copy(number, lead, start, rows):
            out_ref[pl.ds(start, rows), :] = parts[number][lead]

        part_copies(slots_ref, 8 * per_block, panel, cuts, panel * panel_rows, copy)
        return carry

    lax.fori_loop(0, 8 * per_block, fetch, 0)
    half = mine_ref.shape[0]
    width = out_ref.shape[1]
    lane = lax.broadcasted_iota(jnp.int32, (half, PAIR), 1)
    for block, ref in enumerate((q_ref, k_ref, v_ref)):
        for part, rows_ref in enumerate((mine_ref, other_ref)):
            rows = slice(part * half, (part + 1) * half)
            product = dot32(rows_ref[...], out_ref[block * D : (block + 1) * D, :])
            if block == 2:
                ref[rows, :] = product.astype(bf16)
                continue
            cosine, sine = cos_ref[rows, :], sin_ref[rows, :]
            for pair in range(width // PAIR):
                columns = slice(pair * PAIR, (pair + 1) * PAIR)
                turned = rotate(product[:, columns], cosine, sine, lane).astype(bf16)
                if block == 0:
                    turned = (turned.astype(f32) * 0.125).astype(bf16)
                ref[rows, columns] = turned


def project(groups, slots, panel_rows, cuts, mine, other, cosine, sine):
    width = groups[0][0].shape[-1]
    parts = [array.reshape((-1,) + array.shape[-2:]) for group in groups for array in group]
    whole = pl.BlockSpec(memory_space=pltpu.VMEM)
    tall = jax.ShapeDtypeStruct((LEN, width), bf16)
    return pl.pallas_call(
        lambda *refs: project_kernel(panel_rows, cuts, *refs),
        in_specs=[pl.BlockSpec(memory_space=pltpu.SMEM)] + [whole] * (4 * PARTS + 4),
        out_specs=[whole] * 4,
        out_shape=[tall] * 3 + [jax.ShapeDtypeStruct((8 * D, width), bf16)],
        compiler_params=pltpu.CompilerParams(vmem_limit_bytes=project_bytes),
        cost_estimate=pl.CostEstimate(
            flops=2 * LEN * 3 * D * width, bytes_accessed=48 * D * width, transcendentals=0
        ),
        name="project",
    )(slots, *parts, mine, other, cosine, sine)


def feed_kernel(n_ref, g_ref, w_ref, f_ref, d_ref, a_ref, u_ref, n_t_ref, g_t_ref):
    width = w_ref.shape[2]
    rows, grads = n_ref[...], g_ref[...]
    n_t_ref[...] = rows.T
    g_t_ref[...] = grads.T
    pre = [dot32(rows, w_ref[i]) for i in range(2)]
    act_grad = [dot32(grads, w_ref[2 + i]) for i in range(2)]
    acts, pre_grads = [], []
    for i in range(2):
        value = pre[i]
        square = value * value
        turn = jnp.tanh(0.7978845608028654 * (value + 0.044715 * (square * value)))
        share = 0.5 * (1.0 + turn)
        slope = share + (0.5 * value) * (1.0 - turn * turn) * (
            0.7978845608028654 + (3 * 0.044715 * 0.7978845608028654) * square
        )
        acts.append((value * share).astype(bf16))
        pre_grads.append((act_grad[i] * slope).astype(bf16))
        a_ref[:, i * width : (i + 1) * width] = acts[i]
        u_ref[:, i * width : (i + 1) * width] = pre_grads[i]
    f_ref[...] = (dot32(acts[0], w_ref[2], NT) + dot32(acts[1], w_ref[3], NT)).astype(f_ref.dtype)
    d_ref[...] = (dot32(pre_grads[0], w_ref[0], NT) + dot32(pre_grads[1], w_ref[1], NT)).astype(d_ref.dtype)


def feed(rows, grads, stacked, kind):
    half, width = rows.shape[0], stacked.shape[2]
    whole = pl.BlockSpec((half, D), lambda step: (0, 0))
    low, sums = jax.ShapeDtypeStruct((half, D), bf16), jax.ShapeDtypeStruct((half, D), kind)
    return pl.pallas_call(
        feed_kernel,
        grid=(1,),
        in_specs=[whole, whole, pl.BlockSpec((4, D, width), lambda step: (1, 0, 0))],
        out_specs=[whole] * 4 + [pl.BlockSpec((D, half), lambda step: (0, 0))] * 2,
        out_shape=[sums, sums, low, low] + [jax.ShapeDtypeStruct((D, half), bf16)] * 2,
        compiler_params=pltpu.CompilerParams(vmem_limit_bytes=feed_bytes),
        cost_estimate=pl.CostEstimate(
            flops=2 * 4 * half * D * D, bytes_accessed=16 * D * width, transcendentals=half * D
        ),
        name="feed",
    )(rows, grads, stacked)


def inputs_grad_kernel(*refs):
    grads, w_ref, mine_ref, other_ref = refs[:6], refs[6], refs[7], refs[8]
    half = mine_ref.shape[0]
    narrow = grads[0].shape[1]
    for start, out_ref in ((half, other_ref), (0, mine_ref)):
        rows = slice(start, start + half)
        total = None
        for which in range(3):
            for side in range(2):
                weight = w_ref[which, :, side * narrow : (side + 1) * narrow]
                part = dot32(grads[side * 3 + which][rows, :], weight, NT)
                total = part if total is None else total + part
        out_ref[...] = total.astype(out_ref.dtype)


def inputs_grad(grads, stacked):
    width = stacked.shape[2]
    half = LEN // 2
    out = pl.BlockSpec((half, D), lambda step: (0, 0))
    return pl.pallas_call(
        inputs_grad_kernel,
        grid=(1,),
        in_specs=[pl.BlockSpec((LEN, width // 2), lambda step: (0, 0))] * 6
        + [pl.BlockSpec((3, D, width), lambda step: (0, 0, 0))],
        out_specs=[out, out],
        out_shape=[jax.ShapeDtypeStruct((half, D), f32), jax.ShapeDtypeStruct((half, D), bf16)],
        compiler_params=pltpu.CompilerParams(vmem_limit_bytes=vmem_bytes),
        cost_estimate=beside,
        name="inputs_grad",
    )(*grads, stacked)


def gradients_kernel(panel_rows, cuts, lefts, rights, uses, slots_ref, *refs):
    in_count = 1 + max(max(max(pair) for pair in lefts), max(max(pair) for group in rights for _, pair in group))
    inputs, refs = refs[:in_count], refs[in_count:]
    parts, (block_ref,) = refs[: 2 * PARTS], refs[2 * PARTS :]
    tall, side = block_ref.shape[1:]
    half = LEN // 2
    pieces = tall // panel_rows

    def rows_of(pair, part, columns):
        if pair[0] == pair[1]:
            return inputs[pair[0]][part * half : (part + 1) * half, columns]
        return inputs[pair[part]][:, columns]

    for left, right, blocks in uses:
        for left_start in range(0, D, tall):
            product = None
            for part in range(2):
                columns = [rows_of(pair, part, slice(start, start + side)) for start, pair in rights[right]]
                wide = columns[0] if len(columns) == 1 else jnp.concatenate(columns, axis=1)
                term = dot32(inputs[lefts[left][part]][left_start : left_start + tall, :], wide)
                product = term if product is None else product + term
            places = [(block * D + left_start) // tall for block in blocks]
            for number, place in enumerate(places):
                block_ref[place] = product[:, number * side : (number + 1) * side].astype(bf16)

            def send(piece, carry, places=places):
                for place in places:

                    def copy(array, lead, start, rows):
                        parts[array][lead] = block_ref[place, pl.ds(start, rows), :]

                    part_copies(
                        slots_ref, 8 * D // panel_rows, place * pieces + piece, cuts, piece * panel_rows, copy, 2
                    )
                return carry

            lax.fori_loop(0, pieces, send, 0)


def panel_gradients(arrays, lefts, rights, uses, slots, panel_rows, cuts, high_count, width):
    tall = LEN // 2
    outs = [
        jax.ShapeDtypeStruct((8 * high_count, cuts[index + 1] - cuts[index], width), bf16)
        for _ in range(2)
        for index in range(PARTS)
    ]
    outs = pl.pallas_call(
        lambda *refs: gradients_kernel(panel_rows, cuts, lefts, rights, uses, *refs),
        in_specs=[pl.BlockSpec(memory_space=pltpu.SMEM)]
        + [pl.BlockSpec(memory_space=pltpu.VMEM)] * len(arrays),
        out_specs=[pl.BlockSpec(memory_space=pltpu.VMEM)] * (2 * PARTS),
        out_shape=outs,
        scratch_shapes=[pltpu.VMEM((8 * D // tall, tall, width), bf16)],
        compiler_params=pltpu.CompilerParams(vmem_limit_bytes=gradient_bytes),
        cost_estimate=beside,
        name="gradients",
    )(slots, *arrays)
    shaped = [out.reshape((2, 2, 2 * high_count) + out.shape[1:]) for out in outs]
    return shaped[:PARTS], shaped[PARTS:]


def gelu_parts(values):
    share = 0.5 * (1.0 + lax.erf(values * 0.7071067811865476))
    density = 0.3989422804014327 * jnp.exp(-0.5 * values * values)
    return share, density


def in_vmem(kernel, name, inputs, outs, scratch=(), specs=None, out_specs=None, limit=vmem_bytes):
    whole = pl.BlockSpec(memory_space=pltpu.VMEM)
    return pl.pallas_call(
        kernel,
        in_specs=specs or [whole] * len(inputs),
        out_specs=out_specs or [whole] * len(outs),
        out_shape=[jax.ShapeDtypeStruct(shape, kind) for shape, kind in outs],
        scratch_shapes=list(scratch),
        compiler_params=pltpu.CompilerParams(vmem_limit_bytes=limit),
        cost_estimate=beside,
        name=name,
    )(*inputs)


def text_forward_kernel(
    core_ref, table_ref, mine_ref, other_ref, normed_ref, masked_ref, keep_ref, mel_mine_ref, mel_other_ref,
    in_bias_ref, gamma_ref, beta_ref, bias_ref, shift_ref, scale_ref,
    pre_ref, energy_ref, grn_ref, text_ref, stream_ref, first_ref, other_first_ref, first_t_ref, other_first_t_ref, texts_ref,
    hidden_held,
):
    rows = mine_ref.shape[1]
    half = stream_ref.shape[0]

    held = texts_ref

    def fetch(block, carry):
        place = pl.ds(pl.multiple_of(block * rows, 16), rows)
        for part, ref in enumerate((mine_ref, other_ref)):

            @pl.when((block + core_ref[0]) % 2 == part)
            def _():
                texts_ref[place, :] = ref[table_ref[block]]

        return carry

    lax.fori_loop(0, table_ref.shape[0], fetch, 0)
    energy_sum = jnp.zeros((1, TXT_FF), f32)
    for part in range(2):
        frames = slice(part * half, (part + 1) * half)
        pre = dot32(normed_ref[frames, :], held[:TEXT]) + in_bias_ref[...]
        if part == 0:
            pre_ref[...] = pre
        hidden = pre * gelu_parts(pre)[0]
        hidden_held[frames, :] = hidden
        energy_sum = energy_sum + jnp.sum(hidden * hidden, axis=0, keepdims=True)
    energy_ref[...] = energy_sum
    energy = jnp.sqrt(energy_sum)
    ratio = energy / (jnp.mean(energy, axis=-1, keepdims=True) + norm_eps)
    weight = gamma_ref[...] * ratio + 1.0
    for part, mel_ref in enumerate((mel_mine_ref, mel_other_ref)):
        frames = slice(part * half, (part + 1) * half)
        grn_low = (weight * hidden_held[frames, :] + beta_ref[...]).astype(bf16)
        text_out = masked_ref[frames, :] + dot32(grn_low, held[TEXT : 2 * TEXT], NT) + bias_ref[...]
        text_low = (text_out * keep_ref[frames, :]).astype(bf16)
        stream = mel_ref[...].astype(f32) + dot32(text_low, held[2 * TEXT :])
        normed, _ = normalise(stream)
        first = (normed * (1.0 + scale_ref[...]) + shift_ref[...]).astype(bf16)
        if part == 0:
            grn_ref[...] = grn_low
            text_ref[...] = text_low
            stream_ref[...] = stream
            first_ref[...] = first
            first_t_ref[...] = first.T
        else:
            other_first_ref[...] = first
            other_first_t_ref[...] = first.T


def text_forward(core, table, *inputs):
    whole = pl.BlockSpec(memory_space=pltpu.VMEM)
    scalars = pl.BlockSpec(memory_space=pltpu.SMEM)
    half = LEN // 2
    return in_vmem(
        text_forward_kernel,
        "text_forward",
        (core.reshape(1).astype(jnp.int32), table) + inputs,
        [
            ((half, TXT_FF), f32),
            ((1, TXT_FF), f32),
            ((half, TXT_FF), bf16),
            ((half, TEXT), bf16),
            ((half, D), f32),
            ((half, D), bf16),
            ((half, D), bf16),
            ((D, half), bf16),
            ((D, half), bf16),
            ((3 * TEXT, D), bf16),
        ],
        [pltpu.VMEM((LEN, TXT_FF), f32)],
        [scalars, scalars] + [whole] * len(inputs),
        [whole] * 10,
        text_forward_bytes,
    )


def stream_back_kernel(
    core_ref, my_ref, their_ref, stream_ref, later_ref, scale_ref, texts_ref, keep_ref, pre_ref,
    mel_ref, low_ref, shrink_ref, shrink_low_ref, grn_grad_ref, sums_ref, bias_sum_ref, full_ref,
):
    half = mel_ref.shape[0]
    grad = my_ref[...] + their_ref[...].astype(f32)
    normed, scale = normalise(stream_ref[...])
    sums_ref[0:1] = jnp.sum(grad, axis=0, keepdims=True)
    sums_ref[1:2] = jnp.sum(grad * normed, axis=0, keepdims=True)
    mel_grad = later_ref[...] + normalise_back(grad * (1.0 + scale_ref[...]), normed, scale)
    mel_ref[...] = mel_grad
    place = pl.ds(pl.multiple_of(core_ref[0] * half, half), half)
    full_ref[place, :] = mel_ref[...]
    low = mel_grad.astype(bf16)
    low_ref[...] = low
    shrink_grad = dot32(low, texts_ref[2 * TEXT :], NT) * keep_ref[...]
    shrink_ref[...] = shrink_grad
    bias_sum_ref[...] = jnp.sum(shrink_grad, axis=0, keepdims=True)
    shrink_low = shrink_grad.astype(bf16)
    shrink_low_ref[...] = shrink_low
    grn_grad = dot32(shrink_low, texts_ref[TEXT : 2 * TEXT])
    grn_grad_ref[...] = grn_grad
    pre = pre_ref[...]
    sums_ref[2:3] = jnp.sum(grn_grad * (pre * gelu_parts(pre)[0]), axis=0, keepdims=True)
    sums_ref[3:4] = jnp.sum(grn_grad, axis=0, keepdims=True)
    sums_ref[4:8] = jnp.zeros((4, D), f32)


def stream_back(core, *inputs):
    half = inputs[0].shape[0]
    whole = pl.BlockSpec(memory_space=pltpu.VMEM)
    return in_vmem(
        stream_back_kernel,
        "stream_back",
        (core.reshape(1).astype(jnp.int32),) + inputs,
        [
            ((half, D), f32),
            ((half, D), bf16),
            ((half, TEXT), f32),
            ((half, TEXT), bf16),
            ((half, TXT_FF), f32),
            ((8, D), f32),
            ((1, TEXT), f32),
            ((2 * half, D), f32),
        ],
        [],
        [pl.BlockSpec(memory_space=pltpu.SMEM)] + [whole] * len(inputs),
        [whole] * 8,
    )


def text_back_kernel(
    pre_ref, grn_grad_ref, energy_ref, dot_ref, gamma_ref, texts_ref, normed_ref, conv_normed_ref, conv_scale_ref, gain_ref,
    shrink_low_ref, grn_ref, text_ref, low_ref, core_ref, table_ref,
    mixed_ref, sums_ref, wide_sums_ref, *rest,
):
    grads_ref = rest[2] if len(rest) > 1 else rest[0]
    pre = pre_ref[...]
    share, density = gelu_parts(pre)
    energy = jnp.sqrt(energy_ref[...])
    energy_mean = jnp.mean(energy, axis=-1, keepdims=True) + norm_eps
    ratio = energy / energy_mean
    ratio_grad = gamma_ref[...] * dot_ref[...]
    energy_grad = (ratio_grad - jnp.mean(ratio_grad * ratio, axis=-1, keepdims=True)) / energy_mean
    hidden_grad = grn_grad_ref[...] * (gamma_ref[...] * ratio + 1.0) + (pre * share) * (energy_grad / energy)
    expand_grad = hidden_grad * (share + pre * density)
    wide_sums_ref[0:1] = jnp.sum(expand_grad, axis=0, keepdims=True)
    wide_sums_ref[1:2] = ratio
    expand_low = expand_grad.astype(bf16)
    grads_ref[:TEXT] = dot32(normed_ref[...], expand_low, TN).astype(bf16)
    grads_ref[TEXT : 2 * TEXT] = dot32(shrink_low_ref[...], grn_ref[...], TN).astype(bf16)
    grads_ref[2 * TEXT :] = dot32(text_ref[...], low_ref[...], TN).astype(bf16)
    normed_grad = dot32(expand_low, texts_ref[:TEXT], NT)
    conv_normed = conv_normed_ref[...]
    sums_ref[0:1] = jnp.sum(normed_grad * conv_normed, axis=0, keepdims=True)
    sums_ref[1:2] = jnp.sum(normed_grad, axis=0, keepdims=True)
    mixed_grad = normalise_back(normed_grad * gain_ref[...], conv_normed, conv_scale_ref[...])
    sums_ref[2:3] = jnp.sum(mixed_grad, axis=0, keepdims=True)
    mixed_ref[...] = mixed_grad
    if len(rest) == 1:
        return
    keep_ref, send_ref, _ = rest
    rows = keep_ref.shape[1]

    def place(block, carry):
        piece = pl.ds(pl.multiple_of(block * rows, 16), rows)
        for part, ref in enumerate((keep_ref, send_ref)):

            @pl.when((block + core_ref[0]) % 2 == part)
            def _():
                ref[table_ref[block]] = grads_ref[piece, :]

        return carry

    lax.fori_loop(0, table_ref.shape[0], place, 0)


def text_back(core, table, rows, *inputs):
    half = inputs[0].shape[0]
    whole = pl.BlockSpec(memory_space=pltpu.VMEM)
    scalars = pl.BlockSpec(memory_space=pltpu.SMEM)
    outs = [((half, TEXT), f32), ((3, TEXT), f32), ((2, TXT_FF), f32)]
    apart = rows % 16 == 0
    blocks = ((3 * TEXT // (2 * rows), rows, D), bf16)
    return in_vmem(
        text_back_kernel,
        "text_back",
        inputs + (core.reshape(1).astype(jnp.int32), table),
        outs + ([blocks] * 2 if apart else [((3 * TEXT, D), bf16)]),
        [pltpu.VMEM((3 * TEXT, D), bf16)] if apart else [],
        [whole] * len(inputs) + [scalars] * 2,
        [whole] * (5 if apart else 4),
        text_back_bytes,
    )


def conv_back_kernel(
    core_ref, mixed_ref, border_ref, window_ref, kernel_ref, shrink_ref, keep_ref,
    mine_ref, kernel_grad_ref, full_ref, wide,
):
    half = mixed_ref.shape[0]
    edge, margin = border_ref.shape[0], KERNEL // 2
    mixed = mixed_ref[...]
    border = border_ref[...]
    wide[:edge] = jnp.where(core_ref[0] == 1, border, 0.0)
    wide[edge : edge + half] = mixed
    wide[edge + half :] = jnp.where(core_ref[0] == 0, border, 0.0)
    total = shrink_ref[...]
    for j in range(KERNEL):
        start = edge + margin - j
        total = total + wide[start : start + half] * kernel_ref[j : j + 1]
        tap = window_ref[edge - margin + j : edge - margin + j + half]
        kernel_grad_ref[j : j + 1] = jnp.sum(mixed * tap, axis=0, keepdims=True)
    mine_ref[...] = total * keep_ref[...]
    place = pl.ds(pl.multiple_of(core_ref[0] * half, half), half)
    full_ref[place, :] = mine_ref[...]


def conv_back(core, *inputs):
    half = inputs[0].shape[0]
    whole = pl.BlockSpec(memory_space=pltpu.VMEM)
    return in_vmem(
        conv_back_kernel,
        "conv_back",
        (core.reshape(1).astype(jnp.int32),) + inputs,
        [((half, TEXT), f32), ((KERNEL, TEXT), f32), ((2 * half, TEXT), f32)],
        [pltpu.VMEM((half + 2 * inputs[1].shape[0], TEXT), f32)],
        [pl.BlockSpec(memory_space=pltpu.SMEM)] + [whole] * len(inputs),
        [whole] * 3,
    )


def settle_kernel(
    core_ref, my_out_ref, their_out_ref, my_grad_ref, their_grad_ref, stream_ref, attention_ref, cot_ref,
    gate_one_ref, scale_ref, gate_two_ref,
    output_ref, later_ref, attention_grad_ref, sums_ref, full_ref,
):
    half = output_ref.shape[0]
    unit_out = my_out_ref[...] + their_out_ref[...].astype(f32)
    stream = stream_ref[...]
    output_ref[...] = (stream + gate_two_ref[...] * unit_out).astype(bf16)
    place = pl.ds(pl.multiple_of(core_ref[0] * half, half), half)
    full_ref[place, :] = output_ref[...]
    out_grad = cot_ref[...].astype(f32)
    sums_ref[0:1] = jnp.sum(out_grad * unit_out, axis=0, keepdims=True)
    grad = my_grad_ref[...] + their_grad_ref[...].astype(f32)
    normed, scale = normalise(stream)
    sums_ref[1:2] = jnp.sum(grad, axis=0, keepdims=True)
    sums_ref[2:3] = jnp.sum(grad * normed, axis=0, keepdims=True)
    later = out_grad + normalise_back(grad * (1.0 + scale_ref[...]), normed, scale)
    later_ref[...] = later
    sums_ref[3:4] = jnp.sum(later * attention_ref[...], axis=0, keepdims=True)
    attention_grad_ref[...] = (gate_one_ref[...] * later).astype(bf16)


def settle(core, *inputs):
    half = inputs[0].shape[0]
    whole = pl.BlockSpec(memory_space=pltpu.VMEM)
    return in_vmem(
        settle_kernel,
        "settle",
        (core.reshape(1).astype(jnp.int32),) + inputs,
        [((half, D), bf16), ((half, D), f32), ((half, D), bf16), ((4, D), f32), ((2 * half, D), bf16)],
        [],
        [pl.BlockSpec(memory_space=pltpu.SMEM)] + [whole] * len(inputs),
        [whole] * 5,
    )


def dot_split(left, right, dims=NN):
    split = lambda array: (array.astype(bf16), (array - array.astype(bf16).astype(f32)).astype(bf16))
    left_high, left_low = split(left)
    right_high, right_low = split(right)
    return (
        dot32(left_high, right_high, dims)
        + dot32(left_high, right_low, dims)
        + dot32(left_low, right_high, dims)
    )


def rotated_kernel(places, utterances, *refs):
    pieces, refs = refs[: sum(count for _, _, count in places)], refs[sum(count for _, _, count in places) :]
    left_ref, right_ref, master_ref, first_ref, second_ref, weights_ref, moment_ref, variance_ref, grad_ref = refs
    which = 0
    for row, column, count in places:
        total = pieces[which][...].astype(f32)
        for ref in pieces[which + 1 : which + count]:
            total = total + ref[...].astype(f32)
        rows, columns = total.shape
        grad_ref[row : row + rows, column : column + columns] = total / utterances
        which += count
    left, right = left_ref[...], right_ref[...]
    rotated = dot_split(dot_split(left, grad_ref[...], TN), right)
    moment, variance, direction = moments(rotated, first_ref[...], second_ref[...])
    moment_ref[...] = moment
    variance_ref[...] = variance
    turned = dot_split(dot_split(left, direction), right, NT)
    master = master_ref[...]
    weights_ref[...] = apply_step(master, turned, learn_rate)


def rotated_step(pieces, utterances, left, right, master, first, second):
    places = [(row, column, len(arrays)) for row, column, arrays in pieces]
    arrays = [array for _, _, group in pieces for array in group]
    return in_vmem(
        lambda *refs: rotated_kernel(places, utterances, *refs),
        "rotated_step",
        tuple(arrays) + (left, right, master, first, second),
        [(master.shape, f32)] * 3,
        [pltpu.VMEM(master.shape, f32)],
    )


def modulation_kernel(
    utterances, core_ref, time_ref, mine_ref, other_ref, old_ref, first_ref, second_ref,
    weights_ref, moment_ref, variance_ref, sums_ref,
):
    mine = pl.program_id(0) // 3 == core_ref[0]
    table = jnp.where(mine, mine_ref[...], other_ref[...])
    sums_ref[...] = jnp.sum(table, axis=0, keepdims=True)
    grad = dot32(time_ref[...], table.astype(bf16), TN) / utterances
    moment, variance, direction = moments(grad, first_ref[...], second_ref[...])
    moment_ref[...] = moment
    variance_ref[...] = variance
    weights_ref[...] = apply_step(old_ref[...], direction, learn_rate)


def modulation_step(utterances, core, time_rows, mine, other, old, first, second):
    rows, columns = old.shape
    step = columns // 6
    tall = pl.BlockSpec((rows, step), lambda i: (0, i))
    part = pl.BlockSpec((GROUPS, step), lambda i: (0, i % 3))
    return pl.pallas_call(
        lambda *refs: modulation_kernel(utterances, *refs),
        grid=(6,),
        in_specs=[
            pl.BlockSpec(memory_space=pltpu.SMEM),
            pl.BlockSpec((GROUPS, rows), lambda i: (0, 0)),
            part,
            part,
        ]
        + [tall] * 3,
        out_specs=[tall] * 3 + [pl.BlockSpec((1, step), lambda i: (0, i))],
        out_shape=[jax.ShapeDtypeStruct(old.shape, f32)] * 3 + [jax.ShapeDtypeStruct((1, columns), f32)],
        compiler_params=pltpu.CompilerParams(vmem_limit_bytes=vmem_bytes),
        cost_estimate=beside,
        name="modulation_step",
    )(core.reshape(1).astype(jnp.int32), time_rows, mine, other, old, first, second)


def vector_parts(vectors):
    kernel_size = KERNEL * TEXT
    pieces = [vectors[:kernel_size].reshape(KERNEL, TEXT)]
    offset = kernel_size
    for extent in (TEXT, TEXT, TEXT, TEXT, TXT_FF, TXT_FF, TXT_FF, 6 * D):
        pieces.append(vectors[offset : offset + extent])
        offset = offset + extent
    return pieces


def normalise(values):
    center = values - jnp.mean(values, axis=-1, keepdims=True)
    variance = jnp.mean(center * center, axis=-1, keepdims=True)
    scale = lax.rsqrt(variance + norm_eps)
    return center * scale, scale


def normalise_back(grad, normed, scale):
    mean_grad = jnp.mean(grad, axis=-1, keepdims=True)
    mean_dot = jnp.mean(grad * normed, axis=-1, keepdims=True)
    return scale * (grad - mean_grad - normed * mean_dot)


def moments(gradient, first_moment, second_moment):
    first_new = beta_one * first_moment + (1.0 - beta_one) * gradient
    second_new = beta_two * second_moment + (1.0 - beta_two) * gradient * gradient
    bias_first = 1.0 - beta_one**STEP
    bias_second = 1.0 - beta_two**STEP
    direction = first_new / bias_first / (jnp.sqrt(second_new / bias_second) + adam_eps)
    return (first_new, second_new, direction)


def apply_step(weight, direction, rate):
    return weight - rate * (direction + weight_decay * weight)


def rotary_tables(first):
    position = np.arange(LEN)
    frequency = 10000.0 ** (-np.arange(HEAD // 2) * 2.0 / HEAD)
    angle = position[:, None] * frequency[None, :]
    cosine, sine = np.cos(angle), np.sin(angle)
    tables = np.concatenate([cosine] * 4 + [-sine, sine, -sine, sine], axis=1).astype(np.float32)
    tables = lax.dynamic_slice_in_dim(jnp.asarray(np.concatenate([tables, tables])), first, LEN, 0)
    return tables[:, :PAIR], tables[:, PAIR:]


def take_blocks(blocks, index):
    return jnp.take(blocks, index, axis=0, mode="clip")


def both_halves(mine):
    return jnp.concatenate([mine, swap_core(mine)], axis=0)


def sum_halves(multiply, rows, half):
    theirs = multiply(rows[half:]).astype(bf16)
    received = swap_core(theirs)
    return multiply(rows[:half]) + received.astype(f32)


def body(
    mel_frames,
    text_features,
    cotangent,
    time_embedding,
    lengths,
    group_ids,
    text_keep,
    owner_list,
    soap_master,
    soap_first,
    soap_second,
    left_basis,
    right_basis,
    text_matrices,
    text_first,
    text_second,
    modulation_weight,
    modulation_first,
    modulation_second,
    vectors,
    vector_first,
    vector_second,
):
    count = lax.axis_size("dp")
    me, core = lax.axis_index("dp"), lax.axis_index("mp")
    half = LEN // 2
    utterances = lengths.shape[0] * count
    panel_rows, width = soap_master.shape
    share_rows = modulation_weight.shape[0]
    text_rows = text_matrices.shape[0]
    text_half = text_rows // 2
    relative = jnp.arange(count) ^ me

    high_count = count // 16
    cuts = row_cuts(panel_rows)
    panel_table = panel_places(core, owner_list ^ me, high_count)
    gather_table = panel_places(core, owner_list ^ me, high_count, True)
    silu_time = jax.nn.silu(time_embedding.astype(f32)).astype(bf16)
    time_rows = lax.dynamic_slice_in_dim(silu_time, me * share_rows, share_rows, 1)
    weight_half = lax.dynamic_slice_in_dim(modulation_weight, core * 3 * D, 3 * D, 1).astype(bf16)
    own_rows = lax.dynamic_slice_in_dim(text_matrices, core * text_half, text_half, 0)
    text_held = spread_high(own_rows.astype(bf16))
    partial = dot32(time_rows, weight_half)
    held = spread_high(soap_master.astype(bf16))
    text_received, partial_received = tie(swap_bit(text_held, 3), swap_bit(partial, 3))
    text_held = jnp.concatenate([text_held, text_received], axis=0)
    partial = partial + partial_received
    text_received, partial_received, held = tie(
        swap_bits(text_held, phase_bits(text_orders, 0)), swap_bits(partial, phase_bits(text_orders, 0)), held
    )
    held = split_rows(held, cuts)
    text_held = jnp.stack([text_held, text_received])
    partial = partial + partial_received
    received, (text_received, partial_received, far_last) = tie_lists(
        receive(held, 0),
        (
            swap_bits(text_held, phase_bits(text_orders, 1)),
            swap_bits(partial, phase_bits(text_orders, 1)),
            swap_bit(held[1], 3),
        ),
    )
    near = [jnp.stack(pair) for pair in zip(held, received)]
    text_held = jnp.stack([text_held, text_received])
    partial = partial + partial_received
    received, (text_received, partial_received, far_first) = tie_lists(
        receive(near, 1),
        (
            swap_bits(text_held, phase_bits(text_orders, 2)),
            swap_bits(partial, phase_bits(text_orders, 2)),
            swap_bit(held[0], 3),
        ),
    )
    partial = partial + partial_received
    near = [jnp.stack(pair) for pair in zip(near, received)]
    near_received = receive(near, 2)
    far = spread_step([far_first, far_last], 0)
    received = receive(far, 1)
    text_mine = jnp.stack([text_held, text_received]).reshape(count, text_half, D)
    text_other = swap_core(text_mine)
    text_features, mel_frames, cotangent, far = tie(text_features, mel_frames, cotangent, far)
    for bit in range(4, bit_count(count)):
        partial = partial + swap_bit(partial, bit)
    modulation_half = partial
    mine_places, other_places = text_places(core, relative, high_count), text_places(1 - core, relative, high_count)
    text_table = jnp.where(
        core == 0, jnp.stack([mine_places, other_places], 1), jnp.stack([other_places, mine_places], 1)
    ).reshape(-1)
    if text_half % 16:
        source = jnp.arange(2 * count) % 2 != core
        texts = take_blocks(jnp.concatenate([text_mine, text_other]), text_table + count * source)
        text_mine = text_other = texts.reshape(1, 3 * TEXT, D)
        text_table = jnp.zeros((1,), jnp.int32)

    modulation = by_core(core, modulation_half, swap_core(modulation_half), axis=1)
    (
        kernel,
        conv_bias,
        norm_gain,
        norm_bias,
        out_bias,
        in_bias,
        grn_gamma,
        grn_beta,
        modulation_bias,
    ) = vector_parts(vectors)
    group = group_ids[0]
    modulation_row = lax.dynamic_slice_in_dim(modulation, group, 1, 0) + modulation_bias


    first = core * half
    margin = KERNEL // 2
    edge = 8
    keep_all = jnp.pad(text_keep.astype(f32), (edge, edge))[:, None]
    text_all = jnp.pad(text_features, ((edge, edge), (0, 0)))

    def text_start(start):
        window = lax.dynamic_slice_in_dim(text_all, start, half + 2 * edge, 0).astype(f32)
        window = window * lax.dynamic_slice_in_dim(keep_all, start, half + 2 * edge, 0)
        keep = lax.dynamic_slice_in_dim(keep_all, start + edge, half, 0)
        taps = [window[edge - margin + j : edge - margin + j + half] for j in range(KERNEL)]
        mixed = conv_bias[None, :]
        for j in range(KERNEL):
            mixed = mixed + taps[j] * kernel[j][None, :]
        normed, scale = normalise(mixed)
        return window, keep, normed, scale, (normed * norm_gain + norm_bias).astype(bf16)

    window, keep, conv_normed, conv_scale, normed_low = text_start(first)
    window_other, keep_other, _, _, normed_other = text_start(half - first)
    masked_both = jnp.concatenate([window[edge : edge + half], window_other[edge : edge + half]], axis=0)
    keep_both = jnp.concatenate([keep, keep_other], axis=0)
    normed_both = jnp.concatenate([normed_low, normed_other], axis=0)
    mel_mine = lax.dynamic_slice_in_dim(mel_frames, first, half, 0)
    mel_other = lax.dynamic_slice_in_dim(mel_frames, half - first, half, 0)
    cosine, sine = rotary_tables(first)
    received, near_received, (text_other, modulation_row, normed_both, masked_both, cosine, sine) = tie_lists(
        received, near_received, (text_other, modulation_row, normed_both, masked_both, cosine, sine)
    )
    far = [jnp.stack(pair) for pair in zip(far, received)]
    far_received = receive(far, 2)
    shift_one, scale_one, gate_one, shift_two, scale_two, gate_two = (
        modulation_row[:, i * D : (i + 1) * D] for i in range(6)
    )
    expand_pre, energy_sum, grn_low, text_low, stream, first_mine, first_other, first_t, first_other_t, texts = text_forward(
        core,
        text_table,
        text_mine,
        text_other,
        normed_both,
        masked_both,
        keep_both,
        mel_mine,
        mel_other,
        in_bias[None],
        grn_gamma[None],
        grn_beta[None],
        out_bias[None],
        shift_one,
        scale_one,
    )

    cot_mine = lax.dynamic_slice_in_dim(cotangent, first, half, 0)
    cot_other = lax.dynamic_slice_in_dim(cotangent, half - first, half, 0)
    hidden_mine = (gate_two * cot_mine.astype(f32)).astype(bf16)
    hidden_other = (gate_two * cot_other.astype(f32)).astype(bf16)
    first_mine, hidden_mine, hidden_other = tie(first_mine, hidden_mine, hidden_other)
    position = (jnp.arange(LEN) + first) % LEN
    bias = jnp.where(position < lengths[0], 0.0, -1e30).astype(bf16)
    bias = jnp.broadcast_to(bias[:, None], (LEN, PAIR))
    queries, keys, value_rows, stacked = project(
        (near, near_received, far, far_received), gather_table, panel_rows, cuts, first_mine, first_other, cosine, sine
    )
    stacked = stacked.reshape(8, D, width)
    attended, query_aug = attend_forward(queries, keys, value_rows, bias)
    attention_out = sum_halves(lambda rows: dot32(rows, stacked[3], NT), attended, half)
    stream_one = stream + gate_one * attention_out

    normed_two, _ = normalise(stream_one)
    second_mine = (normed_two * (1.0 + scale_two) + shift_two).astype(bf16)
    second_other = swap_core(second_mine)
    their_out, their_grad, act_other, pre_other, second_other_t, hidden_other_t = feed(second_other, hidden_other, stacked, bf16)
    their_out, their_grad = swap_core(their_out), swap_core(their_grad)
    my_out, my_grad, act_mine, pre_mine, second_t, hidden_t = feed(second_mine, hidden_mine, stacked, f32)
    output_mine, stream_one_grad, attention_mine, settle_sums, block_output = settle(
        core,
        my_out,
        their_out,
        my_grad,
        their_grad,
        stream_one,
        attention_out,
        cot_mine,
        gate_one,
        scale_two,
        gate_two,
    )
    gate_two_grad, shift_two_grad, scale_two_grad, gate_one_grad = (settle_sums[i] for i in range(4))
    output_theirs = swap_core(output_mine)

    attention_other = swap_core(attention_mine)
    narrow = width // 2

    def back(side, queries):
        return attend_backward(
            side, queries, keys, value_rows, attended, attention_mine, attention_other, stacked, cosine, sine, bias
        )

    def weight_gradients(side, head_grads):
        column = side * narrow
        return panel_gradients(
            [
                first_t, first_other_t, attention_t, attention_other_t, second_t, second_other_t,
                hidden_t, hidden_other_t, *head_grads, attended, pre_mine, pre_other, act_mine, act_other,
            ],
            [(0, 1), (2, 3), (4, 5), (6, 7)],
            [
                [(0, (8, 8)), (0, (9, 9))],
                [(0, (10, 10))],
                [(column, (11, 11))],
                [(column, (12, 13)), (width + column, (12, 13))],
                [(column, (14, 15)), (width + column, (14, 15))],
            ],
            ((0, 0, (0, 1)), (0, 1, (2,)), (1, 2, (3,)), (2, 3, (4, 5)), (3, 4, (6, 7))),
            panel_table,
            panel_rows,
            cuts,
            high_count,
            narrow,
        )

    *head_grads, attention_t, attention_other_t = back(0, query_aug)
    keep_a, send_a = weight_gradients(0, head_grads)
    send_a, (query_aug,) = tie_lists(send_a, (query_aug,))
    received_a = receive(send_a, 2)
    head_grads += list(back(1, query_aug))
    received_a, head_grads = tie_lists(received_a, head_grads)
    part_a = add_all(keep_a, received_a)
    received_a = receive(seconds(part_a), 1)
    keep_b, send_b = weight_gradients(1, head_grads[3:])
    received_a, send_b, head_grads = tie_lists(received_a, send_b, head_grads)
    part_a = add_all(firsts(part_a), received_a)
    received_a = receive(seconds(part_a), 0)
    my_grad, their_grad = inputs_grad(head_grads, stacked)
    received_a, send_b, (my_grad, their_grad) = tie_lists(received_a, send_b, (my_grad, their_grad))

    part_a = add_all(firsts(part_a), received_a)
    received_b = receive(send_b, 2)
    their_grad = swap_core(their_grad)
    mel_grad_mine, stream_low, shrink_grad, shrink_low, grn_grad, sums, out_bias_grad, mel_gradient = stream_back(
        core, my_grad, their_grad, stream, stream_one_grad, scale_one, texts, keep, expand_pre
    )
    received_b, part_a, (sums, mel_grad_mine) = tie_lists(received_b, part_a, (sums, mel_grad_mine))
    shift_one_grad, scale_one_grad, hidden_dot, beta_grad = sums[0], sums[1], sums[2:3], sums[3]
    out_bias_grad = out_bias_grad[0]
    far_a = [swap_bit(part[high_count:], 3) for part in part_a]
    part_b = add_all(keep_b, received_b)
    received_b = receive(seconds(part_b), 1)
    hidden_dot_all = hidden_dot + swap_core(hidden_dot)
    mixed_grad, text_sums, wide_sums, *text_grads = text_back(
        core,
        text_table,
        text_half,
        expand_pre,
        grn_grad,
        energy_sum,
        hidden_dot_all,
        grn_gamma[None],
        texts,
        normed_low,
        conv_normed,
        conv_scale,
        norm_gain[None],
        shrink_low,
        grn_low,
        text_low,
        stream_low,
    )
    mel_grad_theirs = swap_core(mel_grad_mine)
    gain_grad, norm_bias_grad, conv_bias_grad = text_sums[0], text_sums[1], text_sums[2]
    in_bias_grad, gamma_grad = wide_sums[0], wide_sums[1] * hidden_dot[0]
    if len(text_grads) == 1:
        blocks = text_grads[0].reshape(count, 2, text_half, D)
        order = lambda which: text_slots(which, jnp.arange(count), high_count) ^ me
        text_grads = [
            take_blocks(lax.dynamic_index_in_dim(blocks, which, 1, keepdims=False), order(which))
            for which in (core, 1 - core)
        ]
    received_b, far_a, (mixed_grad, text_keep_half, text_send_half, mel_grad_theirs) = tie_lists(
        received_b, far_a, (mixed_grad, *text_grads, mel_grad_theirs)
    )
    part_b = add_all(firsts(part_b), received_b)
    received_b = receive(seconds(part_b), 0)
    text_received = swap_core(text_send_half)
    border = swap_core(lax.dynamic_slice_in_dim(mixed_grad, (1 - core) * (half - edge), edge, 0))
    text_grad_mine, kernel_grad, text_gradient = conv_back(
        core, mixed_grad, border, window, kernel, shrink_grad, keep
    )

    vector_mine = jnp.concatenate(
        [
            kernel_grad.reshape(-1),
            conv_bias_grad,
            gain_grad,
            norm_bias_grad,
            out_bias_grad,
            in_bias_grad,
            gamma_grad,
            beta_grad,
        ]
    )
    token = jnp.concatenate(
        [shift_one_grad, scale_one_grad, gate_one_grad, shift_two_grad, scale_two_grad, gate_two_grad]
    )
    vector_half = vector_mine.shape[0] // 2
    token_half = 3 * D
    vector_columns = vector_half // GROUPS

    def half_of(values, which, size):
        return lax.dynamic_slice_in_dim(values, which * size, size, 0)

    def both_of(which):
        return jnp.concatenate([half_of(token, which, token_half), half_of(vector_mine, which, vector_half)])

    small = both_of(core)
    small_received = swap_core(both_of(1 - core))
    in_group = (jnp.arange(GROUPS) == group).astype(f32)
    text_grad_theirs = swap_core(text_grad_mine)
    text_part = add_low(text_keep_half, text_received).reshape(2, 2, 2, 2 * high_count, text_half, D)
    mel_gradient = lax.dynamic_update_slice_in_dim(mel_gradient, mel_grad_theirs, half - first, 0)
    received_b, (text_part, small, small_received, mel_gradient) = tie_lists(
        received_b, (text_part, small, small_received, mel_gradient)
    )
    small = small + small_received
    small = jnp.concatenate(
        [in_group[:, None] * small[None, :token_half], small[token_half:].reshape(GROUPS, vector_columns)], axis=1
    )
    part_b = add_all(firsts(part_b), received_b)
    far_b = [swap_bit(part[high_count:], 3) for part in part_b]
    text_received = swap_bits(text_part[1], phase_bits(text_orders, 2))
    small_received = swap_bits(small, (2, 0))
    block_output = lax.dynamic_update_slice_in_dim(block_output, output_theirs, half - first, 0)
    text_gradient = lax.dynamic_update_slice_in_dim(text_gradient, text_grad_theirs, half - first, 0)
    far_b, (text_received, small_received, text_gradient, block_output) = tie_lists(
        far_b, (text_received, small_received, text_gradient, block_output)
    )
    text_part = add_low(text_part[0], text_received)
    text_received = swap_bits(text_part[1], phase_bits(text_orders, 1))
    small = small + small_received
    small_received = swap_bits(small, (0, 1))
    panel_pieces = []
    for side, (parts, others) in enumerate(((part_a, far_a), (part_b, far_b))):
        for index, (part, other) in enumerate(zip(parts, others)):
            if high_count == 1:
                arrays = [part[0], other[0]]
            else:
                arrays = [fold_high(part[:high_count].astype(f32) + other.astype(f32))]
            panel_pieces.append((cuts[index], side * narrow, arrays))
    soap_weights, soap_moment, soap_variance = rotated_step(
        panel_pieces, utterances, left_basis, right_basis, soap_master, soap_first, soap_second
    )
    text_received, small_received, soap_weights, soap_moment, soap_variance = tie(
        text_received, small_received, soap_weights, soap_moment, soap_variance
    )
    text_part = add_low(text_part[0], text_received)
    small = small + small_received
    text_part = fold(text_part, text_orders, 0)
    text_received = swap_bit(text_part[high_count:], 3)
    small = small + swap_bits(small, (1, 2))
    small = small + swap_bit(small, 3)
    own_text = text_part[:high_count].astype(f32) + text_received.astype(f32)
    for bit in range(4, bit_count(count)):
        small = small + swap_bit(small, bit)
    own_text = fold_high(own_text)
    own_text = by_core(core, own_text, swap_core(own_text))
    other = swap_core(small)
    vector_sum = by_core(core, small[:, token_half:].reshape(-1), other[:, token_half:].reshape(-1))

    own_text = own_text / utterances
    text_moment, text_variance, text_direction = moments(own_text, text_first, text_second)
    text_weights = apply_step(text_matrices, text_direction, learn_rate)
    modulation_weights, modulation_moment, modulation_variance, group_sums = modulation_step(
        utterances, core, time_rows, small, other, modulation_weight, modulation_first, modulation_second
    )
    vector_gradient = jnp.concatenate([vector_sum, group_sums[0]]) / utterances
    vector_moment, vector_variance, vector_direction = moments(
        vector_gradient, vector_first, vector_second
    )
    vector_weights = apply_step(vectors, vector_direction, vector_rate)
    return (
        block_output,
        mel_gradient,
        text_gradient,
        soap_weights,
        soap_moment,
        soap_variance,
        text_weights,
        text_moment,
        text_variance,
        modulation_weights,
        modulation_moment,
        modulation_variance,
        vector_weights,
        vector_moment,
        vector_variance,
    )


def solution(mesh):
    rows, quarter, same = P("dp", None), P("dp", "mp"), P()
    return jax.shard_map(
        body,
        mesh=mesh,
        in_specs=(
            (rows,) * 3 + (same,) + (P("dp"),) * 3 + (same,) + (quarter,) * 5 + (rows,) * 6 + (same,) * 3
        ),
        out_specs=(rows,) * 3 + (quarter,) * 3 + (rows,) * 6 + (same,) * 3,
        check_vma=False,
    )
```
